32 devices in a mesh: rows: 8 (over z, x), blk: 4 (over y, core).
Axes of the slice: x: 2, y: 2, z: 4, core: 2. Of those that a mesh axis runs over, the one named last changes fastest.
Arguments:
- inputs: bfloat16 [32, 512, 768], P('rows', 'blk'), may hold values from -6 to 6
- segments: int32 [32, 512], P('rows', 'blk'), may hold values from 0 to 7, as said below
- gain_attn: float32 [768], replicated, may hold values from 0.25 to 1.75
- w_query: bfloat16 [768, 768], P('blk'), may hold values from -0.0546875 to 0.0546875
- w_key: bfloat16 [768, 768], P('blk'), may hold values from -0.21875 to 0.21875
- w_value: bfloat16 [768, 768], P('blk'), may hold values from -0.21875 to 0.21875
- w_out: bfloat16 [768, 768], P('blk'), may hold values from -0.875 to 0.875
- bucket_bias_table: float32 [32, 12], replicated, may hold values from -4 to 4
- gain_ff: float32 [768], replicated, may hold values from 0.25 to 1.75
- w_in: bfloat16 [768, 3072], P('blk'), may hold values from -0.21875 to 0.21875
- w_back: bfloat16 [3072, 768], P('blk'), may hold values from -0.109375 to 0.109375
- cotangent: bfloat16 [32, 512, 768], P('rows', 'blk'), may hold values from -6 to 6
Outputs:
- output: bfloat16 [32, 512, 768], P('rows', 'blk')
- grad_inputs: float32 [32, 512, 768], P('rows', 'blk')
- grad_gain_attn: float32 [768], replicated
- grad_w_query: float32 [768, 768], P('blk')
- grad_w_key: float32 [768, 768], P('blk')
- grad_w_value: float32 [768, 768], P('blk')
- grad_w_out: float32 [768, 768], P('blk')
- grad_bias_table: float32 [32, 12], replicated
- grad_gain_ff: float32 [768], replicated
- grad_w_in: float32 [768, 3072], P('blk')
- grad_w_back: float32 [3072, 768], P('blk')
The draws below stay inside these ranges and needn't reach their ends.
Inputs may be any that keep to these rules, and one draw needn't show every extreme that they name: `segments`: along each row the pair numbers start at 0 and never fall, rising by one at each new pair. In each aligned group of 4 rows (the rows one index of rows holds) one row is a single pair; every other row holds exactly 8 pairs.
All inputs are finite; a program needn't handle non-finite values.
Results may differ from the reference program's by a relative error of at most 0.012.
The reference program's roundings to bfloat16 on the way count: a program that leaves them out, or rounds other values in their place, can miss the bound.
Values may be sent and summed in bfloat16 or wider, within the bound.
No kernel may reach another device: no remote copies, remote signals or barrier semaphores. Data moves between devices by JAX's collectives and lax.ppermute only.
A program may use at most 192 MiB of HBM per device.

```python
import jax
import jax.numpy as jnp
from jax import lax

D = 768
H = 12
DH = 64
FF = 3072
BUCKETS = 32
LEN = 512
SEQS = 4
ROWS = 32


def draw_segments(key, part):
    key = jax.random.fold_in(key, 11)
    key_rows, key_whole = jax.random.split(key)
    pair_count = max(LEN // 64, 2)
    row_keys = jax.random.split(key_rows, ROWS)
    places = jnp.arange(LEN, dtype=jnp.int32)

    def row_starts(row_key):
        order = jax.random.permutation(row_key, LEN - 1).astype(jnp.int32) + 1
        chosen = order[:pair_count - 1]
        return jnp.any(places[:, None] == chosen[None, :], axis=1)
    starts = jax.vmap(row_starts)(row_keys)
    whole_pick = jax.random.randint(key_whole, (ROWS // SEQS,), 0, SEQS)
    row_place = jnp.arange(ROWS) % SEQS
    whole_row = row_place == jnp.repeat(whole_pick, SEQS)
    starts = starts & jnp.logical_not(whole_row)[:, None]
    return jnp.cumsum(starts.astype(jnp.int32), axis=1).astype(jnp.int32)


def levels(key, shape, cuts, smallest, top_value):
    factor_of = 1.0
    for dim, shards_of in cuts:
        steps = jax.random.uniform(jax.random.fold_in(jax.random.fold_in(key, 6), dim), (shards_of,), jnp.float32, smallest / len(cuts), top_value / len(cuts))
        factor_of = factor_of * jnp.repeat(jnp.exp(steps), shape[dim] // shards_of).reshape((-1,) + (1,) * (len(shape) - 1 - dim))
    return factor_of


def bell_draw(key, extent, spread, reach, cuts=(), kind=jnp.bfloat16):
    drawn = jax.random.normal(key, extent, jnp.float32) * spread
    if len(cuts) > 0:
        drawn = levels(key, extent, cuts, -0.22, 0.18) * drawn
    return jnp.clip(drawn, min=-reach, max=reach).astype(kind)


def setup_inputs(seed: int = 0) -> dict:
    arg_keys = jax.random.split(jax.random.key(seed), 13)
    return {
        "inputs": bell_draw(arg_keys[0], (ROWS, LEN, D), 1.0, 6.0, ((0, 8), (1, 4))),
        "segments": draw_segments(jax.random.fold_in(arg_keys[12], 71), 0),
        "gain_attn": jnp.clip(1.0 + 0.15 * jax.random.normal(arg_keys[2], (D,), jnp.float32), 0.25, 1.75),
        "w_query": bell_draw(arg_keys[3], (D, D), (16 * D) ** -0.5, 0.0546875, ((0, 4),)),
        "w_key": bell_draw(arg_keys[4], (D, D), D ** -0.5, 0.21875, ((0, 4),)),
        "w_value": bell_draw(arg_keys[5], (D, D), D ** -0.5, 0.21875, ((0, 4),)),
        "w_out": bell_draw(arg_keys[6], (D, D), (D // 16) ** -0.5, 0.875, ((0, 4),)),
        "bucket_bias_table": bell_draw(arg_keys[7], (BUCKETS, H), 1.0, 4.0, (), jnp.float32),
        "gain_ff": jnp.clip(1.0 + 0.15 * jax.random.normal(arg_keys[8], (D,), jnp.float32), 0.25, 1.75),
        "w_in": bell_draw(arg_keys[9], (D, FF), D ** -0.5, 0.21875, ((0, 4),)),
        "w_back": bell_draw(arg_keys[10], (FF, D), FF ** -0.5, 0.109375, ((0, 4),)),
        "cotangent": bell_draw(arg_keys[11], (ROWS, LEN, D), 1.0, 6.0, ((0, 8), (1, 4))),
    }


EPS = 1e-06
EDGES = (1, 2, 3, 4, 5, 6, 7, 8, 12, 16, 23, 32, 46, 64, 91)
HIGH_PRECISION = lax.Precision.HIGHEST

@jax.custom_vjp
def low(v):
    return lax.optimization_barrier(v.astype(jnp.bfloat16)).astype(jnp.float32)

@jax.custom_vjp
def low_back(v):
    return v

def low_keep(v):
    return (low(v), None)

def low_pass(kept, grad):
    return (grad,)

def back_keep(v):
    return (v, None)

def back_low(kept, grad):
    return (low(grad),)
low.defvjp(low_keep, low_pass)
low_back.defvjp(back_keep, back_low)

def rms_scale(values, gain):
    return values * lax.rsqrt(lax.optimization_barrier(jnp.mean(values * values, axis=-1, keepdims=True)) + EPS) * gain

def matmul_f32(matmul_operand, weight_matrix):
    return jnp.einsum('rld,de->rle', matmul_operand, weight_matrix, precision=HIGH_PRECISION)

def bucket_hot(length, bucket_count):
    places = jnp.arange(length, dtype=jnp.int32)
    offset = places[None, :] - places[:, None]
    distance = jnp.abs(offset)
    bucket_id = jnp.where(offset > 0, bucket_count // 2, 0).astype(jnp.int32)
    for edge_at in EDGES:
        bucket_id = bucket_id + (distance >= edge_at).astype(jnp.int32)
    return (bucket_id[None] == jnp.arange(bucket_count, dtype=jnp.int32)[:, None, None]).astype(jnp.float32)

def reference(inputs, segments, gain_attn, w_query, w_key, w_value, w_out, bucket_bias_table, gain_ff, w_in, w_back, cotangent):
    bucket_indicator = bucket_hot(LEN, BUCKETS)

    def forward(inputs_f32, gain_a, weight_q, weight_k, weight_v, weight_o, lookup_table, gain_f, weight_i, weight_b):
        normed = low(rms_scale(inputs_f32, gain_a))
        queries = low(low_back(matmul_f32(normed, weight_q)))
        keys_low = low(low_back(matmul_f32(normed, weight_k)))
        values_low = low(low_back(matmul_f32(normed, weight_v)))
        relative_position_bias = jnp.einsum('uxp,uw->wxp', bucket_indicator, lookup_table, precision=HIGH_PRECISION)

        def attend(row_data):
            query_row, key_row, value_row, segment_row = row_data
            query_heads = query_row.reshape(LEN, H, DH)
            key_heads = key_row.reshape(LEN, H, DH)
            value_heads = value_row.reshape(LEN, H, DH)
            raw_scores = jnp.einsum('qhd,khd->hqk', query_heads, key_heads, precision=HIGH_PRECISION) + relative_position_bias
            raw_scores = low_back(raw_scores)
            allowed = (segment_row[:, None] == segment_row[None, :])[None]
            scores = jnp.where(allowed, raw_scores, -1e+30)
            probs_low = low(jax.nn.softmax(scores, axis=-1))
            return jnp.einsum('hqk,khd->qhd', probs_low, value_heads, precision=HIGH_PRECISION).reshape(LEN, D)
        mixed = lax.map(jax.checkpoint(attend), (queries, keys_low, values_low, segments))
        mixed = low(low_back(mixed))
        hidden = inputs_f32 + low_back(matmul_f32(mixed, weight_o))
        ff_in = low(rms_scale(hidden, gain_f))
        act = low(jax.nn.gelu(low_back(matmul_f32(ff_in, weight_i))))
        return hidden + matmul_f32(act, weight_b)
    params = (inputs.astype(jnp.float32), gain_attn, w_query.astype(jnp.float32), w_key.astype(jnp.float32), w_value.astype(jnp.float32), w_out.astype(jnp.float32), bucket_bias_table, gain_ff, w_in.astype(jnp.float32), w_back.astype(jnp.float32))
    result, pullback = jax.vjp(forward, *params)
    grads = pullback(cotangent.astype(jnp.float32))
    return (result.astype(jnp.bfloat16), grads[0], grads[1], grads[2], grads[3], grads[4], grads[5], grads[6], grads[7], grads[8], grads[9])
```

```python
import functools

import jax
import jax.numpy as jnp
from jax import lax
from jax.experimental import pallas as pl
from jax.experimental.pallas import tpu as pltpu
from jax.sharding import PartitionSpec as P

EPS = 1e-06
EDGES = (1, 2, 3, 4, 5, 6, 7, 8, 12, 16, 23, 32, 46, 64, 91)
BF = jnp.bfloat16
F32 = jnp.float32
ANY = pl.BlockSpec(memory_space=pl.ANY)
VM = pl.BlockSpec(memory_space=pltpu.VMEM)
SM = pl.BlockSpec(memory_space=pltpu.SMEM)
LOW_ROWS = 8
ORDER = ("y", "x", "z")


def params(mib):
    return pltpu.CompilerParams(vmem_limit_bytes=mib * 1024 * 1024)


def cost(flops, nbytes):
    return pl.CostEstimate(flops=int(flops), bytes_accessed=int(nbytes), transcendentals=0)


def nn(a, b):
    return lax.dot_general(a, b, (((1,), (0,)), ((), ())), preferred_element_type=F32)


def nt(a, b):
    return lax.dot_general(a, b, (((1,), (1,)), ((), ())), preferred_element_type=F32)


def tn(a, b):
    return lax.dot_general(a, b, (((0,), (0,)), ((), ())), preferred_element_type=F32)


def swap(value, rows_bits=0, blk_bits=0):
    rows, blk = lax.axis_size("rows"), lax.axis_size("blk")
    pairs = [
        (r * blk + b, (r ^ rows_bits) * blk + (b ^ blk_bits))
        for r in range(rows)
        for b in range(blk)
    ]
    return lax.ppermute(value, ("rows", "blk"), pairs)


def run_copies(pairs, sems):
    copies = [pltpu.make_async_copy(s, d, sems.at[i]) for i, (s, d) in enumerate(pairs)]
    for c in copies:
        c.start()
    return copies


def wait_all(copies):
    for c in copies:
        c.wait()


def pieces_of(refs, me, half):
    own, core, y, x, yc, xc = refs
    out = []
    for h in (0, 1):
        out.append((own.at[h], me, h))
        out.append((core.at[h], me ^ 1, h))
    out.append((y, me ^ 2, half))
    out.append((x, me ^ 2, 1 - half))
    out.append((yc, me ^ 3, half))
    out.append((xc, me ^ 3, 1 - half))
    return out


def slot_copies(stage, keep, send, me, mr, sub, order):
    sizes = {"y": 2, "x": 2, "z": 4}
    pairs = []
    for sc in (1, 0):
        for i in range(sizes[order[0]]):
            for j in range(sizes[order[1]]):
                for k in range(sizes[order[2]]):
                    at = dict(zip(order, (i, j, k)))
                    owner = me ^ (2 * at["y"] + sc)
                    r = mr ^ (2 * at["z"] + at["x"])
                    src = stage.at[owner, pl.ds(pl.multiple_of(r * sub, sub), sub), :]
                    pairs.append((src, (send if sc else keep).at[i, j, k]))
    return pairs


def slot_shapes(sub, order):
    sizes = {"y": 2, "x": 2, "z": 4}
    dims = tuple(sizes[o] for o in order)
    return [jax.ShapeDtypeStruct(dims + (sub, 256), BF)] * 2


def add_low(a, b):
    if b is None:
        return a
    return (a.astype(F32) + b.astype(F32)).astype(BF)


def reduce_piece(keep, send, order):
    rows = lax.axis_size("rows")
    mine, got = keep, swap(send, blk_bits=1)
    for st in order:
        at = lambda i: add_low(mine[i], None if got is None else got[i])
        if st == "z":
            parts = [at(i) for i in range(4)]
            recv = [swap(parts[i], rows_bits=2 * i) for i in (1, 2, 3)]
            total = parts[0].astype(F32)
            for r in recv:
                total = total + r.astype(F32)
            mine, got = total.astype(BF), None
        else:
            kept, gone = at(0), at(1)
            got = swap(gone, rows_bits=1) if st == "x" else swap(gone, blk_bits=2)
            mine = kept
    total = add_low(mine, got)
    bit = LOW_ROWS
    while bit < rows:
        total = add_low(total, swap(total, rows_bits=bit))
        bit *= 2
    blocks = {(0, 0): total}
    if [o for o in order if o != "y"] == ["x", "z"]:
        zs = [total] + [swap(total, rows_bits=2 * i) for i in (1, 2, 3)]
        zs = jnp.stack(zs)
        xs = swap(zs, rows_bits=1)
        return (zs, xs), [(a, i, a, i) for a in (0, 1) for i in range(4)]
    xs = jnp.stack([total, swap(total, rows_bits=1)])
    zs = [xs] + [swap(xs, rows_bits=2 * i) for i in (1, 2, 3)]
    return tuple(zs), [(i, a, a, i) for i in range(4) for a in (0, 1)]


def qkv_kernel(ids, msg, r1, r2, r3, gain, w0, w1, w2, w3, w4, w5, xs, nrm, nrm_t, q, k, v, seg, wbuf, sbuf, sems):
    me, half = ids[0], ids[2]
    rows = xs.shape[0] // 4
    part = w2.shape[1]
    width = xs.shape[1]
    tok = []
    for s, src in enumerate((msg.at[me], r1, r2, r3)):
        o = me ^ s
        tok.append((src.at[pl.ds(0, rows)], xs.at[pl.ds(pl.multiple_of(o * rows, rows), rows)]))
        tok.append((src.at[pl.ds(rows, 16)], sbuf.at[pl.ds(pl.multiple_of(o * 16, 16), 16)]))
    wts = [
        (ref.at[pl.ds(0, 3)], wbuf.at[:, pl.ds(pl.multiple_of(o * 2 * part + h * part, 16), part)])
        for ref, o, h in pieces_of((w0, w1, w2, w3, w4, w5), me, half)
    ]
    n = len(tok)
    c_tok = run_copies(tok, sems.at[pl.ds(0, n)])
    c_wts = run_copies(wts, sems.at[pl.ds(n, len(wts))])
    wait_all(c_tok)
    seg[...] = jnp.concatenate(
        [sbuf[pl.ds(o * 16, 1), pl.ds(0, rows)].astype(F32) for o in range(4)], axis=1
    )
    for a in range(4):
        x = xs[pl.ds(a * rows, rows), :].astype(F32)
        y = x * lax.rsqrt(jnp.mean(x * x, axis=-1, keepdims=True) + EPS) * gain[...]
        y = y.astype(BF)
        nrm[pl.ds(a * rows, rows), :] = y
        nrm_t[:, pl.ds(a * rows, rows)] = y.T
    wait_all(c_wts)
    for i, out in enumerate((q, k, v)):
        for j in range(0, width, 256):
            out[:, pl.ds(j, 256)] = nn(nrm[...], wbuf[i, :, pl.ds(j, 256)]).astype(BF)


def attn_fwd_kernel(far, q, k, v, near, seg, p, o):
    pair = pl.program_id(0)
    t = near.shape[1]
    length = q.shape[0]
    nblk = length // t
    lane = lax.broadcasted_iota(jnp.int32, (t, 128), 1)
    m0 = (lane < 64).astype(F32).astype(BF)
    m1 = (lane >= 64).astype(F32).astype(BF)
    eye = lax.broadcasted_iota(jnp.int32, (t, t), 0) == lax.broadcasted_iota(jnp.int32, (t, t), 1)
    k2, v2 = k[...], v[...]
    seg_row = seg[...]
    for a in range(nblk):
        q2 = q[pl.ds(a * t, t), :]
        s = nt(jnp.concatenate([q2 * m0, q2 * m1], axis=0), k2)
        seg_col = jnp.sum(
            jnp.where(eye, jnp.broadcast_to(seg_row[:, a * t : (a + 1) * t], (t, t)), 0.0),
            axis=1,
            keepdims=True,
        )
        allowed = seg_col == seg_row
        ps = []
        for h in (0, 1):
            strip = []
            for b in range(nblk):
                rel = b - a
                if abs(rel) <= 1:
                    strip.append(near[h, :, (rel + 1) * t : (rel + 2) * t])
                else:
                    strip.append(jnp.full((t, t), far[int(rel > 0), pair * 2 + h], F32))
            sh = s[h * t : (h + 1) * t] + jnp.concatenate(strip, axis=1)
            sh = jnp.where(allowed, sh, -1e30)
            top = jnp.max(sh, axis=-1, keepdims=True)
            e = jnp.exp(sh - top)
            inv = 1.0 / jnp.sum(e, axis=-1, keepdims=True)
            ph = (e * inv).astype(BF)
            p[h, pl.ds(a * t, t), :] = ph
            ps.append(ph)
        mix = nn(jnp.concatenate(ps, axis=0), v2)
        o[pl.ds(a * t, t), :] = jnp.where(lane < 64, mix[:t], mix[t:]).astype(BF)


def hidden_kernel(ids, xs, mixed, gain, w0, w1, w2, w3, w4, w5, hid, ff, ff_t, wbuf, sems):
    me, half = ids[0], ids[2]
    part = w2.shape[1]
    width = xs.shape[1]
    wts = [
        (ref.at[3], wbuf.at[pl.ds(pl.multiple_of(o * 2 * part + h * part, 16), part)])
        for ref, o, h in pieces_of((w0, w1, w2, w3, w4, w5), me, half)
    ]
    wait_all(run_copies(wts, sems))
    for j in range(0, width, 256):
        hid[:, pl.ds(j, 256)] = nn(mixed[...], wbuf[:, pl.ds(j, 256)]) + xs[:, pl.ds(j, 256)].astype(F32)
    rows = 128
    for a in range(xs.shape[0] // rows):
        x = hid[pl.ds(a * rows, rows), :]
        y = x * lax.rsqrt(jnp.mean(x * x, axis=-1, keepdims=True) + EPS) * gain[...]
        y = y.astype(BF)
        ff[pl.ds(a * rows, rows), :] = y
        ff_t[:, pl.ds(a * rows, rows)] = y.T


def gelu_both(x):
    c = 0.7978845608028654
    x2 = x * x
    th = jnp.tanh(x * (c + (c * 0.044715) * x2))
    half_up = 0.5 + 0.5 * th
    slope = half_up + x * (0.5 - 0.5 * th * th) * (c + (3.0 * c * 0.044715) * x2)
    return x * half_up, slope


def ffn_kernel(first, order, *refs):
    if first:
        (ids, ff, ff_t, cown, c1, c2, c3, p0, p1, p2, p3, p4, p5, oacc, gacc, keep, send, *scratch) = refs
        oin = gin = None
    else:
        (ids, ff, ff_t, cown, c1, c2, c3, p0, p1, p2, p3, p4, p5, oin, gin, oacc, gacc, keep, send, *scratch) = refs
    cot, win, wb, act, gpre, stage, sems = scratch
    me, mr, half = ids[0], ids[3], ids[2]
    d = ff.shape[1]
    rows = cot.shape[0] // 4
    sh = d // 4
    hw, hb = sh // 2, 128
    pairs = []
    for s, src in enumerate((cown.at[me], c1, c2, c3)):
        pairs.append((src, cot.at[pl.ds(pl.multiple_of((me ^ s) * rows, rows), rows)]))
    for ref, o, h in pieces_of((p0, p1, p2, p3, p4, p5), me, half):
        for b in range(4):
            pairs.append((
                ref.at[pl.ds(b * hw, hw)],
                win.at[pl.ds(pl.multiple_of(o * sh + h * hw, 16), hw), pl.ds(b * 256, 256)],
            ))
        for j in range(3):
            pairs.append((
                ref.at[pl.ds(4 * hw + j * hb, hb)],
                wb.at[pl.ds(pl.multiple_of(o * 256 + h * hb, 16), hb), pl.ds(j * 256, 256)],
            ))
    wait_all(run_copies(pairs, sems.at[pl.ds(0, len(pairs))]))

    def hidden_tile(b, _):
        at = pl.ds(pl.multiple_of(b * 256, 256), 256)
        value, slope = gelu_both(nn(ff[...], win[:, at]))
        act[:, at] = value.astype(BF)
        gpre[:, at] = (nt(cot[...], wb[at, :]) * slope).astype(BF)
        return 0

    lax.fori_loop(0, 4, hidden_tile, 0)

    def out_tile(j, _):
        at = pl.ds(pl.multiple_of(j * 256, 256), 256)
        o = nn(act[...], wb[:, at])
        g = nt(gpre[...], win[at, :])
        if not first:
            o = o + oin[:, at]
            g = g + gin[:, at]
        oacc[:, at] = o
        gacc[:, at] = g
        return 0

    lax.fori_loop(0, d // 256, out_tile, 0)

    def grad_tile(b, _):
        at = pl.ds(pl.multiple_of(b * 256, 256), 256)
        gw = nn(ff_t[...], gpre[:, at]).astype(BF)
        for o in range(4):
            stage[o, pl.ds(pl.multiple_of(b * sh, 16), sh), :] = gw[o * sh : (o + 1) * sh]
        gb = tn(act[:, at], cot[...]).astype(BF)
        for j in range(3):
            stage[b, pl.ds(4 * sh + j * 256, 256), :] = gb[:, j * 256 : (j + 1) * 256]
        return 0

    lax.fori_loop(0, 4, grad_tile, 0)
    sub = stage.shape[1] // 8
    wait_all(run_copies(slot_copies(stage, keep, send, me, mr, sub, order), sems.at[pl.ds(0, 32)]))


def after_ff_kernel(ids, hid, oacc, gacc, cown, c1, c2, c3, gain, mixed, w0, w1, w2, w3, w4, w5,
                    o0, o1, o2, o3, ghid, gmix, ggain, gwo, cot, wbuf, ga, obuf, sems):
    me, half = ids[0], ids[2]
    part = w2.shape[1]
    d = hid.shape[1]
    rows = cot.shape[0] // 4
    pairs = []
    for s, src in enumerate((cown.at[me], c1, c2, c3)):
        pairs.append((src, cot.at[pl.ds(pl.multiple_of((me ^ s) * rows, rows), rows)]))
    for ref, o, h in pieces_of((w0, w1, w2, w3, w4, w5), me, half):
        pairs.append((ref.at[3], wbuf.at[pl.ds(pl.multiple_of(o * 2 * part + h * part, 16), part)]))
    wait_all(run_copies(pairs, sems))
    total = jnp.zeros((1, d), F32)
    for a in range(4):
        at = pl.ds(a * rows, rows)
        x = hid[at, :]
        gf = gacc[at, :]
        obuf[at, :] = (x + oacc[at, :]).astype(BF)
        n = lax.rsqrt(jnp.mean(x * x, axis=-1, keepdims=True) + EPS)
        g = gf * gain[...]
        xn = x * n
        total = total + jnp.sum(gf * xn, axis=0, keepdims=True)
        gh = cot[at, :].astype(F32) + n * (g - xn * (n * jnp.mean(g * x, axis=-1, keepdims=True)))
        ghid[at, :] = gh
        ga[at, :] = gh.astype(BF)
    ggain[...] = total
    for s, out in enumerate((o0, o1, o2, o3)):
        out[...] = obuf[pl.ds(pl.multiple_of((me ^ s) * rows, rows), rows), :]
    for j in range(0, d, 256):
        gmix[:, pl.ds(j, 256)] = nt(ga[...], wbuf[pl.ds(j, 256), :]).astype(BF)
    sh = d // 4
    for j in range(3):
        gw = tn(mixed[...], ga[:, pl.ds(j * 256, 256)]).astype(BF)
        for o in range(4):
            gwo[o, pl.ds(j * sh, sh), :] = gw[o * sh : (o + 1) * sh]


def attn_bwd_kernel(with_out, order, *refs):
    if with_out:
        (ids, q, k, v, p, gm, nrm_t, gwo, dq, dk, dv, acc, keep, send, stage, sems) = refs
    else:
        (ids, q, k, v, p, gm, nrm_t, dq, dk, dv, acc, keep, send, stage, sems) = refs
    me, mr = ids[0], ids[3]
    t = 128
    length = q.shape[0]
    nblk = length // t
    lane = lax.broadcasted_iota(jnp.int32, (t, 128), 1)
    m0 = (lane < 64).astype(F32).astype(BF)
    m1 = (lane >= 64).astype(F32).astype(BF)
    base = 0
    if with_out:
        base = gwo.shape[1]
        out_copies = run_copies([(gwo, stage.at[:, pl.ds(0, base), :])], sems.at[pl.ds(0, 1)])
    for pair in (0, 1):
        cols = pl.ds(pair * 128, 128)
        k2, v2 = k[:, cols], v[:, cols]
        dk_t = jnp.zeros((128, length), F32)
        dv_t = jnp.zeros((128, length), F32)
        for a in range(nblk):
            at = pl.ds(a * t, t)
            q2, g2 = q[at, cols], gm[at, cols]
            qm = jnp.concatenate([q2 * m0, q2 * m1], axis=0)
            g_both = jnp.concatenate([g2 * m0, g2 * m1], axis=0)
            dp = nt(g_both, v2)
            pb = jnp.concatenate([p[2 * pair, at, :], p[2 * pair + 1, at, :]], axis=0)
            pf = pb.astype(F32)
            delta = jnp.sum(pf * dp, axis=-1, keepdims=True)
            ds = (pf * (dp - delta)).astype(BF)
            mq = nn(ds, k2)
            dq[at, cols] = jnp.where(lane < 64, mq[:t], mq[t:]).astype(BF)
            dk_t = dk_t + tn(qm, ds)
            dv_t = dv_t + tn(g_both, pb)
            dsf = ds.astype(F32)
            for h in (0, 1):
                for b in range(nblk):
                    rel = b - a
                    place = rel + 1 if abs(rel) <= 1 else (3 if rel < 0 else 4)
                    tile = dsf[h * t : (h + 1) * t, b * t : (b + 1) * t]
                    head = 2 * pair + h
                    lanes = pl.ds(place * t, t)
                    fresh = (a, b) in ((1, 0), (0, 0), (0, 1), (2, 0), (0, 2))
                    if fresh:
                        acc[head, :, lanes] = tile
                    else:
                        acc[head, :, lanes] += tile
        dk[:, cols] = dk_t.T.astype(BF)
        dv[:, cols] = dv_t.T.astype(BF)
    sh = nrm_t.shape[0] // 4
    for i, g in enumerate((dq, dk, dv)):
        gw = nn(nrm_t[...], g[...]).astype(BF)
        for o in range(4):
            stage[o, pl.ds(base + i * sh, sh), :] = gw[o * sh : (o + 1) * sh]
    rest = stage.shape[1] - base - 3 * sh
    if rest:
        stage[:, pl.ds(base + 3 * sh, rest), :] = jnp.zeros((4, rest, 256), BF)
    if with_out:
        wait_all(out_copies)
    sub = stage.shape[1] // 8
    wait_all(run_copies(slot_copies(stage, keep, send, me, mr, sub, order), sems.at[pl.ds(1, 32)]))


def first_norm_kernel(ids, xs, ghid, gain, *refs):
    groups = 3
    dqs, dks, dvs = refs[0:groups], refs[groups : 2 * groups], refs[2 * groups : 3 * groups]
    w = refs[9:15]
    g0, g1, g2, g3, ggain, wbuf, gn, gi, sems = refs[15:]
    me, half = ids[0], ids[2]
    part = w[2].shape[1]
    d = xs.shape[1]
    rows = xs.shape[0] // 4
    wts = [
        (ref.at[pl.ds(0, 3)], wbuf.at[:, pl.ds(pl.multiple_of(o * 2 * part + h * part, 16), part)])
        for ref, o, h in pieces_of(w, me, half)
    ]
    wait_all(run_copies(wts, sems))
    for j in range(0, d, 256):
        out = None
        for i, g in enumerate((dqs, dks, dvs)):
            for c in range(groups):
                term = nt(g[c][...], wbuf[i, pl.ds(j, 256), pl.ds(c * 256, 256)])
                out = term if out is None else out + term
        gn[:, pl.ds(j, 256)] = out
    total = jnp.zeros((1, d), F32)
    for a in range(4):
        at = pl.ds(a * rows, rows)
        x = xs[at, :].astype(F32)
        gf = gn[at, :]
        n = lax.rsqrt(jnp.mean(x * x, axis=-1, keepdims=True) + EPS)
        g = gf * gain[...]
        xn = x * n
        total = total + jnp.sum(gf * xn, axis=0, keepdims=True)
        gi[at, :] = (ghid[at, :] + n * (g - xn * (n * jnp.mean(g * x, axis=-1, keepdims=True)))).astype(BF)
    ggain[...] = total
    for s, out in enumerate((g0, g1, g2, g3)):
        out[...] = gi[pl.ds(pl.multiple_of((me ^ s) * rows, rows), rows), :]


def tokens_kernel(ids, a0, a1, a2, a3, b0, b1, b2, b3, out, gin):
    me = ids[0]
    for s, ref in enumerate((a0, a1, a2, a3)):
        out[me ^ s] = ref[...]
    for s, ref in enumerate((b0, b1, b2, b3)):
        gin[me ^ s] = ref[...].astype(F32)


def block_copies(refs, where, buf, mr, sub, sems):
    pairs = []
    for which, lead, sx, sz in where:
        r = mr ^ (2 * sz + sx)
        pairs.append((refs[which].at[lead], buf.at[pl.ds(pl.multiple_of(r * sub, sub), sub)]))
    return run_copies(pairs, sems)


def ff_shares_kernel(counts, wheres, sub, ids, *refs):
    mr = ids[3]
    n = sum(counts)
    ins, (out_in, out_back, buf, sems) = refs[:n], refs[n:]
    sh = out_in.shape[0]
    copies, at = [], 0
    for k, c in enumerate(counts):
        copies.append(
            block_copies(ins[at : at + c], wheres[k], buf.at[k], mr, sub, sems.at[pl.ds(8 * k, 8)])
        )
        at += c
    for k in range(len(counts)):
        wait_all(copies[k])
        for b in range(4):
            out_in[:, pl.ds((b * 3 + k) * 256, 256)] = buf[k, pl.ds(b * sh, sh), :].astype(F32)
        for j in range(3):
            out_back[pl.ds(k * 256, 256), pl.ds(j * 256, 256)] = buf[
                k, pl.ds(4 * sh + j * 256, 256), :
            ].astype(F32)


def attn_shares_kernel(counts, wheres, subs, ids, *refs):
    mr = ids[3]
    n = sum(counts)
    ins, (wq, wk, wv, wo, buf, sems) = refs[:n], refs[n:]
    sh = wq.shape[0]
    copies, at = [], 0
    for k, c in enumerate(counts):
        copies.append(
            block_copies(ins[at : at + c], wheres[k], buf.at[k], mr, subs[k], sems.at[pl.ds(8 * k, 8)])
        )
        at += c
    for k in range(len(counts)):
        wait_all(copies[k])
        base = 0
        if k == 0:
            base = 3 * sh
            for j in range(3):
                wo[:, pl.ds(j * 256, 256)] = buf[k, pl.ds(j * sh, sh), :].astype(F32)
        for i, out in enumerate((wq, wk, wv)):
            out[:, pl.ds(k * 256, 256)] = buf[k, pl.ds(base + i * sh, sh), :].astype(F32)


def bucket_of(offset, bucket_count):
    distance = jnp.abs(offset)
    bucket = jnp.where(offset > 0, bucket_count // 2, 0).astype(jnp.int32)
    for edge in EDGES:
        bucket = bucket + (distance >= edge).astype(jnp.int32)
    return bucket


def gather_weight(pack, half):
    core = swap(pack, blk_bits=1)
    y = swap(lax.dynamic_index_in_dim(pack, half, 0, keepdims=False), blk_bits=2)
    x = swap(y, rows_bits=1)
    return (pack, core, y, x, swap(y, blk_bits=1), swap(x, blk_bits=1))


def shards(inputs, segments, gain_attn, w_query, w_key, w_value, w_out, bucket_bias_table, gain_ff, w_in, w_back, cotangent):
    seqs, rows, d = inputs.shape
    sh = w_query.shape[0]
    ffs = w_in.shape[1]
    bucket_count, heads = bucket_bias_table.shape
    length = rows * lax.axis_size("blk")
    me = lax.axis_index("blk").astype(jnp.int32)
    mr = lax.axis_index("rows").astype(jnp.int32)
    half = mr & 1
    ids = jnp.stack([me, mr, half, mr & (LOW_ROWS - 1)])
    order = ORDER

    extra = jnp.zeros((seqs, 16, d), BF).at[:, 0, :rows].set(segments.astype(BF))
    msg = jnp.concatenate([inputs, extra], axis=1)
    pick = lambda arr, s: lax.dynamic_index_in_dim(arr, me ^ s, 0, keepdims=False)
    msgs = [swap(pick(msg, s), blk_bits=s) for s in (1, 2, 3)]

    pack_a = jnp.stack([w_query, w_key, w_value, w_out]).reshape(4, 2, sh // 2, d).swapaxes(0, 1)
    wa = gather_weight(pack_a, half)
    part_in = w_in.reshape(2, sh // 2, 4, 3, 256).transpose(3, 0, 2, 1, 4).reshape(3, 2, 2 * sh, 256)
    part_back = w_back.reshape(3, 2, 128, 3, 256).transpose(0, 1, 3, 2, 4).reshape(3, 2, 384, 256)
    packs_f = jnp.concatenate([part_in, part_back], axis=2)
    cots = [swap(pick(cotangent, s), blk_bits=s) for s in (1, 2, 3)]
    wf = [gather_weight(packs_f[k], half) for k in range(3)]

    off = jnp.arange(3 * rows, dtype=jnp.int32)[None, :] - rows - jnp.arange(rows, dtype=jnp.int32)[:, None]
    hot = (bucket_of(off, bucket_count)[None] == jnp.arange(bucket_count, dtype=jnp.int32)[:, None, None])
    near = jnp.einsum("uxp,uw->wxp", hot.astype(F32), bucket_bias_table, precision=lax.Precision.HIGHEST)
    far = jnp.stack([bucket_bias_table[bucket_count // 2 - 1], bucket_bias_table[bucket_count - 1]])

    sds = jax.ShapeDtypeStruct
    row_low, row_f32 = sds((length, d), BF), sds((length, d), F32)
    gain1, gain2 = gain_attn.reshape(1, d), gain_ff.reshape(1, d)
    mm = 2.0 * length * d * d

    xs, nrm, nrm_t, q, k, v, seg = pl.pallas_call(
        qkv_kernel,
        out_shape=[row_low, row_low, sds((d, length), BF), row_low, row_low, row_low, sds((1, length), F32)],
        in_specs=[SM] + [ANY] * 4 + [VM] + [ANY] * 6,
        out_specs=[VM] * 7,
        scratch_shapes=[pltpu.VMEM((3, d, d), BF), pltpu.VMEM((64, d), BF), pltpu.SemaphoreType.DMA((16,))],
        compiler_params=params(40),
        cost_estimate=cost(3 * mm, 8e6),
        name="qkv",
    )(ids, msg, *msgs, gain1, *wa)

    pairs = heads // 2
    lanes = lambda: pl.BlockSpec((length, 128), lambda i: (0, i))
    probs, mixed = pl.pallas_call(
        attn_fwd_kernel,
        grid=(pairs,),
        out_shape=[sds((heads, length, length), BF), row_low],
        in_specs=[
            SM,
            lanes(),
            lanes(),
            lanes(),
            pl.BlockSpec((2, rows, 3 * rows), lambda i: (i, 0, 0)),
            pl.BlockSpec((1, length), lambda i: (0, 0)),
        ],
        out_specs=[pl.BlockSpec((2, length, length), lambda i: (i, 0, 0)), lanes()],
        compiler_params=params(40),
        cost_estimate=cost(2 * mm, 12e6),
        name="attn_fwd",
    )(far, q, k, v, near, seg)

    hid, ff, ff_t = pl.pallas_call(
        hidden_kernel,
        out_shape=[row_f32, row_low, sds((d, length), BF)],
        in_specs=[SM, VM, VM, VM] + [ANY] * 6,
        out_specs=[VM] * 3,
        scratch_shapes=[pltpu.VMEM((d, d), BF), pltpu.SemaphoreType.DMA((8,))],
        compiler_params=params(40),
        cost_estimate=cost(mm, 6e6),
        name="hidden",
    )(ids, xs, mixed, gain2, *wa)

    sub_f = (4 * sh + 768) // 8
    accs, shares_f = (), []
    for c in range(3):
        first = c == 0
        oacc, gacc, keep, send = pl.pallas_call(
            functools.partial(ffn_kernel, first, order),
            out_shape=[row_f32, row_f32] + slot_shapes(sub_f, order),
            in_specs=[SM, VM, VM] + [ANY] * 10 + [VM] * (0 if first else 2),
            out_specs=[VM, VM, ANY, ANY],
            scratch_shapes=[
                pltpu.VMEM((length, d), BF),
                pltpu.VMEM((d, 1024), BF),
                pltpu.VMEM((1024, d), BF),
                pltpu.VMEM((length, 1024), BF),
                pltpu.VMEM((length, 1024), BF),
                pltpu.VMEM((4, 8 * sub_f, 256), BF),
                pltpu.SemaphoreType.DMA((64,)),
            ],
            compiler_params=params(48),
            cost_estimate=cost(8 * mm, 10e6),
            name="ffn",
        )(ids, ff, ff_t, cotangent, *cots, *wf[c], *accs)
        accs = (oacc, gacc)
        shares_f.append(reduce_piece(keep, send, order))
    oacc, gacc = accs

    tok_low = sds((rows, d), BF)
    o0, o1, o2, o3, ghid, gmix, ggain_ff, gwo = pl.pallas_call(
        after_ff_kernel,
        out_shape=[tok_low] * 4 + [row_f32, row_low, sds((1, d), F32), sds((4, 3 * sh, 256), BF)],
        in_specs=[SM, VM, VM, VM] + [ANY] * 4 + [VM, VM] + [ANY] * 6,
        out_specs=[VM] * 8,
        scratch_shapes=[
            pltpu.VMEM((length, d), BF),
            pltpu.VMEM((d, d), BF),
            pltpu.VMEM((length, d), BF),
            pltpu.VMEM((length, d), BF),
            pltpu.SemaphoreType.DMA((12,)),
        ],
        compiler_params=params(48),
        cost_estimate=cost(2 * mm, 12e6),
        name="after_ff",
    )(ids, hid, oacc, gacc, cotangent, *cots, gain2, mixed, *wa)
    outs = [o0] + [swap(o, blk_bits=s) for s, o in ((1, o1), (2, o2), (3, o3))]

    dqs, dks, dvs, baccs, shares_a, subs_a = [], [], [], [], [], []
    for g in range(3):
        with_out = g == 0
        body = 3 * sh * (2 if with_out else 1)
        sub = -(-body // 128) * 16
        quad = lambda: pl.BlockSpec((length, 256), lambda i, g=g: (0, g))
        whole = pl.BlockSpec((length, 256), lambda i: (0, 0))
        dq, dk, dv, bacc, keep, send = pl.pallas_call(
            functools.partial(attn_bwd_kernel, with_out, order),
            grid=(1,),
            out_shape=[sds((length, 256), BF)] * 3 + [sds((4, rows, 5 * rows), F32)] + slot_shapes(sub, order),
            in_specs=[
                SM,
                quad(),
                quad(),
                quad(),
                pl.BlockSpec((4, length, length), lambda i, g=g: (g, 0, 0)),
                quad(),
                pl.BlockSpec((d, length), lambda i: (0, 0)),
            ]
            + [ANY] * with_out,
            out_specs=[whole] * 3 + [pl.BlockSpec((4, rows, 5 * rows), lambda i: (0, 0, 0)), ANY, ANY],
            scratch_shapes=[pltpu.VMEM((4, 8 * sub, 256), BF), pltpu.SemaphoreType.DMA((33,))],
            compiler_params=params(48),
            cost_estimate=cost(3 * mm, 10e6),
            name="attn_bwd",
        )(ids, q, k, v, probs, gmix, nrm_t, *((gwo,) if with_out else ()))
        dqs.append(dq)
        dks.append(dk)
        dvs.append(dv)
        baccs.append(bacc)
        subs_a.append(sub)
        shares_a.append(reduce_piece(keep, send, order))

    g0, g1, g2, g3, ggain_attn = pl.pallas_call(
        first_norm_kernel,
        out_shape=[tok_low] * 4 + [sds((1, d), F32)],
        in_specs=[SM, VM, VM, VM] + [VM] * 9 + [ANY] * 6,
        out_specs=[VM] * 5,
        scratch_shapes=[
            pltpu.VMEM((3, d, d), BF),
            pltpu.VMEM((length, d), F32),
            pltpu.VMEM((length, d), BF),
            pltpu.SemaphoreType.DMA((8,)),
        ],
        compiler_params=params(48),
        cost_estimate=cost(3 * mm, 12e6),
        name="first_norm",
    )(ids, xs, ghid, gain1, *dqs, *dks, *dvs, *wa)
    gins = [g0] + [swap(o, blk_bits=s) for s, o in ((1, g1), (2, g2), (3, g3))]

    place = jnp.concatenate(
        [
            bucket_of(off, bucket_count),
            jnp.full((rows, rows), bucket_count // 2 - 1, jnp.int32),
            jnp.full((rows, rows), bucket_count - 1, jnp.int32),
        ],
        axis=1,
    )
    hot5 = (place[None] == jnp.arange(bucket_count, dtype=jnp.int32)[:, None, None]).astype(F32)
    table = jnp.einsum("uxp,wxp->uw", hot5, jnp.concatenate(baccs, axis=0), precision=lax.Precision.HIGHEST)
    small = jnp.concatenate([ggain_attn.reshape(-1), ggain_ff.reshape(-1), table.reshape(-1)])
    bit = 1
    while bit < lax.axis_size("blk"):
        small = small + swap(small, blk_bits=bit)
        bit *= 2
    bit = 1
    while bit < lax.axis_size("rows"):
        small = small + swap(small, rows_bits=bit)
        bit *= 2
    total_gain_attn, total_gain_ff = small[:d], small[d : 2 * d]
    total_table = small[2 * d :].reshape(bucket_count, heads)

    output, grad_inputs = pl.pallas_call(
        tokens_kernel,
        out_shape=[sds((seqs, rows, d), BF), sds((seqs, rows, d), F32)],
        in_specs=[SM] + [VM] * 8,
        out_specs=[VM] * 2,
        compiler_params=params(32),
        cost_estimate=cost(0, 4e6),
        name="tokens",
    )(ids, *outs, *gins)

    share_in, share_back = pl.pallas_call(
        functools.partial(ff_shares_kernel, [len(s[0]) for s in shares_f], [s[1] for s in shares_f], sub_f),
        out_shape=[sds((sh, ffs), F32), sds(w_back.shape, F32)],
        in_specs=[SM] + [ANY] * sum(len(s[0]) for s in shares_f),
        out_specs=[VM] * 2,
        scratch_shapes=[pltpu.VMEM((3, 8 * sub_f, 256), BF), pltpu.SemaphoreType.DMA((24,))],
        compiler_params=params(32),
        cost_estimate=cost(0, 8e6),
        name="ff_shares",
    )(ids, *[a for s in shares_f for a in s[0]])

    share_q, share_k, share_v, share_o = pl.pallas_call(
        functools.partial(attn_shares_kernel, [len(s[0]) for s in shares_a], [s[1] for s in shares_a], subs_a),
        out_shape=[sds((sh, d), F32)] * 4,
        in_specs=[SM] + [ANY] * sum(len(s[0]) for s in shares_a),
        out_specs=[VM] * 4,
        scratch_shapes=[pltpu.VMEM((3, 8 * max(subs_a), 256), BF), pltpu.SemaphoreType.DMA((24,))],
        compiler_params=params(32),
        cost_estimate=cost(0, 5e6),
        name="attn_shares",
    )(ids, *[a for s in shares_a for a in s[0]])

    return (
        output,
        grad_inputs,
        total_gain_attn,
        share_q,
        share_k,
        share_v,
        share_o,
        total_table,
        total_gain_ff,
        share_in,
        share_back,
    )


def solution(mesh):
    tok, row, rep = P("rows", "blk", None), P("blk", None), P()
    return jax.shard_map(
        shards,
        mesh=mesh,
        in_specs=(tok, P("rows", "blk"), rep, row, row, row, row, rep, rep, row, row, tok),
        out_specs=(tok, tok, rep, row, row, row, row, rep, rep, row, row),
        check_vma=False,
    )
```

```python
import functools

import jax
import jax.numpy as jnp
from jax import lax
from jax.experimental import pallas as pl
from jax.experimental.pallas import tpu as pltpu
from jax.sharding import PartitionSpec as P

EPS = 1e-06
EDGES = (1, 2, 3, 4, 5, 6, 7, 8, 12, 16, 23, 32, 46, 64, 91)
BF = jnp.bfloat16
F32 = jnp.float32
HBM = pl.BlockSpec(memory_space=pltpu.HBM)
VM = pl.BlockSpec(memory_space=pltpu.VMEM)
SM = pl.BlockSpec(memory_space=pltpu.SMEM)
DMA = pltpu.SemaphoreType.DMA
sds = jax.ShapeDtypeStruct
AXES = ("far", "near", "side", "core")
FLIPS = {"near": 4, "side": 2, "core": 1}


def scratch(shape, kind=BF):
    return pltpu.VMEM(shape, kind)


def call(kernel, name, outs, ins, out_specs, scratches, args, flops=1000):
    return pl.pallas_call(
        kernel,
        out_shape=outs,
        in_specs=ins,
        out_specs=out_specs,
        scratch_shapes=scratches,
        compiler_params=pltpu.CompilerParams(vmem_limit_bytes=60 * 1024 * 1024),
        cost_estimate=pl.CostEstimate(flops=flops, bytes_accessed=1000, transcendentals=0),
        name=name,
    )(*args)


def nn(a, b):
    return lax.dot_general(a, b, (((1,), (0,)), ((), ())), preferred_element_type=F32)


def nt(a, b):
    return lax.dot_general(a, b, (((1,), (1,)), ((), ())), preferred_element_type=F32)


def tn(a, b):
    return lax.dot_general(a, b, (((0,), (0,)), ((), ())), preferred_element_type=F32)


def swap(value, *axes):
    flip = sum(FLIPS[a] for a in axes)
    count = 1
    for a in AXES:
        count *= lax.axis_size(a)
    return lax.ppermute(value, AXES, [(i, i ^ flip) for i in range(count)])


def swap_far(value, bits):
    count = 8 * lax.axis_size("far")
    return lax.ppermute(value, AXES, [(i, i ^ (8 * bits)) for i in range(count)])


class Line:
    def __init__(self, ids):
        self.ids = ids

    def gate(self, *values):
        self.ids, *values = lax.optimization_barrier((self.ids, *values))
        return tuple(values)


def pick(arr, index, axis=0):
    return lax.dynamic_index_in_dim(arr, index, axis, keepdims=False)


def add_low(a, b):
    return (a.astype(F32) + b.astype(F32)).astype(BF)


class Sum:
    def __init__(self, line, keep, send):
        self.line, self.keep = line, keep
        self.got = swap(send, "core")

    def first(self):
        (got,) = self.line.gate(self.got)
        keep, h = self.keep, self.keep.shape[2] // 2
        gone_a, gone_b = add_low(keep[1, :, :h], got[1, :, :h]), add_low(keep[:, 1, h:], got[:, 1, h:])
        gone_a, gone_b = self.line.gate(gone_a, gone_b)
        self.a = (add_low(keep[0, :, :h], got[0, :, :h]), swap(gone_a, "side"))
        self.b = (add_low(keep[:, 0, h:], got[:, 0, h:]), swap(gone_b, "near"))

    def second(self):
        (a, b) = self.line.gate(self.a[1], self.b[1])
        gone_a, gone_b = add_low(self.a[0][1], a[1]), add_low(self.b[0][1], b[1])
        gone_a, gone_b = self.line.gate(gone_a, gone_b)
        self.a = (add_low(self.a[0][0], a[0]), swap(gone_a, "near"))
        self.b = (add_low(self.b[0][0], b[0]), swap(gone_b, "side"))

    def total(self):
        (a, b) = self.line.gate(self.a[1], self.b[1])
        return jnp.concatenate([add_low(self.a[0], a), add_low(self.b[0], b)], axis=0)


class FarSum:
    def __init__(self, line, total):
        self.line = line
        total = total.reshape(-1, 256)
        self.plain = lax.axis_size("far") != 4
        if self.plain:
            self.mine = lax.psum(total, "far")
            return
        blocks = total.reshape(4, -1, 256)
        here = lax.axis_index("far")
        self.mine = pick(blocks, here)
        self.got = [swap_far(pick(blocks, here ^ i), i) for i in (1, 2, 3)]

    def gather(self):
        if self.plain:
            return
        got = self.line.gate(*self.got)
        total = self.mine.astype(F32)
        for g in got:
            total = total + g.astype(F32)
        self.mine = total.astype(BF)
        self.got = [swap_far(self.mine, i) for i in (1, 2, 3)]

    def result(self):
        if self.plain:
            return self.mine
        got = self.line.gate(*self.got)
        return jnp.stack([self.mine, *got])


class Gather:
    def __init__(self, line, own, half):
        self.line, self.own = line, own
        self.y = swap(half, "side")
        self.core = swap(own, "core")

    def cross(self):
        self.y, self.core = self.line.gate(self.y, self.core)
        self.x = swap(self.y, "near")
        self.yc = swap(self.y, "core")

    def relay(self):
        self.x, self.yc = self.line.gate(self.x, self.yc)
        self.xc = swap(self.x, "core")

    def done(self):
        (self.xc,) = self.line.gate(self.xc)
        return (self.own, self.core, self.y, self.x, self.yc, self.xc)


class Copies:
    def __init__(self, sems):
        self.sems, self.count = sems, 0

    def start(self, pairs):
        out = []
        for src, dst in pairs:
            out.append(pltpu.make_async_copy(src, dst, self.sems.at[self.count]))
            self.count += 1
            out[-1].start()
        return out


def wait(copies):
    for c in copies:
        c.wait()


def pieces_of(refs, me, half):
    own, core, y, x, yc, xc = refs
    out = []
    for h in (0, 1):
        out.append((own.at[h], me, h))
        out.append((core.at[h], me ^ 1, h))
    out.append((y, me ^ 2, half))
    out.append((x, me ^ 2, 1 - half))
    out.append((yc, me ^ 3, half))
    out.append((xc, me ^ 3, 1 - half))
    return out


def pack_copies(refs, me, half, dst, cut):
    return [(cut(ref), dst.at[o, h]) for ref, o, h in pieces_of(refs, me, half)]


def token_copies(slots, me, dst):
    rows = dst.shape[0] // 4
    return [
        (src, dst.at[pl.ds(pl.multiple_of((me ^ s) * rows, rows), rows)]) for s, src in enumerate(slots)
    ]


def put(stage, owner, row, value):
    half, count = stage.shape[2], value.shape[0]
    first = min(count, max(0, half - row))
    if first:
        stage[owner, 0, pl.ds(row, first), :] = value[:first]
    if first < count:
        stage[owner, 1, pl.ds(row + first - half, count - first), :] = value[first:]


def piece_copies(stage, keep, send, ids):
    me, near, core = ids[0], ids[1], ids[2]
    out = []
    for dst, c in ((send, 1 - core), (keep, core)):
        for sy in (0, 1):
            owner = ((me ^ (2 * sy)) & 2) + c
            for sx in (0, 1):
                out.append((stage.at[owner, near ^ sx], dst.at[sy, sx]))
    return out


def piece_shapes(rows):
    return [sds((2, 2, rows // 2, 256), BF)] * 2


def rows_of(blocks):
    return jnp.concatenate(blocks, axis=0)


def prep_a_kernel(ids, seg, inputs, wq, wk, wv, m0, m1, m2, m3, own0, own1, y0, y1, sems):
    me, half = ids[0], ids[1]
    rows = inputs.shape[1]
    part = wq.shape[0] // 2
    pairs = []
    for g in range(3):
        own, y, at = (own0, y0, 0) if g == 0 else (own1, y1, g - 1)
        for i, w in enumerate((wq, wk, wv)):
            cols, place = pl.ds(g * 256, 256), pl.ds((3 * at + i) * part, part)
            pairs.append((w.at[pl.ds(pl.multiple_of(half * part, 16), part), cols], y.at[place]))
            for h in (0, 1):
                pairs.append((w.at[pl.ds(h * part, part), cols], own.at[h, place]))
    for s, m in enumerate((m0, m1, m2, m3)):
        pairs.append((inputs.at[me ^ s], m.at[pl.ds(0, rows)]))
    copies = Copies(sems).start(pairs)
    for s, m in enumerate((m0, m1, m2, m3)):
        line = seg[pl.ds(me ^ s, 1), :].astype(F32)
        m[pl.ds(rows, 16), pl.ds(0, rows)] = jnp.broadcast_to(line, (16, rows)).astype(BF)
        m[pl.ds(rows, 16), pl.ds(rows, m.shape[1] - rows)] = jnp.zeros((16, m.shape[1] - rows), BF)
    wait(copies)


def prep_b_kernel(ids, w_in, w_back, w_out, cot, own0, own1, own2, y0, y1, y2, k1, k2, k3, sems):
    me, half = ids[0], ids[1]
    hw = w_in.shape[0] // 2
    pairs = [(cot.at[me ^ s], k) for s, k in ((1, k1), (2, k2), (3, k3))]
    for c, (own, y) in enumerate(((own0, y0), (own1, y1), (own2, y2))):
        for dst, h in ((y, half), (own.at[0], 0), (own.at[1], 1)):
            for b in range(4):
                pairs.append((
                    w_in.at[pl.ds(pl.multiple_of(h * hw, 16), hw), pl.ds(b * 768 + c * 256, 256)],
                    dst.at[pl.ds(b * hw, hw)],
                ))
            for j in range(3):
                pairs.append((
                    w_back.at[pl.ds(pl.multiple_of(c * 256 + h * 128, 16), 128), pl.ds(j * 256, 256)],
                    dst.at[pl.ds(4 * hw + j * 128, 128)],
                ))
                if c == 0:
                    pairs.append((
                        w_out.at[pl.ds(pl.multiple_of(h * hw, 16), hw), pl.ds(j * 256, 256)],
                        dst.at[pl.ds(4 * hw + 384 + j * hw, hw)],
                    ))
    wait(Copies(sems).start(pairs))


def norm_kernel(ids, m0, m1, m2, m3, gain, xs, nrm, nrm_t, seg, sbuf, sems):
    me = ids[0]
    rows = xs.shape[0] // 4
    slots = (m0, m1, m2, m3)
    tok = token_copies([m.at[pl.ds(0, rows)] for m in slots], me, xs)
    tok += token_copies([m.at[pl.ds(rows, 16)] for m in slots], me, sbuf)
    wait(Copies(sems).start(tok))
    seg[...] = jnp.concatenate(
        [sbuf[pl.ds(o * 16, 1), pl.ds(0, rows)].astype(F32) for o in range(4)], axis=1
    )
    for a in range(4):
        x = xs[pl.ds(a * rows, rows), :].astype(F32)
        y = x * lax.rsqrt(jnp.mean(x * x, axis=-1, keepdims=True) + EPS) * gain[...]
        y = y.astype(BF)
        nrm[pl.ds(a * rows, rows), :] = y
        nrm_t[:, pl.ds(a * rows, rows)] = y.T


def half_masks(t):
    lane = lax.broadcasted_iota(jnp.int32, (t, 128), 1)
    return lane < 64, (lane < 64).astype(F32).astype(BF), (lane >= 64).astype(F32).astype(BF)


def attn_fwd_kernel(group, ids, far, seg, near_in, nrm_in, w0, w1, w2, w3, w4, w5,
                    q_out, k_out, v_out, p_out, o, near, nrm, wbuf, q, k, v, p, sems):
    me, half = ids[0], ids[1]
    dma = Copies(sems)
    count = wbuf.shape[2]
    part = count // 3
    place = pl.ds(max(group - 1, 0) * count, count)
    loads = dma.start(
        [(nrm_in, nrm)]
        + pack_copies((w0, w1, w2, w3, w4, w5), me, half, wbuf, lambda ref: ref.at[place])
    )
    bias = dma.start([(near_in.at[pl.ds(4 * group, 4)], near)])
    t = near.shape[1]
    length = q.shape[0]
    nblk = length // t
    low, m0, m1 = half_masks(t)
    eye = lax.broadcasted_iota(jnp.int32, (t, t), 0) == lax.broadcasted_iota(jnp.int32, (t, t), 1)
    seg_row = seg[...]
    wait(loads)
    stores = []
    for i, (buf, out) in enumerate(((q, q_out), (k, k_out), (v, v_out))):
        w = rows_of([wbuf[ow, h, pl.ds(i * part, part), :] for ow in range(4) for h in (0, 1)])
        buf[...] = nn(nrm[...], w).astype(BF)
        stores += dma.start([(buf, out)])
    wait(bias)
    for pair in (0, 1):
        at = pl.ds(pair * 128, 128)
        for a in range(nblk):
            seg_col = jnp.sum(
                jnp.where(eye, jnp.broadcast_to(seg_row[:, a * t : (a + 1) * t], (t, t)), 0.0),
                axis=1,
                keepdims=True,
            )
            allowed = seg_col == seg_row
            q2 = q[pl.ds(a * t, t), at]
            s = nt(rows_of([q2 * m0, q2 * m1]), k[:, at])
            ps = []
            for h in (0, 1):
                head = 2 * pair + h
                strip = []
                for b in range(nblk):
                    rel = b - a
                    if abs(rel) <= 1:
                        strip.append(near[head, :, (rel + 1) * t : (rel + 2) * t])
                    else:
                        strip.append(jnp.full((t, t), far[int(rel > 0), group * 4 + head], F32))
                sh = s[h * t : (h + 1) * t] + jnp.concatenate(strip, axis=1)
                sh = jnp.where(allowed, sh, -1e30)
                top = jnp.max(sh, axis=-1, keepdims=True)
                e = jnp.exp(sh - top)
                inv = 1.0 / jnp.sum(e, axis=-1, keepdims=True)
                ph = (e * inv).astype(BF)
                p[head, pl.ds(a * t, t), :] = ph
                ps.append(ph)
            mix = nn(rows_of(ps), v[:, at])
            o[pl.ds(a * t, t), at] = jnp.where(low, mix[:t], mix[t:]).astype(BF)
        stores += dma.start([(p.at[pl.ds(2 * pair, 2)], p_out.at[pl.ds(2 * pair, 2)])])
    wait(stores)


def out_weight(wbuf, j):
    hw = wbuf.shape[2] // 3
    return rows_of([wbuf[o, h, pl.ds(j * hw, hw), :] for o in range(4) for h in (0, 1)])


def out_cut(sh):
    return lambda ref: ref.at[pl.ds(2 * sh + 384, 3 * (sh // 2))]


def hidden_kernel(ids, xs, x0, x1, x2, gain, w0, w1, w2, w3, w4, w5, hid, ff, ff_t, wbuf, sems):
    me, half = ids[0], ids[1]
    width = xs.shape[1]
    wait(Copies(sems).start(pack_copies((w0, w1, w2, w3, w4, w5), me, half, wbuf, out_cut(width // 4))))
    for j in range(3):
        cols = pl.ds(j * 256, 256)
        w = out_weight(wbuf, j)
        acc = xs[:, cols].astype(F32)
        for i, mx in enumerate((x0, x1, x2)):
            acc = acc + nn(mx[...], w[i * 256 : (i + 1) * 256])
        hid[:, cols] = acc
    rows = 128
    for a in range(xs.shape[0] // rows):
        x = hid[pl.ds(a * rows, rows), :]
        y = x * lax.rsqrt(jnp.mean(x * x, axis=-1, keepdims=True) + EPS) * gain[...]
        y = y.astype(BF)
        ff[pl.ds(a * rows, rows), :] = y
        ff_t[:, pl.ds(a * rows, rows)] = y.T


def gelu_both(x):
    c = 0.7978845608028654
    x2 = x * x
    th = jnp.tanh(x * (c + (c * 0.044715) * x2))
    half_up = 0.5 + 0.5 * th
    slope = half_up + x * (0.5 - 0.5 * th * th) * (c + (3.0 * c * 0.044715) * x2)
    return x * half_up, slope


def ffn_kernel(ids, ff, ff_t, cown, c1, c2, c3, p0, p1, p2, p3, p4, p5, act_out, gpre_out, keep, send,
               ffv, fftv, cot, pack, act, gpre, stage, sems):
    me, half = ids[0], ids[1]
    d = ff.shape[1]
    sh = d // 4
    hw = sh // 2
    dma = Copies(sems)
    first = dma.start(
        [(ff, ffv)]
        + pack_copies((p0, p1, p2, p3, p4, p5), me, half, pack, lambda ref: ref.at[pl.ds(0, 4 * hw + 384)])
    )
    second = dma.start(token_copies((cown.at[me], c1, c2, c3), me, cot))
    third = dma.start([(ff_t, fftv)])
    wait(first)
    stores = []
    for b in range(5):
        if b < 4:
            at = pl.ds(b * 256, 256)
            win = rows_of([pack[o, h, pl.ds(b * hw, hw), :] for o in range(4) for h in (0, 1)])
            value, slope = gelu_both(nn(ffv[...], win))
            if b == 0:
                wait(second)
            act[:, at] = value.astype(BF)
            back = 0.0
            for j in range(3):
                wb = rows_of([pack[b, h, pl.ds(4 * hw + j * 128, 128), :] for h in (0, 1)])
                back = back + nt(cot[:, pl.ds(j * 256, 256)], wb)
            gpre[:, at] = (back * slope).astype(BF)
        if b == 3:
            stores += dma.start([(act, act_out), (gpre, gpre_out)])
        if b > 0:
            c = b - 1
            at = pl.ds(c * 256, 256)
            if c == 0:
                wait(third)
            gw = nn(fftv[...], gpre[:, at]).astype(BF)
            for o in range(4):
                put(stage, o, c * sh, gw[o * sh : (o + 1) * sh])
            gb = tn(act[:, at], cot[...]).astype(BF)
            for j in range(3):
                put(stage, c, 4 * sh + j * 256, gb[:, j * 256 : (j + 1) * 256])
    stores += dma.start(piece_copies(stage, keep, send, ids))
    wait(stores)


def after_ff_kernel(ids, gain, hid, g0, g1, g2, cown, c1, c2, c3, x0, x1, x2, *refs):
    packs = (refs[0:6], refs[6:12], refs[12:18])
    ghid, gmix, ggain, gwo, hidv, gv, cot, mx, wbuf, wins, ga, gf, sems = refs[18:]
    me, half = ids[0], ids[1]
    d = hid.shape[1]
    sh = d // 4
    hw = sh // 2
    rows = cot.shape[0] // 4
    dma = Copies(sems)
    loads = [
        dma.start(
            [(g, gv.at[c])]
            + pack_copies(packs[c], me, half, wins.at[c], lambda ref: ref.at[pl.ds(0, 4 * hw)])
        )
        for c, g in enumerate((g0, g1, g2))
    ]
    rest = dma.start([(hid, hidv)] + token_copies((cown.at[me], c1, c2, c3), me, cot))
    last = dma.start(
        pack_copies(packs[0], me, half, wbuf, out_cut(sh))
        + [(x, mx.at[:, pl.ds(i * 256, 256)]) for i, x in enumerate((x0, x1, x2))]
    )
    for c in range(3):
        wait(loads[c])
        acc = None
        for b in range(4):
            w = rows_of([wins[c, o, h, pl.ds(b * hw, hw), :] for o in range(4) for h in (0, 1)])
            term = nt(gv[c, :, pl.ds(b * 256, 256)], w)
            acc = term if acc is None else acc + term
        gf[...] = acc if c == 0 else gf[...] + acc
    wait(rest)
    total = jnp.zeros((1, d), F32)
    for a in range(4):
        at = pl.ds(a * rows, rows)
        x = hidv[at, :]
        gfa = gf[at, :]
        n = lax.rsqrt(jnp.mean(x * x, axis=-1, keepdims=True) + EPS)
        g = gfa * gain[...]
        xn = x * n
        total = total + jnp.sum(gfa * xn, axis=0, keepdims=True)
        gh = cot[at, :].astype(F32) + n * (g - xn * (n * jnp.mean(g * x, axis=-1, keepdims=True)))
        ghid[at, :] = gh
        ga[at, :] = gh.astype(BF)
    ggain[...] = total
    wait(last)
    acc = None
    for j in range(3):
        term = nt(ga[:, pl.ds(j * 256, 256)], out_weight(wbuf, j))
        acc = term if acc is None else acc + term
    gmix[...] = acc.astype(BF)
    for j in range(3):
        gw = tn(mx[...], ga[:, pl.ds(j * 256, 256)]).astype(BF)
        for o in range(4):
            gwo[o, pl.ds(j * sh, sh), :] = gw[o * sh : (o + 1) * sh]


def out_kernel(ids, hid, a0, a1, a2, *refs):
    packs = (refs[0:6], refs[6:12], refs[12:18])
    o0, o1, o2, o3, hidv, av, wb, obuf, sems = refs[18:]
    me, half = ids[0], ids[1]
    d = hid.shape[1]
    hw = d // 8
    rows = hid.shape[0] // 4
    dma = Copies(sems)
    loads = [
        dma.start(
            [(a, av.at[c])]
            + pack_copies(packs[c], me, half, wb.at[c], lambda ref: ref.at[pl.ds(4 * hw, 384)])
        )
        for c, a in enumerate((a0, a1, a2))
    ]
    last = dma.start([(hid, hidv)])
    for c in range(3):
        wait(loads[c])
    wait(last)
    for j in range(3):
        cols = pl.ds(j * 256, 256)
        acc = hidv[:, cols]
        for c in range(3):
            w = rows_of([wb[c, o, h, pl.ds(j * 128, 128), :] for o in range(4) for h in (0, 1)])
            acc = acc + nn(av[c], w)
        obuf[:, cols] = acc.astype(BF)
    for s, out in enumerate((o0, o1, o2, o3)):
        out[...] = obuf[pl.ds(pl.multiple_of((me ^ s) * rows, rows), rows), :]


def diagonals(x):
    width = x.shape[1]
    y = x[0:8]
    for a in range(8, x.shape[0], 8):
        y = y + pltpu.roll(x[a : a + 8], width - a, 1)
    sub = lax.broadcasted_iota(jnp.int32, y.shape, 0)
    for bit in (1, 2, 4):
        y = jnp.where((sub & bit) != 0, pltpu.roll(y, width - bit, 1), y)
    return jnp.sum(y, axis=0, keepdims=True)


def attn_bwd_kernel(with_out, *refs):
    if with_out:
        (ids, q_in, k_in, v_in, p_in, gm_in, nrm_in, gwo, dq_out, dk_out, dv_out, diag, keep, send,
         q, k, v, p, gm, nrm_t, dq, dk, dv, acc, stage, sems) = refs
    else:
        (ids, q_in, k_in, v_in, p_in, gm_in, nrm_in, dq_out, dk_out, dv_out, diag, keep, send,
         q, k, v, p, gm, nrm_t, dq, dk, dv, acc, stage, sems) = refs
    t = 128
    length = q.shape[0]
    nblk = length // t
    low, m0, m1 = half_masks(t)
    dma = Copies(sems)
    first = dma.start([(v_in, v), (gm_in, gm), (p_in.at[pl.ds(0, 2)], p.at[pl.ds(0, 2)]), (k_in, k), (q_in, q)])
    second = dma.start([(p_in.at[pl.ds(2, 2)], p.at[pl.ds(2, 2)])])
    third = dma.start([(nrm_in, nrm_t)])
    base = 0
    if with_out:
        base = gwo.shape[1]
        third += dma.start([(gwo, stage.at[:, 0])])
    wait(first)
    for pair in (0, 1):
        if pair == 1:
            wait(second)
        cols = pl.ds(pair * 128, 128)
        k2, v2 = k[:, cols], v[:, cols]
        dk_t = jnp.zeros((128, length), F32)
        dv_t = jnp.zeros((128, length), F32)
        for a in range(nblk):
            at = pl.ds(a * t, t)
            q2, g2 = q[at, cols], gm[at, cols]
            qm = rows_of([q2 * m0, q2 * m1])
            g_both = rows_of([g2 * m0, g2 * m1])
            dp = nt(g_both, v2)
            pb = rows_of([p[2 * pair, at, :], p[2 * pair + 1, at, :]])
            pf = pb.astype(F32)
            delta = jnp.sum(pf * dp, axis=-1, keepdims=True)
            ds = (pf * (dp - delta)).astype(BF)
            mq = nn(ds, k2)
            dq[at, cols] = jnp.where(low, mq[:t], mq[t:]).astype(BF)
            dk_t = dk_t + tn(qm, ds)
            dv_t = dv_t + tn(g_both, pb)
            dsf = ds.astype(F32)
            for h in (0, 1):
                for b in range(nblk):
                    rel = b - a
                    place = rel + 1 if abs(rel) <= 1 else (3 if rel < 0 else 4)
                    tile = dsf[h * t : (h + 1) * t, b * t : (b + 1) * t]
                    lanes = pl.ds(place * t, t)
                    if (a, b) in ((1, 0), (0, 0), (0, 1), (2, 0), (0, 2)):
                        acc[h, :, lanes] = tile
                    else:
                        acc[h, :, lanes] += tile
        dk[:, cols] = dk_t.T.astype(BF)
        dv[:, cols] = dv_t.T.astype(BF)
        for h in (0, 1):
            near = jnp.concatenate([acc[h, :, pl.ds(0, 3 * t)], jnp.zeros((t, t), F32)], axis=1)
            far = jnp.sum(acc[h, :, pl.ds(3 * t, 2 * t)], axis=0, keepdims=True)
            diag[pl.ds(2 * pair + h, 1), :] = jnp.concatenate([diagonals(near), far], axis=1)
    stores = dma.start([(dq, dq_out), (dk, dk_out), (dv, dv_out)])
    wait(third)
    sh = nrm_t.shape[0] // 4
    for i, g in enumerate((dq, dk, dv)):
        gw = nn(nrm_t[...], g[...]).astype(BF)
        for o in range(4):
            put(stage, o, base + i * sh, gw[o * sh : (o + 1) * sh])
    stores += dma.start(piece_copies(stage, keep, send, ids))
    wait(stores)


def first_norm_kernel(ids, gain, xs, ghid, *refs):
    ins = refs[0:9]
    w0, w1 = refs[9:15], refs[15:21]
    g0, g1, g2, g3, ggain, xv, gv, dall, wbuf0, wbuf1, gn, gi, sems = refs[21:]
    me, half = ids[0], ids[1]
    d = xs.shape[1]
    rows = xs.shape[0] // 4
    dma = Copies(sems)
    loads = dma.start(
        [(g, dall.at[n]) for n, g in enumerate(ins)]
        + pack_copies(w0, me, half, wbuf0, lambda ref: ref)
        + pack_copies(w1, me, half, wbuf1, lambda ref: ref)
    )
    part = wbuf0.shape[2] // 3
    rest = dma.start([(xs, xv), (ghid, gv)])
    wait(loads)
    acc = None
    for i in range(3):
        for c in range(3):
            buf, at = (wbuf0, i) if c == 0 else (wbuf1, 3 * (c - 1) + i)
            wi = rows_of([buf[o, h, pl.ds(at * part, part), :] for o in range(4) for h in (0, 1)])
            term = nt(dall[3 * i + c], wi)
            acc = term if acc is None else acc + term
    gn[...] = acc
    wait(rest)
    total = jnp.zeros((1, d), F32)
    for a in range(4):
        at = pl.ds(a * rows, rows)
        x = xv[at, :].astype(F32)
        gf = gn[at, :]
        n = lax.rsqrt(jnp.mean(x * x, axis=-1, keepdims=True) + EPS)
        g = gf * gain[...]
        xn = x * n
        total = total + jnp.sum(gf * xn, axis=0, keepdims=True)
        gi[at, :] = (gv[at, :] + n * (g - xn * (n * jnp.mean(g * x, axis=-1, keepdims=True)))).astype(BF)
    ggain[...] = total
    for s, out in enumerate((g0, g1, g2, g3)):
        out[...] = gi[pl.ds(pl.multiple_of((me ^ s) * rows, rows), rows), :]


def tokens_kernel(ids, a0, a1, a2, a3, b0, b1, b2, b3, out, gin):
    me = ids[0]
    for s, ref in enumerate((a0, a1, a2, a3)):
        out[me ^ s] = ref[...]
    for s, ref in enumerate((b0, b1, b2, b3)):
        gin[me ^ s] = ref[...].astype(F32)


def half_copies(ref, dst, far):
    if ref.shape == dst.shape:
        return [(ref, dst)]
    n = ref.shape[1]
    return [(ref.at[i], dst.at[pl.ds(pl.multiple_of((far ^ i) * n, 16), n)]) for i in range(ref.shape[0])]


def ff_shares_kernel(ids, z0, x0, z1, x1, z2, x2, out_in, out_back, buf, sems):
    here, far = ids[1], ids[3]
    sh = out_in.shape[0]
    dma = Copies(sems)
    copies = [
        dma.start(half_copies(z, buf.at[k, here], far) + half_copies(x, buf.at[k, 1 - here], far))
        for k, (z, x) in enumerate(((z0, x0), (z1, x1), (z2, x2)))
    ]
    for k in range(3):
        wait(copies[k])
        for b in range(4):
            out_in[:, pl.ds((b * 3 + k) * 256, 256)] = buf[k, 0, pl.ds(b * sh, sh), :].astype(F32)
        for j in range(3):
            out_back[pl.ds(k * 256, 256), pl.ds(j * 256, 256)] = buf[k, 1, pl.ds(j * 256, 256), :].astype(F32)


def attn_shares_kernel(ids, z0, x0, z1, x1, wq, wk, wv, wo, buf0, buf1, sems):
    here, far = ids[1], ids[3]
    sh = wq.shape[0]
    n = buf1.shape[1] // 2
    pairs = []
    for z, x, buf in ((z0, x0, buf0), (z1, x1, buf1)):
        pairs += half_copies(z, buf.at[here], far) + half_copies(x, buf.at[1 - here], far)
    wait(Copies(sems).start(pairs))
    for j in range(3):
        wo[:, pl.ds(j * 256, 256)] = buf0[0, pl.ds(j * sh, sh), :].astype(F32)
    for i, out in enumerate((wq, wk, wv)):
        out[:, pl.ds(0, 256)] = buf0[1, pl.ds(i * sh, sh), :].astype(F32)
        for g in (0, 1):
            whole = rows_of([buf1[0, pl.ds(g * n, n), :], buf1[1, pl.ds(g * n, n), :]])
            out[:, pl.ds((g + 1) * 256, 256)] = whole[i * sh : (i + 1) * sh].astype(F32)


def bucket_of(offset, bucket_count):
    distance = jnp.abs(offset)
    bucket = jnp.where(offset > 0, bucket_count // 2, 0).astype(jnp.int32)
    for edge in EDGES:
        bucket = bucket + (distance >= edge).astype(jnp.int32)
    return bucket


def shards(inputs, segments, gain_attn, w_query, w_key, w_value, w_out, bucket_bias_table, gain_ff, w_in, w_back, cotangent):
    seqs, rows, d = inputs.shape
    sh = w_query.shape[0]
    hw = sh // 2
    ffs = w_in.shape[1]
    bucket_count, heads = bucket_bias_table.shape
    length = rows * seqs
    places = [lax.axis_index(a).astype(jnp.int32) for a in ("near", "side", "core", "far")]
    near_at, side_at, core_at, far_at = places
    line = Line(jnp.stack([2 * side_at + core_at, near_at, core_at, far_at]))
    gate = line.gate
    row_low, row_f32 = sds((length, d), BF), sds((length, d), F32)
    quad_low, tok_low = sds((length, 256), BF), sds((rows, d), BF)
    gain1, gain2 = gain_attn.reshape(1, d), gain_ff.reshape(1, d)
    pack_rows = [4 * hw + 384 + 3 * hw, 4 * hw + 384, 4 * hw + 384]

    m0, m1, m2, m3, own_a, own_b, y_a, y_b = call(
        prep_a_kernel,
        "prep_a",
        [sds((rows + 16, d), BF)] * 4
        + [sds((2, 3 * hw, 256), BF), sds((2, 6 * hw, 256), BF), sds((3 * hw, 256), BF), sds((6 * hw, 256), BF)],
        [SM, VM] + [HBM] * 4,
        [VM] * 8,
        [DMA((31,))],
        (line.ids, segments, inputs, w_query, w_key, w_value),
    )
    wa = Gather(line, own_a, y_a)
    msgs = [swap(m1, "core"), swap(m2, "side"), swap(m3, "side", "core")]
    wb = Gather(line, own_b, y_b)

    own0, own1, own2, y0, y1, y2, k1, k2, k3 = call(
        prep_b_kernel,
        "prep_b",
        [sds((2, r, 256), BF) for r in pack_rows] + [sds((r, 256), BF) for r in pack_rows] + [tok_low] * 3,
        [SM] + [HBM] * 4,
        [VM] * 9,
        [DMA((75,))],
        (line.ids, w_in, w_back, w_out, cotangent),
    )

    off = jnp.arange(3 * rows, dtype=jnp.int32)[None, :] - rows - jnp.arange(rows, dtype=jnp.int32)[:, None]
    hot = (bucket_of(off, bucket_count)[None] == jnp.arange(bucket_count, dtype=jnp.int32)[:, None, None])
    near = jnp.einsum("uxp,uw->wxp", hot.astype(F32), bucket_bias_table, precision=lax.Precision.HIGHEST)
    far = jnp.stack([bucket_bias_table[bucket_count // 2 - 1], bucket_bias_table[bucket_count - 1]])

    own0, near = gate(own0, near)
    wa.cross()
    msgs = gate(*msgs)
    wb.cross()
    y0, own0 = gate(y0, own0)
    wf = [Gather(line, own0, y0)]
    wa.relay()
    xs, nrm, nrm_t, seg = call(
        norm_kernel,
        "norm",
        [row_low, row_low, sds((d, length), BF), sds((1, length), F32)],
        [SM] + [HBM] * 4 + [VM],
        [VM] * 4,
        [scratch((64, d)), DMA((8,))],
        (line.ids, m0, *msgs, gain1),
    )
    (nrm,) = gate(nrm)
    wa = wa.done()
    wb.relay()

    qs, ks, vs, probs, mixed = [], [], [], [], []
    for g in range(3):
        q, k, v, p, mx = call(
            functools.partial(attn_fwd_kernel, g),
            "attn_fwd",
            [quad_low] * 3 + [sds((4, length, length), BF), quad_low],
            [SM, SM, VM] + [HBM] * 8,
            [HBM] * 4 + [VM],
            [
                scratch((4, rows, 3 * rows), F32),
                scratch((length, d)),
                scratch((4, 2, 3 * hw, 256)),
                scratch((length, 256)),
                scratch((length, 256)),
                scratch((length, 256)),
                scratch((4, length, length)),
                DMA((15,)),
            ],
            (line.ids, far, seg, near, nrm, *(wa if g == 0 else wb)),
        )
        (mx,) = gate(mx)
        for have, new in ((qs, q), (ks, k), (vs, v), (probs, p), (mixed, mx)):
            have.append(new)
        if g == 0:
            wb = wb.done()
            wf[0].cross()
            own1, y1 = gate(own1, y1)
            wf.append(Gather(line, own1, y1))
        if g == 1:
            wf[0].relay()
            wf[1].cross()
            own2, y2 = gate(own2, y2)
            wf.append(Gather(line, own2, y2))
    packs = [wf[0].done()]
    wf[1].relay()
    wf[2].cross()
    k1, k2, k3 = gate(k1, k2, k3)
    cots = [swap(k1, "core"), swap(k2, "side"), swap(k3, "side", "core")]

    hid, ff, ff_t = call(
        hidden_kernel,
        "hidden",
        [row_f32, row_low, sds((d, length), BF)],
        [SM] + [VM] * 5 + [HBM] * 6,
        [VM] * 3,
        [scratch((4, 2, 3 * hw, 256)), DMA((8,))],
        (line.ids, xs, *mixed, gain2, *packs[0]),
    )
    (ff,) = gate(ff)
    packs.append(wf[1].done())
    wf[2].relay()
    cots = gate(*cots)

    sums_f, acts, gpres = [], [], []
    for c in range(3):
        act, gpre, keep, send = call(
            ffn_kernel,
            "ffn",
            [sds((length, 1024), BF)] * 2 + piece_shapes(4 * sh + 768),
            [SM] + [HBM] * 12,
            [HBM] * 4,
            [
                scratch((length, d)),
                scratch((d, length)),
                scratch((length, d)),
                scratch((4, 2, 4 * hw + 384, 256)),
                scratch((length, 1024)),
                scratch((length, 1024)),
                scratch((4, 2, 2 * sh + 384, 256)),
                DMA((24,)),
            ],
            (line.ids, ff, ff_t, cotangent, *cots, *packs[c]),
        )
        acts.append(act)
        (gpre,) = gate(gpre)
        gpres.append(gpre)
        sums_f.append(Sum(line, keep, send))
        if c == 0:
            packs.append(wf[2].done())
        if c == 1:
            sums_f[0].first()
        if c == 2:
            sums_f[0].second()
            sums_f[1].first()

    ghid, gmix, ggain_ff, gwo = call(
        after_ff_kernel,
        "after_ff",
        [row_f32, row_low, sds((1, d), F32), sds((4, 3 * sh, 256), BF)],
        [SM, VM] + [HBM] * 29,
        [VM] * 4,
        [
            scratch((length, d), F32),
            scratch((3, length, 1024)),
            scratch((length, d)),
            scratch((length, d)),
            scratch((4, 2, 3 * hw, 256)),
            scratch((3, 4, 2, 4 * hw, 256)),
            scratch((length, d)),
            scratch((length, d), F32),
            DMA((43,)),
        ],
        (line.ids, gain2, hid, *gpres, cotangent, *cots, *mixed, *packs[0], *packs[1], *packs[2]),
    )
    (gmix,) = gate(gmix)
    z0 = lax.psum(sums_f[0].total(), "far")
    sums_f[1].second()
    sums_f[2].first()

    dqs, dks, dvs, diags, sums_a = [], [], [], [], []
    for g in range(3):
        with_out = g == 0
        body = 3 * sh * (2 if with_out else 1)
        dq, dk, dv, diag, keep, send = call(
            functools.partial(attn_bwd_kernel, with_out),
            "attn_bwd",
            [quad_low] * 3 + [sds((4, 6 * rows), F32)] + piece_shapes(body),
            [SM] + [HBM] * (6 + with_out),
            [HBM] * 3 + [VM] + [HBM] * 2,
            [scratch((length, 256))] * 3
            + [scratch((4, length, length)), scratch((length, 256)), scratch((d, length))]
            + [scratch((length, 256))] * 3
            + [scratch((2, rows, 5 * rows), F32), scratch((4, 2, body // 2, 256)), DMA((20,))],
            (line.ids, qs[g], ks[g], vs[g], probs[g], gmix[:, g * 256 : (g + 1) * 256], nrm_t)
            + ((gwo,) if with_out else ()),
        )
        (dq,) = gate(dq)
        for have, new in ((dqs, dq), (dks, dk), (dvs, dv), (diags, diag)):
            have.append(new)
        sums_a.append(Sum(line, keep, send))
        if g == 0:
            z1 = FarSum(line, sums_f[1].total())
            sums_f[2].second()
        if g == 1:
            z1.gather()
            (t2,) = gate(sums_f[2].total())
            sums_a[0].first()
        if g == 2:
            z1 = z1.result()
            x1 = swap(z1, "near")
            z0, t2 = gate(z0, t2)
            x0 = swap(z0, "near")
            z2 = lax.psum(t2, "far")
            sums_a[0].second()
            sums_a[1].first()

    g0, g1, g2, g3, ggain_attn = call(
        first_norm_kernel,
        "first_norm",
        [tok_low] * 4 + [sds((1, d), F32)],
        [SM, VM] + [HBM] * 23,
        [VM] * 5,
        [
            scratch((length, d)),
            scratch((length, d), F32),
            scratch((9, length, 256)),
            scratch((4, 2, 3 * hw, 256)),
            scratch((4, 2, 6 * hw, 256)),
            scratch((length, d), F32),
            scratch((length, d)),
            DMA((27,)),
        ],
        (line.ids, gain1, xs, ghid, *dqs, *dks, *dvs, *wa, *wb),
    )
    (g0,) = gate(g0)
    x0, x1 = gate(x0, x1)
    z3 = FarSum(line, sums_a[0].total())
    sums_a[1].second()
    sums_a[2].first()
    gins = [g0, swap(g1, "core"), swap(g2, "side"), swap(g3, "side", "core")]

    offs = jnp.arange(4 * rows, dtype=jnp.int32)
    offs = jnp.where(offs < 3 * rows, offs - rows, offs - 5 * rows)
    place = jnp.concatenate([
        bucket_of(offs, bucket_count),
        jnp.full((rows,), bucket_count // 2 - 1, jnp.int32),
        jnp.full((rows,), bucket_count - 1, jnp.int32),
    ])
    hot6 = (place[None] == jnp.arange(bucket_count, dtype=jnp.int32)[:, None]).astype(F32)
    table = jnp.einsum("up,wp->uw", hot6, jnp.concatenate(diags, axis=0), precision=lax.Precision.HIGHEST)
    small = jnp.concatenate([ggain_attn.reshape(-1), ggain_ff.reshape(-1), table.reshape(-1)])
    for axis in ("core", "side", "near"):
        small = small + swap(small, axis)
    if lax.axis_size("far") == 4:
        for bits in (1, 2):
            small = small + swap_far(small, bits)
    else:
        small = lax.psum(small, "far")
    total_gain_attn, total_gain_ff = small[:d], small[d : 2 * d]
    total_table = small[2 * d :].reshape(bucket_count, heads)

    o0, o1, o2, o3 = call(
        out_kernel,
        "out",
        [tok_low] * 4,
        [SM] + [HBM] * 22,
        [VM] * 4,
        [
            scratch((length, d), F32),
            scratch((3, length, 1024)),
            scratch((3, 4, 2, 384, 256)),
            scratch((length, d)),
            DMA((28,)),
        ],
        (line.ids, hid, *acts, *packs[0], *packs[1], *packs[2]),
    )
    (o0,) = gate(o0)
    outs = [o0, swap(o1, "core"), swap(o2, "side"), swap(o3, "side", "core")]
    z3.gather()
    sums_a[2].second()

    t4 = sums_a[1].total()
    z3 = z3.result()
    x3 = swap(z3, "near")
    last = jnp.stack([t4, sums_a[2].total()])
    z45 = FarSum(line, last)
    z45.gather()
    z45 = z45.result()
    x45 = swap(z45, "near")
    x2 = swap(z2, "near")
    ids = line.ids

    output, grad_inputs = call(
        tokens_kernel,
        "tokens",
        [sds((seqs, rows, d), BF), sds((seqs, rows, d), F32)],
        [SM] + [VM] * 8,
        [VM] * 2,
        [],
        (ids, *outs, *gins),
    )
    share_in, share_back = call(
        ff_shares_kernel,
        "ff_shares",
        [sds((sh, ffs), F32), sds(w_back.shape, F32)],
        [SM] + [HBM] * 6,
        [VM] * 2,
        [scratch((3, 2, 2 * sh + 384, 256)), DMA((24,))],
        (ids, z0, x0, z1, x1, z2, x2),
    )
    share_q, share_k, share_v, share_o = call(
        attn_shares_kernel,
        "attn_shares",
        [sds((sh, d), F32)] * 4,
        [SM] + [HBM] * 4,
        [VM] * 4,
        [scratch((2, 3 * sh, 256)), scratch((2, 6 * hw, 256)), DMA((16,))],
        (ids, z3, x3, z45, x45),
    )
    return (
        output,
        grad_inputs,
        total_gain_attn,
        share_q,
        share_k,
        share_v,
        share_o,
        total_table,
        total_gain_ff,
        share_in,
        share_back,
    )


def solution(mesh):
    far = mesh.shape["rows"] // 2
    inner = jax.sharding.Mesh(mesh.devices.reshape(far, 2, 2, 2), AXES)
    over_rows, over_blk = ("far", "near"), ("side", "core")
    tok, row, rep = P(over_rows, over_blk, None), P(over_blk, None), P()
    return jax.shard_map(
        shards,
        mesh=inner,
        in_specs=(tok, P(over_rows, over_blk), rep, row, row, row, row, rep, rep, row, row, tok),
        out_specs=(tok, tok, rep, row, row, row, row, rep, rep, row, row),
        check_vma=False,
    )
```

```python
import functools

import jax
import jax.numpy as jnp
from jax import lax
from jax.experimental import pallas as pl
from jax.experimental.pallas import tpu as pltpu
from jax.sharding import PartitionSpec as P

EPS = 1e-06
EDGES = (1, 2, 3, 4, 5, 6, 7, 8, 12, 16, 23, 32, 46, 64, 91)
BF = jnp.bfloat16
F32 = jnp.float32
HBM = pl.BlockSpec(memory_space=pltpu.HBM)
VM = pl.BlockSpec(memory_space=pltpu.VMEM)
SM = pl.BlockSpec(memory_space=pltpu.SMEM)
DMA = pltpu.SemaphoreType.DMA
sds = jax.ShapeDtypeStruct
AXES = ("far", "near", "side", "core")
FLIPS = {"near": 4, "side": 2, "core": 1}


def scratch(shape, kind=BF):
    return pltpu.VMEM(shape, kind)


def call(kernel, name, outs, ins, out_specs, scratches, args, flops=10**10):
    return pl.pallas_call(
        kernel,
        out_shape=outs,
        in_specs=ins,
        out_specs=out_specs,
        scratch_shapes=scratches,
        compiler_params=pltpu.CompilerParams(vmem_limit_bytes=60 * 1024 * 1024),
        cost_estimate=pl.CostEstimate(flops=flops, bytes_accessed=4 * 10**7, transcendentals=0),
        name=name,
    )(*args)


def nn(a, b):
    return lax.dot_general(a, b, (((1,), (0,)), ((), ())), preferred_element_type=F32)


def nt(a, b):
    return lax.dot_general(a, b, (((1,), (1,)), ((), ())), preferred_element_type=F32)


def tn(a, b):
    return lax.dot_general(a, b, (((0,), (0,)), ((), ())), preferred_element_type=F32)


def swap(value, *axes):
    flip = sum(FLIPS[a] for a in axes)
    count = 1
    for a in AXES:
        count *= lax.axis_size(a)
    return lax.ppermute(value, AXES, [(i, i ^ flip) for i in range(count)])


def swap_far(value, bits):
    count = 8 * lax.axis_size("far")
    return lax.ppermute(value, AXES, [(i, i ^ (8 * bits)) for i in range(count)])


class Line:
    def __init__(self, ids):
        self.ids = ids

    def gate(self, *values):
        self.ids, *values = lax.optimization_barrier((self.ids, *values))
        return tuple(values)


def pick(arr, index, axis=0):
    return lax.dynamic_index_in_dim(arr, index, axis, keepdims=False)


def add_low(a, b):
    return (a.astype(F32) + b.astype(F32)).astype(BF)


class Sum:
    def __init__(self, keep, send):
        self.kept = (keep,)
        self.flying = (swap(send, "core"),)

    def first(self):
        (k,), (f,) = self.kept, self.flying
        return [((k, (p, i)), (f, (p, i))) for p in (0, 1) for i in (0, 1)], (None, "side", None, "near")

    def second(self):
        pairs = [((k, (i,)), (f, (i,))) for k, f in zip(self.kept, self.flying) for i in (0, 1)]
        return pairs, (None, "near", None, "side")

    def third(self):
        return [((k, ()), (f, ())) for k, f in zip(self.kept, self.flying)], (None, None)


def add_kernel(pairs, ids, *refs):
    n, outs, bufs, sems = len(refs) - 3 * len(pairs) - 1, None, None, refs[-1]
    outs, bufs = refs[n : n + len(pairs)], refs[n + len(pairs) : -1]
    dma = Copies(sems)
    cut = lambda ref, at: ref.at[at] if at else ref
    loads = [
        dma.start([(cut(refs[r], at), bufs[2 * i + j]) for j, (r, at) in enumerate(pair)])
        for i, pair in enumerate(pairs)
    ]
    stores = []
    for i in range(len(pairs)):
        wait(loads[i])
        a, b = bufs[2 * i], bufs[2 * i + 1]
        a[...] = (a[...].astype(F32) + b[...].astype(F32)).astype(BF)
        stores += dma.start([(a, outs[i])])
    wait(stores)


def add_all(line, pairs):
    arrays = []
    places = []
    for pair in pairs:
        place = []
        for arr, at in pair:
            known = [i for i, other in enumerate(arrays) if other is arr]
            if not known:
                arrays.append(arr)
            place.append((known[0] if known else len(arrays) - 1, at))
        places.append(tuple(place))
    shapes = [p[0][0].shape[len(p[0][1]) :] for p in pairs]
    return call(
        functools.partial(add_kernel, places),
        "add",
        [sds(s, BF) for s in shapes],
        [SM] + [HBM] * len(arrays),
        [HBM] * len(pairs),
        [scratch(s) for s in shapes for _ in (0, 1)] + [DMA((3 * len(pairs),))],
        (line.ids, *arrays),
    )


class FarPairs:
    ORDER = (0, 2, 1, 3)

    def __init__(self, parts):
        total = jnp.concatenate(parts, axis=0)
        self.plain = lax.axis_size("far") != 4
        if self.plain:
            self.kept, self.flying = (lax.psum(total, "far"),), ()
            return
        blocks = total.reshape(4, -1, 256)
        here = lax.axis_index("far")
        at = [pick(blocks, here ^ i) for i in range(4)]
        self.kept, self.flying = (jnp.stack([at[0], at[2]]),), (swap_far(jnp.stack([at[1], at[3]]), 1),)

    def pair(self):
        (kept,), (got,) = self.kept, self.flying
        return [((kept, (i,)), (got, (i,))) for i in (0, 1)], (None, 2)

    def back(self):
        return [((self.kept[0], ()), (self.flying[0], ()))], (0,)

    def last(self):
        both = jnp.stack([self.kept[0], self.flying[0]])
        self.kept, self.flying = (both,), (swap_far(both, 1),)
        return [], ()

    def finish(self):
        if not self.plain:
            self.kept = (jnp.concatenate([self.kept[0], self.flying[0]]),)
        self.flying = (swap(self.kept[0], "near"),)
        return [], ()


def advance(line, *steps, new=()):
    landed = list(line.gate(*[f for piece, _ in steps for f in piece.flying], *new))
    jobs, pairs = [], []
    for piece, step in steps:
        piece.flying = tuple(landed.pop(0) for _ in piece.flying)
        if step is not None and not (step in ("pair", "back", "last") and piece.plain):
            more, where = getattr(piece, step)()
            if more:
                jobs.append((piece, where))
                pairs += more
    fresh = Sum(*landed) if new else None
    if not jobs:
        return fresh
    sums = list(add_all(line, pairs))
    line.gate(sums[0])
    for piece, where in jobs:
        kept, flying = [], []
        for place in where:
            s = sums.pop(0)
            if place is None:
                kept.append(s)
            elif isinstance(place, str):
                flying.append(swap(s, place))
            else:
                if place == 0:
                    kept.append(s)
                flying.append(swap_far(s, 2))
        piece.kept, piece.flying = tuple(kept), tuple(flying)
    return fresh


class Gather:
    def __init__(self, line, own, half):
        self.line, self.own = line, own
        self.y = swap(half, "side")
        self.core = swap(own, "core")

    def cross(self):
        self.y, self.core = self.line.gate(self.y, self.core)
        self.x = swap(self.y, "near")
        self.yc = swap(self.y, "core")

    def relay(self):
        self.x, self.yc = self.line.gate(self.x, self.yc)
        self.xc = swap(self.x, "core")

    def done(self):
        (self.xc,) = self.line.gate(self.xc)
        return (self.own, self.core, self.y, self.x, self.yc, self.xc)


class Copies:
    def __init__(self, sems):
        self.sems, self.count = sems, 0

    def start(self, pairs):
        out = []
        for src, dst in pairs:
            out.append(pltpu.make_async_copy(src, dst, self.sems.at[self.count]))
            self.count += 1
            out[-1].start()
        return out


def wait(copies):
    for c in copies:
        c.wait()


def pieces_of(refs, me, half):
    own, core, y, x, yc, xc = refs
    out = []
    for h in (0, 1):
        out.append((own.at[h], me, h))
        out.append((core.at[h], me ^ 1, h))
    out.append((y, me ^ 2, half))
    out.append((x, me ^ 2, 1 - half))
    out.append((yc, me ^ 3, half))
    out.append((xc, me ^ 3, 1 - half))
    return out


def pack_copies(refs, me, half, dst, cut):
    return [(cut(ref), dst.at[o, h]) for ref, o, h in pieces_of(refs, me, half)]


def token_copies(slots, me, dst):
    rows = dst.shape[0] // 4
    return [
        (src, dst.at[pl.ds(pl.multiple_of((me ^ s) * rows, rows), rows)]) for s, src in enumerate(slots)
    ]


def put(stage, owner, row, value):
    half, count = stage.shape[2], value.shape[0]
    first = min(count, max(0, half - row))
    if first:
        stage[owner, 0, pl.ds(row, first), :] = value[:first]
    if first < count:
        stage[owner, 1, pl.ds(row + first - half, count - first), :] = value[first:]


def piece_copies(stage, keep, send, ids):
    me, near, core = ids[0], ids[1], ids[2]
    h = stage.shape[2] // 2
    out = []
    for dst, c in ((send, 1 - core), (keep, core)):
        for part in (0, 1):
            for first in (0, 1):
                for second in (0, 1):
                    sy, sx = (first, second) if part == 0 else (second, first)
                    owner = ((me ^ (2 * sy)) & 2) + c
                    out.append((stage.at[owner, near ^ sx, pl.ds(part * h, h)], dst.at[part, first, second]))
    return out


def piece_shapes(rows):
    return [sds((2, 2, 2, rows // 4, 256), BF)] * 2


def rows_of(blocks):
    return jnp.concatenate(blocks, axis=0)


def prep_a_kernel(ids, seg, inputs, wq, wk, wv, m0, m1, m2, m3, own0, own1, y0, y1, sems):
    me, half = ids[0], ids[1]
    rows = inputs.shape[1]
    part = wq.shape[0] // 2
    pairs = []
    for g in range(3):
        own, y, at = (own0, y0, 0) if g == 0 else (own1, y1, g - 1)
        for i, w in enumerate((wq, wk, wv)):
            cols, place = pl.ds(g * 256, 256), pl.ds((3 * at + i) * part, part)
            pairs.append((w.at[pl.ds(pl.multiple_of(half * part, 16), part), cols], y.at[place]))
            for h in (0, 1):
                pairs.append((w.at[pl.ds(h * part, part), cols], own.at[h, place]))
    for s, m in enumerate((m0, m1, m2, m3)):
        pairs.append((inputs.at[me ^ s], m.at[pl.ds(0, rows)]))
    copies = Copies(sems).start(pairs)
    for s, m in enumerate((m0, m1, m2, m3)):
        line = seg[pl.ds(me ^ s, 1), :].astype(F32)
        m[pl.ds(rows, 16), pl.ds(0, rows)] = jnp.broadcast_to(line, (16, rows)).astype(BF)
        m[pl.ds(rows, 16), pl.ds(rows, m.shape[1] - rows)] = jnp.zeros((16, m.shape[1] - rows), BF)
    wait(copies)


def prep_b_kernel(ids, w_in, w_back, w_out, cot, own0, own1, own2, y0, y1, y2, k1, k2, k3, sems):
    me, half = ids[0], ids[1]
    hw = w_in.shape[0] // 2
    pairs = [(cot.at[me ^ s], k) for s, k in ((1, k1), (2, k2), (3, k3))]
    for c, (own, y) in enumerate(((own0, y0), (own1, y1), (own2, y2))):
        for dst, h in ((y, half), (own.at[0], 0), (own.at[1], 1)):
            for b in range(4):
                pairs.append((
                    w_in.at[pl.ds(pl.multiple_of(h * hw, 16), hw), pl.ds(b * 768 + c * 256, 256)],
                    dst.at[pl.ds(b * hw, hw)],
                ))
            for j in range(3):
                pairs.append((
                    w_back.at[pl.ds(pl.multiple_of(c * 256 + h * 128, 16), 128), pl.ds(j * 256, 256)],
                    dst.at[pl.ds(4 * hw + j * 128, 128)],
                ))
                if c == 0:
                    pairs.append((
                        w_out.at[pl.ds(pl.multiple_of(h * hw, 16), hw), pl.ds(j * 256, 256)],
                        dst.at[pl.ds(4 * hw + 384 + j * hw, hw)],
                    ))
    wait(Copies(sems).start(pairs))


def norm_kernel(ids, m0, m1, m2, m3, gain, xs, nrm, nrm_t, seg, sbuf, sems):
    me = ids[0]
    rows = xs.shape[0] // 4
    slots = (m0, m1, m2, m3)
    tok = token_copies([m.at[pl.ds(0, rows)] for m in slots], me, xs)
    tok += token_copies([m.at[pl.ds(rows, 16)] for m in slots], me, sbuf)
    wait(Copies(sems).start(tok))
    seg[...] = jnp.concatenate(
        [sbuf[pl.ds(o * 16, 1), pl.ds(0, rows)].astype(F32) for o in range(4)], axis=1
    )
    for a in range(4):
        x = xs[pl.ds(a * rows, rows), :].astype(F32)
        y = x * lax.rsqrt(jnp.mean(x * x, axis=-1, keepdims=True) + EPS) * gain[...]
        y = y.astype(BF)
        nrm[pl.ds(a * rows, rows), :] = y
        nrm_t[:, pl.ds(a * rows, rows)] = y.T


def half_masks(t):
    lane = lax.broadcasted_iota(jnp.int32, (t, 128), 1)
    return lane < 64, (lane < 64).astype(F32).astype(BF), (lane >= 64).astype(F32).astype(BF)


def attn_fwd_kernel(group, ids, far, seg, lines, nrm_in, w0, w1, w2, w3, w4, w5,
                    q_out, k_out, v_out, p_out, o, near, nrm, wbuf, q, k, v, p, sems):
    me, half = ids[0], ids[1]
    dma = Copies(sems)
    count = wbuf.shape[2]
    part = count // 3
    place = pl.ds(max(group - 1, 0) * count, count)
    loads = dma.start(
        [(nrm_in, nrm)]
        + pack_copies((w0, w1, w2, w3, w4, w5), me, half, wbuf, lambda ref: ref.at[place])
    )
    for head in range(4):
        line = jnp.broadcast_to(lines[pl.ds(4 * group + head, 1), :], (near.shape[1], lines.shape[1]))
        near[head] = pltpu.roll(line, 0, 1, stride=1, stride_axis=0)[:, : near.shape[2]]
    t = near.shape[1]
    length = q.shape[0]
    nblk = length // t
    low, m0, m1 = half_masks(t)
    eye = lax.broadcasted_iota(jnp.int32, (t, t), 0) == lax.broadcasted_iota(jnp.int32, (t, t), 1)
    seg_row = seg[...]
    wait(loads)
    stores = []
    for i, (buf, out) in enumerate(((q, q_out), (k, k_out), (v, v_out))):
        w = rows_of([wbuf[ow, h, pl.ds(i * part, part), :] for ow in range(4) for h in (0, 1)])
        buf[...] = nn(nrm[...], w).astype(BF)
        stores += dma.start([(buf, out)])
    for pair in (0, 1):
        at = pl.ds(pair * 128, 128)
        for a in range(nblk):
            seg_col = jnp.sum(
                jnp.where(eye, jnp.broadcast_to(seg_row[:, a * t : (a + 1) * t], (t, t)), 0.0),
                axis=1,
                keepdims=True,
            )
            allowed = seg_col == seg_row
            q2 = q[pl.ds(a * t, t), at]
            s = nt(rows_of([q2 * m0, q2 * m1]), k[:, at])
            ps = []
            for h in (0, 1):
                head = 2 * pair + h
                strip = []
                for b in range(nblk):
                    rel = b - a
                    if abs(rel) <= 1:
                        strip.append(near[head, :, (rel + 1) * t : (rel + 2) * t])
                    else:
                        strip.append(jnp.full((t, t), far[int(rel > 0), group * 4 + head], F32))
                sh = s[h * t : (h + 1) * t] + jnp.concatenate(strip, axis=1)
                sh = jnp.where(allowed, sh, -1e30)
                top = jnp.max(sh, axis=-1, keepdims=True)
                e = jnp.exp(sh - top)
                inv = 1.0 / jnp.sum(e, axis=-1, keepdims=True)
                ph = (e * inv).astype(BF)
                p[head, pl.ds(a * t, t), :] = ph
                ps.append(ph)
            mix = nn(rows_of(ps), v[:, at])
            o[pl.ds(a * t, t), at] = jnp.where(low, mix[:t], mix[t:]).astype(BF)
        stores += dma.start([(p.at[pl.ds(2 * pair, 2)], p_out.at[pl.ds(2 * pair, 2)])])
    wait(stores)


def out_weight(wbuf, j):
    hw = wbuf.shape[2] // 3
    return rows_of([wbuf[o, h, pl.ds(j * hw, hw), :] for o in range(4) for h in (0, 1)])


def out_cut(sh):
    return lambda ref: ref.at[pl.ds(2 * sh + 384, 3 * (sh // 2))]


def hidden_kernel(ids, xs, x0, x1, x2, gain, w0, w1, w2, w3, w4, w5, hid, ff, ff_t, wbuf, sems):
    me, half = ids[0], ids[1]
    width = xs.shape[1]
    wait(Copies(sems).start(pack_copies((w0, w1, w2, w3, w4, w5), me, half, wbuf, out_cut(width // 4))))
    for j in range(3):
        cols = pl.ds(j * 256, 256)
        w = out_weight(wbuf, j)
        acc = xs[:, cols].astype(F32)
        for i, mx in enumerate((x0, x1, x2)):
            acc = acc + nn(mx[...], w[i * 256 : (i + 1) * 256])
        hid[:, cols] = acc
    rows = 128
    for a in range(xs.shape[0] // rows):
        x = hid[pl.ds(a * rows, rows), :]
        y = x * lax.rsqrt(jnp.mean(x * x, axis=-1, keepdims=True) + EPS) * gain[...]
        y = y.astype(BF)
        ff[pl.ds(a * rows, rows), :] = y
        ff_t[:, pl.ds(a * rows, rows)] = y.T


def gelu_both(x):
    c = 0.7978845608028654
    x2 = x * x
    th = jnp.tanh(x * (c + (c * 0.044715) * x2))
    half_up = 0.5 + 0.5 * th
    slope = half_up + x * (0.5 - 0.5 * th * th) * (c + (3.0 * c * 0.044715) * x2)
    return x * half_up, slope


def ffn_kernel(ids, ff, ff_t, cown, c1, c2, c3, p0, p1, p2, p3, p4, p5, act_out, gpre_out, *rest):
    keep, send, ffv, fftv, cot, pack, act, gpre, stage, sems = rest
    me, half = ids[0], ids[1]
    d = ff.shape[1]
    sh = d // 4
    hw = sh // 2
    dma = Copies(sems)
    first = dma.start(
        [(ff, ffv)]
        + pack_copies((p0, p1, p2, p3, p4, p5), me, half, pack, lambda ref: ref.at[pl.ds(0, 4 * hw + 384)])
    )
    second = dma.start(token_copies((cown.at[me], c1, c2, c3), me, cot))
    third = dma.start([(ff_t, fftv)])
    wait(first)
    stores = []
    for b in range(5):
        if b < 4:
            at = pl.ds(b * 256, 256)
            win = rows_of([pack[o, h, pl.ds(b * hw, hw), :] for o in range(4) for h in (0, 1)])
            value, slope = gelu_both(nn(ffv[...], win))
            if b == 0:
                wait(second)
            act[:, at] = value.astype(BF)
            back = 0.0
            for j in range(3):
                wb = rows_of([pack[b, h, pl.ds(4 * hw + j * 128, 128), :] for h in (0, 1)])
                back = back + nt(cot[:, pl.ds(j * 256, 256)], wb)
            gpre[:, at] = (back * slope).astype(BF)
        if b == 3:
            stores += dma.start([(act, act_out), (gpre, gpre_out)])
        if b > 0:
            c = b - 1
            at = pl.ds(c * 256, 256)
            if c == 0:
                wait(third)
            gw = nn(fftv[...], gpre[:, at]).astype(BF)
            for o in range(4):
                put(stage, o, c * sh, gw[o * sh : (o + 1) * sh])
            gb = tn(act[:, at], cot[...]).astype(BF)
            for j in range(3):
                put(stage, c, 4 * sh + j * 256, gb[:, j * 256 : (j + 1) * 256])
    stores += dma.start(piece_copies(stage, keep, send, ids))
    wait(stores)


def after_ff_kernel(ids, gain, hid, g0, g1, g2, cown, c1, c2, c3, x0, x1, x2, *refs):
    packs = (refs[0:6], refs[6:12], refs[12:18])
    ghid, gm0, gm1, gm2, ggain, gwo, hidv, gv, cot, mx, wbuf, wins, ga, gf, sems = refs[18:]
    me, half = ids[0], ids[1]
    d = hid.shape[1]
    sh = d // 4
    hw = sh // 2
    rows = cot.shape[0] // 4
    dma = Copies(sems)
    loads = [
        dma.start(
            [(g, gv.at[c])]
            + pack_copies(packs[c], me, half, wins.at[c], lambda ref: ref.at[pl.ds(0, 4 * hw)])
        )
        for c, g in enumerate((g0, g1, g2))
    ]
    rest = dma.start([(hid, hidv)] + token_copies((cown.at[me], c1, c2, c3), me, cot))
    last = dma.start(
        pack_copies(packs[0], me, half, wbuf, out_cut(sh))
        + [(x, mx.at[:, pl.ds(i * 256, 256)]) for i, x in enumerate((x0, x1, x2))]
    )
    for c in range(3):
        wait(loads[c])
        acc = None
        for b in range(4):
            w = rows_of([wins[c, o, h, pl.ds(b * hw, hw), :] for o in range(4) for h in (0, 1)])
            term = nt(gv[c, :, pl.ds(b * 256, 256)], w)
            acc = term if acc is None else acc + term
        gf[...] = acc if c == 0 else gf[...] + acc
    wait(rest)
    total = jnp.zeros((1, d), F32)
    for a in range(4):
        at = pl.ds(a * rows, rows)
        x = hidv[at, :]
        gfa = gf[at, :]
        n = lax.rsqrt(jnp.mean(x * x, axis=-1, keepdims=True) + EPS)
        g = gfa * gain[...]
        xn = x * n
        total = total + jnp.sum(gfa * xn, axis=0, keepdims=True)
        gh = cot[at, :].astype(F32) + n * (g - xn * (n * jnp.mean(g * x, axis=-1, keepdims=True)))
        ghid[at, :] = gh
        ga[at, :] = gh.astype(BF)
    ggain[...] = total
    wait(last)
    acc = None
    for j in range(3):
        term = nt(ga[:, pl.ds(j * 256, 256)], out_weight(wbuf, j))
        acc = term if acc is None else acc + term
    for i, gm in enumerate((gm0, gm1, gm2)):
        gm[...] = acc[:, i * 256 : (i + 1) * 256].astype(BF)
    for j in range(3):
        gw = tn(mx[...], ga[:, pl.ds(j * 256, 256)]).astype(BF)
        for o in range(4):
            gwo[o, pl.ds(j * sh, sh), :] = gw[o * sh : (o + 1) * sh]


def out_kernel(ids, hid, gin, a0, a1, a2, *refs):
    packs = (refs[0:6], refs[6:12], refs[12:18])
    out, hidv, av, wb, sems = refs[18:]
    me, half = ids[0], ids[1]
    d = hid.shape[1]
    hw = d // 8
    rows = hid.shape[0] // 4
    dma = Copies(sems)
    loads = [
        dma.start(
            [(a, av.at[c])]
            + pack_copies(packs[c], me, half, wb.at[c], lambda ref: ref.at[pl.ds(4 * hw, 384)])
        )
        for c, a in enumerate((a0, a1, a2))
    ]
    last = dma.start([(hid, hidv)])
    grads = dma.start([(gin.at[pl.ds(b * rows, rows)], out.at[b, 1]) for b in range(4)])
    for c in range(3):
        wait(loads[c])
    wait(last)
    for j in range(3):
        cols = pl.ds(j * 256, 256)
        acc = hidv[:, cols]
        for c in range(3):
            w = rows_of([wb[c, o, h, pl.ds(j * 128, 128), :] for o in range(4) for h in (0, 1)])
            acc = acc + nn(av[c], w)
        acc = acc.astype(BF)
        for b in range(4):
            out[b, 0, :, cols] = acc[b * rows : (b + 1) * rows]
    wait(grads)


def diagonals(x):
    width = x.shape[1]
    y = x[0:8]
    for a in range(8, x.shape[0], 8):
        y = y + pltpu.roll(x[a : a + 8], width - a, 1)
    sub = lax.broadcasted_iota(jnp.int32, y.shape, 0)
    for bit in (1, 2, 4):
        y = jnp.where((sub & bit) != 0, pltpu.roll(y, width - bit, 1), y)
    return jnp.sum(y, axis=0, keepdims=True)


def attn_bwd_kernel(plain, carried, ids, q_in, k_in, v_in, p_in, gm_in, nrm_in, *refs):
    carry, refs = refs[:carried], refs[carried:]
    grad, refs = refs[: 1 if plain else 2], refs[1 if plain else 2 :]
    (dq_out, dk_out, dv_out, diag, q, k, v, p, gm, nrm_t, dq, dk, dv, acc, stage, sems) = refs
    t = 128
    length = q.shape[0]
    nblk = length // t
    low, m0, m1 = half_masks(t)
    dma = Copies(sems)
    first = dma.start([(v_in, v), (gm_in, gm), (p_in.at[pl.ds(0, 2)], p.at[pl.ds(0, 2)]), (k_in, k), (q_in, q)])
    second = dma.start([(p_in.at[pl.ds(2, 2)], p.at[pl.ds(2, 2)])])
    third = dma.start([(nrm_in, nrm_t)])
    base, half = 0, stage.shape[2]
    for g in carry:
        count = g.shape[1]
        inside = min(count, half - base) if base < half else 0
        if inside:
            third += dma.start([(g.at[:, pl.ds(0, inside)], stage.at[:, 0, pl.ds(base, inside)])])
        if inside < count:
            rest, at = count - inside, max(0, base - half)
            third += dma.start([(g.at[:, pl.ds(inside, rest)], stage.at[:, 1, pl.ds(at, rest)])])
        base += count
    wait(first)
    for pair in (0, 1):
        if pair == 1:
            wait(second)
        cols = pl.ds(pair * 128, 128)
        k2, v2 = k[:, cols], v[:, cols]
        dk_t = jnp.zeros((128, length), F32)
        dv_t = jnp.zeros((128, length), F32)
        for a in range(nblk):
            at = pl.ds(a * t, t)
            q2, g2 = q[at, cols], gm[at, cols]
            qm = rows_of([q2 * m0, q2 * m1])
            g_both = rows_of([g2 * m0, g2 * m1])
            dp = nt(g_both, v2)
            pb = rows_of([p[2 * pair, at, :], p[2 * pair + 1, at, :]])
            pf = pb.astype(F32)
            delta = jnp.sum(pf * dp, axis=-1, keepdims=True)
            ds = (pf * (dp - delta)).astype(BF)
            mq = nn(ds, k2)
            dq[at, cols] = jnp.where(low, mq[:t], mq[t:]).astype(BF)
            dk_t = dk_t + tn(qm, ds)
            dv_t = dv_t + tn(g_both, pb)
            dsf = ds.astype(F32)
            for h in (0, 1):
                for b in range(nblk):
                    rel = b - a
                    place = rel + 1 if abs(rel) <= 1 else (3 if rel < 0 else 4)
                    tile = dsf[h * t : (h + 1) * t, b * t : (b + 1) * t]
                    lanes = pl.ds(place * t, t)
                    if (a, b) in ((1, 0), (0, 0), (0, 1), (2, 0), (0, 2)):
                        acc[h, :, lanes] = tile
                    else:
                        acc[h, :, lanes] += tile
        dk[:, cols] = dk_t.T.astype(BF)
        dv[:, cols] = dv_t.T.astype(BF)
        for h in (0, 1):
            near = jnp.concatenate([acc[h, :, pl.ds(0, 3 * t)], jnp.zeros((t, t), F32)], axis=1)
            far = jnp.sum(acc[h, :, pl.ds(3 * t, 2 * t)], axis=0, keepdims=True)
            diag[pl.ds(2 * pair + h, 1), :] = jnp.concatenate([diagonals(near), far], axis=1)
    stores = dma.start([(dq, dq_out), (dk, dk_out), (dv, dv_out)])
    wait(third)
    sh = nrm_t.shape[0] // 4
    for i, g in enumerate((dq, dk, dv)):
        gw = nn(nrm_t[...], g[...]).astype(BF)
        for o in range(4):
            put(stage, o, base + i * sh, gw[o * sh : (o + 1) * sh])
    if plain:
        stores += dma.start([(stage.at[:, h], grad[0].at[:, pl.ds(h * half, half)]) for h in (0, 1)])
    else:
        stores += dma.start(piece_copies(stage, *grad, ids))
    wait(stores)


def first_norm_kernel(ids, gain, xs, ghid, *refs):
    ins = refs[0:9]
    w0, w1 = refs[9:15], refs[15:21]
    gi, ggain, xv, gv, dall, wbuf0, wbuf1, gn, sems = refs[21:]
    me, half = ids[0], ids[1]
    d = xs.shape[1]
    rows = xs.shape[0] // 4
    dma = Copies(sems)
    loads = dma.start(
        [(g, dall.at[n]) for n, g in enumerate(ins)]
        + pack_copies(w0, me, half, wbuf0, lambda ref: ref)
        + pack_copies(w1, me, half, wbuf1, lambda ref: ref)
    )
    part = wbuf0.shape[2] // 3
    rest = dma.start([(xs, xv), (ghid, gv)])
    wait(loads)
    acc = None
    for i in range(3):
        for c in range(3):
            buf, at = (wbuf0, i) if c == 0 else (wbuf1, 3 * (c - 1) + i)
            wi = rows_of([buf[o, h, pl.ds(at * part, part), :] for o in range(4) for h in (0, 1)])
            term = nt(dall[3 * i + c], wi)
            acc = term if acc is None else acc + term
    gn[...] = acc
    wait(rest)
    total = jnp.zeros((1, d), F32)
    for a in range(4):
        at = pl.ds(a * rows, rows)
        x = xv[at, :].astype(F32)
        gf = gn[at, :]
        n = lax.rsqrt(jnp.mean(x * x, axis=-1, keepdims=True) + EPS)
        g = gf * gain[...]
        xn = x * n
        total = total + jnp.sum(gf * xn, axis=0, keepdims=True)
        gi[at, :] = (gv[at, :] + n * (g - xn * (n * jnp.mean(g * x, axis=-1, keepdims=True)))).astype(BF)
    ggain[...] = total


def tokens_kernel(ids, tokens, out, gin):
    out[...] = tokens[:, 0]
    gin[...] = tokens[:, 1].astype(F32)


def half_copies(ref, dst, far, order):
    if ref.shape == dst.shape:
        return [(ref, dst)]
    n = ref.shape[1]
    return [(ref.at[i], dst.at[pl.ds(pl.multiple_of((far ^ b) * n, 16), n)]) for i, b in enumerate(order)]


def ff_shares_kernel(ids, za, xa, zb, xb, out_in, out_back, wo, grad_first, buf_a, buf_b, sems):
    here, far = ids[1], ids[3]
    sh = out_in.shape[0]
    order = FarPairs.ORDER
    copies = []
    for z, x, buf in ((za, xa, buf_a), (zb, xb, buf_b)):
        copies += half_copies(z, buf.at[here], far, order) + half_copies(x, buf.at[1 - here], far, order)
    wait(Copies(sems).start(copies))
    half = 2 * sh + 384
    for k, buf, at in ((0, buf_a, 0), (1, buf_a, half), (2, buf_b, 0)):
        for b in range(4):
            out_in[:, pl.ds((b * 3 + k) * 256, 256)] = buf[0, pl.ds(at + b * sh, sh), :].astype(F32)
        for j in range(3):
            out_back[pl.ds(k * 256, 256), pl.ds(j * 256, 256)] = buf[1, pl.ds(at + j * 256, 256), :].astype(F32)
    for i in range(3):
        wo[:, pl.ds(i * 256, 256)] = buf_b[0, pl.ds(half + i * sh, sh), :].astype(F32)
        grad_first[i] = buf_b[1, pl.ds(half + i * sh, sh), :]


def attn_shares_kernel(ids, first, z, x, wq, wk, wv, buf, sems):
    here, far = ids[1], ids[3]
    sh = wq.shape[0]
    order = FarPairs.ORDER
    copies = half_copies(z, buf.at[here], far, order) + half_copies(x, buf.at[1 - here], far, order)
    wait(Copies(sems).start(copies))
    for i, out in enumerate((wq, wk, wv)):
        out[:, pl.ds(0, 256)] = first[i].astype(F32)
        out[:, pl.ds(256, 256)] = buf[0, pl.ds(i * sh, sh), :].astype(F32)
        out[:, pl.ds(512, 256)] = buf[1, pl.ds(i * sh, sh), :].astype(F32)


def bucket_of(offset, bucket_count):
    distance = jnp.abs(offset)
    bucket = jnp.where(offset > 0, bucket_count // 2, 0).astype(jnp.int32)
    for edge in EDGES:
        bucket = bucket + (distance >= edge).astype(jnp.int32)
    return bucket


def shards(inputs, segments, gain_attn, w_query, w_key, w_value, w_out, bucket_bias_table, gain_ff, w_in, w_back, cotangent):
    seqs, rows, d = inputs.shape
    sh = w_query.shape[0]
    hw = sh // 2
    ffs = w_in.shape[1]
    bucket_count, heads = bucket_bias_table.shape
    length = rows * seqs
    places = [lax.axis_index(a).astype(jnp.int32) for a in ("near", "side", "core", "far")]
    near_at, side_at, core_at, far_at = places
    line = Line(jnp.stack([2 * side_at + core_at, near_at, core_at, far_at]))
    gate = line.gate
    row_low, row_f32 = sds((length, d), BF), sds((length, d), F32)
    quad_low, tok_low = sds((length, 256), BF), sds((rows, d), BF)
    gain1, gain2 = gain_attn.reshape(1, d), gain_ff.reshape(1, d)
    pack_rows = [4 * hw + 384 + 3 * hw, 4 * hw + 384, 4 * hw + 384]

    m0, m1, m2, m3, own_a, own_b, y_a, y_b = call(
        prep_a_kernel,
        "prep_a",
        [sds((rows + 16, d), BF)] * 4
        + [sds((2, 3 * hw, 256), BF), sds((2, 6 * hw, 256), BF), sds((3 * hw, 256), BF), sds((6 * hw, 256), BF)],
        [SM, VM] + [HBM] * 4,
        [VM] * 8,
        [DMA((31,))],
        (line.ids, segments, inputs, w_query, w_key, w_value),
    )
    wa = Gather(line, own_a, y_a)
    msgs = [swap(m1, "core"), swap(m2, "side"), swap(m3, "side", "core")]
    wb = Gather(line, own_b, y_b)

    own0, own1, own2, y0, y1, y2, k1, k2, k3 = call(
        prep_b_kernel,
        "prep_b",
        [sds((2, r, 256), BF) for r in pack_rows] + [sds((r, 256), BF) for r in pack_rows] + [tok_low] * 3,
        [SM] + [HBM] * 4,
        [VM] * 9,
        [DMA((75,))],
        (line.ids, w_in, w_back, w_out, cotangent),
    )

    (own0,) = gate(own0)
    wa.cross()
    *msgs, table_in = gate(*msgs, bucket_bias_table)
    wa.relay()

    offs = jnp.arange(4 * rows, dtype=jnp.int32)
    offs = jnp.where(offs < 3 * rows, offs - rows, offs - 5 * rows)
    hot = (bucket_of(offs, bucket_count)[None] == jnp.arange(bucket_count, dtype=jnp.int32)[:, None]).astype(F32)
    lines = jnp.einsum("up,uw->wp", hot, table_in, precision=lax.Precision.HIGHEST)
    far = jnp.stack([table_in[bucket_count // 2 - 1], table_in[bucket_count - 1]])

    y0, own0 = gate(y0, own0)
    wf = [Gather(line, own0, y0)]
    xs, nrm, nrm_t, seg = call(
        norm_kernel,
        "norm",
        [row_low, row_low, sds((d, length), BF), sds((1, length), F32)],
        [SM] + [HBM] * 4 + [VM],
        [VM] * 4,
        [scratch((64, d)), DMA((8,))],
        (line.ids, m0, *msgs, gain1),
    )
    nrm, lines = gate(nrm, lines)
    wb.cross()
    wa = wa.done()

    qs, ks, vs, probs, mixed = [], [], [], [], []
    for g in range(3):
        q, k, v, p, mx = call(
            functools.partial(attn_fwd_kernel, g),
            "attn_fwd",
            [quad_low] * 3 + [sds((4, length, length), BF), quad_low],
            [SM, SM, VM, VM] + [HBM] * 7,
            [HBM] * 4 + [VM],
            [
                scratch((4, rows, 3 * rows), F32),
                scratch((length, d)),
                scratch((4, 2, 3 * hw, 256)),
                scratch((length, 256)),
                scratch((length, 256)),
                scratch((length, 256)),
                scratch((4, length, length)),
                DMA((15,)),
            ],
            (line.ids, far, seg, lines, nrm, *(wa if g == 0 else wb)),
        )
        (mx,) = gate(mx)
        for have, new in ((qs, q), (ks, k), (vs, v), (probs, p), (mixed, mx)):
            have.append(new)
        if g == 0:
            wb.relay()
            wf[0].cross()
            own1, y1 = gate(own1, y1)
            wb = wb.done()
            wf.append(Gather(line, own1, y1))
        if g == 1:
            wf[0].relay()
            wf[1].cross()
            own2, y2 = gate(own2, y2)
            wf.append(Gather(line, own2, y2))
    packs = [wf[0].done()]
    wf[1].relay()
    wf[2].cross()
    k1, k2, k3 = gate(k1, k2, k3)
    cots = [swap(k1, "core"), swap(k2, "side"), swap(k3, "side", "core")]

    hid, ff, ff_t = call(
        hidden_kernel,
        "hidden",
        [row_f32, row_low, sds((d, length), BF)],
        [SM] + [VM] * 5 + [HBM] * 6,
        [VM] * 3,
        [scratch((4, 2, 3 * hw, 256)), DMA((8,))],
        (line.ids, xs, *mixed, gain2, *packs[0]),
    )
    (ff,) = gate(ff)
    packs.append(wf[1].done())
    wf[2].relay()
    cots = gate(*cots)

    sums_f, acts, gpres = [], [], []
    for c in range(3):
        act, gpre, *piece = call(
            ffn_kernel,
            "ffn",
            [sds((length, 1024), BF)] * 2 + piece_shapes(4 * sh + 768),
            [SM] + [HBM] * 12,
            [HBM] * 4,
            [
                scratch((length, d)),
                scratch((d, length)),
                scratch((length, d)),
                scratch((4, 2, 4 * hw + 384, 256)),
                scratch((length, 1024)),
                scratch((length, 1024)),
                scratch((4, 2, 2 * sh + 384, 256)),
                DMA((32,)),
            ],
            (line.ids, ff, ff_t, cotangent, *cots, *packs[c]),
        )
        acts.append(act)
        (gpre,) = gate(gpre)
        gpres.append(gpre)
        if c == 0:
            packs.append(wf[2].done())
        moves = [[], [("first",)], [("second",), ("first",)]][c]
        sums_f.append(advance(line, *[(f, *m) for f, m in zip(sums_f, moves)], new=piece))

    ghid, *gmix, ggain_ff, gwo = call(
        after_ff_kernel,
        "after_ff",
        [row_f32] + [quad_low] * 3 + [sds((1, d), F32), sds((4, 3 * sh, 256), BF)],
        [SM, VM] + [HBM] * 29,
        [VM] * 6,
        [
            scratch((length, d), F32),
            scratch((3, length, 1024)),
            scratch((length, d)),
            scratch((length, d)),
            scratch((4, 2, 3 * hw, 256)),
            scratch((3, 4, 2, 4 * hw, 256)),
            scratch((length, d)),
            scratch((length, d), F32),
            DMA((43,)),
        ],
        (line.ids, gain2, hid, *gpres, cotangent, *cots, *mixed, *packs[0], *packs[1], *packs[2]),
    )
    gmix[0], ggain_ff = gate(gmix[0], ggain_ff)
    advance(line, (sums_f[0], "third"), (sums_f[1], "second"), (sums_f[2], "first"))

    dqs, dks, dvs, diags, sums_a = [], [], [], [], []
    part = sds((4, 3 * sh, 256), BF)
    for g in range(3):
        plain = g == 1
        carry = () if plain else (gwo if g == 0 else grads,)
        body = 3 * sh * (1 + len(carry))
        *grad, dq, dk, dv, diag = call(
            functools.partial(attn_bwd_kernel, plain, len(carry)),
            "attn_bwd",
            ([part] if plain else piece_shapes(body)) + [quad_low] * 3 + [sds((4, 6 * rows), F32)],
            [SM] + [HBM] * (6 + len(carry)),
            [HBM] * ((1 if plain else 2) + 3) + [VM],
            [scratch((length, 256))] * 3
            + [scratch((4, length, length)), scratch((length, 256)), scratch((d, length))]
            + [scratch((length, 256))] * 3
            + [scratch((2, rows, 5 * rows), F32), scratch((4, 2, body // 2, 256)), DMA((32,))],
            (line.ids, qs[g], ks[g], vs[g], probs[g], gmix[g], nrm_t, *carry),
        )
        (dq,) = gate(dq)
        for have, new in ((dqs, dq), (dks, dk), (dvs, dv), (diags, diag)):
            have.append(new)
        if g == 0:
            sums_a.append(advance(line, (sums_f[1], "third"), (sums_f[2], "second"), new=grad))
            far_a = FarPairs([*sums_f[0].kept, *sums_f[1].kept])
        if g == 1:
            grads = grad[0]
            advance(line, (sums_a[0], "first"), (sums_f[2], "third"), (far_a, "pair"))
        if g == 2:
            sums_a.append(advance(line, (sums_a[0], "second"), (far_a, "back"), new=grad))

    gin, ggain_attn = call(
        first_norm_kernel,
        "first_norm",
        [row_low, sds((1, d), F32)],
        [SM, VM] + [HBM] * 23,
        [VM] * 2,
        [
            scratch((length, d)),
            scratch((length, d), F32),
            scratch((9, length, 256)),
            scratch((4, 2, 3 * hw, 256)),
            scratch((4, 2, 6 * hw, 256)),
            scratch((length, d), F32),
            DMA((27,)),
        ],
        (line.ids, gain1, xs, ghid, *dqs, *dks, *dvs, *wa, *wb),
    )
    (gin,) = gate(gin)
    advance(line, (sums_a[0], "third"), (sums_a[1], "first"), (far_a, "last"))
    far_b = FarPairs([*sums_f[2].kept, *sums_a[0].kept])

    hot6 = jnp.concatenate(
        [
            hot,
            jnp.zeros((bucket_count, rows), F32).at[bucket_count // 2 - 1].set(1.0),
            jnp.zeros((bucket_count, rows), F32).at[bucket_count - 1].set(1.0),
        ],
        axis=1,
    )
    table = jnp.einsum("up,wp->uw", hot6, jnp.concatenate(diags, axis=0), precision=lax.Precision.HIGHEST)
    small = jnp.concatenate([ggain_attn.reshape(-1), ggain_ff.reshape(-1), table.reshape(-1)])
    small = small + swap(small, "core")

    (tokens,) = call(
        out_kernel,
        "out",
        [sds((seqs, 2, rows, d), BF)],
        [SM] + [HBM] * 23,
        [VM],
        [
            scratch((length, d), F32),
            scratch((3, length, 1024)),
            scratch((3, 4, 2, 384, 256)),
            DMA((32,)),
        ],
        (line.ids, hid, gin, *acts, *packs[0], *packs[1], *packs[2]),
    )
    tokens, small = gate(tokens, small)
    advance(line, (sums_a[1], "second"), (far_b, "pair"), (far_a, "finish"))
    small = small + swap(small, "side")
    tokens = lax.all_to_all(tokens, ("side", "core"), 0, 0, tiled=True)
    advance(line, (sums_a[1], "third"), (far_b, "back"))
    far_c = FarPairs([*sums_a[1].kept])
    (small,) = gate(small)
    small = small + swap(small, "near")
    advance(line, (far_c, "pair"), (far_b, "last"))
    if far_c.plain:
        small = lax.psum(small, "far")
    else:
        small = small + swap_far(small, 1)
    output, grad_inputs = call(
        tokens_kernel,
        "tokens",
        [sds((seqs, rows, d), BF), sds((seqs, rows, d), F32)],
        [SM, VM],
        [VM] * 2,
        [],
        (line.ids, tokens),
    )
    (output,) = gate(output)
    advance(line, (far_c, "back"), (far_b, "finish"), (far_a, None))
    share_in, share_back, share_o, grad_first = call(
        ff_shares_kernel,
        "ff_shares",
        [sds((sh, ffs), F32), sds(w_back.shape, F32), sds((sh, d), F32), sds((3, sh, 256), BF)],
        [SM] + [HBM] * 4,
        [VM] * 4,
        [scratch((2, 2 * (2 * sh + 384), 256)), scratch((2, 2 * sh + 384 + 3 * sh, 256)), DMA((16,))],
        (line.ids, *far_a.kept, *far_a.flying, *far_b.kept, *far_b.flying),
    )
    (share_in,) = gate(share_in)
    advance(line, (far_c, "last"))
    if not far_c.plain:
        (small,) = gate(small)
        small = small + swap_far(small, 2)
    advance(line, (far_c, "finish"))
    (small,) = gate(small)
    total_gain_attn, total_gain_ff = small[:d], small[d : 2 * d]
    total_table = small[2 * d :].reshape(bucket_count, heads)


    share_q, share_k, share_v = call(
        attn_shares_kernel,
        "attn_shares",
        [sds((sh, d), F32)] * 3,
        [SM, VM] + [HBM] * 2,
        [VM] * 3,
        [scratch((2, 3 * sh, 256)), DMA((8,))],
        (line.ids, grad_first, *far_c.kept, *far_c.flying),
    )
    return (
        output,
        grad_inputs,
        total_gain_attn,
        share_q,
        share_k,
        share_v,
        share_o,
        total_table,
        total_gain_ff,
        share_in,
        share_back,
    )


def solution(mesh):
    far = mesh.shape["rows"] // 2
    inner = jax.sharding.Mesh(mesh.devices.reshape(far, 2, 2, 2), AXES)
    over_rows, over_blk = ("far", "near"), ("side", "core")
    tok, row, rep = P(over_rows, over_blk, None), P(over_blk, None), P()
    return jax.shard_map(
        shards,
        mesh=inner,
        in_specs=(tok, P(over_rows, over_blk), rep, row, row, row, row, rep, rep, row, row, tok),
        out_specs=(tok, tok, rep, row, row, row, row, rep, rep, row, row),
        check_vma=False,
    )
```

```python
import functools

import jax
import jax.numpy as jnp
from jax import lax
from jax.experimental import pallas as pl
from jax.experimental.pallas import tpu as pltpu
from jax.sharding import PartitionSpec as P

EPS = 1e-06
EDGES = (1, 2, 3, 4, 5, 6, 7, 8, 12, 16, 23, 32, 46, 64, 91)
BF = jnp.bfloat16
F32 = jnp.float32
HBM = pl.BlockSpec(memory_space=pltpu.HBM)
VM = pl.BlockSpec(memory_space=pltpu.VMEM)
SM = pl.BlockSpec(memory_space=pltpu.SMEM)
DMA = pltpu.SemaphoreType.DMA
sds = jax.ShapeDtypeStruct
AXES = ("far", "near", "side", "core")
FLIPS = {"near": 4, "side": 2, "core": 1}


def scratch(shape, kind=BF):
    return pltpu.VMEM(shape, kind)


def call(kernel, name, outs, ins, out_specs, scratches, args, flops=10**10):
    return pl.pallas_call(
        kernel,
        out_shape=outs,
        in_specs=ins,
        out_specs=out_specs,
        scratch_shapes=scratches,
        compiler_params=pltpu.CompilerParams(vmem_limit_bytes=63 * 1024 * 1024),
        cost_estimate=pl.CostEstimate(flops=flops, bytes_accessed=4 * 10**7, transcendentals=0),
        name=name,
    )(*args)


def nn(a, b):
    return lax.dot_general(a, b, (((1,), (0,)), ((), ())), preferred_element_type=F32)


def nt(a, b):
    return lax.dot_general(a, b, (((1,), (1,)), ((), ())), preferred_element_type=F32)


def tn(a, b):
    return lax.dot_general(a, b, (((0,), (0,)), ((), ())), preferred_element_type=F32)


def swap(value, *axes):
    flip = sum(FLIPS[a] for a in axes)
    count = 1
    for a in AXES:
        count *= lax.axis_size(a)
    return lax.ppermute(value, AXES, [(i, i ^ flip) for i in range(count)])


def swap_far(value, bits):
    count = 8 * lax.axis_size("far")
    return lax.ppermute(value, AXES, [(i, i ^ (8 * bits)) for i in range(count)])


class Line:
    def __init__(self, ids):
        self.ids = ids

    def gate(self, *values):
        self.ids, *values = lax.optimization_barrier((self.ids, *values))
        return tuple(values)


def pick(arr, index, axis=0):
    return lax.dynamic_index_in_dim(arr, index, axis, keepdims=False)


def add_low(a, b):
    return (a.astype(F32) + b.astype(F32)).astype(BF)


class Sum:
    def __init__(self, keep, send):
        self.kept = (keep,)
        self.flying = (swap(send, "core"),)

    def first(self):
        (k,), (f,) = self.kept, self.flying
        return [((k, (p, i)), (f, (p, i))) for p in (0, 1) for i in (0, 1)], (None, "side", None, "near")

    def second(self):
        pairs = [((k, (i,)), (f, (i,))) for k, f in zip(self.kept, self.flying) for i in (0, 1)]
        return pairs, (None, "near", None, "side")

    def third(self):
        return [((k, ()), (f, ())) for k, f in zip(self.kept, self.flying)], (None, None)


def add_kernel(pairs, ids, *refs):
    n, outs, bufs, sems = len(refs) - 3 * len(pairs) - 1, None, None, refs[-1]
    outs, bufs = refs[n : n + len(pairs)], refs[n + len(pairs) : -1]
    dma = Copies(sems)
    cut = lambda ref, at: ref.at[at] if at else ref
    loads = [
        dma.start([(cut(refs[r], at), bufs[2 * i + j]) for j, (r, at) in enumerate(pair)])
        for i, pair in enumerate(pairs)
    ]
    stores = []
    for i in range(len(pairs)):
        wait(loads[i])
        a, b = bufs[2 * i], bufs[2 * i + 1]
        a[...] = a[...] + b[...]
        stores += dma.start([(a, outs[i])])
    wait(stores)


def add_all(line, pairs):
    arrays = []
    places = []
    for pair in pairs:
        place = []
        for arr, at in pair:
            known = [i for i, other in enumerate(arrays) if other is arr]
            if not known:
                arrays.append(arr)
            place.append((known[0] if known else len(arrays) - 1, at))
        places.append(tuple(place))
    shapes = [p[0][0].shape[len(p[0][1]) :] for p in pairs]
    return call(
        functools.partial(add_kernel, places),
        "add",
        [sds(s, BF) for s in shapes],
        [SM] + [HBM] * len(arrays),
        [HBM] * len(pairs),
        [scratch(s) for s in shapes for _ in (0, 1)] + [DMA((3 * len(pairs),))],
        (line.ids, *arrays),
    )


class FarPairs:
    ORDER = (0, 2, 1, 3)

    def __init__(self, parts):
        total = jnp.concatenate(parts, axis=0)
        self.plain = lax.axis_size("far") != 4
        if self.plain:
            self.kept, self.flying = (lax.psum(total, "far"),), ()
            return
        blocks = total.reshape(4, -1, 256)
        here = lax.axis_index("far")
        at = [pick(blocks, here ^ i) for i in range(4)]
        self.kept, self.flying = (jnp.stack([at[0], at[2]]),), (swap_far(jnp.stack([at[1], at[3]]), 1),)

    def pair(self):
        (kept,), (got,) = self.kept, self.flying
        return [((kept, (i,)), (got, (i,))) for i in (0, 1)], (None, 2)

    def back(self):
        return [((self.kept[0], ()), (self.flying[0], ()))], (0,)

    def last(self):
        both = jnp.stack([self.kept[0], self.flying[0]])
        self.kept, self.flying = (both,), (swap_far(both, 1),)
        return [], ()

    def finish(self):
        if not self.plain:
            self.kept = (jnp.concatenate([self.kept[0], self.flying[0]]),)
        self.flying = (swap(self.kept[0], "near"),)
        return [], ()


class FarBlocks(FarPairs):
    ORDER = (0, 1, 2, 3)

    def __init__(self, parts):
        total = jnp.concatenate(parts, axis=0)
        self.plain = lax.axis_size("far") != 4
        if self.plain:
            self.kept, self.flying = (lax.psum(total, "far"),), ()
            return
        blocks = total.reshape(4, -1, 256)
        here = lax.axis_index("far")
        self.kept = (pick(blocks, here),)
        self.flying = tuple(swap_far(pick(blocks, here ^ i), i) for i in (1, 2, 3))

    def back(self):
        total = self.kept[0].astype(F32)
        for f in self.flying:
            total = total + f.astype(F32)
        self.kept = (total.astype(BF),)
        self.flying = tuple(swap_far(self.kept[0], i) for i in (1, 2, 3))
        return [], ()

    def finish(self):
        if not self.plain:
            self.kept = (jnp.stack([self.kept[0], *self.flying]),)
        self.flying = (swap(self.kept[0], "near"),)
        return [], ()


def advance(line, *steps, new=()):
    landed = list(line.gate(*[f for piece, _ in steps for f in piece.flying], *new))
    jobs, pairs = [], []
    for piece, step in steps:
        piece.flying = tuple(landed.pop(0) for _ in piece.flying)
        if step is not None and not (step in ("pair", "back", "last") and piece.plain):
            more, where = getattr(piece, step)()
            if more:
                jobs.append((piece, where))
                pairs += more
    fresh = Sum(*landed) if new else None
    if not jobs:
        return fresh
    sums = list(add_all(line, pairs))
    line.gate(sums[0])
    for piece, where in jobs:
        kept, flying = [], []
        for place in where:
            s = sums.pop(0)
            if place is None:
                kept.append(s)
            elif isinstance(place, str):
                flying.append(swap(s, place))
            else:
                if place == 0:
                    kept.append(s)
                flying.append(swap_far(s, 2))
        piece.kept, piece.flying = tuple(kept), tuple(flying)
    return fresh


class Gather:
    def __init__(self, line, own, half):
        self.line, self.own = line, own
        self.y = swap(half, "side")
        self.core = swap(own, "core")

    def cross(self):
        self.y, self.core = self.line.gate(self.y, self.core)
        self.x = swap(self.y, "near")

    def relay(self):
        (self.x,) = self.line.gate(self.x)
        self.yc, self.xc = swap(self.y, "core"), swap(self.x, "core")

    def done(self):
        self.yc, self.xc = self.line.gate(self.yc, self.xc)
        return (self.own, self.core, self.y, self.x, self.yc, self.xc)


class Copies:
    def __init__(self, sems):
        self.sems, self.count = sems, 0

    def start(self, pairs):
        out = []
        for src, dst in pairs:
            out.append(pltpu.make_async_copy(src, dst, self.sems.at[self.count]))
            self.count += 1
            out[-1].start()
        return out


def wait(copies):
    for c in copies:
        c.wait()


def pieces_of(refs, me, half):
    own, core, y, x, yc, xc = refs
    out = []
    for h in (0, 1):
        out.append((own.at[h], me, h))
        out.append((core.at[h], me ^ 1, h))
    out.append((y, me ^ 2, half))
    out.append((x, me ^ 2, 1 - half))
    out.append((yc, me ^ 3, half))
    out.append((xc, me ^ 3, 1 - half))
    return out


def pack_copies(refs, me, half, dst, cut):
    return [(cut(ref), dst.at[o, h]) for ref, o, h in pieces_of(refs, me, half)]


def token_copies(slots, me, dst):
    rows = dst.shape[0] // 4
    return [
        (src, dst.at[pl.ds(pl.multiple_of((me ^ s) * rows, rows), rows)]) for s, src in enumerate(slots)
    ]


def put(stage, owner, row, value):
    half, count = stage.shape[2], value.shape[0]
    first = min(count, max(0, half - row))
    if first:
        stage[owner, 0, pl.ds(row, first), :] = value[:first]
    if first < count:
        stage[owner, 1, pl.ds(row + first - half, count - first), :] = value[first:]


def piece_copies(stage, keep, send, ids):
    me, near, core = ids[0], ids[1], ids[2]
    h = stage.shape[2] // 2
    out = []
    for dst, c in ((send, 1 - core), (keep, core)):
        for part in (0, 1):
            for first in (0, 1):
                for second in (0, 1):
                    sy, sx = (first, second) if part == 0 else (second, first)
                    owner = ((me ^ (2 * sy)) & 2) + c
                    out.append((stage.at[owner, near ^ sx, pl.ds(part * h, h)], dst.at[part, first, second]))
    return out


def piece_shapes(rows):
    return [sds((2, 2, 2, rows // 4, 256), BF)] * 2


def rows_of(blocks):
    return jnp.concatenate(blocks, axis=0)


def prep_a_kernel(ids, seg, inputs, wq, wk, wv, m0, m1, m2, m3, own0, own1, y0, y1, sems):
    me, half = ids[0], ids[1]
    rows = inputs.shape[1]
    part = wq.shape[0] // 2
    pairs = []
    for g in range(3):
        own, y, at = (own0, y0, 0) if g == 0 else (own1, y1, g - 1)
        for i, w in enumerate((wq, wk, wv)):
            cols, place = pl.ds(g * 256, 256), pl.ds((3 * at + i) * part, part)
            pairs.append((w.at[pl.ds(pl.multiple_of(half * part, 16), part), cols], y.at[place]))
            for h in (0, 1):
                pairs.append((w.at[pl.ds(h * part, part), cols], own.at[h, place]))
    for s, m in enumerate((m0, m1, m2, m3)):
        pairs.append((inputs.at[me ^ s], m.at[pl.ds(0, rows)]))
    copies = Copies(sems).start(pairs)
    for s, m in enumerate((m0, m1, m2, m3)):
        line = seg[pl.ds(me ^ s, 1), :].astype(F32)
        m[pl.ds(rows, 16), pl.ds(0, rows)] = jnp.broadcast_to(line, (16, rows)).astype(BF)
        m[pl.ds(rows, 16), pl.ds(rows, m.shape[1] - rows)] = jnp.zeros((16, m.shape[1] - rows), BF)
    wait(copies)


def prep_b_kernel(ids, w_in, w_back, w_out, cot, own0, own1, own2, y0, y1, y2, k1, k2, k3, sems):
    me, half = ids[0], ids[1]
    hw = w_in.shape[0] // 2
    pairs = [(cot.at[me ^ s], k) for s, k in ((1, k1), (2, k2), (3, k3))]
    for c, (own, y) in enumerate(((own0, y0), (own1, y1), (own2, y2))):
        for dst, h in ((y, half), (own.at[0], 0), (own.at[1], 1)):
            for b in range(4):
                pairs.append((
                    w_in.at[pl.ds(pl.multiple_of(h * hw, 16), hw), pl.ds(b * 768 + c * 256, 256)],
                    dst.at[pl.ds(b * hw, hw)],
                ))
            for j in range(3):
                pairs.append((
                    w_back.at[pl.ds(pl.multiple_of(c * 256 + h * 128, 16), 128), pl.ds(j * 256, 256)],
                    dst.at[pl.ds(4 * hw + j * 128, 128)],
                ))
                if c == 0:
                    pairs.append((
                        w_out.at[pl.ds(pl.multiple_of(h * hw, 16), hw), pl.ds(j * 256, 256)],
                        dst.at[pl.ds(4 * hw + 384 + j * hw, hw)],
                    ))
    wait(Copies(sems).start(pairs))


def norm_kernel(ids, m0, m1, m2, m3, gain, xs, nrm, nrm_t, seg, sbuf, sems):
    me = ids[0]
    rows = xs.shape[0] // 4
    slots = (m0, m1, m2, m3)
    tok = token_copies([m.at[pl.ds(0, rows)] for m in slots], me, xs)
    tok += token_copies([m.at[pl.ds(rows, 16)] for m in slots], me, sbuf)
    wait(Copies(sems).start(tok))
    seg[...] = jnp.concatenate(
        [sbuf[pl.ds(o * 16, 1), pl.ds(0, rows)].astype(F32) for o in range(4)], axis=1
    )
    for a in range(4):
        x = xs[pl.ds(a * rows, rows), :].astype(F32)
        y = x * lax.rsqrt(jnp.mean(x * x, axis=-1, keepdims=True) + EPS) * gain[...]
        y = y.astype(BF)
        nrm[pl.ds(a * rows, rows), :] = y
        nrm_t[:, pl.ds(a * rows, rows)] = y.T


def half_masks(t):
    lane = lax.broadcasted_iota(jnp.int32, (t, 128), 1)
    return lane < 64, (lane < 64).astype(F32).astype(BF), (lane >= 64).astype(F32).astype(BF)


def attn_fwd_kernel(group, ids, far, seg, lines, nrm_in, w0, w1, w2, w3, w4, w5,
                    q_out, k_out, v_out, p_out, o, near, nrm, wbuf, q, k, v, p, sems):
    me, half = ids[0], ids[1]
    dma = Copies(sems)
    count = wbuf.shape[2]
    part = count // 3
    place = pl.ds(max(group - 1, 0) * count, count)
    loads = dma.start(
        [(nrm_in, nrm)]
        + pack_copies((w0, w1, w2, w3, w4, w5), me, half, wbuf, lambda ref: ref.at[place])
    )
    for head in range(4):
        line = jnp.broadcast_to(lines[pl.ds(4 * group + head, 1), :], (near.shape[1], lines.shape[1]))
        near[head] = pltpu.roll(line, 0, 1, stride=1, stride_axis=0)[:, : near.shape[2]]
    t = near.shape[1]
    length = q.shape[0]
    nblk = length // t
    low, m0, m1 = half_masks(t)
    eye = lax.broadcasted_iota(jnp.int32, (t, t), 0) == lax.broadcasted_iota(jnp.int32, (t, t), 1)
    seg_row = seg[...]
    wait(loads)
    stores = []
    for i, (buf, out) in enumerate(((q, q_out), (k, k_out), (v, v_out))):
        w = rows_of([wbuf[ow, h, pl.ds(i * part, part), :] for ow in range(4) for h in (0, 1)])
        buf[...] = nn(nrm[...], w).astype(BF)
        stores += dma.start([(buf, out)])
    for pair in (0, 1):
        at = pl.ds(pair * 128, 128)
        for a in range(nblk):
            seg_col = jnp.sum(
                jnp.where(eye, jnp.broadcast_to(seg_row[:, a * t : (a + 1) * t], (t, t)), 0.0),
                axis=1,
                keepdims=True,
            )
            allowed = seg_col == seg_row
            q2 = q[pl.ds(a * t, t), at]
            s = nt(rows_of([q2 * m0, q2 * m1]), k[:, at])
            ps = []
            for h in (0, 1):
                head = 2 * pair + h
                strip = []
                for b in range(nblk):
                    rel = b - a
                    if abs(rel) <= 1:
                        strip.append(near[head, :, (rel + 1) * t : (rel + 2) * t])
                    else:
                        strip.append(jnp.full((t, t), far[int(rel > 0), group * 4 + head], F32))
                sh = s[h * t : (h + 1) * t] + jnp.concatenate(strip, axis=1)
                sh = jnp.where(allowed, sh, -1e30)
                top = jnp.max(sh, axis=-1, keepdims=True)
                e = jnp.exp(sh - top)
                inv = 1.0 / jnp.sum(e, axis=-1, keepdims=True)
                ph = (e * inv).astype(BF)
                p[head, pl.ds(a * t, t), :] = ph
                ps.append(ph)
            mix = nn(rows_of(ps), v[:, at])
            o[pl.ds(a * t, t), at] = jnp.where(low, mix[:t], mix[t:]).astype(BF)
        stores += dma.start([(p.at[pl.ds(2 * pair, 2)], p_out.at[pl.ds(2 * pair, 2)])])
    wait(stores)


def out_weight(wbuf, j):
    hw = wbuf.shape[2] // 3
    return rows_of([wbuf[o, h, pl.ds(j * hw, hw), :] for o in range(4) for h in (0, 1)])


def out_cut(sh):
    return lambda ref: ref.at[pl.ds(2 * sh + 384, 3 * (sh // 2))]


def gelu_both(x):
    c = 0.7978845608028654
    x2 = x * x
    th = jnp.tanh(x * (c + (c * 0.044715) * x2))
    half_up = 0.5 + 0.5 * th
    slope = half_up + x * (0.5 - 0.5 * th * th) * (c + (3.0 * c * 0.044715) * x2)
    return x * half_up, slope


def ffn_kernel(lead, ids, *refs):
    if lead:
        gain, xs, x0, x1, x2, cown, c1, c2, c3, p0, p1, p2, p3, p4, p5, *rest = refs
        hid_out, ff_out, fft_out, act_out, gpre_out, keep, send, *rest = rest
        xv, mx, wout, hid, ffv, fftv, cot, pack, act, gpre, stage, sems = rest
    else:
        ff, ff_t, cown, c1, c2, c3, p0, p1, p2, p3, p4, p5, act_out, gpre_out, keep, send, *rest = refs
        ffv, fftv, cot, pack, act, gpre, stage, sems = rest
    me, half = ids[0], ids[1]
    d = ffv.shape[1]
    sh = d // 4
    hw = sh // 2
    packs = (p0, p1, p2, p3, p4, p5)
    dma = Copies(sems)
    weights = pack_copies(packs, me, half, pack, lambda ref: ref.at[pl.ds(0, 4 * hw + 384)])
    stores = []
    if lead:
        early = dma.start(
            pack_copies(packs, me, half, wout, out_cut(sh))
            + [(x, mx.at[:, pl.ds(i * 256, 256)]) for i, x in enumerate((x0, x1, x2))]
            + [(xs, xv)]
        )
        first = dma.start(weights)
    else:
        first = dma.start([(ff, ffv)] + weights)
    second = dma.start(token_copies((cown.at[me], c1, c2, c3), me, cot))
    if lead:
        third = ()
        wait(early)
        for j in range(3):
            cols = pl.ds(j * 256, 256)
            hid[:, cols] = xv[:, cols].astype(F32) + nn(mx[...], out_weight(wout, j))
        rows = 128
        for a in range(xv.shape[0] // rows):
            x = hid[pl.ds(a * rows, rows), :]
            y = x * lax.rsqrt(jnp.mean(x * x, axis=-1, keepdims=True) + EPS) * gain[...]
            y = y.astype(BF)
            ffv[pl.ds(a * rows, rows), :] = y
            fftv[:, pl.ds(a * rows, rows)] = y.T
        stores += dma.start([(hid, hid_out), (ffv, ff_out), (fftv, fft_out)])
    else:
        third = dma.start([(ff_t, fftv)])
    wait(first)
    for b in range(5):
        if b < 4:
            at = pl.ds(b * 256, 256)
            win = rows_of([pack[o, h, pl.ds(b * hw, hw), :] for o in range(4) for h in (0, 1)])
            value, slope = gelu_both(nn(ffv[...], win))
            if b == 0:
                wait(second)
            act[:, at] = value.astype(BF)
            back = 0.0
            for j in range(3):
                wb = rows_of([pack[b, h, pl.ds(4 * hw + j * 128, 128), :] for h in (0, 1)])
                back = back + nt(cot[:, pl.ds(j * 256, 256)], wb)
            gpre[:, at] = (back * slope).astype(BF)
        if b == 3:
            stores += dma.start([(act, act_out), (gpre, gpre_out)])
        if b > 0:
            c = b - 1
            at = pl.ds(c * 256, 256)
            if c == 0:
                wait(third)
            gw = nn(fftv[...], gpre[:, at]).astype(BF)
            for o in range(4):
                put(stage, o, c * sh, gw[o * sh : (o + 1) * sh])
            gb = tn(act[:, at], cot[...]).astype(BF)
            for j in range(3):
                put(stage, c, 4 * sh + j * 256, gb[:, j * 256 : (j + 1) * 256])
    stores += dma.start(piece_copies(stage, keep, send, ids))
    wait(stores)


def after_ff_kernel(ids, gain, hid, g0, g1, g2, cown, c1, c2, c3, x0, x1, x2, *refs):
    packs = (refs[0:6], refs[6:12], refs[12:18])
    ghid, gm0, gm1, gm2, ggain, gwo, hidv, gv, cot, mx, wbuf, wins, ga, gf, sems = refs[18:]
    me, half = ids[0], ids[1]
    d = hid.shape[1]
    sh = d // 4
    hw = sh // 2
    rows = cot.shape[0] // 4
    dma = Copies(sems)
    loads = [
        dma.start(
            [(g, gv.at[c])]
            + pack_copies(packs[c], me, half, wins.at[c], lambda ref: ref.at[pl.ds(0, 4 * hw)])
        )
        for c, g in enumerate((g0, g1, g2))
    ]
    rest = dma.start([(hid, hidv)] + token_copies((cown.at[me], c1, c2, c3), me, cot))
    last = dma.start(
        pack_copies(packs[0], me, half, wbuf, out_cut(sh))
        + [(x, mx.at[:, pl.ds(i * 256, 256)]) for i, x in enumerate((x0, x1, x2))]
    )
    for c in range(3):
        wait(loads[c])
        acc = None
        for b in range(4):
            w = rows_of([wins[c, o, h, pl.ds(b * hw, hw), :] for o in range(4) for h in (0, 1)])
            term = nt(gv[c, :, pl.ds(b * 256, 256)], w)
            acc = term if acc is None else acc + term
        gf[...] = acc if c == 0 else gf[...] + acc
    wait(rest)
    total = jnp.zeros((1, d), F32)
    for a in range(4):
        at = pl.ds(a * rows, rows)
        x = hidv[at, :]
        gfa = gf[at, :]
        n = lax.rsqrt(jnp.mean(x * x, axis=-1, keepdims=True) + EPS)
        g = gfa * gain[...]
        xn = x * n
        total = total + jnp.sum(gfa * xn, axis=0, keepdims=True)
        gh = cot[at, :].astype(F32) + n * (g - xn * (n * jnp.mean(g * x, axis=-1, keepdims=True)))
        ghid[at, :] = gh
        ga[at, :] = gh.astype(BF)
    ggain[...] = total
    wait(last)
    acc = None
    for j in range(3):
        term = nt(ga[:, pl.ds(j * 256, 256)], out_weight(wbuf, j))
        acc = term if acc is None else acc + term
    for i, gm in enumerate((gm0, gm1, gm2)):
        gm[...] = acc[:, i * 256 : (i + 1) * 256].astype(BF)
    for j in range(3):
        gw = tn(mx[...], ga[:, pl.ds(j * 256, 256)]).astype(BF)
        for o in range(4):
            gwo[o, pl.ds(j * sh, sh), :] = gw[o * sh : (o + 1) * sh]


def out_kernel(ids, hid, gin, a0, a1, a2, *refs):
    packs = (refs[0:6], refs[6:12], refs[12:18])
    out, hidv, av, wb, sems = refs[18:]
    me, half = ids[0], ids[1]
    d = hid.shape[1]
    hw = d // 8
    rows = hid.shape[0] // 4
    dma = Copies(sems)
    loads = [
        dma.start(
            [(a, av.at[c])]
            + pack_copies(packs[c], me, half, wb.at[c], lambda ref: ref.at[pl.ds(4 * hw, 384)])
        )
        for c, a in enumerate((a0, a1, a2))
    ]
    last = dma.start([(hid, hidv)])
    grads = dma.start([(gin.at[pl.ds(b * rows, rows)], out.at[b, 1]) for b in range(4)])
    for c in range(3):
        wait(loads[c])
    wait(last)
    for j in range(3):
        cols = pl.ds(j * 256, 256)
        acc = hidv[:, cols]
        for c in range(3):
            w = rows_of([wb[c, o, h, pl.ds(j * 128, 128), :] for o in range(4) for h in (0, 1)])
            acc = acc + nn(av[c], w)
        acc = acc.astype(BF)
        for b in range(4):
            out[b, 0, :, cols] = acc[b * rows : (b + 1) * rows]
    wait(grads)


def diagonals(x):
    width = x.shape[1]
    y = x[0:8]
    for a in range(8, x.shape[0], 8):
        y = y + pltpu.roll(x[a : a + 8], width - a, 1)
    sub = lax.broadcasted_iota(jnp.int32, y.shape, 0)
    for bit in (1, 2, 4):
        y = jnp.where((sub & bit) != 0, pltpu.roll(y, width - bit, 1), y)
    return jnp.sum(y, axis=0, keepdims=True)


def attn_bwd_kernel(plain, carried, ids, q_in, k_in, v_in, p_in, gm_in, nrm_in, *refs):
    carry, refs = refs[:carried], refs[carried:]
    grad, refs = refs[: 1 if plain else 2], refs[1 if plain else 2 :]
    (dq_out, dk_out, dv_out, diag, q, k, v, p, gm, nrm_t, dq, dk, dv, acc, stage, sems) = refs
    t = 128
    length = q.shape[0]
    nblk = length // t
    low, m0, m1 = half_masks(t)
    dma = Copies(sems)
    first = dma.start([(v_in, v), (gm_in, gm), (p_in.at[pl.ds(0, 2)], p.at[pl.ds(0, 2)]), (k_in, k), (q_in, q)])
    second = dma.start([(p_in.at[pl.ds(2, 2)], p.at[pl.ds(2, 2)])])
    third = dma.start([(nrm_in, nrm_t)])
    base, half = 0, stage.shape[2]
    for g in carry:
        count = g.shape[1]
        inside = min(count, half - base) if base < half else 0
        if inside:
            third += dma.start([(g.at[:, pl.ds(0, inside)], stage.at[:, 0, pl.ds(base, inside)])])
        if inside < count:
            rest, at = count - inside, max(0, base - half)
            third += dma.start([(g.at[:, pl.ds(inside, rest)], stage.at[:, 1, pl.ds(at, rest)])])
        base += count
    wait(first)
    for pair in (0, 1):
        if pair == 1:
            wait(second)
        cols = pl.ds(pair * 128, 128)
        k2, v2 = k[:, cols], v[:, cols]
        dk_t = jnp.zeros((128, length), F32)
        dv_t = jnp.zeros((128, length), F32)
        for a in range(nblk):
            at = pl.ds(a * t, t)
            q2, g2 = q[at, cols], gm[at, cols]
            qm = rows_of([q2 * m0, q2 * m1])
            g_both = rows_of([g2 * m0, g2 * m1])
            dp = nt(g_both, v2)
            pb = rows_of([p[2 * pair, at, :], p[2 * pair + 1, at, :]])
            pf = pb.astype(F32)
            delta = jnp.sum(pf * dp, axis=-1, keepdims=True)
            ds = (pf * (dp - delta)).astype(BF)
            mq = nn(ds, k2)
            dq[at, cols] = jnp.where(low, mq[:t], mq[t:]).astype(BF)
            dk_t = dk_t + tn(qm, ds)
            dv_t = dv_t + tn(g_both, pb)
            dsf = ds.astype(F32)
            for h in (0, 1):
                for b in range(nblk):
                    rel = b - a
                    place = rel + 1 if abs(rel) <= 1 else (3 if rel < 0 else 4)
                    tile = dsf[h * t : (h + 1) * t, b * t : (b + 1) * t]
                    lanes = pl.ds(place * t, t)
                    if (a, b) in ((1, 0), (0, 0), (0, 1), (2, 0), (0, 2)):
                        acc[h, :, lanes] = tile
                    else:
                        acc[h, :, lanes] += tile
        dk[:, cols] = dk_t.T.astype(BF)
        dv[:, cols] = dv_t.T.astype(BF)
        for h in (0, 1):
            near = jnp.concatenate([acc[h, :, pl.ds(0, 3 * t)], jnp.zeros((t, t), F32)], axis=1)
            far = jnp.sum(acc[h, :, pl.ds(3 * t, 2 * t)], axis=0, keepdims=True)
            diag[pl.ds(2 * pair + h, 1), :] = jnp.concatenate([diagonals(near), far], axis=1)
    stores = dma.start([(dq, dq_out), (dk, dk_out), (dv, dv_out)])
    wait(third)
    sh = nrm_t.shape[0] // 4
    for i, g in enumerate((dq, dk, dv)):
        gw = nn(nrm_t[...], g[...]).astype(BF)
        for o in range(4):
            put(stage, o, base + i * sh, gw[o * sh : (o + 1) * sh])
    if plain:
        stores += dma.start([(stage.at[:, h], grad[0].at[:, pl.ds(h * half, half)]) for h in (0, 1)])
    else:
        stores += dma.start(piece_copies(stage, *grad, ids))
    wait(stores)


def first_norm_kernel(ids, gain, xs, ghid, *refs):
    ins = refs[0:9]
    w0, w1 = refs[9:15], refs[15:21]
    gi, ggain, xv, gv, dall, wbuf0, wbuf1, gn, sems = refs[21:]
    me, half = ids[0], ids[1]
    d = xs.shape[1]
    rows = xs.shape[0] // 4
    dma = Copies(sems)
    loads = dma.start(
        [(g, dall.at[n]) for n, g in enumerate(ins)]
        + pack_copies(w0, me, half, wbuf0, lambda ref: ref)
        + pack_copies(w1, me, half, wbuf1, lambda ref: ref)
    )
    part = wbuf0.shape[2] // 3
    rest = dma.start([(xs, xv), (ghid, gv)])
    wait(loads)
    acc = None
    for i in range(3):
        for c in range(3):
            buf, at = (wbuf0, i) if c == 0 else (wbuf1, 3 * (c - 1) + i)
            wi = rows_of([buf[o, h, pl.ds(at * part, part), :] for o in range(4) for h in (0, 1)])
            term = nt(dall[3 * i + c], wi)
            acc = term if acc is None else acc + term
    gn[...] = acc
    wait(rest)
    total = jnp.zeros((1, d), F32)
    for a in range(4):
        at = pl.ds(a * rows, rows)
        x = xv[at, :].astype(F32)
        gf = gn[at, :]
        n = lax.rsqrt(jnp.mean(x * x, axis=-1, keepdims=True) + EPS)
        g = gf * gain[...]
        xn = x * n
        total = total + jnp.sum(gf * xn, axis=0, keepdims=True)
        gi[at, :] = (gv[at, :] + n * (g - xn * (n * jnp.mean(g * x, axis=-1, keepdims=True)))).astype(BF)
    ggain[...] = total


def tokens_kernel(ids, tokens, out, gin):
    out[...] = tokens[:, 0]
    gin[...] = tokens[:, 1].astype(F32)


def half_copies(ref, dst, far, order):
    if ref.shape == dst.shape:
        return [(ref, dst)]
    n = ref.shape[1]
    return [(ref.at[i], dst.at[pl.ds(pl.multiple_of((far ^ b) * n, 16), n)]) for i, b in enumerate(order)]


def ff_shares_kernel(ids, za, xa, zb, xb, out_in, out_back, buf_a, buf_b, sems):
    here, far = ids[1], ids[3]
    sh = out_in.shape[0]
    order = FarPairs.ORDER
    copies = []
    for z, x, buf in ((za, xa, buf_a), (zb, xb, buf_b)):
        copies += half_copies(z, buf.at[here], far, order) + half_copies(x, buf.at[1 - here], far, order)
    wait(Copies(sems).start(copies))
    half = 2 * sh + 384
    for k, buf, at in ((0, buf_a, 0), (1, buf_a, half), (2, buf_b, 0)):
        for b in range(4):
            out_in[:, pl.ds((b * 3 + k) * 256, 256)] = buf[0, pl.ds(at + b * sh, sh), :].astype(F32)
        for j in range(3):
            out_back[pl.ds(k * 256, 256), pl.ds(j * 256, 256)] = buf[1, pl.ds(at + j * 256, 256), :].astype(F32)


def attn_shares_kernel(ids, z, x, wq, wk, wv, wo, buf, sems):
    here, far = ids[1], ids[3]
    sh = wq.shape[0]
    order = FarBlocks.ORDER
    copies = half_copies(z, buf.at[here], far, order) + half_copies(x, buf.at[1 - here], far, order)
    wait(Copies(sems).start(copies))
    at = lambda half, n: buf[half, pl.ds(n * sh, sh), :].astype(F32)
    for i in range(3):
        wo[:, pl.ds(i * 256, 256)] = at(0, i)
    for i, out in enumerate((wq, wk, wv)):
        out[:, pl.ds(0, 256)] = at(1, i)
        out[:, pl.ds(256, 256)] = at(0, 3 + i)
        out[:, pl.ds(512, 256)] = at(1, 3 + i)


def bucket_of(offset, bucket_count):
    distance = jnp.abs(offset)
    bucket = jnp.where(offset > 0, bucket_count // 2, 0).astype(jnp.int32)
    for edge in EDGES:
        bucket = bucket + (distance >= edge).astype(jnp.int32)
    return bucket


def shards(inputs, segments, gain_attn, w_query, w_key, w_value, w_out, bucket_bias_table, gain_ff, w_in, w_back, cotangent):
    seqs, rows, d = inputs.shape
    sh = w_query.shape[0]
    hw = sh // 2
    ffs = w_in.shape[1]
    bucket_count, heads = bucket_bias_table.shape
    length = rows * seqs
    places = [lax.axis_index(a).astype(jnp.int32) for a in ("near", "side", "core", "far")]
    near_at, side_at, core_at, far_at = places
    line = Line(jnp.stack([2 * side_at + core_at, near_at, core_at, far_at]))
    gate = line.gate
    row_low, row_f32 = sds((length, d), BF), sds((length, d), F32)
    quad_low, tok_low = sds((length, 256), BF), sds((rows, d), BF)
    gain1, gain2 = gain_attn.reshape(1, d), gain_ff.reshape(1, d)
    pack_rows = [4 * hw + 384 + 3 * hw, 4 * hw + 384, 4 * hw + 384]

    m0, m1, m2, m3, own_a, own_b, y_a, y_b = call(
        prep_a_kernel,
        "prep_a",
        [sds((rows + 16, d), BF)] * 4
        + [sds((2, 3 * hw, 256), BF), sds((2, 6 * hw, 256), BF), sds((3 * hw, 256), BF), sds((6 * hw, 256), BF)],
        [SM, VM] + [HBM] * 4,
        [VM] * 8,
        [DMA((31,))],
        (line.ids, segments, inputs, w_query, w_key, w_value),
    )
    wa = Gather(line, own_a, y_a)
    msgs = [swap(m1, "core"), swap(m2, "side"), swap(m3, "side", "core")]
    wb = Gather(line, own_b, y_b)

    own0, own1, own2, y0, y1, y2, k1, k2, k3 = call(
        prep_b_kernel,
        "prep_b",
        [sds((2, r, 256), BF) for r in pack_rows] + [sds((r, 256), BF) for r in pack_rows] + [tok_low] * 3,
        [SM] + [HBM] * 4,
        [VM] * 9,
        [DMA((75,))],
        (line.ids, w_in, w_back, w_out, cotangent),
    )

    (own0,) = gate(own0)
    wa.cross()
    *msgs, table_in = gate(*msgs, bucket_bias_table)
    wa.relay()

    offs = jnp.arange(4 * rows, dtype=jnp.int32)
    offs = jnp.where(offs < 3 * rows, offs - rows, offs - 5 * rows)
    hot = (bucket_of(offs, bucket_count)[None] == jnp.arange(bucket_count, dtype=jnp.int32)[:, None]).astype(F32)
    lines = jnp.einsum("up,uw->wp", hot, table_in, precision=lax.Precision.HIGHEST)
    far = jnp.stack([table_in[bucket_count // 2 - 1], table_in[bucket_count - 1]])

    y0, own0 = gate(y0, own0)
    wf = [Gather(line, own0, y0)]
    xs, nrm, nrm_t, seg = call(
        norm_kernel,
        "norm",
        [row_low, row_low, sds((d, length), BF), sds((1, length), F32)],
        [SM] + [HBM] * 4 + [VM],
        [VM] * 4,
        [scratch((64, d)), DMA((8,))],
        (line.ids, m0, *msgs, gain1),
    )
    nrm, lines = gate(nrm, lines)
    wb.cross()
    wa = wa.done()

    qs, ks, vs, probs, mixed = [], [], [], [], []
    for g in range(3):
        q, k, v, p, mx = call(
            functools.partial(attn_fwd_kernel, g),
            "attn_fwd",
            [quad_low] * 3 + [sds((4, length, length), BF), quad_low],
            [SM, SM, VM, VM] + [HBM] * 7,
            [HBM] * 4 + [VM],
            [
                scratch((4, rows, 3 * rows), F32),
                scratch((length, d)),
                scratch((4, 2, 3 * hw, 256)),
                scratch((length, 256)),
                scratch((length, 256)),
                scratch((length, 256)),
                scratch((4, length, length)),
                DMA((15,)),
            ],
            (line.ids, far, seg, lines, nrm, *(wa if g == 0 else wb)),
        )
        (mx,) = gate(mx)
        for have, new in ((qs, q), (ks, k), (vs, v), (probs, p), (mixed, mx)):
            have.append(new)
        if g == 0:
            wb.relay()
            wf[0].cross()
            own1, y1 = gate(own1, y1)
            wf.append(Gather(line, own1, y1))
            wb = wb.done()
        if g == 1:
            wf[0].relay()
            wf[1].cross()
            k1, k2, k3 = gate(k1, k2, k3)
            cots = [swap(k1, "core"), swap(k2, "side"), swap(k3, "side", "core")]
    packs = [wf[0].done()]
    cots = gate(*cots)
    wf[1].relay()
    own2, y2 = gate(own2, y2)
    wf.append(Gather(line, own2, y2))

    sums_f, acts, gpres = [], [], []
    for c in range(3):
        lead = c == 0
        *fresh, act, gpre, keep, send = call(
            functools.partial(ffn_kernel, lead),
            "ffn",
            ([row_f32, row_low, sds((d, length), BF)] if lead else [])
            + [sds((length, 1024), BF)] * 2
            + piece_shapes(4 * sh + 768),
            [SM] + ([VM] + [HBM] * 4 if lead else [HBM] * 2) + [HBM] * 10,
            [HBM] * (7 if lead else 4),
            (
                [scratch((length, d)), scratch((length, d)), scratch((4, 2, 3 * hw, 256)), scratch((length, d), F32)]
                if lead
                else []
            )
            + [
                scratch((length, d)),
                scratch((d, length)),
                scratch((length, d)),
                scratch((4, 2, 4 * hw + 384, 256)),
                scratch((length, 1024)),
                scratch((length, 1024)),
                scratch((4, 2, 2 * sh + 384, 256)),
                DMA((52,)),
            ],
            (line.ids, *((gain2, xs, *mixed) if lead else (ff, ff_t)), cotangent, *cots, *packs[c]),
        )
        if lead:
            hid, ff, ff_t = fresh
        piece = (keep, send)
        acts.append(act)
        (gpre,) = gate(gpre)
        gpres.append(gpre)
        if c == 0:
            packs.append(wf[1].done())
            wf[2].cross()
        if c == 1:
            wf[2].relay()
        moves = [[], [("first",)], [("second",), ("first",)]][c]
        sums_f.append(advance(line, *[(f, *m) for f, m in zip(sums_f, moves)], new=piece))
        if c == 1:
            packs.append(wf[2].done())

    ghid, *gmix, ggain_ff, gwo = call(
        after_ff_kernel,
        "after_ff",
        [row_f32] + [quad_low] * 3 + [sds((1, d), F32), sds((4, 3 * sh, 256), BF)],
        [SM, VM] + [HBM] * 29,
        [VM] * 6,
        [
            scratch((length, d), F32),
            scratch((3, length, 1024)),
            scratch((length, d)),
            scratch((length, d)),
            scratch((4, 2, 3 * hw, 256)),
            scratch((3, 4, 2, 4 * hw, 256)),
            scratch((length, d)),
            scratch((length, d), F32),
            DMA((43,)),
        ],
        (line.ids, gain2, hid, *gpres, cotangent, *cots, *mixed, *packs[0], *packs[1], *packs[2]),
    )
    gmix[0], ggain_ff = gate(gmix[0], ggain_ff)
    advance(line, (sums_f[0], "third"), (sums_f[1], "second"), (sums_f[2], "first"))

    dqs, dks, dvs, diags, sums_a = [], [], [], [], []
    part = sds((4, 3 * sh, 256), BF)
    for g in range(3):
        plain = g == 1
        carry = () if plain else (gwo if g == 0 else grads,)
        body = 3 * sh * (1 + len(carry))
        *grad, dq, dk, dv, diag = call(
            functools.partial(attn_bwd_kernel, plain, len(carry)),
            "attn_bwd",
            ([part] if plain else piece_shapes(body)) + [quad_low] * 3 + [sds((4, 6 * rows), F32)],
            [SM] + [HBM] * (6 + len(carry)),
            [HBM] * ((1 if plain else 2) + 3) + [VM],
            [scratch((length, 256))] * 3
            + [scratch((4, length, length)), scratch((length, 256)), scratch((d, length))]
            + [scratch((length, 256))] * 3
            + [scratch((2, rows, 5 * rows), F32), scratch((4, 2, body // 2, 256)), DMA((32,))],
            (line.ids, qs[g], ks[g], vs[g], probs[g], gmix[g], nrm_t, *carry),
        )
        (dq,) = gate(dq)
        for have, new in ((dqs, dq), (dks, dk), (dvs, dv), (diags, diag)):
            have.append(new)
        if g == 0:
            sums_a.append(advance(line, (sums_f[1], "third"), (sums_f[2], "second"), new=grad))
            far_a = FarPairs([*sums_f[0].kept, *sums_f[1].kept])
        if g == 1:
            grads = grad[0]
            advance(line, (sums_a[0], "first"), (sums_f[2], "third"), (far_a, "pair"))
            far_b = FarPairs([*sums_f[2].kept])
        if g == 2:
            sums_a.append(advance(line, (sums_a[0], "second"), (far_a, "back"), (far_b, "pair"), new=grad))

    advance(line, (sums_a[1], "first"), (sums_a[0], "third"), (far_a, "last"))
    gin, ggain_attn = call(
        first_norm_kernel,
        "first_norm",
        [row_low, sds((1, d), F32)],
        [SM, VM] + [HBM] * 23,
        [VM] * 2,
        [
            scratch((length, d)),
            scratch((length, d), F32),
            scratch((9, length, 256)),
            scratch((4, 2, 3 * hw, 256)),
            scratch((4, 2, 6 * hw, 256)),
            scratch((length, d), F32),
            DMA((27,)),
        ],
        (line.ids, gain1, xs, ghid, *dqs, *dks, *dvs, *wa, *wb),
    )
    (gin,) = gate(gin)
    advance(line, (sums_a[1], "second"), (far_a, "finish"), (far_b, "back"))

    (tokens,) = call(
        out_kernel,
        "out",
        [sds((seqs, 2, rows, d), BF)],
        [SM] + [HBM] * 23,
        [VM],
        [
            scratch((length, d), F32),
            scratch((3, length, 1024)),
            scratch((3, 4, 2, 384, 256)),
            DMA((32,)),
        ],
        (line.ids, hid, gin, *acts, *packs[0], *packs[1], *packs[2]),
    )
    tokens, ggain_attn = gate(tokens, ggain_attn)
    tokens = lax.all_to_all(tokens, ("side", "core"), 0, 0, tiled=True)
    advance(line, (sums_a[1], "third"), (far_b, "last"))
    far_c = FarBlocks([*sums_a[0].kept, *sums_a[1].kept])

    hot6 = jnp.concatenate(
        [
            hot,
            jnp.zeros((bucket_count, rows), F32).at[bucket_count // 2 - 1].set(1.0),
            jnp.zeros((bucket_count, rows), F32).at[bucket_count - 1].set(1.0),
        ],
        axis=1,
    )
    table = jnp.einsum("up,wp->uw", hot6, jnp.concatenate(diags, axis=0), precision=lax.Precision.HIGHEST)
    small = jnp.concatenate([ggain_attn.reshape(-1), ggain_ff.reshape(-1), table.reshape(-1)])
    small = small + swap(small, "core")

    advance(line, (far_c, "back"), (far_b, "finish"), (far_a, None))
    (small,) = gate(small)
    small = small + swap(small, "near")
    advance(line, (far_c, "finish"))
    tokens, small = gate(tokens, small)
    small = small + swap(small, "side")

    output, grad_inputs = call(
        tokens_kernel,
        "tokens",
        [sds((seqs, rows, d), BF), sds((seqs, rows, d), F32)],
        [SM, VM],
        [VM] * 2,
        [],
        (line.ids, tokens),
    )
    output, small = gate(output, small)
    small = lax.psum(small, "far") if far_c.plain else small + swap_far(small, 1)
    far_b.flying = gate(*far_b.flying)
    share_in, share_back = call(
        ff_shares_kernel,
        "ff_shares",
        [sds((sh, ffs), F32), sds(w_back.shape, F32)],
        [SM] + [HBM] * 4,
        [VM] * 2,
        [scratch((2, 2 * (2 * sh + 384), 256)), scratch((2, 2 * sh + 384, 256)), DMA((16,))],
        (line.ids, *far_a.kept, *far_a.flying, *far_b.kept, *far_b.flying),
    )
    share_in, small = gate(share_in, small)
    if not far_c.plain:
        small = small + swap_far(small, 2)
    (small,) = gate(small)
    total_gain_attn, total_gain_ff = small[:d], small[d : 2 * d]
    total_table = small[2 * d :].reshape(bucket_count, heads)


    share_q, share_k, share_v, share_o = call(
        attn_shares_kernel,
        "attn_shares",
        [sds((sh, d), F32)] * 4,
        [SM] + [HBM] * 2,
        [VM] * 4,
        [scratch((2, 6 * sh, 256)), DMA((8,))],
        (line.ids, *far_c.kept, *far_c.flying),
    )
    return (
        output,
        grad_inputs,
        total_gain_attn,
        share_q,
        share_k,
        share_v,
        share_o,
        total_table,
        total_gain_ff,
        share_in,
        share_back,
    )


def solution(mesh):
    far = mesh.shape["rows"] // 2
    inner = jax.sharding.Mesh(mesh.devices.reshape(far, 2, 2, 2), AXES)
    over_rows, over_blk = ("far", "near"), ("side", "core")
    tok, row, rep = P(over_rows, over_blk, None), P(over_blk, None), P()
    return jax.shard_map(
        shards,
        mesh=inner,
        in_specs=(tok, P(over_rows, over_blk), rep, row, row, row, row, rep, rep, row, row, tok),
        out_specs=(tok, tok, rep, row, row, row, row, rep, rep, row, row),
        check_vma=False,
    )
```

```python
import functools

import jax
import jax.numpy as jnp
from jax import lax
from jax.experimental import pallas as pl
from jax.experimental.pallas import tpu as pltpu
from jax.sharding import PartitionSpec as P

EPS = 1e-06
EDGES = (1, 2, 3, 4, 5, 6, 7, 8, 12, 16, 23, 32, 46, 64, 91)
BF = jnp.bfloat16
F32 = jnp.float32
HBM = pl.BlockSpec(memory_space=pltpu.HBM)
VM = pl.BlockSpec(memory_space=pltpu.VMEM)
SM = pl.BlockSpec(memory_space=pltpu.SMEM)
DMA = pltpu.SemaphoreType.DMA
sds = jax.ShapeDtypeStruct
AXES = ("far", "near", "side", "core")
FLIPS = {"far2": 16, "far1": 8, "near": 4, "side": 2, "core": 1}


def scratch(shape, kind=BF):
    return pltpu.VMEM(shape, kind)


def call(kernel, name, outs, ins, out_specs, scratches, args, us=10, aliases={}):
    return pl.pallas_call(
        kernel,
        out_shape=outs,
        in_specs=ins,
        out_specs=out_specs,
        scratch_shapes=scratches,
        input_output_aliases=aliases,
        compiler_params=pltpu.CompilerParams(vmem_limit_bytes=63 * 1024 * 1024),
        cost_estimate=pl.CostEstimate(flops=int(us * 10**9), bytes_accessed=int(us * 4 * 10**6), transcendentals=0),
        name=name,
    )(*args)


def nn(a, b):
    return lax.dot_general(a, b, (((1,), (0,)), ((), ())), preferred_element_type=F32)


def nt(a, b):
    return lax.dot_general(a, b, (((1,), (1,)), ((), ())), preferred_element_type=F32)


def tn(a, b):
    return lax.dot_general(a, b, (((0,), (0,)), ((), ())), preferred_element_type=F32)


def swap(value, *axes):
    flip = sum(FLIPS[a] for a in axes)
    count = 1
    for a in AXES:
        count *= lax.axis_size(a)
    return lax.ppermute(value, AXES, [(i, i ^ flip) for i in range(count)])


def swap_far(value, bits):
    count = 8 * lax.axis_size("far")
    return lax.ppermute(value, AXES, [(i, i ^ (8 * bits)) for i in range(count)])


class Line:
    def __init__(self, ids):
        self.ids = ids

    def gate(self, *values):
        self.ids, *values = lax.optimization_barrier((self.ids, *values))
        return tuple(values)


def pick(arr, index, axis=0):
    return lax.dynamic_index_in_dim(arr, index, axis, keepdims=False)


class Sum:
    AXES = (("side", "near"), ("near", "side"))
    ORDER = (0, 2, 1, 3)

    def __init__(self, keep, send):
        self.rows = keep.shape[3]
        places = [(p, i, j) for p in (0, 1) for i in (0, 1) for j in (0, 1)]
        self.kept = {at: (keep, at) for at in places}
        got = swap(send, "core")
        self.flying = {at: (got, at) for at in places}

    def added(self, key):
        return self.kept[key], self.flying[key]

    def land(self, line):
        arrays = []
        for arr, _ in self.flying.values():
            if not any(arr is f for f in arrays):
                arrays.append(arr)
        landed = line.gate(*arrays)
        here = lambda arr: next(l for f, l in zip(arrays, landed) if f is arr)
        self.flying = {key: (here(arr), at) for key, (arr, at) in self.flying.items()}

    def first(self):
        out = []
        for p, i, j in self.kept:
            move = (self.AXES[p][0], (p, j)) if i else None
            out.append((*self.added((p, i, j)), None if i else (p, j), move))
        return self.rows, out

    def second(self):
        out = []
        for p, j in self.kept:
            out.append((*self.added((p, j)), None if j else p, (self.AXES[p][1], p) if j else None))
        return self.rows, out

    def third(self):
        return self.rows, [(*self.added(p), p, None) for p in (0, 1)]

    def spread(self):
        out = []
        cut = lambda block, i: (block[0], (*block[1], ("far", i)))
        for p in (0, 1):
            a, b = self.added(p)
            for i in range(4):
                sent = i & 1
                out.append((cut(a, i), cut(b, i), None if sent else (p, i), ("far1", (p, i - 1)) if sent else None))
        return self.rows // 4, out

    def pair(self):
        out = [(*self.added((p, i)), None if i else p, ("far2", p) if i else None) for p in (0, 1) for i in (0, 2)]
        return self.rows // 4, out

    def back(self):
        return self.rows // 4, [(*self.added(p), (p, 0), ("far2", (p, 2))) for p in (0, 1)]

    def last(self):
        have = {**self.kept, **self.flying}
        out = [(have[p, i], None, (p, i), ("far1", (p, i + 1))) for p in (0, 1) for i in (0, 2)]
        return self.rows // 4, out

    def finish(self):
        have = {**self.kept, **self.flying}
        out = [(have[p, i], None, (p, i), ("near", (p, i))) for p in (0, 1) for i in self.ORDER]
        return self.rows // 4, out


class FarSum:
    def __init__(self, parts):
        total = jnp.concatenate(parts, axis=0)
        self.plain = lax.axis_size("far") != 4
        if self.plain:
            self.kept, self.flying = lax.psum(total, "far"), ()
            return
        blocks = total.reshape(4, -1, 256)
        here = lax.axis_index("far")
        self.kept = pick(blocks, here)
        self.flying = tuple(swap_far(pick(blocks, here ^ i), i) for i in (1, 2, 3))

    def land(self, line):
        if self.flying:
            self.flying = line.gate(*self.flying)

    def back(self):
        if self.plain:
            return
        total = self.kept.astype(F32)
        for f in self.flying:
            total = total + f.astype(F32)
        self.kept = total.astype(BF)
        self.flying = tuple(swap_far(self.kept, i) for i in (1, 2, 3))

    def finish(self, line):
        if not self.plain:
            (self.kept,) = line.gate(jnp.stack([self.kept, *self.flying]))
        self.flying = (swap(self.kept, "near"),)


def add_kernel(jobs, arrays, ids, *refs):
    ins, refs = refs[:arrays], refs[arrays:]
    count = len(jobs)
    bufs, sems = refs[-1 - 2 * count : -1], refs[-1]
    outs = refs[: len(refs) - 1 - 2 * count]
    far = ids[3]
    dma = Copies(sems)

    def view(ref, at, rows):
        if at and isinstance(at[-1], tuple):
            *at, (_, i) = at
            start = at.pop().start if at and hasattr(at[-1], "start") else 0
            at = (*at, pl.ds(pl.multiple_of(start + (far ^ i) * rows, 16), rows))
        return ref.at[tuple(at)] if at else ref

    loads = []
    for n, (rows, a, b, _) in enumerate(jobs):
        loads.append(dma.start([(view(ins[x], at, rows), bufs[2 * n + m]) for m, (x, at) in enumerate((a, b)) if x >= 0]))
    stores = []
    for n, (rows, a, b, places) in enumerate(jobs):
        wait(loads[n])
        buf = bufs[2 * n]
        if b[0] >= 0:
            buf[...] = buf[...] + bufs[2 * n + 1][...]
        stores += dma.start([(buf, outs[o].at[pl.ds(row, rows)]) for o, row in places])
    wait(stores)


def advance(line, *steps, new=()):
    flying = []
    for piece, _ in steps:
        for arr, _ in piece.flying.values():
            if not any(arr is f for f in flying):
                flying.append(arr)
    landed = list(line.gate(*flying, *new))
    here = lambda arr: next(l for f, l in zip(flying, landed) if f is arr)
    fresh = Sum(*landed[len(flying) :]) if new else None
    if not steps:
        return fresh
    arrays, jobs, sizes, marks = [], [], {}, []

    def number(block):
        if block is None:
            return (-1, ())
        arr, at = block
        if not any(arr is x for x in arrays):
            arrays.append(arr)
        return next(n for n, x in enumerate(arrays) if x is arr), at

    for piece, step in steps:
        piece.flying = {key: (here(arr), at) for key, (arr, at) in piece.flying.items()}
        rows, todo = getattr(piece, step)()
        for a, b, key, move in todo:
            places = []
            for name, mark in ((("kept", piece), key), (move[0] if move else None, move[1] if move else None)):
                if mark is None:
                    continue
                row = sizes.get(name, 0)
                sizes[name] = row + rows
                places.append((name, row))
                marks.append((piece, name, mark, row, rows))
            jobs.append((rows, number(a), number(b), places))
    names = list(sizes)
    jobs = [(rows, a, b, tuple((names.index(n), row) for n, row in places)) for rows, a, b, places in jobs]
    sums = call(
        functools.partial(add_kernel, jobs, len(arrays)),
        "add",
        [sds((sizes[n], 256), BF) for n in names],
        [SM] + [HBM] * len(arrays),
        [HBM] * len(names),
        [scratch((rows, 256)) for rows, *_ in jobs for _ in (0, 1)] + [DMA((4 * len(jobs),))],
        (line.ids, *arrays),
        us=3,
    )
    line.gate(sums[0])
    results = {n: v if isinstance(n, tuple) else swap(v, n) for n, v in zip(names, sums)}
    for piece, _ in steps:
        piece.kept, piece.flying = {}, {}
        piece.buffer = results.get(("kept", piece))
    for piece, name, mark, row, rows in marks:
        where = piece.kept if isinstance(name, tuple) else piece.flying
        where[mark] = (results[name], (pl.ds(row, rows),))
    return fresh


class Gather:
    def __init__(self, line, own, half):
        self.line, self.own = line, own
        self.y = swap(half, "side")
        self.core = swap(own, "core")

    def cross(self):
        self.y, self.core = self.line.gate(self.y, self.core)
        self.x = swap(self.y, "near")

    def relay(self):
        (self.x,) = self.line.gate(self.x)
        self.yc, self.xc = swap(self.y, "core"), swap(self.x, "core")

    def done(self):
        self.yc, self.xc = self.line.gate(self.yc, self.xc)
        return (self.own, self.core, self.y, self.x, self.yc, self.xc)


class Copies:
    def __init__(self, sems):
        self.sems, self.count = sems, 0

    def start(self, pairs):
        out = []
        for src, dst in pairs:
            out.append(pltpu.make_async_copy(src, dst, self.sems.at[self.count]))
            self.count += 1
            out[-1].start()
        return out


def wait(copies):
    for c in copies:
        c.wait()


def pieces_of(refs, me, half):
    own, core, y, x, yc, xc = refs
    out = []
    for h in (0, 1):
        out.append((own.at[h], me, h))
        out.append((core.at[h], me ^ 1, h))
    out.append((y, me ^ 2, half))
    out.append((x, me ^ 2, 1 - half))
    out.append((yc, me ^ 3, half))
    out.append((xc, me ^ 3, 1 - half))
    return out


def pack_copies(refs, me, half, dst, cut):
    return [(cut(ref), dst.at[o, h]) for ref, o, h in pieces_of(refs, me, half)]


def token_copies(slots, me, dst):
    rows = dst.shape[0] // 4
    return [
        (src, dst.at[pl.ds(pl.multiple_of((me ^ s) * rows, rows), rows)]) for s, src in enumerate(slots)
    ]


def put(stage, owner, row, value):
    half, count = stage.shape[2], value.shape[0]
    first = min(count, max(0, half - row))
    if first:
        stage[owner, 0, pl.ds(row, first), :] = value[:first]
    if first < count:
        stage[owner, 1, pl.ds(row + first - half, count - first), :] = value[first:]


def piece_copies(stage, keep, send, ids):
    me, near, core = ids[0], ids[1], ids[2]
    h = stage.shape[2] // 2
    out = []
    for dst, c in ((send, 1 - core), (keep, core)):
        for part in (0, 1):
            for first in (0, 1):
                for second in (0, 1):
                    sy, sx = (first, second) if part == 0 else (second, first)
                    owner = ((me ^ (2 * sy)) & 2) + c
                    out.append((stage.at[owner, near ^ sx, pl.ds(part * h, h)], dst.at[part, first, second]))
    return out


def piece_shapes(rows):
    return [sds((2, 2, 2, rows // 4, 256), BF)] * 2


def rows_of(blocks):
    return jnp.concatenate(blocks, axis=0)


def prep_a_kernel(ids, seg, inputs, wq, wk, wv, m0, m1, m2, m3, own0, own1, y0, y1, sems):
    me, half = ids[0], ids[1]
    rows = inputs.shape[1]
    part = wq.shape[0] // 2
    pairs = []
    for g in range(3):
        own, y, at = (own0, y0, 0) if g == 0 else (own1, y1, g - 1)
        for i, w in enumerate((wq, wk, wv)):
            cols, place = pl.ds(g * 256, 256), pl.ds((3 * at + i) * part, part)
            pairs.append((w.at[pl.ds(pl.multiple_of(half * part, 16), part), cols], y.at[place]))
            for h in (0, 1):
                pairs.append((w.at[pl.ds(h * part, part), cols], own.at[h, place]))
    for s, m in enumerate((m0, m1, m2, m3)):
        pairs.append((inputs.at[me ^ s], m.at[pl.ds(0, rows)]))
    copies = Copies(sems).start(pairs)
    for s, m in enumerate((m0, m1, m2, m3)):
        line = seg[pl.ds(me ^ s, 1), :].astype(F32)
        m[pl.ds(rows, 16), pl.ds(0, rows)] = jnp.broadcast_to(line, (16, rows)).astype(BF)
        m[pl.ds(rows, 16), pl.ds(rows, m.shape[1] - rows)] = jnp.zeros((16, m.shape[1] - rows), BF)
    wait(copies)


def prep_b_kernel(ids, w_in, w_back, w_out, cot, own0, own1, own2, y0, y1, y2, k1, k2, k3, sems):
    me, half = ids[0], ids[1]
    hw = w_in.shape[0] // 2
    pairs = [(cot.at[me ^ s], k) for s, k in ((1, k1), (2, k2), (3, k3))]
    for c, (own, y) in enumerate(((own0, y0), (own1, y1), (own2, y2))):
        for dst, h in ((y, half), (own.at[0], 0), (own.at[1], 1)):
            for b in range(4):
                pairs.append((
                    w_in.at[pl.ds(pl.multiple_of(h * hw, 16), hw), pl.ds(b * 768 + c * 256, 256)],
                    dst.at[pl.ds(b * hw, hw)],
                ))
            for j in range(3):
                pairs.append((
                    w_back.at[pl.ds(pl.multiple_of(c * 256 + h * 128, 16), 128), pl.ds(j * 256, 256)],
                    dst.at[pl.ds(4 * hw + j * 128, 128)],
                ))
                if c == 0:
                    pairs.append((
                        w_out.at[pl.ds(pl.multiple_of(h * hw, 16), hw), pl.ds(j * 256, 256)],
                        dst.at[pl.ds(4 * hw + 384 + j * hw, hw)],
                    ))
    wait(Copies(sems).start(pairs))


def norm_kernel(ids, m0, m1, m2, m3, gain, xs, nrm, nrm_t, seg, sbuf, sems):
    me = ids[0]
    rows = xs.shape[0] // 4
    slots = (m0, m1, m2, m3)
    tok = token_copies([m.at[pl.ds(0, rows)] for m in slots], me, xs)
    tok += token_copies([m.at[pl.ds(rows, 16)] for m in slots], me, sbuf)
    wait(Copies(sems).start(tok))
    seg[...] = jnp.concatenate(
        [sbuf[pl.ds(o * 16, 1), pl.ds(0, rows)].astype(F32) for o in range(4)], axis=1
    )
    for a in range(4):
        x = xs[pl.ds(a * rows, rows), :].astype(F32)
        y = x * lax.rsqrt(jnp.mean(x * x, axis=-1, keepdims=True) + EPS) * gain[...]
        y = y.astype(BF)
        nrm[pl.ds(a * rows, rows), :] = y
        nrm_t[:, pl.ds(a * rows, rows)] = y.T


def half_masks(t):
    lane = lax.broadcasted_iota(jnp.int32, (t, 128), 1)
    return lane < 64, (lane < 64).astype(F32).astype(BF), (lane >= 64).astype(F32).astype(BF)


def attn_fwd_kernel(group, ids, far, seg, lines, nrm_in, w0, w1, w2, w3, w4, w5,
                    q_out, k_out, v_out, p_out, o, near, nrm, wbuf, q, k, v, p, sems):
    me, half = ids[0], ids[1]
    dma = Copies(sems)
    count = wbuf.shape[2]
    part = count // 3
    place = pl.ds(max(group - 1, 0) * count, count)
    loads = dma.start(
        [(nrm_in, nrm)]
        + pack_copies((w0, w1, w2, w3, w4, w5), me, half, wbuf, lambda ref: ref.at[place])
    )
    for head in range(4):
        line = jnp.broadcast_to(lines[pl.ds(4 * group + head, 1), :], (near.shape[1], lines.shape[1]))
        near[head] = pltpu.roll(line, 0, 1, stride=1, stride_axis=0)[:, : near.shape[2]]
    t = near.shape[1]
    length = q.shape[0]
    nblk = length // t
    low, m0, m1 = half_masks(t)
    eye = lax.broadcasted_iota(jnp.int32, (t, t), 0) == lax.broadcasted_iota(jnp.int32, (t, t), 1)
    seg_row = seg[...]
    wait(loads)
    stores = []
    for i, (buf, out) in enumerate(((q, q_out), (k, k_out), (v, v_out))):
        w = rows_of([wbuf[ow, h, pl.ds(i * part, part), :] for ow in range(4) for h in (0, 1)])
        buf[...] = nn(nrm[...], w).astype(BF)
        stores += dma.start([(buf, out)])
    for pair in (0, 1):
        at = pl.ds(pair * 128, 128)
        for a in range(nblk):
            seg_col = jnp.sum(
                jnp.where(eye, jnp.broadcast_to(seg_row[:, a * t : (a + 1) * t], (t, t)), 0.0),
                axis=1,
                keepdims=True,
            )
            allowed = seg_col == seg_row
            q2 = q[pl.ds(a * t, t), at]
            s = nt(rows_of([q2 * m0, q2 * m1]), k[:, at])
            ps = []
            for h in (0, 1):
                head = 2 * pair + h
                strip = []
                for b in range(nblk):
                    rel = b - a
                    if abs(rel) <= 1:
                        strip.append(near[head, :, (rel + 1) * t : (rel + 2) * t])
                    else:
                        strip.append(jnp.full((t, t), far[int(rel > 0), group * 4 + head], F32))
                sh = s[h * t : (h + 1) * t] + jnp.concatenate(strip, axis=1)
                sh = jnp.where(allowed, sh, -1e30)
                top = jnp.max(sh, axis=-1, keepdims=True)
                e = jnp.exp(sh - top)
                inv = 1.0 / jnp.sum(e, axis=-1, keepdims=True)
                ph = (e * inv).astype(BF)
                p[head, pl.ds(a * t, t), :] = ph
                ps.append(ph)
            mix = nn(rows_of(ps), v[:, at])
            o[pl.ds(a * t, t), at] = jnp.where(low, mix[:t], mix[t:]).astype(BF)
        stores += dma.start([(p.at[pl.ds(2 * pair, 2)], p_out.at[pl.ds(2 * pair, 2)])])
    wait(stores)


def out_weight(wbuf, j):
    hw = wbuf.shape[2] // 3
    return rows_of([wbuf[o, h, pl.ds(j * hw, hw), :] for o in range(4) for h in (0, 1)])


def out_cut(sh):
    return lambda ref: ref.at[pl.ds(2 * sh + 384, 3 * (sh // 2))]


def gelu_both(x):
    c = 0.7978845608028654
    x2 = x * x
    th = jnp.tanh(x * (c + (c * 0.044715) * x2))
    half_up = 0.5 + 0.5 * th
    slope = half_up + x * (0.5 - 0.5 * th * th) * (c + (3.0 * c * 0.044715) * x2)
    return x * half_up, slope


def ffn_kernel(lead, ids, *refs):
    if lead:
        gain, xs, x0, x1, x2, cown, c1, c2, c3, p0, p1, p2, p3, p4, p5, *rest = refs
        hid_out, ff_out, fft_out, act_out, gpre_out, keep, send, *rest = rest
        xv, mx, wout, hid, ffv, fftv, cot, pack, act, gpre, stage, sems = rest
    else:
        ff, ff_t, cown, c1, c2, c3, p0, p1, p2, p3, p4, p5, act_out, gpre_out, keep, send, *rest = refs
        ffv, fftv, cot, pack, act, gpre, stage, sems = rest
    me, half = ids[0], ids[1]
    d = ffv.shape[1]
    sh = d // 4
    hw = sh // 2
    packs = (p0, p1, p2, p3, p4, p5)
    dma = Copies(sems)
    weights = pack_copies(packs, me, half, pack, lambda ref: ref.at[pl.ds(0, 4 * hw + 384)])
    stores = []
    if lead:
        early = dma.start(
            pack_copies(packs, me, half, wout, out_cut(sh))
            + [(x, mx.at[:, pl.ds(i * 256, 256)]) for i, x in enumerate((x0, x1, x2))]
            + [(xs, xv)]
        )
        first = dma.start(weights)
    else:
        first = dma.start([(ff, ffv)] + weights)
    second = dma.start(token_copies((cown.at[me], c1, c2, c3), me, cot))
    if lead:
        third = ()
        wait(early)
        for j in range(3):
            cols = pl.ds(j * 256, 256)
            hid[:, cols] = xv[:, cols].astype(F32) + nn(mx[...], out_weight(wout, j))
        rows = 128
        for a in range(xv.shape[0] // rows):
            x = hid[pl.ds(a * rows, rows), :]
            y = x * lax.rsqrt(jnp.mean(x * x, axis=-1, keepdims=True) + EPS) * gain[...]
            y = y.astype(BF)
            ffv[pl.ds(a * rows, rows), :] = y
            fftv[:, pl.ds(a * rows, rows)] = y.T
        stores += dma.start([(hid, hid_out), (ffv, ff_out), (fftv, fft_out)])
    else:
        third = dma.start([(ff_t, fftv)])
    wait(first)
    for b in range(5):
        if b < 4:
            at = pl.ds(b * 256, 256)
            win = rows_of([pack[o, h, pl.ds(b * hw, hw), :] for o in range(4) for h in (0, 1)])
            value, slope = gelu_both(nn(ffv[...], win))
            if b == 0:
                wait(second)
            act[:, at] = value.astype(BF)
            back = 0.0
            for j in range(3):
                wb = rows_of([pack[b, h, pl.ds(4 * hw + j * 128, 128), :] for h in (0, 1)])
                back = back + nt(cot[:, pl.ds(j * 256, 256)], wb)
            gpre[:, at] = (back * slope).astype(BF)
        if b == 3:
            stores += dma.start([(act, act_out), (gpre, gpre_out)])
        if b > 0:
            c = b - 1
            at = pl.ds(c * 256, 256)
            if c == 0:
                wait(third)
            gw = nn(fftv[...], gpre[:, at]).astype(BF)
            for o in range(4):
                put(stage, o, c * sh, gw[o * sh : (o + 1) * sh])
            gb = tn(act[:, at], cot[...]).astype(BF)
            for j in range(3):
                put(stage, c, 4 * sh + j * 256, gb[:, j * 256 : (j + 1) * 256])
    stores += dma.start(piece_copies(stage, keep, send, ids))
    wait(stores)


def after_ff_kernel(ids, gain, hid, g0, g1, g2, cown, c1, c2, c3, x0, x1, x2, *refs):
    packs = (refs[0:6], refs[6:12], refs[12:18])
    ghid, gm0, gm1, gm2, ggain, gwo, hidv, gv, cot, mx, wbuf, wins, ga, gf, sems = refs[18:]
    me, half = ids[0], ids[1]
    d = hid.shape[1]
    sh = d // 4
    hw = sh // 2
    rows = cot.shape[0] // 4
    dma = Copies(sems)
    loads = [
        dma.start(
            [(g, gv.at[c])]
            + pack_copies(packs[c], me, half, wins.at[c], lambda ref: ref.at[pl.ds(0, 4 * hw)])
        )
        for c, g in enumerate((g0, g1, g2))
    ]
    rest = dma.start([(hid, hidv)] + token_copies((cown.at[me], c1, c2, c3), me, cot))
    last = dma.start(
        pack_copies(packs[0], me, half, wbuf, out_cut(sh))
        + [(x, mx.at[:, pl.ds(i * 256, 256)]) for i, x in enumerate((x0, x1, x2))]
    )
    for c in range(3):
        wait(loads[c])
        acc = None
        for b in range(4):
            w = rows_of([wins[c, o, h, pl.ds(b * hw, hw), :] for o in range(4) for h in (0, 1)])
            term = nt(gv[c, :, pl.ds(b * 256, 256)], w)
            acc = term if acc is None else acc + term
        gf[...] = acc if c == 0 else gf[...] + acc
    wait(rest)
    total = jnp.zeros((1, d), F32)
    for a in range(4):
        at = pl.ds(a * rows, rows)
        x = hidv[at, :]
        gfa = gf[at, :]
        n = lax.rsqrt(jnp.mean(x * x, axis=-1, keepdims=True) + EPS)
        g = gfa * gain[...]
        xn = x * n
        total = total + jnp.sum(gfa * xn, axis=0, keepdims=True)
        gh = cot[at, :].astype(F32) + n * (g - xn * (n * jnp.mean(g * x, axis=-1, keepdims=True)))
        ghid[at, :] = gh
        ga[at, :] = gh.astype(BF)
    ggain[...] = total
    wait(last)
    acc = None
    for j in range(3):
        term = nt(ga[:, pl.ds(j * 256, 256)], out_weight(wbuf, j))
        acc = term if acc is None else acc + term
    for i, gm in enumerate((gm0, gm1, gm2)):
        gm[...] = acc[:, i * 256 : (i + 1) * 256].astype(BF)
    for j in range(3):
        gw = tn(mx[...], ga[:, pl.ds(j * 256, 256)]).astype(BF)
        for o in range(4):
            gwo[o, pl.ds(j * sh, sh), :] = gw[o * sh : (o + 1) * sh]


def out_kernel(ids, hid, gin, a0, a1, a2, *refs):
    packs = (refs[0:6], refs[6:12], refs[12:18])
    out, hidv, av, wb, sems = refs[18:]
    me, half = ids[0], ids[1]
    d = hid.shape[1]
    hw = d // 8
    rows = hid.shape[0] // 4
    dma = Copies(sems)
    loads = [
        dma.start(
            [(a, av.at[c])]
            + pack_copies(packs[c], me, half, wb.at[c], lambda ref: ref.at[pl.ds(4 * hw, 384)])
        )
        for c, a in enumerate((a0, a1, a2))
    ]
    last = dma.start([(hid, hidv)])
    grads = dma.start([(gin.at[pl.ds(b * rows, rows)], out.at[b, 1]) for b in range(4)])
    for c in range(3):
        wait(loads[c])
    wait(last)
    for j in range(3):
        cols = pl.ds(j * 256, 256)
        acc = hidv[:, cols]
        for c in range(3):
            w = rows_of([wb[c, o, h, pl.ds(j * 128, 128), :] for o in range(4) for h in (0, 1)])
            acc = acc + nn(av[c], w)
        acc = acc.astype(BF)
        for b in range(4):
            out[b, 0, :, cols] = acc[b * rows : (b + 1) * rows]
    wait(grads)


def diagonals(x):
    width = x.shape[1]
    y = x[0:8]
    for a in range(8, x.shape[0], 8):
        y = y + pltpu.roll(x[a : a + 8], width - a, 1)
    sub = lax.broadcasted_iota(jnp.int32, y.shape, 0)
    for bit in (1, 2, 4):
        y = jnp.where((sub & bit) != 0, pltpu.roll(y, width - bit, 1), y)
    return jnp.sum(y, axis=0, keepdims=True)


def attn_bwd_kernel(groups, carried, ids, nrm_in, *refs):
    ins, refs = refs[: 5 * groups], refs[5 * groups :]
    carry, refs = refs[:carried], refs[carried:]
    keep, send, *refs = refs
    outs, refs = refs[: 3 * groups], refs[3 * groups :]
    (diag, q, k, v, p, gm, nrm_t, dq, dk, dv, acc, stage, sems) = refs
    t = 128
    length = nrm_t.shape[1]
    nblk = length // t
    low, m0, m1 = half_masks(t)
    dma = Copies(sems)
    loads = []
    for n in range(groups):
        q_in, k_in, v_in, p_in, gm_in = ins[5 * n : 5 * n + 5]
        whole = [(v_in, v.at[n]), (gm_in, gm.at[n]), (k_in, k.at[n]), (q_in, q.at[n])]
        halves = [[(p_in.at[pl.ds(2 * i, 2)], p.at[pl.ds(4 * n + 2 * i, 2)])] for i in (0, 1)]
        loads += [dma.start(whole + halves[0]), dma.start(halves[1])]
        if n == 0:
            last = dma.start([(nrm_in, nrm_t)])
    base, half = 0, stage.shape[2]
    for g in carry:
        count = g.shape[1]
        inside = min(count, half - base) if base < half else 0
        if inside:
            last += dma.start([(g.at[:, pl.ds(0, inside)], stage.at[:, 0, pl.ds(base, inside)])])
        if inside < count:
            rest, at = count - inside, max(0, base - half)
            last += dma.start([(g.at[:, pl.ds(inside, rest)], stage.at[:, 1, pl.ds(at, rest)])])
        base += count
    sh = nrm_t.shape[0] // 4
    stores = []
    for n in range(groups):
        for pair in (0, 1):
            wait(loads[2 * n + pair])
            cols = pl.ds(pair * 128, 128)
            k2, v2 = k[n, :, cols], v[n, :, cols]
            dk_t = jnp.zeros((128, length), F32)
            dv_t = jnp.zeros((128, length), F32)
            for a in range(nblk):
                at = pl.ds(a * t, t)
                q2, g2 = q[n, at, cols], gm[n, at, cols]
                qm = rows_of([q2 * m0, q2 * m1])
                g_both = rows_of([g2 * m0, g2 * m1])
                dp = nt(g_both, v2)
                pb = rows_of([p[4 * n + 2 * pair, at, :], p[4 * n + 2 * pair + 1, at, :]])
                pf = pb.astype(F32)
                delta = jnp.sum(pf * dp, axis=-1, keepdims=True)
                ds = (pf * (dp - delta)).astype(BF)
                mq = nn(ds, k2)
                dq[n, at, cols] = jnp.where(low, mq[:t], mq[t:]).astype(BF)
                dk_t = dk_t + tn(qm, ds)
                dv_t = dv_t + tn(g_both, pb)
                dsf = ds.astype(F32)
                for h in (0, 1):
                    for b in range(nblk):
                        rel = b - a
                        place = rel + 1 if abs(rel) <= 1 else (3 if rel < 0 else 4)
                        tile = dsf[h * t : (h + 1) * t, b * t : (b + 1) * t]
                        lanes = pl.ds(place * t, t)
                        if (a, b) in ((1, 0), (0, 0), (0, 1), (2, 0), (0, 2)):
                            acc[h, :, lanes] = tile
                        else:
                            acc[h, :, lanes] += tile
            dk[n, :, cols] = dk_t.T.astype(BF)
            dv[n, :, cols] = dv_t.T.astype(BF)
            for h in (0, 1):
                near = jnp.concatenate([acc[h, :, pl.ds(0, 3 * t)], jnp.zeros((t, t), F32)], axis=1)
                far = jnp.sum(acc[h, :, pl.ds(3 * t, 2 * t)], axis=0, keepdims=True)
                diag[pl.ds(4 * n + 2 * pair + h, 1), :] = jnp.concatenate([diagonals(near), far], axis=1)
        stores += dma.start([(d.at[n], out) for d, out in zip((dq, dk, dv), outs[3 * n : 3 * n + 3])])
        if n == 0:
            wait(last)
        for i, g in enumerate((dq, dk, dv)):
            gw = nn(nrm_t[...], g[n]).astype(BF)
            for o in range(4):
                put(stage, o, base + i * sh, gw[o * sh : (o + 1) * sh])
        base += 3 * sh
    stores += dma.start(piece_copies(stage, keep, send, ids))
    wait(stores)


def first_norm_kernel(ids, gain, xs, ghid, *refs):
    ins = refs[0:9]
    w0, w1 = refs[9:15], refs[15:21]
    gi, ggain, xv, gv, dall, wbuf0, wbuf1, gn, sems = refs[21:]
    me, half = ids[0], ids[1]
    d = xs.shape[1]
    rows = xs.shape[0] // 4
    dma = Copies(sems)
    loads = dma.start(
        [(g, dall.at[n]) for n, g in enumerate(ins)]
        + pack_copies(w0, me, half, wbuf0, lambda ref: ref)
        + pack_copies(w1, me, half, wbuf1, lambda ref: ref)
    )
    part = wbuf0.shape[2] // 3
    rest = dma.start([(xs, xv), (ghid, gv)])
    wait(loads)
    acc = None
    for i in range(3):
        for c in range(3):
            buf, at = (wbuf0, i) if c == 0 else (wbuf1, 3 * (c - 1) + i)
            wi = rows_of([buf[o, h, pl.ds(at * part, part), :] for o in range(4) for h in (0, 1)])
            term = nt(dall[3 * i + c], wi)
            acc = term if acc is None else acc + term
    gn[...] = acc
    wait(rest)
    total = jnp.zeros((1, d), F32)
    for a in range(4):
        at = pl.ds(a * rows, rows)
        x = xv[at, :].astype(F32)
        gf = gn[at, :]
        n = lax.rsqrt(jnp.mean(x * x, axis=-1, keepdims=True) + EPS)
        g = gf * gain[...]
        xn = x * n
        total = total + jnp.sum(gf * xn, axis=0, keepdims=True)
        gi[at, :] = (gv[at, :] + n * (g - xn * (n * jnp.mean(g * x, axis=-1, keepdims=True)))).astype(BF)
    ggain[...] = total


def tokens_kernel(ids, tokens, out, gin):
    out[...] = tokens[:, 0]
    gin[...] = tokens[:, 1].astype(F32)


def ff_shares_kernel(quad, thirds, starts, ids, *refs):
    ins, (out_in, out_back, buf, part_in, part_back, sems) = refs, refs[-6:]
    here, far = ids[1], ids[3]
    sh = out_in.shape[0]
    dma = Copies(sems)
    n = (2 * sh + 384) // 8
    copies = []
    for k in range(len(thirds)):
        pairs = []
        for m, h in ((2 * k, here), (2 * k + 1, 1 - here)):
            src = ins[m].at[pl.ds(starts[m], 8 * n)]
            if not quad:
                pairs.append((src, buf.at[k, h]))
                continue
            for p in (0, 1):
                for q, i in enumerate(Sum.ORDER):
                    row = pl.multiple_of(p * 4 * n + (far ^ i) * n, 16)
                    pairs.append((src.at[pl.ds((4 * p + q) * n, n)], buf.at[k, h, pl.ds(row, n)]))
        copies.append(dma.start(pairs))
    stores = []
    for m, k in enumerate(thirds):
        wait(copies[m])
        for b in range(4):
            part_in[m, :, pl.ds(b * 256, 256)] = buf[m, 0, pl.ds(b * sh, sh), :].astype(F32)
        stores += dma.start([
            (part_in.at[m, :, pl.ds(b * 256, 256)], out_in.at[:, pl.ds((b * 3 + k) * 256, 256)]) for b in range(4)
        ])
        for j in range(3):
            part_back[m, :, pl.ds(j * 256, 256)] = buf[m, 1, pl.ds(j * 256, 256), :].astype(F32)
        stores += dma.start([(part_back.at[m], out_back.at[pl.ds(k * 256, 256)])])
    wait(stores)


def attn_shares_kernel(plain, ids, z, x, wq, wk, wv, wo, buf, sems):
    here, far = ids[1], ids[3]
    sh = wq.shape[0]
    pairs = []
    for src, h in ((z, here), (x, 1 - here)):
        if plain:
            pairs.append((src, buf.at[h]))
        else:
            n = src.shape[1]
            pairs += [(src.at[i], buf.at[h, pl.ds(pl.multiple_of((far ^ i) * n, 16), n)]) for i in range(4)]
    wait(Copies(sems).start(pairs))
    at = lambda half, n: buf[half, pl.ds(n * sh, sh), :].astype(F32)
    for i in range(3):
        wo[:, pl.ds(i * 256, 256)] = at(0, i)
    for i, out in enumerate((wq, wk, wv)):
        out[:, pl.ds(0, 256)] = at(1, i)
        out[:, pl.ds(256, 256)] = at(0, 3 + i)
        out[:, pl.ds(512, 256)] = at(1, 3 + i)


def bucket_of(offset, bucket_count):
    distance = jnp.abs(offset)
    bucket = jnp.where(offset > 0, bucket_count // 2, 0).astype(jnp.int32)
    for edge in EDGES:
        bucket = bucket + (distance >= edge).astype(jnp.int32)
    return bucket


def shards(inputs, segments, gain_attn, w_query, w_key, w_value, w_out, bucket_bias_table, gain_ff, w_in, w_back, cotangent):
    seqs, rows, d = inputs.shape
    sh = w_query.shape[0]
    hw = sh // 2
    ffs = w_in.shape[1]
    bucket_count, heads = bucket_bias_table.shape
    length = rows * seqs
    places = [lax.axis_index(a).astype(jnp.int32) for a in ("near", "side", "core", "far")]
    near_at, side_at, core_at, far_at = places
    line = Line(jnp.stack([2 * side_at + core_at, near_at, core_at, far_at]))
    gate = line.gate
    row_low, row_f32 = sds((length, d), BF), sds((length, d), F32)
    quad_low, tok_low = sds((length, 256), BF), sds((rows, d), BF)
    gain1, gain2 = gain_attn.reshape(1, d), gain_ff.reshape(1, d)
    pack_rows = [4 * hw + 384 + 3 * hw, 4 * hw + 384, 4 * hw + 384]

    m0, m1, m2, m3, own_a, own_b, y_a, y_b = call(
        prep_a_kernel,
        "prep_a",
        [sds((rows + 16, d), BF)] * 4
        + [sds((2, 3 * hw, 256), BF), sds((2, 6 * hw, 256), BF), sds((3 * hw, 256), BF), sds((6 * hw, 256), BF)],
        [SM, VM] + [HBM] * 4,
        [VM] * 8,
        [DMA((31,))],
        (line.ids, segments, inputs, w_query, w_key, w_value),
    )
    wa = Gather(line, own_a, y_a)
    msgs = [swap(m1, "core"), swap(m2, "side"), swap(m3, "side", "core")]
    wb = Gather(line, own_b, y_b)

    own0, own1, own2, y0, y1, y2, k1, k2, k3 = call(
        prep_b_kernel,
        "prep_b",
        [sds((2, r, 256), BF) for r in pack_rows] + [sds((r, 256), BF) for r in pack_rows] + [tok_low] * 3,
        [SM] + [HBM] * 4,
        [VM] * 9,
        [DMA((75,))],
        (line.ids, w_in, w_back, w_out, cotangent),
    )

    (own0,) = gate(own0)
    wa.cross()
    *msgs, table_in = gate(*msgs, bucket_bias_table)
    wa.relay()

    offs = jnp.arange(4 * rows, dtype=jnp.int32)
    offs = jnp.where(offs < 3 * rows, offs - rows, offs - 5 * rows)
    hot = (bucket_of(offs, bucket_count)[None] == jnp.arange(bucket_count, dtype=jnp.int32)[:, None]).astype(F32)
    lines = jnp.einsum("up,uw->wp", hot, table_in, precision=lax.Precision.HIGHEST)
    far = jnp.stack([table_in[bucket_count // 2 - 1], table_in[bucket_count - 1]])

    y0, own0 = gate(y0, own0)
    wf = [Gather(line, own0, y0)]
    xs, nrm, nrm_t, seg = call(
        norm_kernel,
        "norm",
        [row_low, row_low, sds((d, length), BF), sds((1, length), F32)],
        [SM] + [HBM] * 4 + [VM],
        [VM] * 4,
        [scratch((64, d)), DMA((8,))],
        (line.ids, m0, *msgs, gain1),
    )
    nrm, lines = gate(nrm, lines)
    wb.cross()
    wa = wa.done()

    qs, ks, vs, probs, mixed = [], [], [], [], []
    for g in range(3):
        q, k, v, p, mx = call(
            functools.partial(attn_fwd_kernel, g),
            "attn_fwd",
            [quad_low] * 3 + [sds((4, length, length), BF), quad_low],
            [SM, SM, VM, VM] + [HBM] * 7,
            [HBM] * 4 + [VM],
            [
                scratch((4, rows, 3 * rows), F32),
                scratch((length, d)),
                scratch((4, 2, 3 * hw, 256)),
                scratch((length, 256)),
                scratch((length, 256)),
                scratch((length, 256)),
                scratch((4, length, length)),
                DMA((15,)),
            ],
            (line.ids, far, seg, lines, nrm, *(wa if g == 0 else wb)),
        )
        (mx,) = gate(mx)
        for have, new in ((qs, q), (ks, k), (vs, v), (probs, p), (mixed, mx)):
            have.append(new)
        if g == 0:
            wb.relay()
            wf[0].cross()
            own1, y1 = gate(own1, y1)
            wf.append(Gather(line, own1, y1))
            wb = wb.done()
        if g == 1:
            wf[0].relay()
            wf[1].cross()
            k1, k2, k3 = gate(k1, k2, k3)
            cots = [swap(k1, "core"), swap(k2, "side"), swap(k3, "side", "core")]
    packs = [wf[0].done()]
    cots = gate(*cots)
    wf[1].relay()
    own2, y2 = gate(own2, y2)
    wf.append(Gather(line, own2, y2))

    sums_f, acts, gpres = [], [], []
    for c in range(3):
        lead = c == 0
        *fresh, act, gpre, keep, send = call(
            functools.partial(ffn_kernel, lead),
            "ffn",
            ([row_f32, row_low, sds((d, length), BF)] if lead else [])
            + [sds((length, 1024), BF)] * 2
            + piece_shapes(4 * sh + 768),
            [SM] + ([VM] + [HBM] * 4 if lead else [HBM] * 2) + [HBM] * 10,
            [HBM] * (7 if lead else 4),
            (
                [scratch((length, d)), scratch((length, d)), scratch((4, 2, 3 * hw, 256)), scratch((length, d), F32)]
                if lead
                else []
            )
            + [
                scratch((length, d)),
                scratch((d, length)),
                scratch((length, d)),
                scratch((4, 2, 4 * hw + 384, 256)),
                scratch((length, 1024)),
                scratch((length, 1024)),
                scratch((4, 2, 2 * sh + 384, 256)),
                DMA((52,)),
            ],
            (line.ids, *((gain2, xs, *mixed) if lead else (ff, ff_t)), cotangent, *cots, *packs[c]),
        )
        if lead:
            hid, ff, ff_t = fresh
        piece = (keep, send)
        acts.append(act)
        (gpre,) = gate(gpre)
        gpres.append(gpre)
        if c == 0:
            packs.append(wf[1].done())
            wf[2].cross()
        if c == 1:
            wf[2].relay()
        moves = [[], [("first",)], [("second",), ("first",)]][c]
        sums_f.append(advance(line, *[(f, *m) for f, m in zip(sums_f, moves)], new=piece))
        if c == 1:
            packs.append(wf[2].done())

    ghid, *gmix, ggain_ff, gwo = call(
        after_ff_kernel,
        "after_ff",
        [row_f32] + [quad_low] * 3 + [sds((1, d), F32), sds((4, 3 * sh, 256), BF)],
        [SM, VM] + [HBM] * 29,
        [VM] * 6,
        [
            scratch((length, d), F32),
            scratch((3, length, 1024)),
            scratch((length, d)),
            scratch((length, d)),
            scratch((4, 2, 3 * hw, 256)),
            scratch((3, 4, 2, 4 * hw, 256)),
            scratch((length, d)),
            scratch((length, d), F32),
            DMA((43,)),
        ],
        (line.ids, gain2, hid, *gpres, cotangent, *cots, *mixed, *packs[0], *packs[1], *packs[2]),
    )
    gmix[0], ggain_ff = gate(gmix[0], ggain_ff)
    quad = lax.axis_size("far") == 4
    third = "spread" if quad else "third"
    far_steps = lambda *steps: steps if quad else ()
    advance(line, (sums_f[0], third), (sums_f[1], "second"), (sums_f[2], "first"))

    dqs, dks, dvs, diags, sums_a = [], [], [], [], []
    for first, groups in ((0, 1), (1, 2)):
        carry = (gwo,) if first == 0 else ()
        body = 3 * sh * (groups + len(carry))
        some = range(first, first + groups)
        keep, send, *grads, diag = call(
            functools.partial(attn_bwd_kernel, groups, len(carry)),
            "attn_bwd",
            piece_shapes(body) + [quad_low] * (3 * groups) + [sds((4 * groups, 6 * rows), F32)],
            [SM] + [HBM] * (1 + 5 * groups + len(carry)),
            [HBM] * (2 + 3 * groups) + [VM],
            [scratch((groups, length, 256))] * 3
            + [scratch((4 * groups, length, length)), scratch((groups, length, 256)), scratch((d, length))]
            + [scratch((groups, length, 256))] * 3
            + [scratch((2, rows, 5 * rows), F32), scratch((4, 2, body // 2, 256)), DMA((48,))],
            (line.ids, nrm_t, *[a for g in some for a in (qs[g], ks[g], vs[g], probs[g], gmix[g])], *carry),
            us=10 * groups,
        )
        (grads[0],) = gate(grads[0])
        for n in range(groups):
            for have, new in zip((dqs, dks, dvs), grads[3 * n : 3 * n + 3]):
                have.append(new)
        diags.append(diag)
        if first == 0:
            steps = ((sums_f[1], third), (sums_f[2], "second"), *far_steps((sums_f[0], "pair")))
        else:
            steps = ((sums_a[0], "first"), (sums_f[2], third))
            steps += far_steps((sums_f[0], "back"), (sums_f[1], "pair"))
        sums_a.append(advance(line, *steps, new=(keep, send)))

    gin, ggain_attn = call(
        first_norm_kernel,
        "first_norm",
        [row_low, sds((1, d), F32)],
        [SM, VM] + [HBM] * 23,
        [VM] * 2,
        [
            scratch((length, d)),
            scratch((length, d), F32),
            scratch((9, length, 256)),
            scratch((4, 2, 3 * hw, 256)),
            scratch((4, 2, 6 * hw, 256)),
            scratch((length, d), F32),
            DMA((27,)),
        ],
        (line.ids, gain1, xs, ghid, *dqs, *dks, *dvs, *wa, *wb),
    )
    gin, ggain_attn = gate(gin, ggain_attn)
    steps = far_steps((sums_f[0], "last"), (sums_f[1], "back"), (sums_f[2], "pair"))
    advance(line, (sums_a[1], "first"), (sums_a[0], "second"), *steps)
    (tokens,) = call(
        out_kernel,
        "out",
        [sds((seqs, 2, rows, d), BF)],
        [SM] + [HBM] * 23,
        [VM],
        [
            scratch((length, d), F32),
            scratch((3, length, 1024)),
            scratch((3, 4, 2, 384, 256)),
            DMA((32,)),
        ],
        (line.ids, hid, gin, *acts, *packs[0], *packs[1], *packs[2]),
    )
    tokens, ggain_attn = gate(tokens, ggain_attn)
    steps = far_steps((sums_f[0], "finish"), (sums_f[1], "last"), (sums_f[2], "back"))
    advance(line, (sums_a[1], "second"), (sums_a[0], "third"), *steps)
    first_total = sums_a[0].buffer


    hot6 = jnp.concatenate(
        [
            hot,
            jnp.zeros((bucket_count, rows), F32).at[bucket_count // 2 - 1].set(1.0),
            jnp.zeros((bucket_count, rows), F32).at[bucket_count - 1].set(1.0),
        ],
        axis=1,
    )
    table = jnp.einsum("up,wp->uw", hot6, jnp.concatenate(diags, axis=0), precision=lax.Precision.HIGHEST)
    small = jnp.concatenate([ggain_attn.reshape(-1), ggain_ff.reshape(-1), table.reshape(-1)])
    small = small + swap(small, "near")
    tokens = lax.all_to_all(tokens, ("side", "core"), 0, 0, tiled=True)
    advance(line, (sums_a[1], "third"), *far_steps((sums_f[1], "finish"), (sums_f[2], "last")))
    far_c = FarSum([first_total, sums_a[1].buffer])

    (small,) = gate(small)
    sums_f[1].land(line)
    far_c.land(line)
    far_c.back()
    if quad:
        advance(line, (sums_f[2], "finish"))
    else:
        for f in sums_f:
            whole = lax.psum(f.buffer, "far")
            f.buffer, f.flying = whole, {0: (swap(whole, "near"), ())}
    far_c.land(line)
    far_c.finish(line)
    tokens, small = gate(tokens, small)
    small = small + swap(small, "side")

    output, grad_inputs = call(
        tokens_kernel,
        "tokens",
        [sds((seqs, rows, d), BF), sds((seqs, rows, d), F32)],
        [SM, VM],
        [VM] * 2,
        [],
        (line.ids, tokens),
        us=1,
    )
    output, small = gate(output, small)
    small = small + swap(small, "core")
    shares = []
    shapes = [sds((sh, ffs), F32), sds(w_back.shape, F32)]
    for thirds in ((0, 1), (2,)):
        if thirds == (2,):
            sums_f[2].land(line)
            far_c.land(line)
            if not far_c.plain:
                small = small + swap_far(small, 2)
            share_q, share_k, share_v, share_o = call(
                functools.partial(attn_shares_kernel, far_c.plain),
                "attn_shares",
                [sds((sh, d), F32)] * 4,
                [SM] + [HBM] * 2,
                [VM] * 4,
                [scratch((2, 6 * sh, 256)), DMA((8,))],
                (line.ids, far_c.kept, *far_c.flying),
            )
            share_q, small = gate(share_q, small)
        parts, starts = [], []
        for f in [sums_f[k] for k in thirds]:
            arr, at = next(iter(f.flying.values()))
            parts += [f.buffer, *gate(arr)]
            starts += [0, at[0].start if at else 0]
        n = len(thirds)
        shares = list(call(
            functools.partial(ff_shares_kernel, quad, thirds, starts),
            "ff_shares",
            shapes,
            [SM] + [HBM] * (2 * n + len(shares)),
            [HBM] * 2,
            [
                scratch((n, 2, 2 * sh + 384, 256)),
                scratch((n, sh, 1024), F32),
                scratch((n, 256, d), F32),
                DMA((16 * n + 5 * n,)),
            ],
            (line.ids, *parts, *shares),
            aliases={1 + 2 * n + i: i for i in range(len(shares))},
            us=1,
        ))
        shares[0], small = gate(shares[0], small)
        if thirds == (0, 1):
            small = lax.psum(small, "far") if far_c.plain else small + swap_far(small, 1)
    share_in, share_back = shares
    total_gain_attn, total_gain_ff = small[:d], small[d : 2 * d]
    total_table = small[2 * d :].reshape(bucket_count, heads)


    return (
        output,
        grad_inputs,
        total_gain_attn,
        share_q,
        share_k,
        share_v,
        share_o,
        total_table,
        total_gain_ff,
        share_in,
        share_back,
    )


def solution(mesh):
    far = mesh.shape["rows"] // 2
    inner = jax.sharding.Mesh(mesh.devices.reshape(far, 2, 2, 2), AXES)
    over_rows, over_blk = ("far", "near"), ("side", "core")
    tok, row, rep = P(over_rows, over_blk, None), P(over_blk, None), P()
    return jax.shard_map(
        shards,
        mesh=inner,
        in_specs=(tok, P(over_rows, over_blk), rep, row, row, row, row, rep, rep, row, row, tok),
        out_specs=(tok, tok, rep, row, row, row, row, rep, rep, row, row),
        check_vma=False,
    )
```

```python
import functools

import jax
import jax.numpy as jnp
from jax import lax
from jax.experimental import pallas as pl
from jax.experimental.pallas import tpu as pltpu
from jax.sharding import PartitionSpec as P

EPS = 1e-06
EDGES = (1, 2, 3, 4, 5, 6, 7, 8, 12, 16, 23, 32, 46, 64, 91)
BF = jnp.bfloat16
F32 = jnp.float32
HBM = pl.BlockSpec(memory_space=pltpu.HBM)
VM = pl.BlockSpec(memory_space=pltpu.VMEM)
SM = pl.BlockSpec(memory_space=pltpu.SMEM)
DMA = pltpu.SemaphoreType.DMA
sds = jax.ShapeDtypeStruct
AXES = ("far", "near", "side", "core")
FLIPS = {"far2": 16, "far1": 8, "near": 4, "whole": 4, "side": 2, "core": 1}


def scratch(shape, kind=BF):
    return pltpu.VMEM(shape, kind)


def call(kernel, name, outs, ins, out_specs, scratches, args, us=10, aliases={}):
    return pl.pallas_call(
        kernel,
        out_shape=outs,
        in_specs=ins,
        out_specs=out_specs,
        scratch_shapes=scratches,
        input_output_aliases=aliases,
        compiler_params=pltpu.CompilerParams(vmem_limit_bytes=63 * 1024 * 1024),
        cost_estimate=pl.CostEstimate(flops=int(us * 10**9), bytes_accessed=int(us * 4 * 10**6), transcendentals=0),
        name=name,
    )(*args)


def nn(a, b):
    return lax.dot_general(a, b, (((1,), (0,)), ((), ())), preferred_element_type=F32)


def nt(a, b):
    return lax.dot_general(a, b, (((1,), (1,)), ((), ())), preferred_element_type=F32)


def tn(a, b):
    return lax.dot_general(a, b, (((0,), (0,)), ((), ())), preferred_element_type=F32)


def swap(value, *axes):
    flip = sum(FLIPS[a] for a in axes)
    count = 1
    for a in AXES:
        count *= lax.axis_size(a)
    return lax.ppermute(value, AXES, [(i, i ^ flip) for i in range(count)])


def swap_far(value, bits):
    count = 8 * lax.axis_size("far")
    return lax.ppermute(value, AXES, [(i, i ^ (8 * bits)) for i in range(count)])


class Line:
    def __init__(self, ids):
        self.ids = ids

    def gate(self, *values):
        self.ids, *values = lax.optimization_barrier((self.ids, *values))
        return tuple(values)


def pick(arr, index, axis=0):
    return lax.dynamic_index_in_dim(arr, index, axis, keepdims=False)


class Sum:
    AXES = (("side", "near"), ("near", "side"))
    ORDER = (0, 2, 1, 3)

    def __init__(self, keep, send):
        self.rows = keep.shape[3]
        places = [(p, i, j) for p in (0, 1) for i in (0, 1) for j in (0, 1)]
        self.kept = {at: (keep, at) for at in places}
        got = swap(send, "core")
        self.flying = {at: (got, at) for at in places}

    def added(self, key):
        return self.kept[key], self.flying[key]

    def land(self, line):
        arrays = []
        for arr, _ in self.flying.values():
            if not any(arr is f for f in arrays):
                arrays.append(arr)
        landed = line.gate(*arrays)
        here = lambda arr: next(l for f, l in zip(arrays, landed) if f is arr)
        self.flying = {key: (here(arr), at) for key, (arr, at) in self.flying.items()}

    def first(self):
        out = []
        for p, i, j in self.kept:
            move = (self.AXES[p][0], (p, j)) if i else None
            out.append((*self.added((p, i, j)), None if i else (p, j), move))
        return self.rows, out

    def second(self):
        out = []
        for p, j in self.kept:
            out.append((*self.added((p, j)), None if j else p, (self.AXES[p][1], p) if j else None))
        return self.rows, out

    def third(self):
        return self.rows, [(*self.added(p), p, None) for p in (0, 1)]

    def spread(self):
        out = []
        cut = lambda block, i: (block[0], (*block[1], ("far", i)))
        for p in (0, 1):
            a, b = self.added(p)
            for i in range(4):
                sent = i & 1
                out.append((cut(a, i), cut(b, i), None if sent else (p, i), ("far1", (p, i - 1)) if sent else None))
        return self.rows // 4, out

    def pair(self):
        out = [(*self.added((p, i)), None if i else p, ("far2", p) if i else None) for p in (0, 1) for i in (0, 2)]
        return self.rows // 4, out

    def back(self):
        return self.rows // 4, [(*self.added(p), (p, 0), ("far2", (p, 2))) for p in (0, 1)]

    def last(self):
        have = {**self.kept, **self.flying}
        out = [(have[p, i], None, (p, i), ("far1", (p, i + 1))) for p in (0, 1) for i in (0, 2)]
        return self.rows // 4, out

    def finish(self):
        have = {**self.kept, **self.flying}
        out = [(have[p, i], None, (p, i), ("whole", (p, i))) for p in (0, 1) for i in self.ORDER]
        return self.rows // 4, out


class FarSum:
    def __init__(self, parts):
        total = jnp.concatenate(parts, axis=0)
        self.plain = lax.axis_size("far") != 4
        if self.plain:
            self.kept, self.flying = lax.psum(total, "far"), ()
            return
        blocks = total.reshape(4, -1, 256)
        here = lax.axis_index("far")
        self.kept = pick(blocks, here)
        self.flying = tuple(swap_far(pick(blocks, here ^ i), i) for i in (1, 2, 3))

    def land(self, line):
        if self.flying:
            self.flying = line.gate(*self.flying)

    def back(self):
        if self.plain:
            return
        total = self.kept.astype(F32)
        for f in self.flying:
            total = total + f.astype(F32)
        self.kept = total.astype(BF)
        self.flying = tuple(swap_far(self.kept, i) for i in (1, 2, 3))

    def finish(self, line):
        if self.plain:
            self.result = (self.kept, swap(self.kept, "near"))
            return
        (whole,) = line.gate(jnp.stack([self.kept, *self.flying]))
        self.flying = (swap(whole, "near"),)
        self.result = (whole, *self.flying)


def add_kernel(jobs, arrays, ids, *refs):
    ins, refs = refs[:arrays], refs[arrays:]
    count = len(jobs)
    bufs, sems = refs[-1 - 2 * count : -1], refs[-1]
    outs = refs[: len(refs) - 1 - 2 * count]
    far = ids[3]
    dma = Copies(sems)

    def view(ref, at, rows):
        if at and isinstance(at[-1], tuple):
            *at, (_, i) = at
            start = at.pop().start if at and hasattr(at[-1], "start") else 0
            at = (*at, pl.ds(pl.multiple_of(start + (far ^ i) * rows, 16), rows))
        return ref.at[tuple(at)] if at else ref

    loads = []
    for n, (rows, a, b, _) in enumerate(jobs):
        loads.append(dma.start([(view(ins[x], at, rows), bufs[2 * n + m]) for m, (x, at) in enumerate((a, b)) if x >= 0]))
    stores = []
    for n, (rows, a, b, places) in enumerate(jobs):
        wait(loads[n])
        buf = bufs[2 * n]
        if b[0] >= 0:
            buf[...] = buf[...] + bufs[2 * n + 1][...]
        stores += dma.start([(buf, outs[o].at[pl.ds(row, rows)]) for o, row in places])
    wait(stores)


def advance(line, *steps, new=()):
    flying = []
    for piece, _ in steps:
        for arr, _ in piece.flying.values():
            if not any(arr is f for f in flying):
                flying.append(arr)
    landed = list(line.gate(*flying, *new))
    here = lambda arr: next(l for f, l in zip(flying, landed) if f is arr)
    fresh = Sum(*landed[len(flying) :]) if new else None
    if not steps:
        return fresh
    arrays, jobs, sizes, marks = [], [], {}, []

    def number(block):
        if block is None:
            return (-1, ())
        arr, at = block
        if not any(arr is x for x in arrays):
            arrays.append(arr)
        return next(n for n, x in enumerate(arrays) if x is arr), at

    for piece, step in steps:
        piece.flying = {key: (here(arr), at) for key, (arr, at) in piece.flying.items()}
        rows, todo = getattr(piece, step)()
        for a, b, key, move in todo:
            places = []
            for name, mark in ((("kept", piece), key), (move[0] if move else None, move[1] if move else None)):
                if mark is None:
                    continue
                row = sizes.get(name, 0)
                sizes[name] = row + rows
                places.append((name, row))
                marks.append((piece, name, mark, row, rows))
            jobs.append((rows, number(a), number(b), places))
    names = list(sizes)
    jobs = [(rows, a, b, tuple((names.index(n), row) for n, row in places)) for rows, a, b, places in jobs]
    sums = call(
        functools.partial(add_kernel, jobs, len(arrays)),
        "add",
        [sds((sizes[n], 256), BF) for n in names],
        [SM] + [HBM] * len(arrays),
        [HBM] * len(names),
        [scratch((rows, 256)) for rows, *_ in jobs for _ in (0, 1)] + [DMA((4 * len(jobs),))],
        (line.ids, *arrays),
        us=3,
    )
    line.gate(sums[0])
    results = {n: v if isinstance(n, tuple) else swap(v, n) for n, v in zip(names, sums)}
    for piece, _ in steps:
        piece.kept, piece.flying = {}, {}
        piece.buffer = results.get(("kept", piece))
    for piece, name, mark, row, rows in marks:
        where = piece.kept if isinstance(name, tuple) else piece.flying
        where[mark] = (results[name], (pl.ds(row, rows),))
    return fresh


class Gather:
    def __init__(self, line, own, half):
        self.line, self.own = line, own
        self.y = swap(half, "side")
        self.core = swap(own, "core")

    def cross(self):
        self.y, self.core = self.line.gate(self.y, self.core)
        self.x = swap(self.y, "near")

    def relay(self):
        (self.x,) = self.line.gate(self.x)
        self.yc, self.xc = swap(self.y, "core"), swap(self.x, "core")

    def done(self):
        self.yc, self.xc = self.line.gate(self.yc, self.xc)
        return (self.own, self.core, self.y, self.x, self.yc, self.xc)


class Copies:
    def __init__(self, sems):
        self.sems, self.count = sems, 0

    def start(self, pairs):
        out = []
        for src, dst in pairs:
            out.append(pltpu.make_async_copy(src, dst, self.sems.at[self.count]))
            self.count += 1
            out[-1].start()
        return out


def wait(copies):
    for c in copies:
        c.wait()


def pieces_of(refs, me, half):
    own, core, y, x, yc, xc = refs
    out = []
    for h in (0, 1):
        out.append((own.at[h], me, h))
        out.append((core.at[h], me ^ 1, h))
    out.append((y, me ^ 2, half))
    out.append((x, me ^ 2, 1 - half))
    out.append((yc, me ^ 3, half))
    out.append((xc, me ^ 3, 1 - half))
    return out


def pack_copies(refs, me, half, dst, cut):
    return [(cut(ref), dst.at[o, h]) for ref, o, h in pieces_of(refs, me, half)]


def token_copies(slots, me, dst):
    rows = dst.shape[0] // 4
    return [
        (src, dst.at[pl.ds(pl.multiple_of((me ^ s) * rows, rows), rows)]) for s, src in enumerate(slots)
    ]


def put(stage, owner, row, value):
    half, count = stage.shape[2], value.shape[0]
    first = min(count, max(0, half - row))
    if first:
        stage[owner, 0, pl.ds(row, first), :] = value[:first]
    if first < count:
        stage[owner, 1, pl.ds(row + first - half, count - first), :] = value[first:]


def piece_copies(stage, keep, send, ids):
    me, near, core = ids[0], ids[1], ids[2]
    h = stage.shape[2] // 2
    out = []
    for dst, c in ((send, 1 - core), (keep, core)):
        for part in (0, 1):
            for first in (0, 1):
                for second in (0, 1):
                    sy, sx = (first, second) if part == 0 else (second, first)
                    owner = ((me ^ (2 * sy)) & 2) + c
                    out.append((stage.at[owner, near ^ sx, pl.ds(part * h, h)], dst.at[part, first, second]))
    return out


class Either:
    def __init__(self, dma, stage, keep, send, ids, owner, half, part):
        me, near = ids[0], ids[1]
        rows = stage.shape[2] // 2
        sem = dma.sems.at[dma.count]
        dma.count += 1
        sy, sx = ((me ^ owner) >> 1) & 1, near ^ half
        at = (part, sy, sx) if part == 0 else (part, sx, sy)
        src = stage.at[owner, half, pl.ds(part * rows, rows)]
        self.stays = ((me ^ owner) & 1) == 0
        self.copies = [pltpu.make_async_copy(src, dst.at[at], sem) for dst in (keep, send)]
        self.each("start")

    def each(self, name):
        for copy, taken in zip(self.copies, (self.stays, jnp.logical_not(self.stays))):
            pl.when(taken)(getattr(copy, name))

    def wait(self):
        self.each("wait")


def piece_shapes(rows):
    return [sds((2, 2, 2, rows // 4, 256), BF)] * 2


def rows_of(blocks):
    return jnp.concatenate(blocks, axis=0)


def prep_a_kernel(ids, seg, inputs, wq, wk, wv, m0, m1, m2, m3, own0, own1, y0, y1, sems):
    me, half = ids[0], ids[1]
    rows = inputs.shape[1]
    part = wq.shape[0] // 2
    pairs = []
    for g in range(3):
        own, y, at = (own0, y0, 0) if g == 0 else (own1, y1, g - 1)
        for i, w in enumerate((wq, wk, wv)):
            cols, place = pl.ds(g * 256, 256), pl.ds((3 * at + i) * part, part)
            pairs.append((w.at[pl.ds(pl.multiple_of(half * part, 16), part), cols], y.at[place]))
            for h in (0, 1):
                pairs.append((w.at[pl.ds(h * part, part), cols], own.at[h, place]))
    for s, m in enumerate((m0, m1, m2, m3)):
        pairs.append((inputs.at[me ^ s], m.at[pl.ds(0, rows)]))
    copies = Copies(sems).start(pairs)
    for s, m in enumerate((m0, m1, m2, m3)):
        line = seg[pl.ds(me ^ s, 1), :].astype(F32)
        m[pl.ds(rows, 16), pl.ds(0, rows)] = jnp.broadcast_to(line, (16, rows)).astype(BF)
        m[pl.ds(rows, 16), pl.ds(rows, m.shape[1] - rows)] = jnp.zeros((16, m.shape[1] - rows), BF)
    wait(copies)


def prep_b_kernel(ids, w_in, w_back, w_out, cot, own0, own1, own2, y0, y1, y2, k1, k2, k3, sems):
    me, half = ids[0], ids[1]
    hw = w_in.shape[0] // 2
    pairs = [(cot.at[me ^ s], k) for s, k in ((1, k1), (2, k2), (3, k3))]
    for c, (own, y) in enumerate(((own0, y0), (own1, y1), (own2, y2))):
        for dst, h in ((y, half), (own.at[0], 0), (own.at[1], 1)):
            for b in range(4):
                pairs.append((
                    w_in.at[pl.ds(pl.multiple_of(h * hw, 16), hw), pl.ds(b * 768 + c * 256, 256)],
                    dst.at[pl.ds(b * hw, hw)],
                ))
            for j in range(3):
                pairs.append((
                    w_back.at[pl.ds(pl.multiple_of(c * 256 + h * 128, 16), 128), pl.ds(j * 256, 256)],
                    dst.at[pl.ds(4 * hw + j * 128, 128)],
                ))
                if c == 0:
                    pairs.append((
                        w_out.at[pl.ds(pl.multiple_of(h * hw, 16), hw), pl.ds(j * 256, 256)],
                        dst.at[pl.ds(4 * hw + 384 + j * hw, hw)],
                    ))
    wait(Copies(sems).start(pairs))


def norm_kernel(ids, m0, m1, m2, m3, gain, xs, nrm, nrm_t, seg, sbuf, sems):
    me = ids[0]
    rows = xs.shape[0] // 4
    slots = (m0, m1, m2, m3)
    tok = token_copies([m.at[pl.ds(0, rows)] for m in slots], me, xs)
    tok += token_copies([m.at[pl.ds(rows, 16)] for m in slots], me, sbuf)
    wait(Copies(sems).start(tok))
    seg[...] = jnp.concatenate(
        [sbuf[pl.ds(o * 16, 1), pl.ds(0, rows)].astype(F32) for o in range(4)], axis=1
    )
    for a in range(4):
        x = xs[pl.ds(a * rows, rows), :].astype(F32)
        y = x * lax.rsqrt(jnp.mean(x * x, axis=-1, keepdims=True) + EPS) * gain[...]
        y = y.astype(BF)
        nrm[pl.ds(a * rows, rows), :] = y
        nrm_t[:, pl.ds(a * rows, rows)] = y.T


def half_masks(t):
    lane = lax.broadcasted_iota(jnp.int32, (t, 128), 1)
    return lane < 64, (lane < 64).astype(F32).astype(BF), (lane >= 64).astype(F32).astype(BF)


def attn_fwd_kernel(group, ids, far, seg, lines, nrm_in, w0, w1, w2, w3, w4, w5,
                    q_out, k_out, v_out, p_out, o, near, nrm, wbuf, q, k, v, p, sems):
    me, half = ids[0], ids[1]
    dma = Copies(sems)
    count = wbuf.shape[2]
    part = count // 3
    place = pl.ds(max(group - 1, 0) * count, count)
    loads = dma.start(
        [(nrm_in, nrm)]
        + pack_copies((w0, w1, w2, w3, w4, w5), me, half, wbuf, lambda ref: ref.at[place])
    )
    for head in range(4):
        line = jnp.broadcast_to(lines[pl.ds(4 * group + head, 1), :], (near.shape[1], lines.shape[1]))
        near[head] = pltpu.roll(line, 0, 1, stride=1, stride_axis=0)[:, : near.shape[2]]
    t = near.shape[1]
    length = q.shape[0]
    nblk = length // t
    low, m0, m1 = half_masks(t)
    eye = lax.broadcasted_iota(jnp.int32, (t, t), 0) == lax.broadcasted_iota(jnp.int32, (t, t), 1)
    seg_row = seg[...]
    wait(loads)
    stores = []
    for i, (buf, out) in enumerate(((q, q_out), (k, k_out), (v, v_out))):
        w = rows_of([wbuf[ow, h, pl.ds(i * part, part), :] for ow in range(4) for h in (0, 1)])
        buf[...] = nn(nrm[...], w).astype(BF)
        stores += dma.start([(buf, out)])
    for pair in (0, 1):
        at = pl.ds(pair * 128, 128)
        for a in range(nblk):
            seg_col = jnp.sum(
                jnp.where(eye, jnp.broadcast_to(seg_row[:, a * t : (a + 1) * t], (t, t)), 0.0),
                axis=1,
                keepdims=True,
            )
            allowed = seg_col == seg_row
            q2 = q[pl.ds(a * t, t), at]
            s = nt(rows_of([q2 * m0, q2 * m1]), k[:, at])
            ps = []
            for h in (0, 1):
                head = 2 * pair + h
                strip = []
                for b in range(nblk):
                    rel = b - a
                    if abs(rel) <= 1:
                        strip.append(near[head, :, (rel + 1) * t : (rel + 2) * t])
                    else:
                        strip.append(jnp.full((t, t), far[int(rel > 0), group * 4 + head], F32))
                sh = s[h * t : (h + 1) * t] + jnp.concatenate(strip, axis=1)
                sh = jnp.where(allowed, sh, -1e30)
                top = jnp.max(sh, axis=-1, keepdims=True)
                e = jnp.exp(sh - top)
                inv = 1.0 / jnp.sum(e, axis=-1, keepdims=True)
                ph = (e * inv).astype(BF)
                p[head, pl.ds(a * t, t), :] = ph
                ps.append(ph)
            mix = nn(rows_of(ps), v[:, at])
            o[pl.ds(a * t, t), at] = jnp.where(low, mix[:t], mix[t:]).astype(BF)
        stores += dma.start([(p.at[pl.ds(2 * pair, 2)], p_out.at[pl.ds(2 * pair, 2)])])
    wait(stores)


def out_weight(wbuf, j):
    hw = wbuf.shape[2] // 3
    return rows_of([wbuf[o, h, pl.ds(j * hw, hw), :] for o in range(4) for h in (0, 1)])


def out_cut(sh):
    return lambda ref: ref.at[pl.ds(2 * sh + 384, 3 * (sh // 2))]


def gelu_both(x):
    c = 0.7978845608028654
    x2 = x * x
    th = jnp.tanh(x * (c + (c * 0.044715) * x2))
    half_up = 0.5 + 0.5 * th
    slope = half_up + x * (0.5 - 0.5 * th * th) * (c + (3.0 * c * 0.044715) * x2)
    return x * half_up, slope


def ffn_kernel(lead, ids, *refs):
    if lead:
        gain, xs, x0, x1, x2, cown, c1, c2, c3, p0, p1, p2, p3, p4, p5, *rest = refs
        hid_out, ff_out, fft_out, act_out, gpre_out, keep, send, *rest = rest
        xv, mx, wout, hid, ffv, fftv, cot, pack, act, gpre, stage, sems = rest
    else:
        ff, ff_t, cown, c1, c2, c3, p0, p1, p2, p3, p4, p5, act_out, gpre_out, keep, send, *rest = refs
        ffv, fftv, cot, pack, act, gpre, stage, sems = rest
    me, half = ids[0], ids[1]
    d = ffv.shape[1]
    sh = d // 4
    hw = sh // 2
    packs = (p0, p1, p2, p3, p4, p5)
    dma = Copies(sems)
    split = lambda at, n: [
        (ref.at[pl.ds(at, n)], pack.at[o, h, pl.ds(at, n)]) for ref, o, h in pieces_of(packs, me, half)
    ]
    weights, back_weights = split(0, 4 * hw), split(4 * hw, 384)
    stores = []
    if lead:
        early = dma.start(
            pack_copies(packs, me, half, wout, out_cut(sh))
            + [(x, mx.at[:, pl.ds(i * 256, 256)]) for i, x in enumerate((x0, x1, x2))]
            + [(xs, xv)]
        )
        first = dma.start(weights)
    else:
        first = dma.start([(ff, ffv)] + weights)
    second = dma.start(token_copies((cown.at[me], c1, c2, c3), me, cot) + back_weights)
    if lead:
        third = ()
        wait(early)
        for j in range(3):
            cols = pl.ds(j * 256, 256)
            hid[:, cols] = xv[:, cols].astype(F32) + nn(mx[...], out_weight(wout, j))
        rows = 128
        for a in range(xv.shape[0] // rows):
            x = hid[pl.ds(a * rows, rows), :]
            y = x * lax.rsqrt(jnp.mean(x * x, axis=-1, keepdims=True) + EPS) * gain[...]
            y = y.astype(BF)
            ffv[pl.ds(a * rows, rows), :] = y
            fftv[:, pl.ds(a * rows, rows)] = y.T
        stores += dma.start([(hid, hid_out), (ffv, ff_out), (fftv, fft_out)])
    else:
        third = dma.start([(ff_t, fftv)])
    wait(first)
    for b in range(5):
        if b < 4:
            at = pl.ds(b * 256, 256)
            win = rows_of([pack[o, h, pl.ds(b * hw, hw), :] for o in range(4) for h in (0, 1)])
            value, slope = gelu_both(nn(ffv[...], win))
            if b == 0:
                wait(second)
            act[:, at] = value.astype(BF)
            back = 0.0
            for j in range(3):
                wb = rows_of([pack[b, h, pl.ds(4 * hw + j * 128, 128), :] for h in (0, 1)])
                back = back + nt(cot[:, pl.ds(j * 256, 256)], wb)
            gpre[:, at] = (back * slope).astype(BF)
        if b == 3:
            stores += dma.start([(act, act_out), (gpre, gpre_out)])
        if b > 0:
            c = b - 1
            at = pl.ds(c * 256, 256)
            if c == 0:
                wait(third)
            gw = nn(fftv[...], gpre[:, at]).astype(BF)
            for o in range(4):
                put(stage, o, c * sh, gw[o * sh : (o + 1) * sh])
            gb = tn(act[:, at], cot[...]).astype(BF)
            for j in range(3):
                put(stage, c, 4 * sh + j * 256, gb[:, j * 256 : (j + 1) * 256])
            stores += [Either(dma, stage, keep, send, ids, c, 1, part) for part in (0, 1)]
            if c & 1:
                stores += [Either(dma, stage, keep, send, ids, o, 0, c // 2) for o in range(4)]
    wait(stores)


def after_ff_kernel(ids, gain, hid, g0, g1, g2, cown, c1, c2, c3, x0, x1, x2, *refs):
    packs = (refs[0:6], refs[6:12], refs[12:18])
    ghid_out, gm0, gm1, gm2, ggain, gwo_out, hidv, gv, cot, mx, wbuf, wins, ga, gf, ghid, gmv, gwo, sems = refs[18:]
    stores = []
    me, half = ids[0], ids[1]
    d = hid.shape[1]
    sh = d // 4
    hw = sh // 2
    rows = cot.shape[0] // 4
    dma = Copies(sems)
    loads = [
        dma.start(
            [(g, gv.at[c])]
            + pack_copies(packs[c], me, half, wins.at[c], lambda ref: ref.at[pl.ds(0, 4 * hw)])
        )
        for c, g in enumerate((g0, g1, g2))
    ]
    rest = dma.start([(hid, hidv)] + token_copies((cown.at[me], c1, c2, c3), me, cot))
    last = dma.start(
        pack_copies(packs[0], me, half, wbuf, out_cut(sh))
        + [(x, mx.at[:, pl.ds(i * 256, 256)]) for i, x in enumerate((x0, x1, x2))]
    )
    for c in range(3):
        wait(loads[c])
        acc = None
        for b in range(4):
            w = rows_of([wins[c, o, h, pl.ds(b * hw, hw), :] for o in range(4) for h in (0, 1)])
            term = nt(gv[c, :, pl.ds(b * 256, 256)], w)
            acc = term if acc is None else acc + term
        gf[...] = acc if c == 0 else gf[...] + acc
    wait(rest)
    total = jnp.zeros((1, d), F32)
    for a in range(4):
        at = pl.ds(a * rows, rows)
        x = hidv[at, :]
        gfa = gf[at, :]
        n = lax.rsqrt(jnp.mean(x * x, axis=-1, keepdims=True) + EPS)
        g = gfa * gain[...]
        xn = x * n
        total = total + jnp.sum(gfa * xn, axis=0, keepdims=True)
        gh = cot[at, :].astype(F32) + n * (g - xn * (n * jnp.mean(g * x, axis=-1, keepdims=True)))
        ghid[at, :] = gh
        ga[at, :] = gh.astype(BF)
    ggain[...] = total
    stores += dma.start([(ghid, ghid_out)])
    wait(last)
    acc = None
    for j in range(3):
        term = nt(ga[:, pl.ds(j * 256, 256)], out_weight(wbuf, j))
        acc = term if acc is None else acc + term
    for i, gm in enumerate((gm0, gm1, gm2)):
        gmv[i] = acc[:, i * 256 : (i + 1) * 256].astype(BF)
        stores += dma.start([(gmv.at[i], gm)])
    for j in range(3):
        gw = tn(mx[...], ga[:, pl.ds(j * 256, 256)]).astype(BF)
        for o in range(4):
            gwo[o, pl.ds(j * sh, sh), :] = gw[o * sh : (o + 1) * sh]
        rows_j = pl.ds(j * sh, sh)
        stores += dma.start([(gwo.at[:, rows_j], gwo_out.at[:, rows_j])])
    wait(stores)


def out_kernel(ids, hid, gin, a0, a1, a2, *refs):
    packs = (refs[0:6], refs[6:12], refs[12:18])
    out, hidv, av, wb, sems = refs[18:]
    me, half = ids[0], ids[1]
    d = hid.shape[1]
    hw = d // 8
    rows = hid.shape[0] // 4
    dma = Copies(sems)
    loads = [
        dma.start(
            [(a, av.at[c])]
            + pack_copies(packs[c], me, half, wb.at[c], lambda ref: ref.at[pl.ds(4 * hw, 384)])
        )
        for c, a in enumerate((a0, a1, a2))
    ]
    last = dma.start([(hid, hidv)])
    grads = dma.start([(gin.at[pl.ds(b * rows, rows)], out.at[b, 1]) for b in range(4)])
    for c in range(3):
        wait(loads[c])
    wait(last)
    for j in range(3):
        cols = pl.ds(j * 256, 256)
        acc = hidv[:, cols]
        for c in range(3):
            w = rows_of([wb[c, o, h, pl.ds(j * 128, 128), :] for o in range(4) for h in (0, 1)])
            acc = acc + nn(av[c], w)
        acc = acc.astype(BF)
        for b in range(4):
            out[b, 0, :, cols] = acc[b * rows : (b + 1) * rows]
    wait(grads)


def diagonals(x):
    width = x.shape[1]
    y = x[0:8]
    for a in range(8, x.shape[0], 8):
        y = y + pltpu.roll(x[a : a + 8], width - a, 1)
    sub = lax.broadcasted_iota(jnp.int32, y.shape, 0)
    for bit in (1, 2, 4):
        y = jnp.where((sub & bit) != 0, pltpu.roll(y, width - bit, 1), y)
    return jnp.sum(y, axis=0, keepdims=True)


def attn_bwd_kernel(groups, carried, ids, nrm_in, *refs):
    ins, refs = refs[: 5 * groups], refs[5 * groups :]
    carry, refs = refs[:carried], refs[carried:]
    keep, send, *refs = refs
    outs, refs = refs[: 3 * groups], refs[3 * groups :]
    (diag, q, k, v, p, gm, nrm_t, dq, dk, dv, acc, stage, sems) = refs
    t = 128
    length = nrm_t.shape[1]
    nblk = length // t
    low, m0, m1 = half_masks(t)
    dma = Copies(sems)
    loads = []
    for n in range(groups):
        q_in, k_in, v_in, p_in, gm_in = ins[5 * n : 5 * n + 5]
        whole = [(v_in, v.at[n]), (gm_in, gm.at[n]), (k_in, k.at[n]), (q_in, q.at[n])]
        halves = [[(p_in.at[pl.ds(2 * i, 2)], p.at[pl.ds(4 * n + 2 * i, 2)])] for i in (0, 1)]
        loads += [dma.start(whole + halves[0]), dma.start(halves[1])]
        if n == 0:
            last = dma.start([(nrm_in, nrm_t)])
    base, half = 0, stage.shape[2]
    for g in carry:
        count = g.shape[1]
        inside = min(count, half - base) if base < half else 0
        if inside:
            last += dma.start([(g.at[:, pl.ds(0, inside)], stage.at[:, 0, pl.ds(base, inside)])])
        if inside < count:
            rest, at = count - inside, max(0, base - half)
            last += dma.start([(g.at[:, pl.ds(inside, rest)], stage.at[:, 1, pl.ds(at, rest)])])
        base += count
    sh = nrm_t.shape[0] // 4
    stores = []
    for n in range(groups):
        for pair in (0, 1):
            wait(loads[2 * n + pair])
            cols = pl.ds(pair * 128, 128)
            k2, v2 = k[n, :, cols], v[n, :, cols]
            dk_t = jnp.zeros((128, length), F32)
            dv_t = jnp.zeros((128, length), F32)
            for a in range(nblk):
                at = pl.ds(a * t, t)
                q2, g2 = q[n, at, cols], gm[n, at, cols]
                qm = rows_of([q2 * m0, q2 * m1])
                g_both = rows_of([g2 * m0, g2 * m1])
                dp = nt(g_both, v2)
                pb = rows_of([p[4 * n + 2 * pair, at, :], p[4 * n + 2 * pair + 1, at, :]])
                pf = pb.astype(F32)
                delta = jnp.sum(pf * dp, axis=-1, keepdims=True)
                ds = (pf * (dp - delta)).astype(BF)
                mq = nn(ds, k2)
                dq[n, at, cols] = jnp.where(low, mq[:t], mq[t:]).astype(BF)
                dk_t = dk_t + tn(qm, ds)
                dv_t = dv_t + tn(g_both, pb)
                dsf = ds.astype(F32)
                for h in (0, 1):
                    for b in range(nblk):
                        rel = b - a
                        place = rel + 1 if abs(rel) <= 1 else (3 if rel < 0 else 4)
                        tile = dsf[h * t : (h + 1) * t, b * t : (b + 1) * t]
                        lanes = pl.ds(place * t, t)
                        if (a, b) in ((1, 0), (0, 0), (0, 1), (2, 0), (0, 2)):
                            acc[h, :, lanes] = tile
                        else:
                            acc[h, :, lanes] += tile
            dk[n, :, cols] = dk_t.T.astype(BF)
            dv[n, :, cols] = dv_t.T.astype(BF)
            for h in (0, 1):
                near = jnp.concatenate([acc[h, :, pl.ds(0, 3 * t)], jnp.zeros((t, t), F32)], axis=1)
                far = jnp.sum(acc[h, :, pl.ds(3 * t, 2 * t)], axis=0, keepdims=True)
                diag[pl.ds(4 * n + 2 * pair + h, 1), :] = jnp.concatenate([diagonals(near), far], axis=1)
        stores += dma.start([(d.at[n], out) for d, out in zip((dq, dk, dv), outs[3 * n : 3 * n + 3])])
        if n == 0:
            wait(last)
        for i, g in enumerate((dq, dk, dv)):
            gw = nn(nrm_t[...], g[n]).astype(BF)
            for o in range(4):
                put(stage, o, base + i * sh, gw[o * sh : (o + 1) * sh])
        base += 3 * sh
    stores += dma.start(piece_copies(stage, keep, send, ids))
    wait(stores)


def first_norm_kernel(ids, gain, xs, ghid, *refs):
    ins = refs[0:9]
    w0, w1 = refs[9:15], refs[15:21]
    gi, ggain, xv, gv, dall, wbuf0, wbuf1, gn, sems = refs[21:]
    me, half = ids[0], ids[1]
    d = xs.shape[1]
    rows = xs.shape[0] // 4
    dma = Copies(sems)
    loads = dma.start(
        [(g, dall.at[n]) for n, g in enumerate(ins)]
        + pack_copies(w0, me, half, wbuf0, lambda ref: ref)
        + pack_copies(w1, me, half, wbuf1, lambda ref: ref)
    )
    part = wbuf0.shape[2] // 3
    rest = dma.start([(xs, xv), (ghid, gv)])
    wait(loads)
    acc = None
    for i in range(3):
        for c in range(3):
            buf, at = (wbuf0, i) if c == 0 else (wbuf1, 3 * (c - 1) + i)
            wi = rows_of([buf[o, h, pl.ds(at * part, part), :] for o in range(4) for h in (0, 1)])
            term = nt(dall[3 * i + c], wi)
            acc = term if acc is None else acc + term
    gn[...] = acc
    wait(rest)
    total = jnp.zeros((1, d), F32)
    for a in range(4):
        at = pl.ds(a * rows, rows)
        x = xv[at, :].astype(F32)
        gf = gn[at, :]
        n = lax.rsqrt(jnp.mean(x * x, axis=-1, keepdims=True) + EPS)
        g = gf * gain[...]
        xn = x * n
        total = total + jnp.sum(gf * xn, axis=0, keepdims=True)
        gi[at, :] = (gv[at, :] + n * (g - xn * (n * jnp.mean(g * x, axis=-1, keepdims=True)))).astype(BF)
    ggain[...] = total


def tokens_kernel(ids, tokens, out, gin):
    out[...] = tokens[:, 0]
    gin[...] = tokens[:, 1].astype(F32)


def ff_shares_kernel(quad, thirds, starts, ids, *refs):
    ins, (out_in, out_back, buf, part_in, part_back, sems) = refs, refs[-6:]
    here, far = ids[1], ids[3]
    sh = out_in.shape[0]
    dma = Copies(sems)
    n = (2 * sh + 384) // 8
    copies = []
    for k in range(len(thirds)):
        pairs = []
        for m, h in ((2 * k, here), (2 * k + 1, 1 - here)):
            src = ins[m].at[pl.ds(starts[m], 8 * n)]
            if not quad:
                pairs.append((src, buf.at[k, h]))
                continue
            for p in (0, 1):
                for q, i in enumerate(Sum.ORDER):
                    row = pl.multiple_of(p * 4 * n + (far ^ i) * n, 16)
                    pairs.append((src.at[pl.ds((4 * p + q) * n, n)], buf.at[k, h, pl.ds(row, n)]))
        copies.append(dma.start(pairs))
    stores = []
    for m, k in enumerate(thirds):
        wait(copies[m])
        for b in range(4):
            part_in[m, :, pl.ds(b * 256, 256)] = buf[m, 0, pl.ds(b * sh, sh), :].astype(F32)
        stores += dma.start([
            (part_in.at[m, :, pl.ds(b * 256, 256)], out_in.at[:, pl.ds((b * 3 + k) * 256, 256)]) for b in range(4)
        ])
        for j in range(3):
            part_back[m, :, pl.ds(j * 256, 256)] = buf[m, 1, pl.ds(j * 256, 256), :].astype(F32)
        stores += dma.start([(part_back.at[m], out_back.at[pl.ds(k * 256, 256)])])
    wait(stores)


def attn_shares_kernel(plain, ids, *refs):
    ins, (wq, wk, wv, wo, buf, sems) = refs[:-6], refs[-6:]
    here, far = ids[1], ids[3]
    sh = wq.shape[0]
    pairs = []
    for m, h in ((0, here), (1, 1 - here)):
        if plain:
            pairs.append((ins[m], buf.at[h]))
            continue
        n = ins[m].shape[1]
        pairs += [(ins[m].at[i], buf.at[h, pl.ds(pl.multiple_of((far ^ i) * n, 16), n)]) for i in range(4)]
    wait(Copies(sems).start(pairs))
    at = lambda half, n: buf[half, pl.ds(n * sh, sh), :].astype(F32)
    for i in range(3):
        wo[:, pl.ds(i * 256, 256)] = at(0, i)
    for i, out in enumerate((wq, wk, wv)):
        out[:, pl.ds(0, 256)] = at(1, i)
        out[:, pl.ds(256, 256)] = at(0, 3 + i)
        out[:, pl.ds(512, 256)] = at(1, 3 + i)


def bucket_of(offset, bucket_count):
    distance = jnp.abs(offset)
    bucket = jnp.where(offset > 0, bucket_count // 2, 0).astype(jnp.int32)
    for edge in EDGES:
        bucket = bucket + (distance >= edge).astype(jnp.int32)
    return bucket


def shards(inputs, segments, gain_attn, w_query, w_key, w_value, w_out, bucket_bias_table, gain_ff, w_in, w_back, cotangent):
    seqs, rows, d = inputs.shape
    sh = w_query.shape[0]
    hw = sh // 2
    ffs = w_in.shape[1]
    bucket_count, heads = bucket_bias_table.shape
    length = rows * seqs
    places = [lax.axis_index(a).astype(jnp.int32) for a in ("near", "side", "core", "far")]
    near_at, side_at, core_at, far_at = places
    line = Line(jnp.stack([2 * side_at + core_at, near_at, core_at, far_at]))
    gate = line.gate
    row_low, row_f32 = sds((length, d), BF), sds((length, d), F32)
    quad_low, tok_low = sds((length, 256), BF), sds((rows, d), BF)
    gain1, gain2 = gain_attn.reshape(1, d), gain_ff.reshape(1, d)
    pack_rows = [4 * hw + 384 + 3 * hw, 4 * hw + 384, 4 * hw + 384]

    m0, m1, m2, m3, own_a, own_b, y_a, y_b = call(
        prep_a_kernel,
        "prep_a",
        [sds((rows + 16, d), BF)] * 4
        + [sds((2, 3 * hw, 256), BF), sds((2, 6 * hw, 256), BF), sds((3 * hw, 256), BF), sds((6 * hw, 256), BF)],
        [SM, VM] + [HBM] * 4,
        [VM] * 8,
        [DMA((31,))],
        (line.ids, segments, inputs, w_query, w_key, w_value),
    )
    wa = Gather(line, own_a, y_a)
    msgs = [swap(m1, "core"), swap(m2, "side"), swap(m3, "side", "core")]
    wb = Gather(line, own_b, y_b)

    own0, own1, own2, y0, y1, y2, k1, k2, k3 = call(
        prep_b_kernel,
        "prep_b",
        [sds((2, r, 256), BF) for r in pack_rows] + [sds((r, 256), BF) for r in pack_rows] + [tok_low] * 3,
        [SM] + [HBM] * 4,
        [VM] * 9,
        [DMA((75,))],
        (line.ids, w_in, w_back, w_out, cotangent),
    )

    (own0,) = gate(own0)
    wa.cross()
    *msgs, table_in = gate(*msgs, bucket_bias_table)
    wa.relay()

    offs = jnp.arange(4 * rows, dtype=jnp.int32)
    offs = jnp.where(offs < 3 * rows, offs - rows, offs - 5 * rows)
    hot = (bucket_of(offs, bucket_count)[None] == jnp.arange(bucket_count, dtype=jnp.int32)[:, None]).astype(F32)
    lines = jnp.einsum("up,uw->wp", hot, table_in, precision=lax.Precision.HIGHEST)
    far = jnp.stack([table_in[bucket_count // 2 - 1], table_in[bucket_count - 1]])

    y0, own0 = gate(y0, own0)
    wf = [Gather(line, own0, y0)]
    xs, nrm, nrm_t, seg = call(
        norm_kernel,
        "norm",
        [row_low, row_low, sds((d, length), BF), sds((1, length), F32)],
        [SM] + [HBM] * 4 + [VM],
        [VM] * 4,
        [scratch((64, d)), DMA((8,))],
        (line.ids, m0, *msgs, gain1),
    )
    nrm, lines = gate(nrm, lines)
    wb.cross()
    wa = wa.done()

    qs, ks, vs, probs, mixed = [], [], [], [], []
    for g in range(3):
        q, k, v, p, mx = call(
            functools.partial(attn_fwd_kernel, g),
            "attn_fwd",
            [quad_low] * 3 + [sds((4, length, length), BF), quad_low],
            [SM, SM, VM, VM] + [HBM] * 7,
            [HBM] * 4 + [VM],
            [
                scratch((4, rows, 3 * rows), F32),
                scratch((length, d)),
                scratch((4, 2, 3 * hw, 256)),
                scratch((length, 256)),
                scratch((length, 256)),
                scratch((length, 256)),
                scratch((4, length, length)),
                DMA((15,)),
            ],
            (line.ids, far, seg, lines, nrm, *(wa if g == 0 else wb)),
        )
        (mx,) = gate(mx)
        for have, new in ((qs, q), (ks, k), (vs, v), (probs, p), (mixed, mx)):
            have.append(new)
        if g == 0:
            wb.relay()
            wf[0].cross()
            own1, y1 = gate(own1, y1)
            wf.append(Gather(line, own1, y1))
            wb = wb.done()
        if g == 1:
            wf[0].relay()
            wf[1].cross()
            k1, k2, k3 = gate(k1, k2, k3)
            cots = [swap(k1, "core"), swap(k2, "side"), swap(k3, "side", "core")]
    packs = [wf[0].done()]
    cots = gate(*cots)
    wf[1].relay()
    own2, y2 = gate(own2, y2)
    wf.append(Gather(line, own2, y2))

    sums_f, acts, gpres = [], [], []
    for c in range(3):
        lead = c == 0
        *fresh, act, gpre, keep, send = call(
            functools.partial(ffn_kernel, lead),
            "ffn",
            ([row_f32, row_low, sds((d, length), BF)] if lead else [])
            + [sds((length, 1024), BF)] * 2
            + piece_shapes(4 * sh + 768),
            [SM] + ([VM] + [HBM] * 4 if lead else [HBM] * 2) + [HBM] * 10,
            [HBM] * (7 if lead else 4),
            (
                [scratch((length, d)), scratch((length, d)), scratch((4, 2, 3 * hw, 256)), scratch((length, d), F32)]
                if lead
                else []
            )
            + [
                scratch((length, d)),
                scratch((d, length)),
                scratch((length, d)),
                scratch((4, 2, 4 * hw + 384, 256)),
                scratch((length, 1024)),
                scratch((length, 1024)),
                scratch((4, 2, 2 * sh + 384, 256)),
                DMA((60,)),
            ],
            (line.ids, *((gain2, xs, *mixed) if lead else (ff, ff_t)), cotangent, *cots, *packs[c]),
        )
        if lead:
            hid, ff, ff_t = fresh
        piece = (keep, send)
        acts.append(act)
        (gpre,) = gate(gpre)
        gpres.append(gpre)
        if c == 0:
            packs.append(wf[1].done())
            wf[2].cross()
        if c == 1:
            wf[2].relay()
        moves = [[], [("first",)], [("second",), ("first",)]][c]
        sums_f.append(advance(line, *[(f, *m) for f, m in zip(sums_f, moves)], new=piece))
        if c == 1:
            packs.append(wf[2].done())

    ghid, *gmix, ggain_ff, gwo = call(
        after_ff_kernel,
        "after_ff",
        [row_f32] + [quad_low] * 3 + [sds((1, d), F32), sds((4, 3 * sh, 256), BF)],
        [SM, VM] + [HBM] * 29,
        [HBM] * 4 + [VM, HBM],
        [
            scratch((length, d), F32),
            scratch((3, length, 1024)),
            scratch((length, d)),
            scratch((length, d)),
            scratch((4, 2, 3 * hw, 256)),
            scratch((3, 4, 2, 4 * hw, 256)),
            scratch((length, d)),
            scratch((length, d), F32),
            scratch((length, d), F32),
            scratch((3, length, 256)),
            scratch((4, 3 * sh, 256)),
            DMA((52,)),
        ],
        (line.ids, gain2, hid, *gpres, cotangent, *cots, *mixed, *packs[0], *packs[1], *packs[2]),
    )
    gmix[0], ggain_ff = gate(gmix[0], ggain_ff)
    quad = lax.axis_size("far") == 4
    third = "spread" if quad else "third"
    far_steps = lambda *steps: steps if quad else ()
    advance(line, (sums_f[0], third), (sums_f[1], "second"), (sums_f[2], "first"))

    dqs, dks, dvs, diags, sums_a = [], [], [], [], []
    for first, groups in ((0, 1), (1, 2)):
        carry = (gwo,) if first == 0 else ()
        body = 3 * sh * (groups + len(carry))
        some = range(first, first + groups)
        keep, send, *grads, diag = call(
            functools.partial(attn_bwd_kernel, groups, len(carry)),
            "attn_bwd",
            piece_shapes(body) + [quad_low] * (3 * groups) + [sds((4 * groups, 6 * rows), F32)],
            [SM] + [HBM] * (1 + 5 * groups + len(carry)),
            [HBM] * (2 + 3 * groups) + [VM],
            [scratch((groups, length, 256))] * 3
            + [scratch((4 * groups, length, length)), scratch((groups, length, 256)), scratch((d, length))]
            + [scratch((groups, length, 256))] * 3
            + [scratch((2, rows, 5 * rows), F32), scratch((4, 2, body // 2, 256)), DMA((48,))],
            (line.ids, nrm_t, *[a for g in some for a in (qs[g], ks[g], vs[g], probs[g], gmix[g])], *carry),
            us=10 * groups,
        )
        (grads[0],) = gate(grads[0])
        for n in range(groups):
            for have, new in zip((dqs, dks, dvs), grads[3 * n : 3 * n + 3]):
                have.append(new)
        diags.append(diag)
        if first == 0:
            steps = ((sums_f[1], third), (sums_f[2], "second"), *far_steps((sums_f[0], "pair")))
        else:
            steps = ((sums_a[0], "first"), (sums_f[2], third))
            steps += far_steps((sums_f[0], "back"), (sums_f[1], "pair"))
        sums_a.append(advance(line, *steps, new=(keep, send)))

    gin, ggain_attn = call(
        first_norm_kernel,
        "first_norm",
        [row_low, sds((1, d), F32)],
        [SM, VM] + [HBM] * 23,
        [VM] * 2,
        [
            scratch((length, d)),
            scratch((length, d), F32),
            scratch((9, length, 256)),
            scratch((4, 2, 3 * hw, 256)),
            scratch((4, 2, 6 * hw, 256)),
            scratch((length, d), F32),
            DMA((27,)),
        ],
        (line.ids, gain1, xs, ghid, *dqs, *dks, *dvs, *wa, *wb),
    )
    gin, ggain_attn = gate(gin, ggain_attn)
    steps = far_steps((sums_f[0], "last"), (sums_f[1], "back"), (sums_f[2], "pair"))
    advance(line, (sums_a[1], "first"), (sums_a[0], "second"), *steps)
    (tokens,) = call(
        out_kernel,
        "out",
        [sds((seqs, 2, rows, d), BF)],
        [SM] + [HBM] * 23,
        [VM],
        [
            scratch((length, d), F32),
            scratch((3, length, 1024)),
            scratch((3, 4, 2, 384, 256)),
            DMA((32,)),
        ],
        (line.ids, hid, gin, *acts, *packs[0], *packs[1], *packs[2]),
    )
    tokens, ggain_attn = gate(tokens, ggain_attn)
    steps = far_steps((sums_f[0], "finish"), (sums_f[1], "last"), (sums_f[2], "back"))
    advance(line, (sums_a[1], "second"), (sums_a[0], "third"), *steps)
    first_total = sums_a[0].buffer


    hot6 = jnp.concatenate(
        [
            hot,
            jnp.zeros((bucket_count, rows), F32).at[bucket_count // 2 - 1].set(1.0),
            jnp.zeros((bucket_count, rows), F32).at[bucket_count - 1].set(1.0),
        ],
        axis=1,
    )
    table = jnp.einsum("up,wp->uw", hot6, jnp.concatenate(diags, axis=0), precision=lax.Precision.HIGHEST)
    small = jnp.concatenate([ggain_attn.reshape(-1), ggain_ff.reshape(-1), table.reshape(-1)])
    tokens = lax.all_to_all(tokens, ("side", "core"), 0, 0, tiled=True)
    advance(line, (sums_a[1], "third"), *far_steps((sums_f[1], "finish"), (sums_f[2], "last")))
    far_c = FarSum([first_total, sums_a[1].buffer])

    sums_f[1].land(line)
    far_c.land(line)
    far_c.back()
    if quad:
        advance(line, (sums_f[2], "finish"))
    else:
        for f in sums_f:
            whole = lax.psum(f.buffer, "far")
            f.buffer, f.flying = whole, {0: (swap(whole, "near"), ())}
    (small,) = gate(small)
    small = small + swap(small, "core")

    def ff_shares(thirds, have):
        parts, starts = [], []
        for f in [sums_f[k] for k in thirds]:
            arr, at = next(iter(f.flying.values()))
            parts += [f.buffer, *gate(arr)]
            starts += [0, at[0].start if at else 0]
        n = len(thirds)
        return call(
            functools.partial(ff_shares_kernel, quad, thirds, starts),
            "ff_shares",
            [sds((sh, ffs), F32), sds(w_back.shape, F32)],
            [SM] + [HBM] * (2 * n + len(have)),
            [HBM] * 2,
            [
                scratch((n, 2, 2 * sh + 384, 256)),
                scratch((n, sh, 1024), F32),
                scratch((n, 256, d), F32),
                DMA((21 * n,)),
            ],
            (line.ids, *parts, *have),
            aliases={1 + 2 * n + i: i for i in range(len(have))},
            us=1,
        )

    shares = gate(*ff_shares((0, 1), ()))
    sums_f[2].land(line)
    far_c.land(line)
    far_c.finish(line)
    (small,) = gate(small)
    small = small + swap(small, "side")
    tokens, small = gate(tokens, small)
    small = small + swap_far(small, 1) if quad else lax.psum(small, "far")
    output, grad_inputs = call(
        tokens_kernel,
        "tokens",
        [sds((seqs, rows, d), BF), sds((seqs, rows, d), F32)],
        [SM, VM],
        [VM] * 2,
        [],
        (line.ids, tokens),
        us=1,
    )
    output, small = gate(output, small)
    if quad:
        small = small + swap_far(small, 2)
    *shares_c, small = gate(*far_c.result, small)
    small = small + swap(small, "near")
    share_q, share_k, share_v, share_o = call(
        functools.partial(attn_shares_kernel, far_c.plain),
        "attn_shares",
        [sds((sh, d), F32)] * 4,
        [SM] + [HBM] * len(shares_c),
        [VM] * 4,
        [scratch((2, 6 * sh, 256)), DMA((8,))],
        (line.ids, *shares_c),
        us=1,
    )
    share_q, small = gate(share_q, small)
    share_in, share_back = ff_shares((2,), shares)
    total_gain_attn, total_gain_ff = small[:d], small[d : 2 * d]
    total_table = small[2 * d :].reshape(bucket_count, heads)


    return (
        output,
        grad_inputs,
        total_gain_attn,
        share_q,
        share_k,
        share_v,
        share_o,
        total_table,
        total_gain_ff,
        share_in,
        share_back,
    )


def solution(mesh):
    far = mesh.shape["rows"] // 2
    inner = jax.sharding.Mesh(mesh.devices.reshape(far, 2, 2, 2), AXES)
    over_rows, over_blk = ("far", "near"), ("side", "core")
    tok, row, rep = P(over_rows, over_blk, None), P(over_blk, None), P()
    return jax.shard_map(
        shards,
        mesh=inner,
        in_specs=(tok, P(over_rows, over_blk), rep, row, row, row, row, rep, rep, row, row, tok),
        out_specs=(tok, tok, rep, row, row, row, row, rep, rep, row, row),
        check_vma=False,
    )
```

```python
import functools

import jax
import jax.numpy as jnp
from jax import lax
from jax.experimental import pallas as pl
from jax.experimental.pallas import tpu as pltpu
from jax.sharding import PartitionSpec as P

EPS = 1e-06
EDGES = (1, 2, 3, 4, 5, 6, 7, 8, 12, 16, 23, 32, 46, 64, 91)
BF = jnp.bfloat16
F32 = jnp.float32
HBM = pl.BlockSpec(memory_space=pltpu.HBM)
VM = pl.BlockSpec(memory_space=pltpu.VMEM)
SM = pl.BlockSpec(memory_space=pltpu.SMEM)
DMA = pltpu.SemaphoreType.DMA
sds = jax.ShapeDtypeStruct
AXES = ("far", "near", "side", "core")
FLIPS = {"far2": 16, "far1": 8, "near": 4, "whole": 4, "side": 2, "core": 1}


def scratch(shape, kind=BF):
    return pltpu.VMEM(shape, kind)


def call(kernel, name, outs, ins, out_specs, scratches, args, us=10, aliases={}):
    return pl.pallas_call(
        kernel,
        out_shape=outs,
        in_specs=ins,
        out_specs=out_specs,
        scratch_shapes=scratches,
        input_output_aliases=aliases,
        compiler_params=pltpu.CompilerParams(vmem_limit_bytes=63 * 1024 * 1024),
        cost_estimate=pl.CostEstimate(flops=int(us * 10**9), bytes_accessed=int(us * 4 * 10**6), transcendentals=0),
        name=name,
    )(*args)


def nn(a, b):
    return lax.dot_general(a, b, (((1,), (0,)), ((), ())), preferred_element_type=F32)


def nt(a, b):
    return lax.dot_general(a, b, (((1,), (1,)), ((), ())), preferred_element_type=F32)


def tn(a, b):
    return lax.dot_general(a, b, (((0,), (0,)), ((), ())), preferred_element_type=F32)


def swap(value, *axes):
    flip = sum(FLIPS[a] for a in axes)
    count = 1
    for a in AXES:
        count *= lax.axis_size(a)
    return lax.ppermute(value, AXES, [(i, i ^ flip) for i in range(count)])


def swap_far(value, bits):
    count = 8 * lax.axis_size("far")
    return lax.ppermute(value, AXES, [(i, i ^ (8 * bits)) for i in range(count)])


class Line:
    def __init__(self, ids):
        self.ids = ids

    def gate(self, *values):
        self.ids, *values = lax.optimization_barrier((self.ids, *values))
        return tuple(values)


def pick(arr, index, axis=0):
    return lax.dynamic_index_in_dim(arr, index, axis, keepdims=False)


class Sum:
    AXES = (("side", "near"), ("near", "side"))
    ORDER = (0, 2, 1, 3)

    def __init__(self, keep, send):
        self.rows = keep.shape[3]
        places = [(p, i, j) for p in (0, 1) for i in (0, 1) for j in (0, 1)]
        self.kept = {at: (keep, at) for at in places}
        got = swap(send, "core")
        self.flying = {at: (got, at) for at in places}

    def added(self, key):
        return self.kept[key], self.flying[key]

    def land(self, line):
        arrays = []
        for arr, _ in self.flying.values():
            if not any(arr is f for f in arrays):
                arrays.append(arr)
        landed = line.gate(*arrays)
        here = lambda arr: next(l for f, l in zip(arrays, landed) if f is arr)
        self.flying = {key: (here(arr), at) for key, (arr, at) in self.flying.items()}

    def first(self):
        out = []
        for p, i, j in self.kept:
            move = (self.AXES[p][0], (p, j)) if i else None
            out.append((*self.added((p, i, j)), None if i else (p, j), move))
        return self.rows, out

    def second(self):
        out = []
        for p, j in self.kept:
            out.append((*self.added((p, j)), None if j else p, (self.AXES[p][1], p) if j else None))
        return self.rows, out

    def third(self):
        return self.rows, [(*self.added(p), p, None) for p in (0, 1)]

    def spread(self):
        out = []
        cut = lambda block, i: (block[0], (*block[1], ("far", i)))
        for p in (0, 1):
            a, b = self.added(p)
            for i in range(4):
                sent = i & 1
                out.append((cut(a, i), cut(b, i), None if sent else (p, i), ("far1", (p, i - 1)) if sent else None))
        return self.rows // 4, out

    def pair(self):
        out = [(*self.added((p, i)), None if i else p, ("far2", p) if i else None) for p in (0, 1) for i in (0, 2)]
        return self.rows // 4, out

    def back(self):
        return self.rows // 4, [(*self.added(p), (p, 0), ("far2", (p, 2))) for p in (0, 1)]

    def last(self):
        have = {**self.kept, **self.flying}
        out = [(have[p, i], None, (p, i), ("far1", (p, i + 1))) for p in (0, 1) for i in (0, 2)]
        return self.rows // 4, out

    def finish(self):
        have = {**self.kept, **self.flying}
        out = [(have[p, i], None, (p, i), ("whole", (p, i))) for p in (0, 1) for i in self.ORDER]
        return self.rows // 4, out


class FarSum:
    def __init__(self, parts):
        total = jnp.concatenate(parts, axis=0)
        self.plain = lax.axis_size("far") != 4
        if self.plain:
            self.kept, self.flying = lax.psum(total, "far"), ()
            return
        blocks = total.reshape(4, -1, 256)
        here = lax.axis_index("far")
        self.kept = pick(blocks, here)
        self.flying = tuple(swap_far(pick(blocks, here ^ i), i) for i in (1, 2, 3))

    def land(self, line):
        if self.flying:
            self.flying = line.gate(*self.flying)

    def back(self):
        if self.plain:
            return
        total = self.kept.astype(F32)
        for f in self.flying:
            total = total + f.astype(F32)
        self.kept = total.astype(BF)
        self.flying = tuple(swap_far(self.kept, i) for i in (1, 2, 3))

    def finish(self, line):
        if self.plain:
            self.result = (self.kept, swap(self.kept, "near"))
            return
        (whole,) = line.gate(jnp.stack([self.kept, *self.flying]))
        self.flying = (swap(whole, "near"),)
        self.result = (whole, *self.flying)


def add_kernel(jobs, arrays, ids, *refs):
    ins, refs = refs[:arrays], refs[arrays:]
    count = len(jobs)
    bufs, sems = refs[-1 - 2 * count : -1], refs[-1]
    outs = refs[: len(refs) - 1 - 2 * count]
    far = ids[3]
    dma = Copies(sems)

    def view(ref, at, rows):
        if at and isinstance(at[-1], tuple):
            *at, (_, i) = at
            start = at.pop().start if at and hasattr(at[-1], "start") else 0
            at = (*at, pl.ds(pl.multiple_of(start + (far ^ i) * rows, 16), rows))
        return ref.at[tuple(at)] if at else ref

    loads = []
    for n, (rows, a, b, _) in enumerate(jobs):
        loads.append(dma.start([(view(ins[x], at, rows), bufs[2 * n + m]) for m, (x, at) in enumerate((a, b)) if x >= 0]))
    stores = []
    for n, (rows, a, b, places) in enumerate(jobs):
        wait(loads[n])
        buf = bufs[2 * n]
        if b[0] >= 0:
            buf[...] = buf[...] + bufs[2 * n + 1][...]
        stores += dma.start([(buf, outs[o].at[pl.ds(row, rows)]) for o, row in places])
    wait(stores)


def advance(line, *steps, new=()):
    flying = []
    for piece, _ in steps:
        for arr, _ in piece.flying.values():
            if not any(arr is f for f in flying):
                flying.append(arr)
    landed = list(line.gate(*flying, *new))
    here = lambda arr: next(l for f, l in zip(flying, landed) if f is arr)
    fresh = Sum(*landed[len(flying) :]) if new else None
    if not steps:
        return fresh
    arrays, jobs, sizes, marks = [], [], {}, []

    def number(block):
        if block is None:
            return (-1, ())
        arr, at = block
        if not any(arr is x for x in arrays):
            arrays.append(arr)
        return next(n for n, x in enumerate(arrays) if x is arr), at

    for piece, step in steps:
        piece.flying = {key: (here(arr), at) for key, (arr, at) in piece.flying.items()}
        rows, todo = getattr(piece, step)()
        for a, b, key, move in todo:
            places = []
            for name, mark in ((("kept", piece), key), (move[0] if move else None, move[1] if move else None)):
                if mark is None:
                    continue
                row = sizes.get(name, 0)
                sizes[name] = row + rows
                places.append((name, row))
                marks.append((piece, name, mark, row, rows))
            jobs.append((rows, number(a), number(b), places))
    names = list(sizes)
    jobs = [(rows, a, b, tuple((names.index(n), row) for n, row in places)) for rows, a, b, places in jobs]
    sums = call(
        functools.partial(add_kernel, jobs, len(arrays)),
        "add",
        [sds((sizes[n], 256), BF) for n in names],
        [SM] + [HBM] * len(arrays),
        [HBM] * len(names),
        [scratch((rows, 256)) for rows, *_ in jobs for _ in (0, 1)] + [DMA((4 * len(jobs),))],
        (line.ids, *arrays),
        us=3,
    )
    line.gate(sums[0])
    results = {n: v if isinstance(n, tuple) else swap(v, n) for n, v in zip(names, sums)}
    for piece, _ in steps:
        piece.kept, piece.flying = {}, {}
        piece.buffer = results.get(("kept", piece))
    for piece, name, mark, row, rows in marks:
        where = piece.kept if isinstance(name, tuple) else piece.flying
        where[mark] = (results[name], (pl.ds(row, rows),))
    return fresh


class Gather:
    def __init__(self, line, own, half):
        self.line, self.own = line, own
        self.y = swap(half, "side")
        self.core = swap(own, "core")

    def cross(self):
        self.y, self.core = self.line.gate(self.y, self.core)
        self.x = swap(self.y, "near")

    def relay(self):
        (self.x,) = self.line.gate(self.x)
        self.yc, self.xc = swap(self.y, "core"), swap(self.x, "core")

    def done(self):
        self.yc, self.xc = self.line.gate(self.yc, self.xc)
        return (self.own, self.core, self.y, self.x, self.yc, self.xc)


class Copies:
    def __init__(self, sems):
        self.sems, self.count = sems, 0

    def start(self, pairs):
        out = []
        for src, dst in pairs:
            out.append(pltpu.make_async_copy(src, dst, self.sems.at[self.count]))
            self.count += 1
            out[-1].start()
        return out


def wait(copies):
    for c in copies:
        c.wait()


def pieces_of(refs, me, half):
    own, core, y, x, yc, xc = refs
    out = []
    for h in (0, 1):
        out.append((own.at[h], me, h))
        out.append((core.at[h], me ^ 1, h))
    out.append((y, me ^ 2, half))
    out.append((x, me ^ 2, 1 - half))
    out.append((yc, me ^ 3, half))
    out.append((xc, me ^ 3, 1 - half))
    return out


def pack_copies(refs, me, half, dst, cut):
    return [(cut(ref), dst.at[o, h]) for ref, o, h in pieces_of(refs, me, half)]


def token_copies(slots, me, dst):
    rows = dst.shape[0] // 4
    return [
        (src, dst.at[pl.ds(pl.multiple_of((me ^ s) * rows, rows), rows)]) for s, src in enumerate(slots)
    ]


def put(stage, owner, row, value):
    half, count = stage.shape[2], value.shape[0]
    first = min(count, max(0, half - row))
    if first:
        stage[owner, 0, pl.ds(row, first), :] = value[:first]
    if first < count:
        stage[owner, 1, pl.ds(row + first - half, count - first), :] = value[first:]


def piece_copies(stage, keep, send, ids):
    me, near, core = ids[0], ids[1], ids[2]
    h = stage.shape[2] // 2
    out = []
    for dst, c in ((send, 1 - core), (keep, core)):
        for part in (0, 1):
            for first in (0, 1):
                for second in (0, 1):
                    sy, sx = (first, second) if part == 0 else (second, first)
                    owner = ((me ^ (2 * sy)) & 2) + c
                    out.append((stage.at[owner, near ^ sx, pl.ds(part * h, h)], dst.at[part, first, second]))
    return out


class Either:
    def __init__(self, dma, stage, keep, send, ids, owner, half, part):
        me, near = ids[0], ids[1]
        rows = stage.shape[2] // 2
        sem = dma.sems.at[dma.count]
        dma.count += 1
        sy, sx = ((me ^ owner) >> 1) & 1, near ^ half
        at = (part, sy, sx) if part == 0 else (part, sx, sy)
        src = stage.at[owner, half, pl.ds(part * rows, rows)]
        self.stays = ((me ^ owner) & 1) == 0
        self.copies = [pltpu.make_async_copy(src, dst.at[at], sem) for dst in (keep, send)]
        self.each("start")

    def each(self, name):
        for copy, taken in zip(self.copies, (self.stays, jnp.logical_not(self.stays))):
            pl.when(taken)(getattr(copy, name))

    def wait(self):
        self.each("wait")


def piece_shapes(rows):
    return [sds((2, 2, 2, rows // 4, 256), BF)] * 2


def rows_of(blocks):
    return jnp.concatenate(blocks, axis=0)


def prep_a_kernel(ids, seg, inputs, wq, wk, wv, m0, m1, m2, m3, own0, own1, y0, y1, sems):
    me, half = ids[0], ids[1]
    rows = inputs.shape[1]
    part = wq.shape[0] // 2
    pairs = []
    for g in range(3):
        own, y, at = (own0, y0, 0) if g == 0 else (own1, y1, g - 1)
        for i, w in enumerate((wq, wk, wv)):
            cols, place = pl.ds(g * 256, 256), pl.ds((3 * at + i) * part, part)
            pairs.append((w.at[pl.ds(pl.multiple_of(half * part, 16), part), cols], y.at[place]))
            for h in (0, 1):
                pairs.append((w.at[pl.ds(h * part, part), cols], own.at[h, place]))
    for s, m in enumerate((m0, m1, m2, m3)):
        pairs.append((inputs.at[me ^ s], m.at[pl.ds(0, rows)]))
    copies = Copies(sems).start(pairs)
    for s, m in enumerate((m0, m1, m2, m3)):
        line = seg[pl.ds(me ^ s, 1), :].astype(F32)
        m[pl.ds(rows, 16), pl.ds(0, rows)] = jnp.broadcast_to(line, (16, rows)).astype(BF)
        m[pl.ds(rows, 16), pl.ds(rows, m.shape[1] - rows)] = jnp.zeros((16, m.shape[1] - rows), BF)
    wait(copies)


def prep_b_kernel(ids, w_in, w_back, w_out, cot, own0, own1, own2, y0, y1, y2, k1, k2, k3, sems):
    me, half = ids[0], ids[1]
    hw = w_in.shape[0] // 2
    pairs = [(cot.at[me ^ s], k) for s, k in ((1, k1), (2, k2), (3, k3))]
    for c, (own, y) in enumerate(((own0, y0), (own1, y1), (own2, y2))):
        for dst, h in ((y, half), (own.at[0], 0), (own.at[1], 1)):
            for b in range(4):
                pairs.append((
                    w_in.at[pl.ds(pl.multiple_of(h * hw, 16), hw), pl.ds(b * 768 + c * 256, 256)],
                    dst.at[pl.ds(b * hw, hw)],
                ))
            for j in range(3):
                pairs.append((
                    w_back.at[pl.ds(pl.multiple_of(c * 256 + h * 128, 16), 128), pl.ds(j * 256, 256)],
                    dst.at[pl.ds(4 * hw + j * 128, 128)],
                ))
                if c == 0:
                    pairs.append((
                        w_out.at[pl.ds(pl.multiple_of(h * hw, 16), hw), pl.ds(j * 256, 256)],
                        dst.at[pl.ds(4 * hw + 384 + j * hw, hw)],
                    ))
    wait(Copies(sems).start(pairs))


def norm_kernel(ids, m0, m1, m2, m3, gain, xs, nrm, nrm_t, seg, sbuf, sems):
    me = ids[0]
    rows = xs.shape[0] // 4
    slots = (m0, m1, m2, m3)
    tok = token_copies([m.at[pl.ds(0, rows)] for m in slots], me, xs)
    tok += token_copies([m.at[pl.ds(rows, 16)] for m in slots], me, sbuf)
    wait(Copies(sems).start(tok))
    seg[...] = jnp.concatenate(
        [sbuf[pl.ds(o * 16, 1), pl.ds(0, rows)].astype(F32) for o in range(4)], axis=1
    )
    for a in range(4):
        x = xs[pl.ds(a * rows, rows), :].astype(F32)
        y = x * lax.rsqrt(jnp.mean(x * x, axis=-1, keepdims=True) + EPS) * gain[...]
        y = y.astype(BF)
        nrm[pl.ds(a * rows, rows), :] = y
        nrm_t[:, pl.ds(a * rows, rows)] = y.T


def half_masks(t):
    lane = lax.broadcasted_iota(jnp.int32, (t, 128), 1)
    return lane < 64, (lane < 64).astype(F32).astype(BF), (lane >= 64).astype(F32).astype(BF)


def attn_fwd_kernel(group, ids, far, seg, lines, nrm_in, w0, w1, w2, w3, w4, w5,
                    q_out, k_out, v_out, p_out, o, near, nrm, wbuf, q, k, v, p, sems):
    me, half = ids[0], ids[1]
    dma = Copies(sems)
    count = wbuf.shape[2]
    part = count // 3
    place = pl.ds(max(group - 1, 0) * count, count)
    loads = dma.start(
        [(nrm_in, nrm)]
        + pack_copies((w0, w1, w2, w3, w4, w5), me, half, wbuf, lambda ref: ref.at[place])
    )
    for head in range(4):
        line = jnp.broadcast_to(lines[pl.ds(4 * group + head, 1), :], (near.shape[1], lines.shape[1]))
        near[head] = pltpu.roll(line, 0, 1, stride=1, stride_axis=0)[:, : near.shape[2]]
    t = near.shape[1]
    length = q.shape[0]
    nblk = length // t
    low, m0, m1 = half_masks(t)
    eye = lax.broadcasted_iota(jnp.int32, (t, t), 0) == lax.broadcasted_iota(jnp.int32, (t, t), 1)
    seg_row = seg[...]
    wait(loads)
    stores = []
    for i, (buf, out) in enumerate(((q, q_out), (k, k_out), (v, v_out))):
        w = rows_of([wbuf[ow, h, pl.ds(i * part, part), :] for ow in range(4) for h in (0, 1)])
        buf[...] = nn(nrm[...], w).astype(BF)
        stores += dma.start([(buf, out)])
    for pair in (0, 1):
        at = pl.ds(pair * 128, 128)
        for a in range(nblk):
            seg_col = jnp.sum(
                jnp.where(eye, jnp.broadcast_to(seg_row[:, a * t : (a + 1) * t], (t, t)), 0.0),
                axis=1,
                keepdims=True,
            )
            allowed = seg_col == seg_row
            q2 = q[pl.ds(a * t, t), at]
            s = nt(rows_of([q2 * m0, q2 * m1]), k[:, at])
            ps = []
            for h in (0, 1):
                head = 2 * pair + h
                strip = []
                for b in range(nblk):
                    rel = b - a
                    if abs(rel) <= 1:
                        strip.append(near[head, :, (rel + 1) * t : (rel + 2) * t])
                    else:
                        strip.append(jnp.full((t, t), far[int(rel > 0), group * 4 + head], F32))
                sh = s[h * t : (h + 1) * t] + jnp.concatenate(strip, axis=1)
                sh = jnp.where(allowed, sh, -1e30)
                top = jnp.max(sh, axis=-1, keepdims=True)
                e = jnp.exp(sh - top)
                inv = 1.0 / jnp.sum(e, axis=-1, keepdims=True)
                ph = (e * inv).astype(BF)
                p[head, pl.ds(a * t, t), :] = ph
                ps.append(ph)
            mix = nn(rows_of(ps), v[:, at])
            o[pl.ds(a * t, t), at] = jnp.where(low, mix[:t], mix[t:]).astype(BF)
        stores += dma.start([(p.at[pl.ds(2 * pair, 2)], p_out.at[pl.ds(2 * pair, 2)])])
    wait(stores)


def out_weight(wbuf, j):
    hw = wbuf.shape[2] // 3
    return rows_of([wbuf[o, h, pl.ds(j * hw, hw), :] for o in range(4) for h in (0, 1)])


def out_cut(sh):
    return lambda ref: ref.at[pl.ds(2 * sh + 384, 3 * (sh // 2))]


def gelu_both(x):
    c = 0.7978845608028654
    x2 = x * x
    th = jnp.tanh(x * (c + (c * 0.044715) * x2))
    half_up = 0.5 + 0.5 * th
    slope = half_up + x * (0.5 - 0.5 * th * th) * (c + (3.0 * c * 0.044715) * x2)
    return x * half_up, slope


def ffn_kernel(lead, ids, *refs):
    if lead:
        gain, xs, x0, x1, x2, cown, c1, c2, c3, p0, p1, p2, p3, p4, p5, *rest = refs
        hid_out, ff_out, fft_out, act_out, gpre_out, keep, send, *rest = rest
        xv, mx, wout, hid, ffv, fftv, cot, pack, act, gpre, stage, sems = rest
    else:
        ff, ff_t, cown, c1, c2, c3, p0, p1, p2, p3, p4, p5, act_out, gpre_out, keep, send, *rest = refs
        ffv, fftv, cot, pack, act, gpre, stage, sems = rest
    me, half = ids[0], ids[1]
    d = ffv.shape[1]
    sh = d // 4
    hw = sh // 2
    packs = (p0, p1, p2, p3, p4, p5)
    dma = Copies(sems)
    split = lambda at, n: [
        (ref.at[pl.ds(at, n)], pack.at[o, h, pl.ds(at, n)]) for ref, o, h in pieces_of(packs, me, half)
    ]
    weights, back_weights = split(0, 4 * hw), split(4 * hw, 384)
    stores = []
    if lead:
        early = dma.start(
            pack_copies(packs, me, half, wout, out_cut(sh))
            + [(x, mx.at[:, pl.ds(i * 256, 256)]) for i, x in enumerate((x0, x1, x2))]
            + [(xs, xv)]
        )
        first = dma.start(weights)
    else:
        first = dma.start([(ff, ffv)] + weights)
    second = dma.start(token_copies((cown.at[me], c1, c2, c3), me, cot) + back_weights)
    if lead:
        third = ()
        wait(early)
        for j in range(3):
            cols = pl.ds(j * 256, 256)
            hid[:, cols] = xv[:, cols].astype(F32) + nn(mx[...], out_weight(wout, j))
        rows = 128
        for a in range(xv.shape[0] // rows):
            x = hid[pl.ds(a * rows, rows), :]
            y = x * lax.rsqrt(jnp.mean(x * x, axis=-1, keepdims=True) + EPS) * gain[...]
            y = y.astype(BF)
            ffv[pl.ds(a * rows, rows), :] = y
            fftv[:, pl.ds(a * rows, rows)] = y.T
        stores += dma.start([(hid, hid_out), (ffv, ff_out), (fftv, fft_out)])
    else:
        third = dma.start([(ff_t, fftv)])
    wait(first)
    for b in range(5):
        if b < 4:
            at = pl.ds(b * 256, 256)
            win = rows_of([pack[o, h, pl.ds(b * hw, hw), :] for o in range(4) for h in (0, 1)])
            value, slope = gelu_both(nn(ffv[...], win))
            if b == 0:
                wait(second)
            act[:, at] = value.astype(BF)
            back = 0.0
            for j in range(3):
                wb = rows_of([pack[b, h, pl.ds(4 * hw + j * 128, 128), :] for h in (0, 1)])
                back = back + nt(cot[:, pl.ds(j * 256, 256)], wb)
            gpre[:, at] = (back * slope).astype(BF)
        if b == 3:
            stores += dma.start([(act, act_out), (gpre, gpre_out)])
        if b > 0:
            c = b - 1
            at = pl.ds(c * 256, 256)
            if c == 0:
                wait(third)
            gw = nn(fftv[...], gpre[:, at]).astype(BF)
            for o in range(4):
                put(stage, o, c * sh, gw[o * sh : (o + 1) * sh])
            gb = tn(act[:, at], cot[...]).astype(BF)
            for j in range(3):
                put(stage, c, 4 * sh + j * 256, gb[:, j * 256 : (j + 1) * 256])
            stores += [Either(dma, stage, keep, send, ids, c, 1, part) for part in (0, 1)]
            if c & 1:
                stores += [Either(dma, stage, keep, send, ids, o, 0, c // 2) for o in range(4)]
    wait(stores)


def after_ff_kernel(ids, gain, hid, g0, g1, g2, cown, c1, c2, c3, x0, x1, x2, *refs):
    packs = (refs[0:6], refs[6:12], refs[12:18])
    ghid_out, gm0, gm1, gm2, ggain, gwo_out, hidv, gv, cot, mx, wbuf, wins, ga, gf, ghid, gmv, gwo, sems = refs[18:]
    stores = []
    me, half = ids[0], ids[1]
    d = hid.shape[1]
    sh = d // 4
    hw = sh // 2
    rows = cot.shape[0] // 4
    dma = Copies(sems)
    loads = [
        dma.start(
            [(g, gv.at[c])]
            + pack_copies(packs[c], me, half, wins.at[c], lambda ref: ref.at[pl.ds(0, 4 * hw)])
        )
        for c, g in enumerate((g0, g1, g2))
    ]
    rest = dma.start([(hid, hidv)] + token_copies((cown.at[me], c1, c2, c3), me, cot))
    last = dma.start(
        pack_copies(packs[0], me, half, wbuf, out_cut(sh))
        + [(x, mx.at[:, pl.ds(i * 256, 256)]) for i, x in enumerate((x0, x1, x2))]
    )
    for c in range(3):
        wait(loads[c])
        acc = None
        for b in range(4):
            w = rows_of([wins[c, o, h, pl.ds(b * hw, hw), :] for o in range(4) for h in (0, 1)])
            term = nt(gv[c, :, pl.ds(b * 256, 256)], w)
            acc = term if acc is None else acc + term
        gf[...] = acc if c == 0 else gf[...] + acc
    wait(rest)
    total = jnp.zeros((1, d), F32)
    for a in range(4):
        at = pl.ds(a * rows, rows)
        x = hidv[at, :]
        gfa = gf[at, :]
        n = lax.rsqrt(jnp.mean(x * x, axis=-1, keepdims=True) + EPS)
        g = gfa * gain[...]
        xn = x * n
        total = total + jnp.sum(gfa * xn, axis=0, keepdims=True)
        gh = cot[at, :].astype(F32) + n * (g - xn * (n * jnp.mean(g * x, axis=-1, keepdims=True)))
        ghid[at, :] = gh
        ga[at, :] = gh.astype(BF)
    ggain[...] = total
    stores += dma.start([(ghid, ghid_out)])
    wait(last)
    acc = None
    for j in range(3):
        term = nt(ga[:, pl.ds(j * 256, 256)], out_weight(wbuf, j))
        acc = term if acc is None else acc + term
    for i, gm in enumerate((gm0, gm1, gm2)):
        gmv[i] = acc[:, i * 256 : (i + 1) * 256].astype(BF)
        stores += dma.start([(gmv.at[i], gm)])
    for j in range(3):
        gw = tn(mx[...], ga[:, pl.ds(j * 256, 256)]).astype(BF)
        for o in range(4):
            gwo[o, pl.ds(j * sh, sh), :] = gw[o * sh : (o + 1) * sh]
        rows_j = pl.ds(j * sh, sh)
        stores += dma.start([(gwo.at[:, rows_j], gwo_out.at[:, rows_j])])
    wait(stores)


def out_kernel(ids, hid, gin, a0, a1, a2, *refs):
    packs = (refs[0:6], refs[6:12], refs[12:18])
    out, hidv, av, wb, sems = refs[18:]
    me, half = ids[0], ids[1]
    d = hid.shape[1]
    hw = d // 8
    rows = hid.shape[0] // 4
    dma = Copies(sems)
    loads = [
        dma.start(
            [(a, av.at[c])]
            + pack_copies(packs[c], me, half, wb.at[c], lambda ref: ref.at[pl.ds(4 * hw, 384)])
        )
        for c, a in enumerate((a0, a1, a2))
    ]
    last = dma.start([(hid, hidv)])
    grads = dma.start([(gin.at[pl.ds(b * rows, rows)], out.at[b, 1]) for b in range(4)])
    for c in range(3):
        wait(loads[c])
    wait(last)
    for j in range(3):
        cols = pl.ds(j * 256, 256)
        acc = hidv[:, cols]
        for c in range(3):
            w = rows_of([wb[c, o, h, pl.ds(j * 128, 128), :] for o in range(4) for h in (0, 1)])
            acc = acc + nn(av[c], w)
        acc = acc.astype(BF)
        for b in range(4):
            out[b, 0, :, cols] = acc[b * rows : (b + 1) * rows]
    wait(grads)


def diagonals(x):
    width = x.shape[1]
    y = x[0:8]
    for a in range(8, x.shape[0], 8):
        y = y + pltpu.roll(x[a : a + 8], width - a, 1)
    sub = lax.broadcasted_iota(jnp.int32, y.shape, 0)
    for bit in (1, 2, 4):
        y = jnp.where((sub & bit) != 0, pltpu.roll(y, width - bit, 1), y)
    return jnp.sum(y, axis=0, keepdims=True)


def attn_bwd_kernel(groups, carried, ids, nrm_in, *refs):
    ins, refs = refs[: 5 * groups], refs[5 * groups :]
    carry, refs = refs[:carried], refs[carried:]
    keep, send, *refs = refs
    outs, refs = refs[: 3 * groups], refs[3 * groups :]
    (diag, q, k, v, p, gm, nrm_t, dq, dk, dv, acc, stage, sems) = refs
    t = 128
    length = nrm_t.shape[1]
    nblk = length // t
    low, m0, m1 = half_masks(t)
    dma = Copies(sems)
    loads = []
    for n in range(groups):
        q_in, k_in, v_in, p_in, gm_in = ins[5 * n : 5 * n + 5]
        whole = [(v_in, v.at[n]), (gm_in, gm.at[n]), (k_in, k.at[n]), (q_in, q.at[n])]
        halves = [[(p_in.at[pl.ds(2 * i, 2)], p.at[pl.ds(4 * n + 2 * i, 2)])] for i in (0, 1)]
        loads += [dma.start(whole + halves[0]), dma.start(halves[1])]
        if n == 0:
            last = dma.start([(nrm_in, nrm_t)])
    base, half = 0, stage.shape[2]
    for g in carry:
        count = g.shape[1]
        inside = min(count, half - base) if base < half else 0
        if inside:
            last += dma.start([(g.at[:, pl.ds(0, inside)], stage.at[:, 0, pl.ds(base, inside)])])
        if inside < count:
            rest, at = count - inside, max(0, base - half)
            last += dma.start([(g.at[:, pl.ds(inside, rest)], stage.at[:, 1, pl.ds(at, rest)])])
        base += count
    sh = nrm_t.shape[0] // 4
    stores = []
    for n in range(groups):
        for pair in (0, 1):
            wait(loads[2 * n + pair])
            cols = pl.ds(pair * 128, 128)
            k2, v2 = k[n, :, cols], v[n, :, cols]
            dk_t = jnp.zeros((128, length), F32)
            dv_t = jnp.zeros((128, length), F32)
            for a in range(nblk):
                at = pl.ds(a * t, t)
                q2, g2 = q[n, at, cols], gm[n, at, cols]
                qm = rows_of([q2 * m0, q2 * m1])
                g_both = rows_of([g2 * m0, g2 * m1])
                dp = nt(g_both, v2)
                pb = rows_of([p[4 * n + 2 * pair, at, :], p[4 * n + 2 * pair + 1, at, :]])
                pf = pb.astype(F32)
                delta = jnp.sum(pf * dp, axis=-1, keepdims=True)
                ds = (pf * (dp - delta)).astype(BF)
                mq = nn(ds, k2)
                dq[n, at, cols] = jnp.where(low, mq[:t], mq[t:]).astype(BF)
                dk_t = dk_t + tn(qm, ds)
                dv_t = dv_t + tn(g_both, pb)
                dsf = ds.astype(F32)
                for h in (0, 1):
                    for b in range(nblk):
                        rel = b - a
                        place = rel + 1 if abs(rel) <= 1 else (3 if rel < 0 else 4)
                        tile = dsf[h * t : (h + 1) * t, b * t : (b + 1) * t]
                        lanes = pl.ds(place * t, t)
                        if (a, b) in ((1, 0), (0, 0), (0, 1), (2, 0), (0, 2)):
                            acc[h, :, lanes] = tile
                        else:
                            acc[h, :, lanes] += tile
            dk[n, :, cols] = dk_t.T.astype(BF)
            dv[n, :, cols] = dv_t.T.astype(BF)
            for h in (0, 1):
                near = jnp.concatenate([acc[h, :, pl.ds(0, 3 * t)], jnp.zeros((t, t), F32)], axis=1)
                far = jnp.sum(acc[h, :, pl.ds(3 * t, 2 * t)], axis=0, keepdims=True)
                diag[pl.ds(4 * n + 2 * pair + h, 1), :] = jnp.concatenate([diagonals(near), far], axis=1)
        stores += dma.start([(d.at[n], out) for d, out in zip((dq, dk, dv), outs[3 * n : 3 * n + 3])])
        if n == 0:
            wait(last)
        for i, g in enumerate((dq, dk, dv)):
            gw = nn(nrm_t[...], g[n]).astype(BF)
            for o in range(4):
                put(stage, o, base + i * sh, gw[o * sh : (o + 1) * sh])
        base += 3 * sh
    stores += dma.start(piece_copies(stage, keep, send, ids))
    wait(stores)


def first_norm_kernel(ids, gain, xs, ghid, *refs):
    ins = refs[0:9]
    w0, w1 = refs[9:15], refs[15:21]
    gi, ggain, xv, gv, dall, wbuf0, wbuf1, gn, sems = refs[21:]
    me, half = ids[0], ids[1]
    d = xs.shape[1]
    rows = xs.shape[0] // 4
    dma = Copies(sems)
    loads = dma.start(
        [(g, dall.at[n]) for n, g in enumerate(ins)]
        + pack_copies(w0, me, half, wbuf0, lambda ref: ref)
        + pack_copies(w1, me, half, wbuf1, lambda ref: ref)
    )
    part = wbuf0.shape[2] // 3
    rest = dma.start([(xs, xv), (ghid, gv)])
    wait(loads)
    acc = None
    for i in range(3):
        for c in range(3):
            buf, at = (wbuf0, i) if c == 0 else (wbuf1, 3 * (c - 1) + i)
            wi = rows_of([buf[o, h, pl.ds(at * part, part), :] for o in range(4) for h in (0, 1)])
            term = nt(dall[3 * i + c], wi)
            acc = term if acc is None else acc + term
    gn[...] = acc
    wait(rest)
    total = jnp.zeros((1, d), F32)
    for a in range(4):
        at = pl.ds(a * rows, rows)
        x = xv[at, :].astype(F32)
        gf = gn[at, :]
        n = lax.rsqrt(jnp.mean(x * x, axis=-1, keepdims=True) + EPS)
        g = gf * gain[...]
        xn = x * n
        total = total + jnp.sum(gf * xn, axis=0, keepdims=True)
        gi[at, :] = (gv[at, :] + n * (g - xn * (n * jnp.mean(g * x, axis=-1, keepdims=True)))).astype(BF)
    ggain[...] = total


def tokens_kernel(ids, tokens, out, gin):
    out[...] = tokens[:, 0]
    gin[...] = tokens[:, 1].astype(F32)


def ff_shares_kernel(quad, thirds, starts, ids, *refs):
    ins, (out_in, out_back, buf, part_in, part_back, sems) = refs, refs[-6:]
    here, far = ids[1], ids[3]
    sh = out_in.shape[0]
    dma = Copies(sems)
    n = (2 * sh + 384) // 8
    copies = []
    for k in range(len(thirds)):
        pairs = []
        for m, h in ((2 * k, here), (2 * k + 1, 1 - here)):
            src = ins[m].at[pl.ds(starts[m], 8 * n)]
            if not quad:
                pairs.append((src, buf.at[k, h]))
                continue
            for p in (0, 1):
                for q, i in enumerate(Sum.ORDER):
                    row = pl.multiple_of(p * 4 * n + (far ^ i) * n, 16)
                    pairs.append((src.at[pl.ds((4 * p + q) * n, n)], buf.at[k, h, pl.ds(row, n)]))
        copies.append(dma.start(pairs))
    stores = []
    for m, k in enumerate(thirds):
        wait(copies[m])
        for b in range(4):
            part_in[m, :, pl.ds(b * 256, 256)] = buf[m, 0, pl.ds(b * sh, sh), :].astype(F32)
        stores += dma.start([
            (part_in.at[m, :, pl.ds(b * 256, 256)], out_in.at[:, pl.ds((b * 3 + k) * 256, 256)]) for b in range(4)
        ])
        for j in range(3):
            part_back[m, :, pl.ds(j * 256, 256)] = buf[m, 1, pl.ds(j * 256, 256), :].astype(F32)
        stores += dma.start([(part_back.at[m], out_back.at[pl.ds(k * 256, 256)])])
    wait(stores)


def attn_shares_kernel(plain, ids, *refs):
    ins, (wq, wk, wv, wo, buf, sems) = refs[:-6], refs[-6:]
    here, far = ids[1], ids[3]
    sh = wq.shape[0]
    pairs = []
    for m, h in ((0, here), (1, 1 - here)):
        if plain:
            pairs.append((ins[m], buf.at[h]))
            continue
        n = ins[m].shape[1]
        pairs += [(ins[m].at[i], buf.at[h, pl.ds(pl.multiple_of((far ^ i) * n, 16), n)]) for i in range(4)]
    wait(Copies(sems).start(pairs))
    at = lambda half, n: buf[half, pl.ds(n * sh, sh), :].astype(F32)
    for i in range(3):
        wo[:, pl.ds(i * 256, 256)] = at(0, i)
    for i, out in enumerate((wq, wk, wv)):
        out[:, pl.ds(0, 256)] = at(1, i)
        out[:, pl.ds(256, 256)] = at(0, 3 + i)
        out[:, pl.ds(512, 256)] = at(1, 3 + i)


def bucket_of(offset, bucket_count):
    distance = jnp.abs(offset)
    bucket = jnp.where(offset > 0, bucket_count // 2, 0).astype(jnp.int32)
    for edge in EDGES:
        bucket = bucket + (distance >= edge).astype(jnp.int32)
    return bucket


def shards(inputs, segments, gain_attn, w_query, w_key, w_value, w_out, bucket_bias_table, gain_ff, w_in, w_back, cotangent):
    seqs, rows, d = inputs.shape
    sh = w_query.shape[0]
    hw = sh // 2
    ffs = w_in.shape[1]
    bucket_count, heads = bucket_bias_table.shape
    length = rows * seqs
    places = [lax.axis_index(a).astype(jnp.int32) for a in ("near", "side", "core", "far")]
    near_at, side_at, core_at, far_at = places
    line = Line(jnp.stack([2 * side_at + core_at, near_at, core_at, far_at]))
    gate = line.gate
    row_low, row_f32 = sds((length, d), BF), sds((length, d), F32)
    quad_low, tok_low = sds((length, 256), BF), sds((rows, d), BF)
    gain1, gain2 = gain_attn.reshape(1, d), gain_ff.reshape(1, d)
    pack_rows = [4 * hw + 384 + 3 * hw, 4 * hw + 384, 4 * hw + 384]

    m0, m1, m2, m3, own_a, own_b, y_a, y_b = call(
        prep_a_kernel,
        "prep_a",
        [sds((rows + 16, d), BF)] * 4
        + [sds((2, 3 * hw, 256), BF), sds((2, 6 * hw, 256), BF), sds((3 * hw, 256), BF), sds((6 * hw, 256), BF)],
        [SM, VM] + [HBM] * 4,
        [VM] * 8,
        [DMA((31,))],
        (line.ids, segments, inputs, w_query, w_key, w_value),
    )
    wa = Gather(line, own_a, y_a)
    msgs = [swap(m1, "core"), swap(m2, "side"), swap(m3, "side", "core")]
    wb = Gather(line, own_b, y_b)

    own0, own1, own2, y0, y1, y2, k1, k2, k3 = call(
        prep_b_kernel,
        "prep_b",
        [sds((2, r, 256), BF) for r in pack_rows] + [sds((r, 256), BF) for r in pack_rows] + [tok_low] * 3,
        [SM] + [HBM] * 4,
        [VM] * 9,
        [DMA((75,))],
        (line.ids, w_in, w_back, w_out, cotangent),
    )

    (own0,) = gate(own0)
    wa.cross()
    *msgs, table_in = gate(*msgs, bucket_bias_table)
    wa.relay()

    offs = jnp.arange(4 * rows, dtype=jnp.int32)
    offs = jnp.where(offs < 3 * rows, offs - rows, offs - 5 * rows)
    hot = (bucket_of(offs, bucket_count)[None] == jnp.arange(bucket_count, dtype=jnp.int32)[:, None]).astype(F32)
    lines = jnp.einsum("up,uw->wp", hot, table_in, precision=lax.Precision.HIGHEST)
    far = jnp.stack([table_in[bucket_count // 2 - 1], table_in[bucket_count - 1]])

    y0, own0 = gate(y0, own0)
    wf = [Gather(line, own0, y0)]
    xs, nrm, nrm_t, seg = call(
        norm_kernel,
        "norm",
        [row_low, row_low, sds((d, length), BF), sds((1, length), F32)],
        [SM] + [HBM] * 4 + [VM],
        [VM] * 4,
        [scratch((64, d)), DMA((8,))],
        (line.ids, m0, *msgs, gain1),
    )
    nrm, lines = gate(nrm, lines)
    wb.cross()
    wa = wa.done()

    qs, ks, vs, probs, mixed = [], [], [], [], []
    for g in range(3):
        q, k, v, p, mx = call(
            functools.partial(attn_fwd_kernel, g),
            "attn_fwd",
            [quad_low] * 3 + [sds((4, length, length), BF), quad_low],
            [SM, SM, VM, VM] + [HBM] * 7,
            [HBM] * 4 + [VM],
            [
                scratch((4, rows, 3 * rows), F32),
                scratch((length, d)),
                scratch((4, 2, 3 * hw, 256)),
                scratch((length, 256)),
                scratch((length, 256)),
                scratch((length, 256)),
                scratch((4, length, length)),
                DMA((15,)),
            ],
            (line.ids, far, seg, lines, nrm, *(wa if g == 0 else wb)),
        )
        (mx,) = gate(mx)
        for have, new in ((qs, q), (ks, k), (vs, v), (probs, p), (mixed, mx)):
            have.append(new)
        if g == 0:
            wb.relay()
            wf[0].cross()
            own1, y1 = gate(own1, y1)
            wf.append(Gather(line, own1, y1))
            wb = wb.done()
        if g == 1:
            wf[0].relay()
            wf[1].cross()
            k1, k2, k3 = gate(k1, k2, k3)
            cots = [swap(k1, "core"), swap(k2, "side"), swap(k3, "side", "core")]
    packs = [wf[0].done()]
    cots = gate(*cots)
    wf[1].relay()
    own2, y2 = gate(own2, y2)
    wf.append(Gather(line, own2, y2))

    sums_f, acts, gpres = [], [], []
    for c in range(3):
        lead = c == 0
        *fresh, act, gpre, keep, send = call(
            functools.partial(ffn_kernel, lead),
            "ffn",
            ([row_f32, row_low, sds((d, length), BF)] if lead else [])
            + [sds((length, 1024), BF)] * 2
            + piece_shapes(4 * sh + 768),
            [SM] + ([VM] + [HBM] * 4 if lead else [HBM] * 2) + [HBM] * 10,
            [HBM] * (7 if lead else 4),
            (
                [scratch((length, d)), scratch((length, d)), scratch((4, 2, 3 * hw, 256)), scratch((length, d), F32)]
                if lead
                else []
            )
            + [
                scratch((length, d)),
                scratch((d, length)),
                scratch((length, d)),
                scratch((4, 2, 4 * hw + 384, 256)),
                scratch((length, 1024)),
                scratch((length, 1024)),
                scratch((4, 2, 2 * sh + 384, 256)),
                DMA((60,)),
            ],
            (line.ids, *((gain2, xs, *mixed) if lead else (ff, ff_t)), cotangent, *cots, *packs[c]),
        )
        if lead:
            hid, ff, ff_t = fresh
        piece = (keep, send)
        acts.append(act)
        (gpre,) = gate(gpre)
        gpres.append(gpre)
        if c == 0:
            packs.append(wf[1].done())
            wf[2].cross()
        if c == 1:
            wf[2].relay()
        moves = [[], [("first",)], [("second",), ("first",)]][c]
        sums_f.append(advance(line, *[(f, *m) for f, m in zip(sums_f, moves)], new=piece))
        if c == 1:
            packs.append(wf[2].done())

    ghid, *gmix, ggain_ff, gwo = call(
        after_ff_kernel,
        "after_ff",
        [row_f32] + [quad_low] * 3 + [sds((1, d), F32), sds((4, 3 * sh, 256), BF)],
        [SM, VM] + [HBM] * 29,
        [HBM] * 4 + [VM, HBM],
        [
            scratch((length, d), F32),
            scratch((3, length, 1024)),
            scratch((length, d)),
            scratch((length, d)),
            scratch((4, 2, 3 * hw, 256)),
            scratch((3, 4, 2, 4 * hw, 256)),
            scratch((length, d)),
            scratch((length, d), F32),
            scratch((length, d), F32),
            scratch((3, length, 256)),
            scratch((4, 3 * sh, 256)),
            DMA((52,)),
        ],
        (line.ids, gain2, hid, *gpres, cotangent, *cots, *mixed, *packs[0], *packs[1], *packs[2]),
    )
    gmix[0], ggain_ff = gate(gmix[0], ggain_ff)
    quad = lax.axis_size("far") == 4
    third = "spread" if quad else "third"
    far_steps = lambda *steps: steps if quad else ()
    advance(line, (sums_f[0], third), (sums_f[1], "second"), (sums_f[2], "first"))

    dqs, dks, dvs, diags, sums_a = [], [], [], [], []
    for first, groups in ((0, 1), (1, 2)):
        carry = (gwo,) if first == 0 else ()
        body = 3 * sh * (groups + len(carry))
        some = range(first, first + groups)
        keep, send, *grads, diag = call(
            functools.partial(attn_bwd_kernel, groups, len(carry)),
            "attn_bwd",
            piece_shapes(body) + [quad_low] * (3 * groups) + [sds((4 * groups, 6 * rows), F32)],
            [SM] + [HBM] * (1 + 5 * groups + len(carry)),
            [HBM] * (2 + 3 * groups) + [VM],
            [scratch((groups, length, 256))] * 3
            + [scratch((4 * groups, length, length)), scratch((groups, length, 256)), scratch((d, length))]
            + [scratch((groups, length, 256))] * 3
            + [scratch((2, rows, 5 * rows), F32), scratch((4, 2, body // 2, 256)), DMA((48,))],
            (line.ids, nrm_t, *[a for g in some for a in (qs[g], ks[g], vs[g], probs[g], gmix[g])], *carry),
            us=10 * groups,
        )
        (grads[0],) = gate(grads[0])
        for n in range(groups):
            for have, new in zip((dqs, dks, dvs), grads[3 * n : 3 * n + 3]):
                have.append(new)
        diags.append(diag)
        if first == 0:
            steps = ((sums_f[1], third), (sums_f[2], "second"), *far_steps((sums_f[0], "pair")))
        else:
            steps = ((sums_a[0], "first"), (sums_f[2], third))
            steps += far_steps((sums_f[0], "back"), (sums_f[1], "pair"))
        sums_a.append(advance(line, *steps, new=(keep, send)))

    gin, ggain_attn = call(
        first_norm_kernel,
        "first_norm",
        [row_low, sds((1, d), F32)],
        [SM, VM] + [HBM] * 23,
        [VM] * 2,
        [
            scratch((length, d)),
            scratch((length, d), F32),
            scratch((9, length, 256)),
            scratch((4, 2, 3 * hw, 256)),
            scratch((4, 2, 6 * hw, 256)),
            scratch((length, d), F32),
            DMA((27,)),
        ],
        (line.ids, gain1, xs, ghid, *dqs, *dks, *dvs, *wa, *wb),
    )
    gin, ggain_attn = gate(gin, ggain_attn)
    steps = far_steps((sums_f[0], "last"), (sums_f[1], "back"), (sums_f[2], "pair"))
    advance(line, (sums_a[1], "first"), (sums_a[0], "second"), *steps)
    (tokens,) = call(
        out_kernel,
        "out",
        [sds((seqs, 2, rows, d), BF)],
        [SM] + [HBM] * 23,
        [VM],
        [
            scratch((length, d), F32),
            scratch((3, length, 1024)),
            scratch((3, 4, 2, 384, 256)),
            DMA((32,)),
        ],
        (line.ids, hid, gin, *acts, *packs[0], *packs[1], *packs[2]),
    )
    tokens, ggain_attn = gate(tokens, ggain_attn)
    steps = far_steps((sums_f[0], "finish"), (sums_f[1], "last"), (sums_f[2], "back"))
    advance(line, (sums_a[1], "second"), (sums_a[0], "third"), *steps)
    first_total = sums_a[0].buffer


    hot6 = jnp.concatenate(
        [
            hot,
            jnp.zeros((bucket_count, rows), F32).at[bucket_count // 2 - 1].set(1.0),
            jnp.zeros((bucket_count, rows), F32).at[bucket_count - 1].set(1.0),
        ],
        axis=1,
    )
    table = jnp.einsum("up,wp->uw", hot6, jnp.concatenate(diags, axis=0), precision=lax.Precision.HIGHEST)
    small = jnp.concatenate([ggain_attn.reshape(-1), ggain_ff.reshape(-1), table.reshape(-1)])
    tokens = lax.all_to_all(tokens, ("side", "core"), 0, 0, tiled=True)
    advance(line, (sums_a[1], "third"), *far_steps((sums_f[1], "finish"), (sums_f[2], "last")))
    far_c = FarSum([first_total, sums_a[1].buffer])

    sums_f[1].land(line)
    far_c.land(line)
    far_c.back()
    if quad:
        advance(line, (sums_f[2], "finish"))
    else:
        for f in sums_f:
            whole = lax.psum(f.buffer, "far")
            f.buffer, f.flying = whole, {0: (swap(whole, "near"), ())}
    (small,) = gate(small)
    small = small + swap(small, "core")

    def ff_shares(thirds, have):
        parts, starts = [], []
        for f in [sums_f[k] for k in thirds]:
            arr, at = next(iter(f.flying.values()))
            parts += [f.buffer, *gate(arr)]
            starts += [0, at[0].start if at else 0]
        n = len(thirds)
        return call(
            functools.partial(ff_shares_kernel, quad, thirds, starts),
            "ff_shares",
            [sds((sh, ffs), F32), sds(w_back.shape, F32)],
            [SM] + [HBM] * (2 * n + len(have)),
            [HBM] * 2,
            [
                scratch((n, 2, 2 * sh + 384, 256)),
                scratch((n, sh, 1024), F32),
                scratch((n, 256, d), F32),
                DMA((21 * n,)),
            ],
            (line.ids, *parts, *have),
            aliases={1 + 2 * n + i: i for i in range(len(have))},
            us=1,
        )

    shares = gate(*ff_shares((0, 1), ()))
    sums_f[2].land(line)
    far_c.land(line)
    far_c.finish(line)
    (small,) = gate(small)
    small = small + swap(small, "side")
    tokens, small = gate(tokens, small)
    small = small + swap_far(small, 1) if quad else lax.psum(small, "far")
    output, grad_inputs = call(
        tokens_kernel,
        "tokens",
        [sds((seqs, rows, d), BF), sds((seqs, rows, d), F32)],
        [SM, VM],
        [VM] * 2,
        [],
        (line.ids, tokens),
        us=1,
    )
    output, small = gate(output, small)
    if quad:
        small = small + swap_far(small, 2)
    share_in, share_back = gate(*ff_shares((2,), shares))
    *shares_c, small = gate(*far_c.result, small)
    small = small + swap(small, "near")
    share_q, share_k, share_v, share_o = call(
        functools.partial(attn_shares_kernel, far_c.plain),
        "attn_shares",
        [sds((sh, d), F32)] * 4,
        [SM] + [HBM] * len(shares_c),
        [VM] * 4,
        [scratch((2, 6 * sh, 256)), DMA((8,))],
        (line.ids, *shares_c),
        us=1,
    )
    total_gain_attn, total_gain_ff = small[:d], small[d : 2 * d]
    total_table = small[2 * d :].reshape(bucket_count, heads)


    return (
        output,
        grad_inputs,
        total_gain_attn,
        share_q,
        share_k,
        share_v,
        share_o,
        total_table,
        total_gain_ff,
        share_in,
        share_back,
    )


def solution(mesh):
    far = mesh.shape["rows"] // 2
    inner = jax.sharding.Mesh(mesh.devices.reshape(far, 2, 2, 2), AXES)
    over_rows, over_blk = ("far", "near"), ("side", "core")
    tok, row, rep = P(over_rows, over_blk, None), P(over_blk, None), P()
    return jax.shard_map(
        shards,
        mesh=inner,
        in_specs=(tok, P(over_rows, over_blk), rep, row, row, row, row, rep, rep, row, row, tok),
        out_specs=(tok, tok, rep, row, row, row, row, rep, rep, row, row),
        check_vma=False,
    )
```

```python
import functools

import jax
import jax.numpy as jnp
from jax import lax
from jax.experimental import pallas as pl
from jax.experimental.pallas import tpu as pltpu
from jax.sharding import PartitionSpec as P

EPS = 1e-06
EDGES = (1, 2, 3, 4, 5, 6, 7, 8, 12, 16, 23, 32, 46, 64, 91)
BF = jnp.bfloat16
F32 = jnp.float32
HBM = pl.BlockSpec(memory_space=pltpu.HBM)
VM = pl.BlockSpec(memory_space=pltpu.VMEM)
SM = pl.BlockSpec(memory_space=pltpu.SMEM)
DMA = pltpu.SemaphoreType.DMA
sds = jax.ShapeDtypeStruct
AXES = ("far", "near", "side", "core")
FLIPS = {"far2": 16, "far1": 8, "near": 4, "whole": 4, "side": 2, "core": 1}


def scratch(shape, kind=BF):
    return pltpu.VMEM(shape, kind)


def call(kernel, name, outs, ins, out_specs, scratches, args, us=20, aliases={}):
    return pl.pallas_call(
        kernel,
        out_shape=outs,
        in_specs=ins,
        out_specs=out_specs,
        scratch_shapes=scratches,
        input_output_aliases=aliases,
        compiler_params=pltpu.CompilerParams(vmem_limit_bytes=63 * 1024 * 1024),
        cost_estimate=pl.CostEstimate(flops=int(us * 10**9), bytes_accessed=int(us * 4 * 10**6), transcendentals=0),
        name=name,
    )(*args)


def nn(a, b):
    return lax.dot_general(a, b, (((1,), (0,)), ((), ())), preferred_element_type=F32)


def nt(a, b):
    return lax.dot_general(a, b, (((1,), (1,)), ((), ())), preferred_element_type=F32)


def tn(a, b):
    return lax.dot_general(a, b, (((0,), (0,)), ((), ())), preferred_element_type=F32)


def swap(value, *axes):
    flip = sum(FLIPS[a] for a in axes)
    count = 1
    for a in AXES:
        count *= lax.axis_size(a)
    return lax.ppermute(value, AXES, [(i, i ^ flip) for i in range(count)])


def swap_far(value, bits):
    count = 8 * lax.axis_size("far")
    return lax.ppermute(value, AXES, [(i, i ^ (8 * bits)) for i in range(count)])


class Line:
    def __init__(self, ids):
        self.ids = ids

    def gate(self, *values):
        self.ids, *values = lax.optimization_barrier((self.ids, *values))
        return tuple(values)


def pick(arr, index, axis=0):
    return lax.dynamic_index_in_dim(arr, index, axis, keepdims=False)


class Sum:
    AXES = (("side", "near"), ("near", "side"))
    ORDER = (0, 2, 1, 3)

    def __init__(self, keep, send):
        self.rows = keep.shape[3]
        places = [(p, i, j) for p in (0, 1) for i in (0, 1) for j in (0, 1)]
        self.kept = {at: (keep, at) for at in places}
        got = swap(send, "core")
        self.flying = {at: (got, at) for at in places}

    def added(self, key):
        return self.kept[key], self.flying[key]

    def land(self, line):
        arrays = []
        for arr, _ in self.flying.values():
            if not any(arr is f for f in arrays):
                arrays.append(arr)
        landed = line.gate(*arrays)
        here = lambda arr: next(l for f, l in zip(arrays, landed) if f is arr)
        self.flying = {key: (here(arr), at) for key, (arr, at) in self.flying.items()}

    def first(self):
        out = []
        for p, i, j in self.kept:
            move = (self.AXES[p][0], (p, j)) if i else None
            out.append((*self.added((p, i, j)), None if i else (p, j), move))
        return self.rows, out

    def second(self):
        out = []
        for p, j in self.kept:
            out.append((*self.added((p, j)), None if j else p, (self.AXES[p][1], p) if j else None))
        return self.rows, out

    def third(self):
        return self.rows, [(*self.added(p), p, None) for p in (0, 1)]

    def spread(self):
        out = []
        cut = lambda block, i: (block[0], (*block[1], ("far", i)))
        for p in (0, 1):
            a, b = self.added(p)
            for i in range(4):
                sent = i & 1
                out.append((cut(a, i), cut(b, i), None if sent else (p, i), ("far1", (p, i - 1)) if sent else None))
        return self.rows // 4, out

    def pair(self):
        out = [(*self.added((p, i)), None if i else p, ("far2", p) if i else None) for p in (0, 1) for i in (0, 2)]
        return self.rows // 4, out

    def back(self):
        return self.rows // 4, [(*self.added(p), (p, 0), ("far2", (p, 2))) for p in (0, 1)]

    def last(self):
        have = {**self.kept, **self.flying}
        out = [(have[p, i], None, (p, i), ("far1", (p, i + 1))) for p in (0, 1) for i in (0, 2)]
        return self.rows // 4, out

    def finish(self):
        have = {**self.kept, **self.flying}
        out = [(have[p, i], None, (p, i), ("whole", (p, i))) for p in (0, 1) for i in self.ORDER]
        return self.rows // 4, out


class FarSum:
    def __init__(self, parts):
        total = jnp.concatenate(parts, axis=0)
        self.plain = lax.axis_size("far") != 4
        if self.plain:
            self.kept, self.flying = lax.psum(total, "far"), ()
            return
        blocks = total.reshape(4, -1, 256)
        here = lax.axis_index("far")
        self.kept = pick(blocks, here)
        self.flying = tuple(swap_far(pick(blocks, here ^ i), i) for i in (1, 2, 3))

    def land(self, line):
        if self.flying:
            self.flying = line.gate(*self.flying)

    def back(self):
        if self.plain:
            return
        total = self.kept.astype(F32)
        for f in self.flying:
            total = total + f.astype(F32)
        self.kept = total.astype(BF)
        self.flying = tuple(swap_far(self.kept, i) for i in (1, 2, 3))

    def finish(self, line):
        if self.plain:
            self.result = (self.kept, swap(self.kept, "near"))
            return
        (whole,) = line.gate(jnp.stack([self.kept, *self.flying]))
        self.flying = (swap(whole, "near"),)
        self.result = (whole, *self.flying)


def add_kernel(jobs, arrays, ids, *refs):
    ins, refs = refs[:arrays], refs[arrays:]
    count = len(jobs)
    bufs, sems = refs[-1 - 2 * count : -1], refs[-1]
    outs = refs[: len(refs) - 1 - 2 * count]
    far = ids[3]
    dma = Copies(sems)

    def view(ref, at, rows):
        if at and isinstance(at[-1], tuple):
            *at, (_, i) = at
            start = at.pop().start if at and hasattr(at[-1], "start") else 0
            at = (*at, pl.ds(pl.multiple_of(start + (far ^ i) * rows, 16), rows))
        return ref.at[tuple(at)] if at else ref

    loads = []
    for n, (rows, a, b, _) in enumerate(jobs):
        loads.append(dma.start([(view(ins[x], at, rows), bufs[2 * n + m]) for m, (x, at) in enumerate((a, b)) if x >= 0]))
    stores = []
    for n, (rows, a, b, places) in enumerate(jobs):
        wait(loads[n])
        buf = bufs[2 * n]
        if b[0] >= 0:
            buf[...] = buf[...] + bufs[2 * n + 1][...]
        stores += dma.start([(buf, outs[o].at[pl.ds(row, rows)]) for o, row in places])
    wait(stores)


def advance(line, *steps, new=()):
    flying = []
    for piece, _ in steps:
        for arr, _ in piece.flying.values():
            if not any(arr is f for f in flying):
                flying.append(arr)
    landed = list(line.gate(*flying, *new))
    here = lambda arr: next(l for f, l in zip(flying, landed) if f is arr)
    fresh = Sum(*landed[len(flying) :]) if new else None
    if not steps:
        return fresh
    arrays, jobs, sizes, marks = [], [], {}, []

    def number(block):
        if block is None:
            return (-1, ())
        arr, at = block
        if not any(arr is x for x in arrays):
            arrays.append(arr)
        return next(n for n, x in enumerate(arrays) if x is arr), at

    for piece, step in steps:
        piece.flying = {key: (here(arr), at) for key, (arr, at) in piece.flying.items()}
        rows, todo = getattr(piece, step)()
        for a, b, key, move in todo:
            places = []
            for name, mark in ((("kept", piece), key), (move[0] if move else None, move[1] if move else None)):
                if mark is None:
                    continue
                row = sizes.get(name, 0)
                sizes[name] = row + rows
                places.append((name, row))
                marks.append((piece, name, mark, row, rows))
            jobs.append((rows, number(a), number(b), places))
    names = list(sizes)
    jobs = [(rows, a, b, tuple((names.index(n), row) for n, row in places)) for rows, a, b, places in jobs]
    sums = call(
        functools.partial(add_kernel, jobs, len(arrays)),
        "add",
        [sds((sizes[n], 256), BF) for n in names],
        [SM] + [HBM] * len(arrays),
        [HBM] * len(names),
        [scratch((rows, 256)) for rows, *_ in jobs for _ in (0, 1)] + [DMA((4 * len(jobs),))],
        (line.ids, *arrays),
        us=3,
    )
    line.gate(sums[0])
    results = {n: v if isinstance(n, tuple) else swap(v, n) for n, v in zip(names, sums)}
    for piece, _ in steps:
        piece.kept, piece.flying = {}, {}
        piece.buffer = results.get(("kept", piece))
    for piece, name, mark, row, rows in marks:
        where = piece.kept if isinstance(name, tuple) else piece.flying
        where[mark] = (results[name], (pl.ds(row, rows),))
    return fresh


class Gather:
    def __init__(self, line, own, half):
        self.line, self.own = line, own
        self.y = swap(half, "side")
        self.core = swap(own, "core")

    def cross(self):
        self.y, self.core = self.line.gate(self.y, self.core)
        self.x = swap(self.y, "near")

    def relay(self):
        (self.x,) = self.line.gate(self.x)
        self.yc, self.xc = swap(self.y, "core"), swap(self.x, "core")

    def done(self):
        self.yc, self.xc = self.line.gate(self.yc, self.xc)
        return (self.own, self.core, self.y, self.x, self.yc, self.xc)


class Copies:
    def __init__(self, sems):
        self.sems, self.count = sems, 0

    def start(self, pairs):
        out = []
        for src, dst in pairs:
            out.append(pltpu.make_async_copy(src, dst, self.sems.at[self.count]))
            self.count += 1
            out[-1].start()
        return out


def wait(copies):
    for c in copies:
        c.wait()


def pieces_of(refs, me, half):
    own, core, y, x, yc, xc = refs
    out = []
    for h in (0, 1):
        out.append((own.at[h], me, h))
        out.append((core.at[h], me ^ 1, h))
    out.append((y, me ^ 2, half))
    out.append((x, me ^ 2, 1 - half))
    out.append((yc, me ^ 3, half))
    out.append((xc, me ^ 3, 1 - half))
    return out


def pack_copies(refs, me, half, dst, cut):
    return [(cut(ref), dst.at[o, h]) for ref, o, h in pieces_of(refs, me, half)]


def token_copies(slots, me, dst):
    rows = dst.shape[0] // 4
    return [
        (src, dst.at[pl.ds(pl.multiple_of((me ^ s) * rows, rows), rows)]) for s, src in enumerate(slots)
    ]


def put(stage, owner, row, value):
    half, count = stage.shape[2], value.shape[0]
    first = min(count, max(0, half - row))
    if first:
        stage[owner, 0, pl.ds(row, first), :] = value[:first]
    if first < count:
        stage[owner, 1, pl.ds(row + first - half, count - first), :] = value[first:]


def piece_copies(stage, keep, send, ids):
    me, near, core = ids[0], ids[1], ids[2]
    h = stage.shape[2] // 2
    out = []
    for dst, c in ((send, 1 - core), (keep, core)):
        for part in (0, 1):
            for first in (0, 1):
                for second in (0, 1):
                    sy, sx = (first, second) if part == 0 else (second, first)
                    owner = ((me ^ (2 * sy)) & 2) + c
                    out.append((stage.at[owner, near ^ sx, pl.ds(part * h, h)], dst.at[part, first, second]))
    return out


class Either:
    def __init__(self, dma, stage, keep, send, ids, owner, half, part):
        me, near = ids[0], ids[1]
        rows = stage.shape[2] // 2
        sem = dma.sems.at[dma.count]
        dma.count += 1
        sy, sx = ((me ^ owner) >> 1) & 1, near ^ half
        at = (part, sy, sx) if part == 0 else (part, sx, sy)
        src = stage.at[owner, half, pl.ds(part * rows, rows)]
        self.stays = ((me ^ owner) & 1) == 0
        self.copies = [pltpu.make_async_copy(src, dst.at[at], sem) for dst in (keep, send)]
        self.each("start")

    def each(self, name):
        for copy, taken in zip(self.copies, (self.stays, jnp.logical_not(self.stays))):
            pl.when(taken)(getattr(copy, name))

    def wait(self):
        self.each("wait")


def piece_shapes(rows):
    return [sds((2, 2, 2, rows // 4, 256), BF)] * 2


def rows_of(blocks):
    return jnp.concatenate(blocks, axis=0)


def prep_a_kernel(ids, seg, inputs, wq, wk, wv, m0, m1, m2, m3, own0, own1, y0, y1, sems):
    me, half = ids[0], ids[1]
    rows = inputs.shape[1]
    part = wq.shape[0] // 2
    pairs = []
    for g in range(3):
        own, y, at = (own0, y0, 0) if g == 0 else (own1, y1, g - 1)
        for i, w in enumerate((wq, wk, wv)):
            cols, place = pl.ds(g * 256, 256), pl.ds((3 * at + i) * part, part)
            pairs.append((w.at[pl.ds(pl.multiple_of(half * part, 16), part), cols], y.at[place]))
            for h in (0, 1):
                pairs.append((w.at[pl.ds(h * part, part), cols], own.at[h, place]))
    for s, m in enumerate((m0, m1, m2, m3)):
        pairs.append((inputs.at[me ^ s], m.at[pl.ds(0, rows)]))
    copies = Copies(sems).start(pairs)
    for s, m in enumerate((m0, m1, m2, m3)):
        line = seg[pl.ds(me ^ s, 1), :].astype(F32)
        m[pl.ds(rows, 16), pl.ds(0, rows)] = jnp.broadcast_to(line, (16, rows)).astype(BF)
        m[pl.ds(rows, 16), pl.ds(rows, m.shape[1] - rows)] = jnp.zeros((16, m.shape[1] - rows), BF)
    wait(copies)


def prep_b_kernel(ids, w_in, w_back, w_out, cot, own0, own1, own2, y0, y1, y2, k1, k2, k3, sems):
    me, half = ids[0], ids[1]
    hw = w_in.shape[0] // 2
    pairs = [(cot.at[me ^ s], k) for s, k in ((1, k1), (2, k2), (3, k3))]
    for c, (own, y) in enumerate(((own0, y0), (own1, y1), (own2, y2))):
        for dst, h in ((y, half), (own.at[0], 0), (own.at[1], 1)):
            for b in range(4):
                pairs.append((
                    w_in.at[pl.ds(pl.multiple_of(h * hw, 16), hw), pl.ds(b * 768 + c * 256, 256)],
                    dst.at[pl.ds(b * hw, hw)],
                ))
            for j in range(3):
                pairs.append((
                    w_back.at[pl.ds(pl.multiple_of(c * 256 + h * 128, 16), 128), pl.ds(j * 256, 256)],
                    dst.at[pl.ds(4 * hw + j * 128, 128)],
                ))
                if c == 0:
                    pairs.append((
                        w_out.at[pl.ds(pl.multiple_of(h * hw, 16), hw), pl.ds(j * 256, 256)],
                        dst.at[pl.ds(4 * hw + 384 + j * hw, hw)],
                    ))
    wait(Copies(sems).start(pairs))


def norm_kernel(ids, m0, m1, m2, m3, gain, xs, nrm, nrm_t, seg, sbuf, sems):
    me = ids[0]
    rows = xs.shape[0] // 4
    slots = (m0, m1, m2, m3)
    tok = token_copies([m.at[pl.ds(0, rows)] for m in slots], me, xs)
    tok += token_copies([m.at[pl.ds(rows, 16)] for m in slots], me, sbuf)
    wait(Copies(sems).start(tok))
    seg[...] = jnp.concatenate(
        [sbuf[pl.ds(o * 16, 1), pl.ds(0, rows)].astype(F32) for o in range(4)], axis=1
    )
    for a in range(4):
        x = xs[pl.ds(a * rows, rows), :].astype(F32)
        y = x * lax.rsqrt(jnp.mean(x * x, axis=-1, keepdims=True) + EPS) * gain[...]
        y = y.astype(BF)
        nrm[pl.ds(a * rows, rows), :] = y
        nrm_t[:, pl.ds(a * rows, rows)] = y.T


def half_masks(t):
    lane = lax.broadcasted_iota(jnp.int32, (t, 128), 1)
    return lane < 64, (lane < 64).astype(F32).astype(BF), (lane >= 64).astype(F32).astype(BF)


def attn_fwd_kernel(group, ids, far, seg, lines, nrm_in, w0, w1, w2, w3, w4, w5,
                    q_out, k_out, v_out, p_out, o, near, nrm, wbuf, q, k, v, p, sems):
    me, half = ids[0], ids[1]
    dma = Copies(sems)
    count = wbuf.shape[2]
    part = count // 3
    place = pl.ds(max(group - 1, 0) * count, count)
    loads = dma.start(
        [(nrm_in, nrm)]
        + pack_copies((w0, w1, w2, w3, w4, w5), me, half, wbuf, lambda ref: ref.at[place])
    )
    for head in range(4):
        line = jnp.broadcast_to(lines[pl.ds(4 * group + head, 1), :], (near.shape[1], lines.shape[1]))
        near[head] = pltpu.roll(line, 0, 1, stride=1, stride_axis=0)[:, : near.shape[2]]
    t = near.shape[1]
    length = q.shape[0]
    nblk = length // t
    low, m0, m1 = half_masks(t)
    eye = lax.broadcasted_iota(jnp.int32, (t, t), 0) == lax.broadcasted_iota(jnp.int32, (t, t), 1)
    seg_row = seg[...]
    wait(loads)
    stores = []
    for i, (buf, out) in enumerate(((q, q_out), (k, k_out), (v, v_out))):
        w = rows_of([wbuf[ow, h, pl.ds(i * part, part), :] for ow in range(4) for h in (0, 1)])
        buf[...] = nn(nrm[...], w).astype(BF)
        stores += dma.start([(buf, out)])
    for pair in (0, 1):
        at = pl.ds(pair * 128, 128)
        for a in range(nblk):
            seg_col = jnp.sum(
                jnp.where(eye, jnp.broadcast_to(seg_row[:, a * t : (a + 1) * t], (t, t)), 0.0),
                axis=1,
                keepdims=True,
            )
            allowed = seg_col == seg_row
            q2 = q[pl.ds(a * t, t), at]
            s = nt(rows_of([q2 * m0, q2 * m1]), k[:, at])
            ps = []
            for h in (0, 1):
                head = 2 * pair + h
                strip = []
                for b in range(nblk):
                    rel = b - a
                    if abs(rel) <= 1:
                        strip.append(near[head, :, (rel + 1) * t : (rel + 2) * t])
                    else:
                        strip.append(jnp.full((t, t), far[int(rel > 0), group * 4 + head], F32))
                sh = s[h * t : (h + 1) * t] + jnp.concatenate(strip, axis=1)
                sh = jnp.where(allowed, sh, -1e30)
                top = jnp.max(sh, axis=-1, keepdims=True)
                e = jnp.exp(sh - top)
                inv = 1.0 / jnp.sum(e, axis=-1, keepdims=True)
                ph = (e * inv).astype(BF)
                p[head, pl.ds(a * t, t), :] = ph
                ps.append(ph)
            mix = nn(rows_of(ps), v[:, at])
            o[pl.ds(a * t, t), at] = jnp.where(low, mix[:t], mix[t:]).astype(BF)
        stores += dma.start([(p.at[pl.ds(2 * pair, 2)], p_out.at[pl.ds(2 * pair, 2)])])
    wait(stores)


def out_weight(wbuf, j):
    hw = wbuf.shape[2] // 3
    return rows_of([wbuf[o, h, pl.ds(j * hw, hw), :] for o in range(4) for h in (0, 1)])


def out_cut(sh):
    return lambda ref: ref.at[pl.ds(2 * sh + 384, 3 * (sh // 2))]


def gelu_both(x):
    c = 0.7978845608028654
    x2 = x * x
    th = jnp.tanh(x * (c + (c * 0.044715) * x2))
    half_up = 0.5 + 0.5 * th
    slope = half_up + x * (0.5 - 0.5 * th * th) * (c + (3.0 * c * 0.044715) * x2)
    return x * half_up, slope


def ffn_kernel(lead, ids, *refs):
    if lead:
        gain, xs, x0, x1, x2, cown, c1, c2, c3, p0, p1, p2, p3, p4, p5, *rest = refs
        hid_out, ff_out, fft_out, act_out, gpre_out, keep, send, *rest = rest
        xv, mx, wout, hid, ffv, fftv, cot, pack, act, gpre, stage, sems = rest
    else:
        ff, ff_t, cown, c1, c2, c3, p0, p1, p2, p3, p4, p5, act_out, gpre_out, keep, send, *rest = refs
        ffv, fftv, cot, pack, act, gpre, stage, sems = rest
    me, half = ids[0], ids[1]
    d = ffv.shape[1]
    sh = d // 4
    hw = sh // 2
    packs = (p0, p1, p2, p3, p4, p5)
    dma = Copies(sems)
    split = lambda at, n: [
        (ref.at[pl.ds(at, n)], pack.at[o, h, pl.ds(at, n)]) for ref, o, h in pieces_of(packs, me, half)
    ]
    weights, back_weights = split(0, 4 * hw), split(4 * hw, 384)
    stores = []
    if lead:
        early = dma.start(
            pack_copies(packs, me, half, wout, out_cut(sh))
            + [(x, mx.at[:, pl.ds(i * 256, 256)]) for i, x in enumerate((x0, x1, x2))]
            + [(xs, xv)]
        )
        first = dma.start(weights)
    else:
        first = dma.start([(ff, ffv)] + weights)
    second = dma.start(token_copies((cown.at[me], c1, c2, c3), me, cot) + back_weights)
    if lead:
        third = ()
        wait(early)
        for j in range(3):
            cols = pl.ds(j * 256, 256)
            hid[:, cols] = xv[:, cols].astype(F32) + nn(mx[...], out_weight(wout, j))
        rows = 128
        for a in range(xv.shape[0] // rows):
            x = hid[pl.ds(a * rows, rows), :]
            y = x * lax.rsqrt(jnp.mean(x * x, axis=-1, keepdims=True) + EPS) * gain[...]
            y = y.astype(BF)
            ffv[pl.ds(a * rows, rows), :] = y
            fftv[:, pl.ds(a * rows, rows)] = y.T
        stores += dma.start([(hid, hid_out), (ffv, ff_out), (fftv, fft_out)])
    else:
        third = dma.start([(ff_t, fftv)])
    wait(first)
    for b in range(5):
        if b < 4:
            at = pl.ds(b * 256, 256)
            win = rows_of([pack[o, h, pl.ds(b * hw, hw), :] for o in range(4) for h in (0, 1)])
            value, slope = gelu_both(nn(ffv[...], win))
            if b == 0:
                wait(second)
            act[:, at] = value.astype(BF)
            back = 0.0
            for j in range(3):
                wb = rows_of([pack[b, h, pl.ds(4 * hw + j * 128, 128), :] for h in (0, 1)])
                back = back + nt(cot[:, pl.ds(j * 256, 256)], wb)
            gpre[:, at] = (back * slope).astype(BF)
        if b == 3:
            stores += dma.start([(act, act_out), (gpre, gpre_out)])
        if b > 0:
            c = b - 1
            at = pl.ds(c * 256, 256)
            if c == 0:
                wait(third)
            gw = nn(fftv[...], gpre[:, at]).astype(BF)
            for o in range(4):
                put(stage, o, c * sh, gw[o * sh : (o + 1) * sh])
            gb = tn(act[:, at], cot[...]).astype(BF)
            for j in range(3):
                put(stage, c, 4 * sh + j * 256, gb[:, j * 256 : (j + 1) * 256])
            stores += [Either(dma, stage, keep, send, ids, c, 1, part) for part in (0, 1)]
            if c & 1:
                stores += [Either(dma, stage, keep, send, ids, o, 0, c // 2) for o in range(4)]
    wait(stores)


def after_ff_kernel(ids, gain, hid, g0, g1, g2, cown, c1, c2, c3, x0, x1, x2, *refs):
    packs = (refs[0:6], refs[6:12], refs[12:18])
    ghid_out, gm0, gm1, gm2, ggain, gwo_out, hidv, gv, cot, mx, wbuf, wins, ga, gf, ghid, gmv, gwo, sems = refs[18:]
    stores = []
    me, half = ids[0], ids[1]
    d = hid.shape[1]
    sh = d // 4
    hw = sh // 2
    rows = cot.shape[0] // 4
    dma = Copies(sems)
    loads = [
        dma.start(
            [(g, gv.at[c])]
            + pack_copies(packs[c], me, half, wins.at[c], lambda ref: ref.at[pl.ds(0, 4 * hw)])
        )
        for c, g in enumerate((g0, g1, g2))
    ]
    rest = dma.start([(hid, hidv)] + token_copies((cown.at[me], c1, c2, c3), me, cot))
    last = dma.start(
        pack_copies(packs[0], me, half, wbuf, out_cut(sh))
        + [(x, mx.at[:, pl.ds(i * 256, 256)]) for i, x in enumerate((x0, x1, x2))]
    )
    for c in range(3):
        wait(loads[c])
        acc = None
        for b in range(4):
            w = rows_of([wins[c, o, h, pl.ds(b * hw, hw), :] for o in range(4) for h in (0, 1)])
            term = nt(gv[c, :, pl.ds(b * 256, 256)], w)
            acc = term if acc is None else acc + term
        gf[...] = acc if c == 0 else gf[...] + acc
    wait(rest)
    total = jnp.zeros((1, d), F32)
    for a in range(4):
        at = pl.ds(a * rows, rows)
        x = hidv[at, :]
        gfa = gf[at, :]
        n = lax.rsqrt(jnp.mean(x * x, axis=-1, keepdims=True) + EPS)
        g = gfa * gain[...]
        xn = x * n
        total = total + jnp.sum(gfa * xn, axis=0, keepdims=True)
        gh = cot[at, :].astype(F32) + n * (g - xn * (n * jnp.mean(g * x, axis=-1, keepdims=True)))
        ghid[at, :] = gh
        ga[at, :] = gh.astype(BF)
    ggain[...] = total
    stores += dma.start([(ghid, ghid_out)])
    wait(last)
    acc = None
    for j in range(3):
        term = nt(ga[:, pl.ds(j * 256, 256)], out_weight(wbuf, j))
        acc = term if acc is None else acc + term
    for i, gm in enumerate((gm0, gm1, gm2)):
        gmv[i] = acc[:, i * 256 : (i + 1) * 256].astype(BF)
        stores += dma.start([(gmv.at[i], gm)])
    for j in range(3):
        gw = tn(mx[...], ga[:, pl.ds(j * 256, 256)]).astype(BF)
        for o in range(4):
            gwo[o, pl.ds(j * sh, sh), :] = gw[o * sh : (o + 1) * sh]
        rows_j = pl.ds(j * sh, sh)
        stores += dma.start([(gwo.at[:, rows_j], gwo_out.at[:, rows_j])])
    wait(stores)


def out_kernel(ids, hid, gin, a0, a1, a2, *refs):
    packs = (refs[0:6], refs[6:12], refs[12:18])
    out, hidv, av, wb, sems = refs[18:]
    me, half = ids[0], ids[1]
    d = hid.shape[1]
    hw = d // 8
    rows = hid.shape[0] // 4
    dma = Copies(sems)
    loads = [
        dma.start(
            [(a, av.at[c])]
            + pack_copies(packs[c], me, half, wb.at[c], lambda ref: ref.at[pl.ds(4 * hw, 384)])
        )
        for c, a in enumerate((a0, a1, a2))
    ]
    last = dma.start([(hid, hidv)])
    grads = dma.start([(gin.at[pl.ds(b * rows, rows)], out.at[b, 1]) for b in range(4)])
    for c in range(3):
        wait(loads[c])
    wait(last)
    for j in range(3):
        cols = pl.ds(j * 256, 256)
        acc = hidv[:, cols]
        for c in range(3):
            w = rows_of([wb[c, o, h, pl.ds(j * 128, 128), :] for o in range(4) for h in (0, 1)])
            acc = acc + nn(av[c], w)
        acc = acc.astype(BF)
        for b in range(4):
            out[b, 0, :, cols] = acc[b * rows : (b + 1) * rows]
    wait(grads)


def diagonals(x):
    width = x.shape[1]
    y = x[0:8]
    for a in range(8, x.shape[0], 8):
        y = y + pltpu.roll(x[a : a + 8], width - a, 1)
    sub = lax.broadcasted_iota(jnp.int32, y.shape, 0)
    for bit in (1, 2, 4):
        y = jnp.where((sub & bit) != 0, pltpu.roll(y, width - bit, 1), y)
    return jnp.sum(y, axis=0, keepdims=True)


def attn_bwd_kernel(groups, carried, ids, nrm_in, *refs):
    ins, refs = refs[: 5 * groups], refs[5 * groups :]
    carry, refs = refs[:carried], refs[carried:]
    keep, send, *refs = refs
    outs, refs = refs[: 3 * groups], refs[3 * groups :]
    (diag, q, k, v, p, gm, nrm_t, dq, dk, dv, acc, stage, sems) = refs
    t = 128
    length = nrm_t.shape[1]
    nblk = length // t
    low, m0, m1 = half_masks(t)
    dma = Copies(sems)
    loads = []
    for n in range(groups):
        q_in, k_in, v_in, p_in, gm_in = ins[5 * n : 5 * n + 5]
        whole = [(v_in, v.at[n]), (gm_in, gm.at[n]), (k_in, k.at[n]), (q_in, q.at[n])]
        halves = [[(p_in.at[pl.ds(2 * i, 2)], p.at[pl.ds(4 * n + 2 * i, 2)])] for i in (0, 1)]
        loads += [dma.start(whole + halves[0]), dma.start(halves[1])]
        if n == 0:
            last = dma.start([(nrm_in, nrm_t)])
    base, half = 0, stage.shape[2]
    for g in carry:
        count = g.shape[1]
        inside = min(count, half - base) if base < half else 0
        if inside:
            last += dma.start([(g.at[:, pl.ds(0, inside)], stage.at[:, 0, pl.ds(base, inside)])])
        if inside < count:
            rest, at = count - inside, max(0, base - half)
            last += dma.start([(g.at[:, pl.ds(inside, rest)], stage.at[:, 1, pl.ds(at, rest)])])
        base += count
    sh = nrm_t.shape[0] // 4
    stores = []
    for n in range(groups):
        for pair in (0, 1):
            wait(loads[2 * n + pair])
            cols = pl.ds(pair * 128, 128)
            k2, v2 = k[n, :, cols], v[n, :, cols]
            dk_t = jnp.zeros((128, length), F32)
            dv_t = jnp.zeros((128, length), F32)
            for a in range(nblk):
                at = pl.ds(a * t, t)
                q2, g2 = q[n, at, cols], gm[n, at, cols]
                qm = rows_of([q2 * m0, q2 * m1])
                g_both = rows_of([g2 * m0, g2 * m1])
                dp = nt(g_both, v2)
                pb = rows_of([p[4 * n + 2 * pair, at, :], p[4 * n + 2 * pair + 1, at, :]])
                pf = pb.astype(F32)
                delta = jnp.sum(pf * dp, axis=-1, keepdims=True)
                ds = (pf * (dp - delta)).astype(BF)
                mq = nn(ds, k2)
                dq[n, at, cols] = jnp.where(low, mq[:t], mq[t:]).astype(BF)
                dk_t = dk_t + tn(qm, ds)
                dv_t = dv_t + tn(g_both, pb)
                dsf = ds.astype(F32)
                for h in (0, 1):
                    for b in range(nblk):
                        rel = b - a
                        place = rel + 1 if abs(rel) <= 1 else (3 if rel < 0 else 4)
                        tile = dsf[h * t : (h + 1) * t, b * t : (b + 1) * t]
                        lanes = pl.ds(place * t, t)
                        if (a, b) in ((1, 0), (0, 0), (0, 1), (2, 0), (0, 2)):
                            acc[h, :, lanes] = tile
                        else:
                            acc[h, :, lanes] += tile
            dk[n, :, cols] = dk_t.T.astype(BF)
            dv[n, :, cols] = dv_t.T.astype(BF)
            for h in (0, 1):
                near = jnp.concatenate([acc[h, :, pl.ds(0, 3 * t)], jnp.zeros((t, t), F32)], axis=1)
                far = jnp.sum(acc[h, :, pl.ds(3 * t, 2 * t)], axis=0, keepdims=True)
                diag[pl.ds(4 * n + 2 * pair + h, 1), :] = jnp.concatenate([diagonals(near), far], axis=1)
        stores += dma.start([(d.at[n], out) for d, out in zip((dq, dk, dv), outs[3 * n : 3 * n + 3])])
        if n == 0:
            wait(last)
        for i, g in enumerate((dq, dk, dv)):
            gw = nn(nrm_t[...], g[n]).astype(BF)
            for o in range(4):
                put(stage, o, base + i * sh, gw[o * sh : (o + 1) * sh])
        base += 3 * sh
    stores += dma.start(piece_copies(stage, keep, send, ids))
    wait(stores)


def first_norm_kernel(ids, gain, xs, ghid, *refs):
    ins = refs[0:9]
    w0, w1 = refs[9:15], refs[15:21]
    gi, ggain, xv, gv, dall, wbuf0, wbuf1, gn, sems = refs[21:]
    me, half = ids[0], ids[1]
    d = xs.shape[1]
    rows = xs.shape[0] // 4
    dma = Copies(sems)
    loads = dma.start(
        [(g, dall.at[n]) for n, g in enumerate(ins)]
        + pack_copies(w0, me, half, wbuf0, lambda ref: ref)
        + pack_copies(w1, me, half, wbuf1, lambda ref: ref)
    )
    part = wbuf0.shape[2] // 3
    rest = dma.start([(xs, xv), (ghid, gv)])
    wait(loads)
    acc = None
    for i in range(3):
        for c in range(3):
            buf, at = (wbuf0, i) if c == 0 else (wbuf1, 3 * (c - 1) + i)
            wi = rows_of([buf[o, h, pl.ds(at * part, part), :] for o in range(4) for h in (0, 1)])
            term = nt(dall[3 * i + c], wi)
            acc = term if acc is None else acc + term
    gn[...] = acc
    wait(rest)
    total = jnp.zeros((1, d), F32)
    for a in range(4):
        at = pl.ds(a * rows, rows)
        x = xv[at, :].astype(F32)
        gf = gn[at, :]
        n = lax.rsqrt(jnp.mean(x * x, axis=-1, keepdims=True) + EPS)
        g = gf * gain[...]
        xn = x * n
        total = total + jnp.sum(gf * xn, axis=0, keepdims=True)
        gi[at, :] = (gv[at, :] + n * (g - xn * (n * jnp.mean(g * x, axis=-1, keepdims=True)))).astype(BF)
    ggain[...] = total


def tokens_kernel(ids, tokens, out, gin):
    out[...] = tokens[:, 0]
    gin[...] = tokens[:, 1].astype(F32)


def ff_shares_kernel(quad, thirds, starts, ids, *refs):
    ins, (out_in, out_back, buf, part_in, part_back, sems) = refs, refs[-6:]
    here, far = ids[1], ids[3]
    sh = out_in.shape[0]
    dma = Copies(sems)
    n = (2 * sh + 384) // 8
    copies = []
    for k in range(len(thirds)):
        pairs = []
        for m, h in ((2 * k, here), (2 * k + 1, 1 - here)):
            src = ins[m].at[pl.ds(starts[m], 8 * n)]
            if not quad:
                pairs.append((src, buf.at[k, h]))
                continue
            for p in (0, 1):
                for q, i in enumerate(Sum.ORDER):
                    row = pl.multiple_of(p * 4 * n + (far ^ i) * n, 16)
                    pairs.append((src.at[pl.ds((4 * p + q) * n, n)], buf.at[k, h, pl.ds(row, n)]))
        copies.append(dma.start(pairs))
    stores = []
    for m, k in enumerate(thirds):
        wait(copies[m])
        for b in range(4):
            part_in[m, :, pl.ds(b * 256, 256)] = buf[m, 0, pl.ds(b * sh, sh), :].astype(F32)
        stores += dma.start([
            (part_in.at[m, :, pl.ds(b * 256, 256)], out_in.at[:, pl.ds((b * 3 + k) * 256, 256)]) for b in range(4)
        ])
        for j in range(3):
            part_back[m, :, pl.ds(j * 256, 256)] = buf[m, 1, pl.ds(j * 256, 256), :].astype(F32)
        stores += dma.start([(part_back.at[m], out_back.at[pl.ds(k * 256, 256)])])
    wait(stores)


def attn_shares_kernel(plain, ids, *refs):
    ins, (wq, wk, wv, wo, buf, sems) = refs[:-6], refs[-6:]
    here, far = ids[1], ids[3]
    sh = wq.shape[0]
    pairs = []
    for m, h in ((0, here), (1, 1 - here)):
        if plain:
            pairs.append((ins[m], buf.at[h]))
            continue
        n = ins[m].shape[1]
        pairs += [(ins[m].at[i], buf.at[h, pl.ds(pl.multiple_of((far ^ i) * n, 16), n)]) for i in range(4)]
    wait(Copies(sems).start(pairs))
    at = lambda half, n: buf[half, pl.ds(n * sh, sh), :].astype(F32)
    for i in range(3):
        wo[:, pl.ds(i * 256, 256)] = at(0, i)
    for i, out in enumerate((wq, wk, wv)):
        out[:, pl.ds(0, 256)] = at(1, i)
        out[:, pl.ds(256, 256)] = at(0, 3 + i)
        out[:, pl.ds(512, 256)] = at(1, 3 + i)


def bucket_of(offset, bucket_count):
    distance = jnp.abs(offset)
    bucket = jnp.where(offset > 0, bucket_count // 2, 0).astype(jnp.int32)
    for edge in EDGES:
        bucket = bucket + (distance >= edge).astype(jnp.int32)
    return bucket


def shards(inputs, segments, gain_attn, w_query, w_key, w_value, w_out, bucket_bias_table, gain_ff, w_in, w_back, cotangent):
    seqs, rows, d = inputs.shape
    sh = w_query.shape[0]
    hw = sh // 2
    ffs = w_in.shape[1]
    bucket_count, heads = bucket_bias_table.shape
    length = rows * seqs
    places = [lax.axis_index(a).astype(jnp.int32) for a in ("near", "side", "core", "far")]
    near_at, side_at, core_at, far_at = places
    line = Line(jnp.stack([2 * side_at + core_at, near_at, core_at, far_at]))
    gate = line.gate
    row_low, row_f32 = sds((length, d), BF), sds((length, d), F32)
    quad_low, tok_low = sds((length, 256), BF), sds((rows, d), BF)
    gain1, gain2 = gain_attn.reshape(1, d), gain_ff.reshape(1, d)
    pack_rows = [4 * hw + 384 + 3 * hw, 4 * hw + 384, 4 * hw + 384]

    m0, m1, m2, m3, own_a, own_b, y_a, y_b = call(
        prep_a_kernel,
        "prep_a",
        [sds((rows + 16, d), BF)] * 4
        + [sds((2, 3 * hw, 256), BF), sds((2, 6 * hw, 256), BF), sds((3 * hw, 256), BF), sds((6 * hw, 256), BF)],
        [SM, VM] + [HBM] * 4,
        [VM] * 8,
        [DMA((31,))],
        (line.ids, segments, inputs, w_query, w_key, w_value),
    )
    wa = Gather(line, own_a, y_a)
    msgs = [swap(m1, "core"), swap(m2, "side"), swap(m3, "side", "core")]
    wb = Gather(line, own_b, y_b)

    own0, own1, own2, y0, y1, y2, k1, k2, k3 = call(
        prep_b_kernel,
        "prep_b",
        [sds((2, r, 256), BF) for r in pack_rows] + [sds((r, 256), BF) for r in pack_rows] + [tok_low] * 3,
        [SM] + [HBM] * 4,
        [VM] * 9,
        [DMA((75,))],
        (line.ids, w_in, w_back, w_out, cotangent),
    )

    (own0,) = gate(own0)
    wa.cross()
    *msgs, table_in = gate(*msgs, bucket_bias_table)
    wa.relay()

    offs = jnp.arange(4 * rows, dtype=jnp.int32)
    offs = jnp.where(offs < 3 * rows, offs - rows, offs - 5 * rows)
    hot = (bucket_of(offs, bucket_count)[None] == jnp.arange(bucket_count, dtype=jnp.int32)[:, None]).astype(F32)
    lines = jnp.einsum("up,uw->wp", hot, table_in, precision=lax.Precision.HIGHEST)
    far = jnp.stack([table_in[bucket_count // 2 - 1], table_in[bucket_count - 1]])

    y0, own0 = gate(y0, own0)
    wf = [Gather(line, own0, y0)]
    xs, nrm, nrm_t, seg = call(
        norm_kernel,
        "norm",
        [row_low, row_low, sds((d, length), BF), sds((1, length), F32)],
        [SM] + [HBM] * 4 + [VM],
        [VM] * 4,
        [scratch((64, d)), DMA((8,))],
        (line.ids, m0, *msgs, gain1),
    )
    nrm, lines = gate(nrm, lines)
    wb.cross()
    wa = wa.done()

    qs, ks, vs, probs, mixed = [], [], [], [], []
    for g in range(3):
        q, k, v, p, mx = call(
            functools.partial(attn_fwd_kernel, g),
            "attn_fwd",
            [quad_low] * 3 + [sds((4, length, length), BF), quad_low],
            [SM, SM, VM, VM] + [HBM] * 7,
            [HBM] * 4 + [VM],
            [
                scratch((4, rows, 3 * rows), F32),
                scratch((length, d)),
                scratch((4, 2, 3 * hw, 256)),
                scratch((length, 256)),
                scratch((length, 256)),
                scratch((length, 256)),
                scratch((4, length, length)),
                DMA((15,)),
            ],
            (line.ids, far, seg, lines, nrm, *(wa if g == 0 else wb)),
        )
        (mx,) = gate(mx)
        for have, new in ((qs, q), (ks, k), (vs, v), (probs, p), (mixed, mx)):
            have.append(new)
        if g == 0:
            wb.relay()
            wf[0].cross()
            own1, y1 = gate(own1, y1)
            wf.append(Gather(line, own1, y1))
            wb = wb.done()
        if g == 1:
            wf[0].relay()
            wf[1].cross()
            k1, k2, k3 = gate(k1, k2, k3)
            cots = [swap(k1, "core"), swap(k2, "side"), swap(k3, "side", "core")]
    packs = [wf[0].done()]
    cots = gate(*cots)
    wf[1].relay()
    own2, y2 = gate(own2, y2)
    wf.append(Gather(line, own2, y2))

    sums_f, acts, gpres = [], [], []
    for c in range(3):
        lead = c == 0
        *fresh, act, gpre, keep, send = call(
            functools.partial(ffn_kernel, lead),
            "ffn",
            ([row_f32, row_low, sds((d, length), BF)] if lead else [])
            + [sds((length, 1024), BF)] * 2
            + piece_shapes(4 * sh + 768),
            [SM] + ([VM] + [HBM] * 4 if lead else [HBM] * 2) + [HBM] * 10,
            [HBM] * (7 if lead else 4),
            (
                [scratch((length, d)), scratch((length, d)), scratch((4, 2, 3 * hw, 256)), scratch((length, d), F32)]
                if lead
                else []
            )
            + [
                scratch((length, d)),
                scratch((d, length)),
                scratch((length, d)),
                scratch((4, 2, 4 * hw + 384, 256)),
                scratch((length, 1024)),
                scratch((length, 1024)),
                scratch((4, 2, 2 * sh + 384, 256)),
                DMA((60,)),
            ],
            (line.ids, *((gain2, xs, *mixed) if lead else (ff, ff_t)), cotangent, *cots, *packs[c]),
        )
        if lead:
            hid, ff, ff_t = fresh
        piece = (keep, send)
        acts.append(act)
        (gpre,) = gate(gpre)
        gpres.append(gpre)
        if c == 0:
            packs.append(wf[1].done())
            wf[2].cross()
        if c == 1:
            wf[2].relay()
        moves = [[], [("first",)], [("second",), ("first",)]][c]
        sums_f.append(advance(line, *[(f, *m) for f, m in zip(sums_f, moves)], new=piece))
        if c == 1:
            packs.append(wf[2].done())

    ghid, *gmix, ggain_ff, gwo = call(
        after_ff_kernel,
        "after_ff",
        [row_f32] + [quad_low] * 3 + [sds((1, d), F32), sds((4, 3 * sh, 256), BF)],
        [SM, VM] + [HBM] * 29,
        [HBM] * 4 + [VM, HBM],
        [
            scratch((length, d), F32),
            scratch((3, length, 1024)),
            scratch((length, d)),
            scratch((length, d)),
            scratch((4, 2, 3 * hw, 256)),
            scratch((3, 4, 2, 4 * hw, 256)),
            scratch((length, d)),
            scratch((length, d), F32),
            scratch((length, d), F32),
            scratch((3, length, 256)),
            scratch((4, 3 * sh, 256)),
            DMA((52,)),
        ],
        (line.ids, gain2, hid, *gpres, cotangent, *cots, *mixed, *packs[0], *packs[1], *packs[2]),
    )
    gmix[0], ggain_ff = gate(gmix[0], ggain_ff)
    quad = lax.axis_size("far") == 4
    third = "spread" if quad else "third"
    far_steps = lambda *steps: steps if quad else ()
    advance(line, (sums_f[0], third), (sums_f[1], "second"), (sums_f[2], "first"))

    dqs, dks, dvs, diags, sums_a = [], [], [], [], []
    for first, groups in ((0, 1), (1, 2)):
        carry = (gwo,) if first == 0 else ()
        body = 3 * sh * (groups + len(carry))
        some = range(first, first + groups)
        keep, send, *grads, diag = call(
            functools.partial(attn_bwd_kernel, groups, len(carry)),
            "attn_bwd",
            piece_shapes(body) + [quad_low] * (3 * groups) + [sds((4 * groups, 6 * rows), F32)],
            [SM] + [HBM] * (1 + 5 * groups + len(carry)),
            [HBM] * (2 + 3 * groups) + [VM],
            [scratch((groups, length, 256))] * 3
            + [scratch((4 * groups, length, length)), scratch((groups, length, 256)), scratch((d, length))]
            + [scratch((groups, length, 256))] * 3
            + [scratch((2, rows, 5 * rows), F32), scratch((4, 2, body // 2, 256)), DMA((48,))],
            (line.ids, nrm_t, *[a for g in some for a in (qs[g], ks[g], vs[g], probs[g], gmix[g])], *carry),
            us=10 * groups,
        )
        (grads[0],) = gate(grads[0])
        for n in range(groups):
            for have, new in zip((dqs, dks, dvs), grads[3 * n : 3 * n + 3]):
                have.append(new)
        diags.append(diag)
        if first == 0:
            steps = ((sums_f[1], third), (sums_f[2], "second"), *far_steps((sums_f[0], "pair")))
        else:
            steps = ((sums_a[0], "first"), (sums_f[2], third))
            steps += far_steps((sums_f[0], "back"), (sums_f[1], "pair"))
        sums_a.append(advance(line, *steps, new=(keep, send)))

    gin, ggain_attn = call(
        first_norm_kernel,
        "first_norm",
        [row_low, sds((1, d), F32)],
        [SM, VM] + [HBM] * 23,
        [VM] * 2,
        [
            scratch((length, d)),
            scratch((length, d), F32),
            scratch((9, length, 256)),
            scratch((4, 2, 3 * hw, 256)),
            scratch((4, 2, 6 * hw, 256)),
            scratch((length, d), F32),
            DMA((27,)),
        ],
        (line.ids, gain1, xs, ghid, *dqs, *dks, *dvs, *wa, *wb),
    )
    gin, ggain_attn = gate(gin, ggain_attn)
    steps = far_steps((sums_f[0], "last"), (sums_f[1], "back"), (sums_f[2], "pair"))
    advance(line, (sums_a[1], "first"), (sums_a[0], "second"), *steps)
    (tokens,) = call(
        out_kernel,
        "out",
        [sds((seqs, 2, rows, d), BF)],
        [SM] + [HBM] * 23,
        [VM],
        [
            scratch((length, d), F32),
            scratch((3, length, 1024)),
            scratch((3, 4, 2, 384, 256)),
            DMA((32,)),
        ],
        (line.ids, hid, gin, *acts, *packs[0], *packs[1], *packs[2]),
    )
    tokens, ggain_attn = gate(tokens, ggain_attn)
    steps = far_steps((sums_f[0], "finish"), (sums_f[1], "last"), (sums_f[2], "back"))
    advance(line, (sums_a[1], "second"), (sums_a[0], "third"), *steps)
    first_total = sums_a[0].buffer


    hot6 = jnp.concatenate(
        [
            hot,
            jnp.zeros((bucket_count, rows), F32).at[bucket_count // 2 - 1].set(1.0),
            jnp.zeros((bucket_count, rows), F32).at[bucket_count - 1].set(1.0),
        ],
        axis=1,
    )
    table = jnp.einsum("up,wp->uw", hot6, jnp.concatenate(diags, axis=0), precision=lax.Precision.HIGHEST)
    small = jnp.concatenate([ggain_attn.reshape(-1), ggain_ff.reshape(-1), table.reshape(-1)])
    tokens = lax.all_to_all(tokens, ("side", "core"), 0, 0, tiled=True)
    advance(line, (sums_a[1], "third"), *far_steps((sums_f[1], "finish"), (sums_f[2], "last")))
    far_c = FarSum([first_total, sums_a[1].buffer])

    sums_f[1].land(line)
    far_c.land(line)
    far_c.back()
    if quad:
        advance(line, (sums_f[2], "finish"))
    else:
        for f in sums_f:
            whole = lax.psum(f.buffer, "far")
            f.buffer, f.flying = whole, {0: (swap(whole, "near"), ())}
    (small,) = gate(small)
    small = small + swap(small, "core")

    def ff_shares(thirds, have):
        parts, starts = [], []
        for f in [sums_f[k] for k in thirds]:
            arr, at = next(iter(f.flying.values()))
            parts += [f.buffer, *gate(arr)]
            starts += [0, at[0].start if at else 0]
        n = len(thirds)
        return call(
            functools.partial(ff_shares_kernel, quad, thirds, starts),
            "ff_shares",
            [sds((sh, ffs), F32), sds(w_back.shape, F32)],
            [SM] + [HBM] * (2 * n + len(have)),
            [HBM] * 2,
            [
                scratch((n, 2, 2 * sh + 384, 256)),
                scratch((n, sh, 1024), F32),
                scratch((n, 256, d), F32),
                DMA((21 * n,)),
            ],
            (line.ids, *parts, *have),
            aliases={1 + 2 * n + i: i for i in range(len(have))},
            us=1,
        )

    shares = gate(*ff_shares((0, 1), ()))
    sums_f[2].land(line)
    far_c.land(line)
    far_c.finish(line)
    (small,) = gate(small)
    small = small + swap(small, "side")
    tokens, small = gate(tokens, small)
    small = small + swap_far(small, 1) if quad else lax.psum(small, "far")
    output, grad_inputs = call(
        tokens_kernel,
        "tokens",
        [sds((seqs, rows, d), BF), sds((seqs, rows, d), F32)],
        [SM, VM],
        [VM] * 2,
        [],
        (line.ids, tokens),
        us=1,
    )
    output, small = gate(output, small)
    if quad:
        small = small + swap_far(small, 2)
    share_in, share_back = gate(*ff_shares((2,), shares))
    *shares_c, small = gate(*far_c.result, small)
    small = small + swap(small, "near")
    share_q, share_k, share_v, share_o = call(
        functools.partial(attn_shares_kernel, far_c.plain),
        "attn_shares",
        [sds((sh, d), F32)] * 4,
        [SM] + [HBM] * len(shares_c),
        [VM] * 4,
        [scratch((2, 6 * sh, 256)), DMA((8,))],
        (line.ids, *shares_c),
        us=1,
    )
    total_gain_attn, total_gain_ff = small[:d], small[d : 2 * d]
    total_table = small[2 * d :].reshape(bucket_count, heads)


    return (
        output,
        grad_inputs,
        total_gain_attn,
        share_q,
        share_k,
        share_v,
        share_o,
        total_table,
        total_gain_ff,
        share_in,
        share_back,
    )


def solution(mesh):
    far = mesh.shape["rows"] // 2
    inner = jax.sharding.Mesh(mesh.devices.reshape(far, 2, 2, 2), AXES)
    over_rows, over_blk = ("far", "near"), ("side", "core")
    tok, row, rep = P(over_rows, over_blk, None), P(over_blk, None), P()
    return jax.shard_map(
        shards,
        mesh=inner,
        in_specs=(tok, P(over_rows, over_blk), rep, row, row, row, row, rep, rep, row, row, tok),
        out_specs=(tok, tok, rep, row, row, row, row, rep, rep, row, row),
        check_vma=False,
    )
```

```python
import functools

import jax
import jax.numpy as jnp
from jax import lax
from jax.experimental import pallas as pl
from jax.experimental.pallas import tpu as pltpu
from jax.sharding import PartitionSpec as P

EPS = 1e-06
EDGES = (1, 2, 3, 4, 5, 6, 7, 8, 12, 16, 23, 32, 46, 64, 91)
BF = jnp.bfloat16
F32 = jnp.float32
HBM = pl.BlockSpec(memory_space=pltpu.HBM)
VM = pl.BlockSpec(memory_space=pltpu.VMEM)
SM = pl.BlockSpec(memory_space=pltpu.SMEM)
DMA = pltpu.SemaphoreType.DMA
sds = jax.ShapeDtypeStruct
AXES = ("far", "near", "side", "core")
FLIPS = {"far2": 16, "far1": 8, "near": 4, "whole": 4, "side": 2, "core": 1}


def scratch(shape, kind=BF):
    return pltpu.VMEM(shape, kind)


def call(kernel, name, outs, ins, out_specs, scratches, args, us=20, aliases={}):
    return pl.pallas_call(
        kernel,
        out_shape=outs,
        in_specs=ins,
        out_specs=out_specs,
        scratch_shapes=scratches,
        input_output_aliases=aliases,
        compiler_params=pltpu.CompilerParams(vmem_limit_bytes=63 * 1024 * 1024),
        cost_estimate=pl.CostEstimate(flops=int(us * 10**9), bytes_accessed=int(us * 4 * 10**6), transcendentals=0),
        name=name,
    )(*args)


def nn(a, b):
    return lax.dot_general(a, b, (((1,), (0,)), ((), ())), preferred_element_type=F32)


def nt(a, b):
    return lax.dot_general(a, b, (((1,), (1,)), ((), ())), preferred_element_type=F32)


def tn(a, b):
    return lax.dot_general(a, b, (((0,), (0,)), ((), ())), preferred_element_type=F32)


def swap(value, *axes):
    flip = sum(FLIPS[a] for a in axes)
    count = 1
    for a in AXES:
        count *= lax.axis_size(a)
    return lax.ppermute(value, AXES, [(i, i ^ flip) for i in range(count)])


def swap_far(value, bits):
    count = 8 * lax.axis_size("far")
    return lax.ppermute(value, AXES, [(i, i ^ (8 * bits)) for i in range(count)])


class Line:
    def __init__(self, ids):
        self.ids = ids

    def gate(self, *values):
        self.ids, *values = lax.optimization_barrier((self.ids, *values))
        return tuple(values)


def pick(arr, index, axis=0):
    return lax.dynamic_index_in_dim(arr, index, axis, keepdims=False)


class Sum:
    AXES = (("side", "near"), ("near", "side"))
    ORDER = (0, 2, 1, 3)

    def __init__(self, keep, send):
        self.rows = keep.shape[3]
        places = [(p, i, j) for p in (0, 1) for i in (0, 1) for j in (0, 1)]
        self.kept = {at: (keep, at) for at in places}
        got = swap(send, "core")
        self.flying = {at: (got, at) for at in places}

    def added(self, key):
        return self.kept[key], self.flying[key]

    def land(self, line):
        arrays = []
        for arr, _ in self.flying.values():
            if not any(arr is f for f in arrays):
                arrays.append(arr)
        landed = line.gate(*arrays)
        here = lambda arr: next(l for f, l in zip(arrays, landed) if f is arr)
        self.flying = {key: (here(arr), at) for key, (arr, at) in self.flying.items()}

    def first(self):
        out = []
        for p, i, j in self.kept:
            move = (self.AXES[p][0], (p, j)) if i else None
            out.append((*self.added((p, i, j)), None if i else (p, j), move))
        return self.rows, out

    def second(self):
        out = []
        for p, j in self.kept:
            out.append((*self.added((p, j)), None if j else p, (self.AXES[p][1], p) if j else None))
        return self.rows, out

    def third(self):
        return self.rows, [(*self.added(p), p, None) for p in (0, 1)]

    def spread(self):
        out = []
        cut = lambda block, i: (block[0], (*block[1], ("far", i)))
        for p in (0, 1):
            a, b = self.added(p)
            for i in range(4):
                sent = i & 1
                out.append((cut(a, i), cut(b, i), None if sent else (p, i), ("far1", (p, i - 1)) if sent else None))
        return self.rows // 4, out

    def pair(self):
        out = [(*self.added((p, i)), None if i else p, ("far2", p) if i else None) for p in (0, 1) for i in (0, 2)]
        return self.rows // 4, out

    def back(self):
        return self.rows // 4, [(*self.added(p), (p, 0), ("far2", (p, 2))) for p in (0, 1)]

    def last(self):
        have = {**self.kept, **self.flying}
        out = [(have[p, i], None, (p, i), ("far1", (p, i + 1))) for p in (0, 1) for i in (0, 2)]
        return self.rows // 4, out

    def finish(self):
        have = {**self.kept, **self.flying}
        out = [(have[p, i], None, (p, i), ("whole", (p, i))) for p in (0, 1) for i in self.ORDER]
        return self.rows // 4, out


class FarSum:
    def __init__(self, parts):
        total = jnp.concatenate(parts, axis=0)
        self.plain = lax.axis_size("far") != 4
        if self.plain:
            self.kept, self.flying = lax.psum(total, "far"), ()
            return
        blocks = total.reshape(4, -1, 256)
        here = lax.axis_index("far")
        self.kept = pick(blocks, here)
        self.flying = tuple(swap_far(pick(blocks, here ^ i), i) for i in (1, 2, 3))

    def land(self, line):
        if self.flying:
            self.flying = line.gate(*self.flying)

    def back(self):
        if self.plain:
            return
        total = self.kept.astype(F32)
        for f in self.flying:
            total = total + f.astype(F32)
        self.kept = total.astype(BF)
        self.flying = tuple(swap_far(self.kept, i) for i in (1, 2, 3))

    def finish(self, line):
        if self.plain:
            self.result = (self.kept, swap(self.kept, "near"))
            return
        (whole,) = line.gate(jnp.stack([self.kept, *self.flying]))
        self.flying = (swap(whole, "near"),)
        self.result = (whole, *self.flying)


def add_kernel(jobs, arrays, ids, *refs):
    ins, refs = refs[:arrays], refs[arrays:]
    count = len(jobs)
    bufs, sems = refs[-1 - 2 * count : -1], refs[-1]
    outs = refs[: len(refs) - 1 - 2 * count]
    far = ids[3]
    dma = Copies(sems)

    def view(ref, at, rows):
        if at and isinstance(at[-1], tuple):
            *at, (_, i) = at
            start = at.pop().start if at and hasattr(at[-1], "start") else 0
            at = (*at, pl.ds(pl.multiple_of(start + (far ^ i) * rows, 16), rows))
        return ref.at[tuple(at)] if at else ref

    loads = []
    for n, (rows, a, b, _) in enumerate(jobs):
        loads.append(dma.start([(view(ins[x], at, rows), bufs[2 * n + m]) for m, (x, at) in enumerate((a, b)) if x >= 0]))
    stores = []
    for n, (rows, a, b, places) in enumerate(jobs):
        wait(loads[n])
        buf = bufs[2 * n]
        if b[0] >= 0:
            buf[...] = buf[...] + bufs[2 * n + 1][...]
        stores += dma.start([(buf, outs[o].at[pl.ds(row, rows)]) for o, row in places])
    wait(stores)


def advance(line, *steps, new=()):
    flying = []
    for piece, _ in steps:
        for arr, _ in piece.flying.values():
            if not any(arr is f for f in flying):
                flying.append(arr)
    landed = list(line.gate(*flying, *new))
    here = lambda arr: next(l for f, l in zip(flying, landed) if f is arr)
    fresh = Sum(*landed[len(flying) :]) if new else None
    if not steps:
        return fresh
    arrays, jobs, sizes, marks = [], [], {}, []

    def number(block):
        if block is None:
            return (-1, ())
        arr, at = block
        if not any(arr is x for x in arrays):
            arrays.append(arr)
        return next(n for n, x in enumerate(arrays) if x is arr), at

    for piece, step in steps:
        piece.flying = {key: (here(arr), at) for key, (arr, at) in piece.flying.items()}
        rows, todo = getattr(piece, step)()
        for a, b, key, move in todo:
            places = []
            for name, mark in ((("kept", piece), key), (move[0] if move else None, move[1] if move else None)):
                if mark is None:
                    continue
                row = sizes.get(name, 0)
                sizes[name] = row + rows
                places.append((name, row))
                marks.append((piece, name, mark, row, rows))
            jobs.append((rows, number(a), number(b), places))
    names = list(sizes)
    jobs = [(rows, a, b, tuple((names.index(n), row) for n, row in places)) for rows, a, b, places in jobs]
    sums = call(
        functools.partial(add_kernel, jobs, len(arrays)),
        "add",
        [sds((sizes[n], 256), BF) for n in names],
        [SM] + [HBM] * len(arrays),
        [HBM] * len(names),
        [scratch((rows, 256)) for rows, *_ in jobs for _ in (0, 1)] + [DMA((4 * len(jobs),))],
        (line.ids, *arrays),
        us=3,
    )
    line.gate(sums[0])
    results = {n: v if isinstance(n, tuple) else swap(v, n) for n, v in zip(names, sums)}
    for piece, _ in steps:
        piece.kept, piece.flying = {}, {}
        piece.buffer = results.get(("kept", piece))
    for piece, name, mark, row, rows in marks:
        where = piece.kept if isinstance(name, tuple) else piece.flying
        where[mark] = (results[name], (pl.ds(row, rows),))
    return fresh


class Gather:
    def __init__(self, line, own, half):
        self.line, self.own = line, own
        self.y = swap(half, "side")
        self.core = swap(own, "core")

    def cross(self):
        self.y, self.core = self.line.gate(self.y, self.core)
        self.x = swap(self.y, "near")

    def relay(self):
        (self.x,) = self.line.gate(self.x)
        self.yc, self.xc = swap(self.y, "core"), swap(self.x, "core")

    def done(self):
        self.yc, self.xc = self.line.gate(self.yc, self.xc)
        return (self.own, self.core, self.y, self.x, self.yc, self.xc)


class Copies:
    def __init__(self, sems):
        self.sems, self.count = sems, 0

    def start(self, pairs):
        out = []
        for src, dst in pairs:
            out.append(pltpu.make_async_copy(src, dst, self.sems.at[self.count]))
            self.count += 1
            out[-1].start()
        return out


def wait(copies):
    for c in copies:
        c.wait()


def pieces_of(refs, me, half):
    own, core, y, x, yc, xc = refs
    out = []
    for h in (0, 1):
        out.append((own.at[h], me, h))
        out.append((core.at[h], me ^ 1, h))
    out.append((y, me ^ 2, half))
    out.append((x, me ^ 2, 1 - half))
    out.append((yc, me ^ 3, half))
    out.append((xc, me ^ 3, 1 - half))
    return out


def pack_copies(refs, me, half, dst, cut):
    return [(cut(ref), dst.at[o, h]) for ref, o, h in pieces_of(refs, me, half)]


def token_copies(slots, me, dst):
    rows = dst.shape[0] // 4
    return [
        (src, dst.at[pl.ds(pl.multiple_of((me ^ s) * rows, rows), rows)]) for s, src in enumerate(slots)
    ]


def put(stage, owner, row, value):
    half, count = stage.shape[2], value.shape[0]
    first = min(count, max(0, half - row))
    if first:
        stage[owner, 0, pl.ds(row, first), :] = value[:first]
    if first < count:
        stage[owner, 1, pl.ds(row + first - half, count - first), :] = value[first:]


class Either:
    def __init__(self, dma, stage, keep, send, ids, owner, half, part):
        me, near = ids[0], ids[1]
        rows = stage.shape[2] // 2
        sem = dma.sems.at[dma.count]
        dma.count += 1
        sy, sx = ((me ^ owner) >> 1) & 1, near ^ half
        at = (part, sy, sx) if part == 0 else (part, sx, sy)
        src = stage.at[owner, half, pl.ds(part * rows, rows)]
        self.stays = ((me ^ owner) & 1) == 0
        self.copies = [pltpu.make_async_copy(src, dst.at[at], sem) for dst in (keep, send)]
        self.each("start")

    def each(self, name):
        for copy, taken in zip(self.copies, (self.stays, jnp.logical_not(self.stays))):
            pl.when(taken)(getattr(copy, name))

    def wait(self):
        self.each("wait")


def piece_shapes(rows):
    return [sds((2, 2, 2, rows // 4, 256), BF)] * 2


def rows_of(blocks):
    return jnp.concatenate(blocks, axis=0)


def prep_a_kernel(ids, seg, inputs, wq, wk, wv, m0, m1, m2, m3, own0, own1, y0, y1, sems):
    me, half = ids[0], ids[1]
    rows = inputs.shape[1]
    part = wq.shape[0] // 2
    pairs = []
    for g in range(3):
        own, y, at = (own0, y0, 0) if g == 0 else (own1, y1, g - 1)
        for i, w in enumerate((wq, wk, wv)):
            cols, place = pl.ds(g * 256, 256), pl.ds((3 * at + i) * part, part)
            pairs.append((w.at[pl.ds(pl.multiple_of(half * part, 16), part), cols], y.at[place]))
            for h in (0, 1):
                pairs.append((w.at[pl.ds(h * part, part), cols], own.at[h, place]))
    for s, m in enumerate((m0, m1, m2, m3)):
        pairs.append((inputs.at[me ^ s], m.at[pl.ds(0, rows)]))
    copies = Copies(sems).start(pairs)
    for s, m in enumerate((m0, m1, m2, m3)):
        line = seg[pl.ds(me ^ s, 1), :].astype(F32)
        m[pl.ds(rows, 16), pl.ds(0, rows)] = jnp.broadcast_to(line, (16, rows)).astype(BF)
        m[pl.ds(rows, 16), pl.ds(rows, m.shape[1] - rows)] = jnp.zeros((16, m.shape[1] - rows), BF)
    wait(copies)


def prep_b_kernel(ids, w_in, w_back, w_out, cot, own0, own1, own2, y0, y1, y2, k1, k2, k3, sems):
    me, half = ids[0], ids[1]
    hw = w_in.shape[0] // 2
    pairs = [(cot.at[me ^ s], k) for s, k in ((1, k1), (2, k2), (3, k3))]
    for c, (own, y) in enumerate(((own0, y0), (own1, y1), (own2, y2))):
        for dst, h in ((y, half), (own.at[0], 0), (own.at[1], 1)):
            for b in range(4):
                pairs.append((
                    w_in.at[pl.ds(pl.multiple_of(h * hw, 16), hw), pl.ds(b * 768 + c * 256, 256)],
                    dst.at[pl.ds(b * hw, hw)],
                ))
            for j in range(3):
                pairs.append((
                    w_back.at[pl.ds(pl.multiple_of(c * 256 + h * 128, 16), 128), pl.ds(j * 256, 256)],
                    dst.at[pl.ds(4 * hw + j * 128, 128)],
                ))
                if c == 0:
                    pairs.append((
                        w_out.at[pl.ds(pl.multiple_of(h * hw, 16), hw), pl.ds(j * 256, 256)],
                        dst.at[pl.ds(4 * hw + 384 + j * hw, hw)],
                    ))
    wait(Copies(sems).start(pairs))


def norm_kernel(ids, m0, m1, m2, m3, gain, xs, nrm, nrm_t, seg, sbuf, sems):
    me = ids[0]
    rows = xs.shape[0] // 4
    slots = (m0, m1, m2, m3)
    tok = token_copies([m.at[pl.ds(0, rows)] for m in slots], me, xs)
    tok += token_copies([m.at[pl.ds(rows, 16)] for m in slots], me, sbuf)
    wait(Copies(sems).start(tok))
    seg[...] = jnp.concatenate(
        [sbuf[pl.ds(o * 16, 1), pl.ds(0, rows)].astype(F32) for o in range(4)], axis=1
    )
    for a in range(4):
        x = xs[pl.ds(a * rows, rows), :].astype(F32)
        y = x * lax.rsqrt(jnp.mean(x * x, axis=-1, keepdims=True) + EPS) * gain[...]
        y = y.astype(BF)
        nrm[pl.ds(a * rows, rows), :] = y
        nrm_t[:, pl.ds(a * rows, rows)] = y.T


def half_masks(t):
    lane = lax.broadcasted_iota(jnp.int32, (t, 128), 1)
    return lane < 64, (lane < 64).astype(F32).astype(BF), (lane >= 64).astype(F32).astype(BF)


def attn_fwd_kernel(group, ids, table, seg, lines, nrm_in, w0, w1, w2, w3, w4, w5,
                    q_out, k_out, v_out, p_out, o, near, nrm, wbuf, q, k, v, p, sems):
    me, half = ids[0], ids[1]
    dma = Copies(sems)
    count = wbuf.shape[2]
    count_b = table.shape[0]
    part = count // 3
    place = pl.ds(max(group - 1, 0) * count, count)
    loads = dma.start(
        [(nrm_in, nrm)]
        + pack_copies((w0, w1, w2, w3, w4, w5), me, half, wbuf, lambda ref: ref.at[place])
    )
    for head in range(4):
        line = jnp.broadcast_to(lines[pl.ds(4 * group + head, 1), :], (near.shape[1], lines.shape[1]))
        near[head] = pltpu.roll(line, 0, 1, stride=1, stride_axis=0)[:, : near.shape[2]]
    t = near.shape[1]
    length = q.shape[0]
    nblk = length // t
    low, m0, m1 = half_masks(t)
    eye = lax.broadcasted_iota(jnp.int32, (t, t), 0) == lax.broadcasted_iota(jnp.int32, (t, t), 1)
    seg_row = seg[...]
    wait(loads)
    stores = []
    for i, (buf, out) in enumerate(((q, q_out), (k, k_out), (v, v_out))):
        w = rows_of([wbuf[ow, h, pl.ds(i * part, part), :] for ow in range(4) for h in (0, 1)])
        buf[...] = nn(nrm[...], w).astype(BF)
        stores += dma.start([(buf, out)])
    for pair in (0, 1):
        at = pl.ds(pair * 128, 128)
        for a in range(nblk):
            seg_col = jnp.sum(
                jnp.where(eye, jnp.broadcast_to(seg_row[:, a * t : (a + 1) * t], (t, t)), 0.0),
                axis=1,
                keepdims=True,
            )
            allowed = seg_col == seg_row
            q2 = q[pl.ds(a * t, t), at]
            s = nt(rows_of([q2 * m0, q2 * m1]), k[:, at])
            ps = []
            for h in (0, 1):
                head = 2 * pair + h
                strip = []
                for b in range(nblk):
                    rel = b - a
                    if abs(rel) <= 1:
                        strip.append(near[head, :, (rel + 1) * t : (rel + 2) * t])
                    else:
                        strip.append(jnp.full((t, t), table[(count_b // 2 if rel < 0 else count_b) - 1, group * 4 + head], F32))
                sh = s[h * t : (h + 1) * t] + jnp.concatenate(strip, axis=1)
                sh = jnp.where(allowed, sh, -1e30)
                top = jnp.max(sh, axis=-1, keepdims=True)
                e = jnp.exp(sh - top)
                inv = 1.0 / jnp.sum(e, axis=-1, keepdims=True)
                ph = (e * inv).astype(BF)
                p[head, pl.ds(a * t, t), :] = ph
                ps.append(ph)
            mix = nn(rows_of(ps), v[:, at])
            o[pl.ds(a * t, t), at] = jnp.where(low, mix[:t], mix[t:]).astype(BF)
        stores += dma.start([(p.at[pl.ds(2 * pair, 2)], p_out.at[pl.ds(2 * pair, 2)])])
    wait(stores)


def out_weight(wbuf, j):
    hw = wbuf.shape[2] // 3
    return rows_of([wbuf[o, h, pl.ds(j * hw, hw), :] for o in range(4) for h in (0, 1)])


def out_cut(sh):
    return lambda ref: ref.at[pl.ds(2 * sh + 384, 3 * (sh // 2))]


def gelu_both(x):
    c = 0.7978845608028654
    x2 = x * x
    th = jnp.tanh(x * (c + (c * 0.044715) * x2))
    half_up = 0.5 + 0.5 * th
    slope = half_up + x * (0.5 - 0.5 * th * th) * (c + (3.0 * c * 0.044715) * x2)
    return x * half_up, slope


def ffn_kernel(lead, ids, *refs):
    if lead:
        gain, xs, x0, x1, x2, cown, c1, c2, c3, p0, p1, p2, p3, p4, p5, *rest = refs
        hid_out, ff_out, fft_out, act_out, gpre_out, keep, send, *rest = rest
        xv, mx, wout, hid, ffv, fftv, cot, pack, act, gpre, stage, sems = rest
    else:
        ff, ff_t, cown, c1, c2, c3, p0, p1, p2, p3, p4, p5, act_out, gpre_out, keep, send, *rest = refs
        ffv, fftv, cot, pack, act, gpre, stage, sems = rest
    me, half = ids[0], ids[1]
    d = ffv.shape[1]
    sh = d // 4
    hw = sh // 2
    packs = (p0, p1, p2, p3, p4, p5)
    dma = Copies(sems)
    split = lambda at, n: [
        (ref.at[pl.ds(at, n)], pack.at[o, h, pl.ds(at, n)]) for ref, o, h in pieces_of(packs, me, half)
    ]
    weights, back_weights = split(0, 4 * hw), split(4 * hw, 384)
    stores = []
    if lead:
        early = dma.start(
            pack_copies(packs, me, half, wout, out_cut(sh))
            + [(x, mx.at[:, pl.ds(i * 256, 256)]) for i, x in enumerate((x0, x1, x2))]
            + [(xs, xv)]
        )
        first = dma.start(weights)
    else:
        first = dma.start([(ff, ffv)] + weights)
    second = dma.start(token_copies((cown.at[me], c1, c2, c3), me, cot) + back_weights)
    if lead:
        third = ()
        wait(early)
        for j in range(3):
            cols = pl.ds(j * 256, 256)
            hid[:, cols] = xv[:, cols].astype(F32) + nn(mx[...], out_weight(wout, j))
        rows = 128
        for a in range(xv.shape[0] // rows):
            x = hid[pl.ds(a * rows, rows), :]
            y = x * lax.rsqrt(jnp.mean(x * x, axis=-1, keepdims=True) + EPS) * gain[...]
            y = y.astype(BF)
            ffv[pl.ds(a * rows, rows), :] = y
            fftv[:, pl.ds(a * rows, rows)] = y.T
        stores += dma.start([(hid, hid_out), (ffv, ff_out), (fftv, fft_out)])
    else:
        third = dma.start([(ff_t, fftv)])
    wait(first)
    for b in range(5):
        if b < 4:
            at = pl.ds(b * 256, 256)
            win = rows_of([pack[o, h, pl.ds(b * hw, hw), :] for o in range(4) for h in (0, 1)])
            value, slope = gelu_both(nn(ffv[...], win))
            if b == 0:
                wait(second)
            act[:, at] = value.astype(BF)
            back = 0.0
            for j in range(3):
                wb = rows_of([pack[b, h, pl.ds(4 * hw + j * 128, 128), :] for h in (0, 1)])
                back = back + nt(cot[:, pl.ds(j * 256, 256)], wb)
            gpre[:, at] = (back * slope).astype(BF)
        if b == 3:
            stores += dma.start([(act, act_out), (gpre, gpre_out)])
        if b > 0:
            c = b - 1
            at = pl.ds(c * 256, 256)
            if c == 0:
                wait(third)
            gw = nn(fftv[...], gpre[:, at]).astype(BF)
            for o in range(4):
                put(stage, o, c * sh, gw[o * sh : (o + 1) * sh])
            gb = tn(act[:, at], cot[...]).astype(BF)
            for j in range(3):
                put(stage, c, 4 * sh + j * 256, gb[:, j * 256 : (j + 1) * 256])
            stores += [Either(dma, stage, keep, send, ids, c, 1, part) for part in (0, 1)]
            if c & 1:
                stores += [Either(dma, stage, keep, send, ids, o, 0, c // 2) for o in range(4)]
    wait(stores)


def after_ff_kernel(ids, gain, hid, g0, g1, g2, cown, c1, c2, c3, x0, x1, x2, *refs):
    packs = (refs[0:6], refs[6:12], refs[12:18])
    ghid_out, gm0, gm1, gm2, ggain, gwo_out, hidv, gv, cot, mx, wbuf, wins, ga, gf, ghid, gmv, gwo, sems = refs[18:]
    stores = []
    me, half = ids[0], ids[1]
    d = hid.shape[1]
    sh = d // 4
    hw = sh // 2
    rows = cot.shape[0] // 4
    dma = Copies(sems)
    loads = [
        dma.start(
            [(g, gv.at[c])]
            + pack_copies(packs[c], me, half, wins.at[c], lambda ref: ref.at[pl.ds(0, 4 * hw)])
        )
        for c, g in enumerate((g0, g1, g2))
    ]
    rest = dma.start([(hid, hidv)] + token_copies((cown.at[me], c1, c2, c3), me, cot))
    last = dma.start(
        pack_copies(packs[0], me, half, wbuf, out_cut(sh))
        + [(x, mx.at[:, pl.ds(i * 256, 256)]) for i, x in enumerate((x0, x1, x2))]
    )
    for c in range(3):
        wait(loads[c])
        acc = None
        for b in range(4):
            w = rows_of([wins[c, o, h, pl.ds(b * hw, hw), :] for o in range(4) for h in (0, 1)])
            term = nt(gv[c, :, pl.ds(b * 256, 256)], w)
            acc = term if acc is None else acc + term
        gf[...] = acc if c == 0 else gf[...] + acc
    wait(rest)
    total = jnp.zeros((1, d), F32)
    for a in range(4):
        at = pl.ds(a * rows, rows)
        x = hidv[at, :]
        gfa = gf[at, :]
        n = lax.rsqrt(jnp.mean(x * x, axis=-1, keepdims=True) + EPS)
        g = gfa * gain[...]
        xn = x * n
        total = total + jnp.sum(gfa * xn, axis=0, keepdims=True)
        gh = cot[at, :].astype(F32) + n * (g - xn * (n * jnp.mean(g * x, axis=-1, keepdims=True)))
        ghid[at, :] = gh
        ga[at, :] = gh.astype(BF)
    ggain[...] = total
    stores += dma.start([(ghid, ghid_out)])
    wait(last)
    acc = None
    for j in range(3):
        term = nt(ga[:, pl.ds(j * 256, 256)], out_weight(wbuf, j))
        acc = term if acc is None else acc + term
    for i, gm in enumerate((gm0, gm1, gm2)):
        gmv[i] = acc[:, i * 256 : (i + 1) * 256].astype(BF)
        stores += dma.start([(gmv.at[i], gm)])
    for j in range(3):
        gw = tn(mx[...], ga[:, pl.ds(j * 256, 256)]).astype(BF)
        for o in range(4):
            gwo[o, pl.ds(j * sh, sh), :] = gw[o * sh : (o + 1) * sh]
        rows_j = pl.ds(j * sh, sh)
        stores += dma.start([(gwo.at[:, rows_j], gwo_out.at[:, rows_j])])
    wait(stores)


def out_kernel(ids, hid, gin, a0, a1, a2, *refs):
    packs = (refs[0:6], refs[6:12], refs[12:18])
    out, hidv, av, wb, sems = refs[18:]
    me, half = ids[0], ids[1]
    d = hid.shape[1]
    hw = d // 8
    rows = hid.shape[0] // 4
    dma = Copies(sems)
    loads = [
        dma.start(
            [(a, av.at[c])]
            + pack_copies(packs[c], me, half, wb.at[c], lambda ref: ref.at[pl.ds(4 * hw, 384)])
        )
        for c, a in enumerate((a0, a1, a2))
    ]
    last = dma.start([(hid, hidv)])
    grads = dma.start([(gin.at[pl.ds(b * rows, rows)], out.at[b, 1]) for b in range(4)])
    for c in range(3):
        wait(loads[c])
    wait(last)
    for j in range(3):
        cols = pl.ds(j * 256, 256)
        acc = hidv[:, cols]
        for c in range(3):
            w = rows_of([wb[c, o, h, pl.ds(j * 128, 128), :] for o in range(4) for h in (0, 1)])
            acc = acc + nn(av[c], w)
        acc = acc.astype(BF)
        for b in range(4):
            out[b, 0, :, cols] = acc[b * rows : (b + 1) * rows]
    wait(grads)


def diagonals(x):
    width = x.shape[1]
    y = x[0:8]
    for a in range(8, x.shape[0], 8):
        y = y + pltpu.roll(x[a : a + 8], width - a, 1)
    sub = lax.broadcasted_iota(jnp.int32, y.shape, 0)
    for bit in (1, 2, 4):
        y = jnp.where((sub & bit) != 0, pltpu.roll(y, width - bit, 1), y)
    return jnp.sum(y, axis=0, keepdims=True)


def attn_bwd_kernel(groups, carried, ids, nrm_in, *refs):
    ins, refs = refs[: 5 * groups], refs[5 * groups :]
    carry, refs = refs[:carried], refs[carried:]
    keep, send, *refs = refs
    outs, refs = refs[: 3 * groups], refs[3 * groups :]
    (diag, q, k, v, p, gm, nrm_t, dq, dk, dv, acc, stage, sems) = refs
    t = 128
    length = nrm_t.shape[1]
    nblk = length // t
    low, m0, m1 = half_masks(t)
    dma = Copies(sems)
    loads = []
    for n in range(groups):
        q_in, k_in, v_in, p_in, gm_in = ins[5 * n : 5 * n + 5]
        whole = [(v_in, v.at[n]), (gm_in, gm.at[n]), (k_in, k.at[n]), (q_in, q.at[n])]
        halves = [[(p_in.at[pl.ds(2 * i, 2)], p.at[pl.ds(4 * n + 2 * i, 2)])] for i in (0, 1)]
        loads += [dma.start(whole + halves[0]), dma.start(halves[1])]
        if n == 0:
            last = dma.start([(nrm_in, nrm_t)])
    base, half = 0, stage.shape[2]
    for g in carry:
        count = g.shape[1]
        inside = min(count, half - base) if base < half else 0
        if inside:
            last += dma.start([(g.at[:, pl.ds(0, inside)], stage.at[:, 0, pl.ds(base, inside)])])
        if inside < count:
            rest, at = count - inside, max(0, base - half)
            last += dma.start([(g.at[:, pl.ds(inside, rest)], stage.at[:, 1, pl.ds(at, rest)])])
        base += count
    sh = nrm_t.shape[0] // 4
    finished = lambda h: [
        Either(dma, stage, keep, send, ids, o, h, part) for o in range(4) for part in (0, 1)
    ]
    stores = []
    for n in range(groups):
        for pair in (0, 1):
            wait(loads[2 * n + pair])
            cols = pl.ds(pair * 128, 128)
            k2, v2 = k[n, :, cols], v[n, :, cols]
            dk_t = jnp.zeros((128, length), F32)
            dv_t = jnp.zeros((128, length), F32)
            for a in range(nblk):
                at = pl.ds(a * t, t)
                q2, g2 = q[n, at, cols], gm[n, at, cols]
                qm = rows_of([q2 * m0, q2 * m1])
                g_both = rows_of([g2 * m0, g2 * m1])
                dp = nt(g_both, v2)
                pb = rows_of([p[4 * n + 2 * pair, at, :], p[4 * n + 2 * pair + 1, at, :]])
                pf = pb.astype(F32)
                delta = jnp.sum(pf * dp, axis=-1, keepdims=True)
                ds = (pf * (dp - delta)).astype(BF)
                mq = nn(ds, k2)
                dq[n, at, cols] = jnp.where(low, mq[:t], mq[t:]).astype(BF)
                dk_t = dk_t + tn(qm, ds)
                dv_t = dv_t + tn(g_both, pb)
                dsf = ds.astype(F32)
                for h in (0, 1):
                    for b in range(nblk):
                        rel = b - a
                        place = rel + 1 if abs(rel) <= 1 else (3 if rel < 0 else 4)
                        tile = dsf[h * t : (h + 1) * t, b * t : (b + 1) * t]
                        lanes = pl.ds(place * t, t)
                        if (a, b) in ((1, 0), (0, 0), (0, 1), (2, 0), (0, 2)):
                            acc[h, :, lanes] = tile
                        else:
                            acc[h, :, lanes] += tile
            dk[n, :, cols] = dk_t.T.astype(BF)
            dv[n, :, cols] = dv_t.T.astype(BF)
            for h in (0, 1):
                near = jnp.concatenate([acc[h, :, pl.ds(0, 3 * t)], jnp.zeros((t, t), F32)], axis=1)
                far = jnp.sum(acc[h, :, pl.ds(3 * t, 2 * t)], axis=0, keepdims=True)
                diag[pl.ds(4 * n + 2 * pair + h, 1), :] = jnp.concatenate([diagonals(near), far], axis=1)
        stores += dma.start([(d.at[n], out) for d, out in zip((dq, dk, dv), outs[3 * n : 3 * n + 3])])
        if n == 0:
            wait(last)
        for i, g in enumerate((dq, dk, dv)):
            if base == half and i == 0:
                stores += finished(0)
            gw = nn(nrm_t[...], g[n]).astype(BF)
            for o in range(4):
                put(stage, o, base + i * sh, gw[o * sh : (o + 1) * sh])
        base += 3 * sh
    stores += finished(1)
    wait(stores)


def first_norm_kernel(ids, gain, xs, ghid, *refs):
    ins = refs[0:9]
    w0, w1 = refs[9:15], refs[15:21]
    gi, ggain, xv, gv, dall, wbuf0, wbuf1, gn, sems = refs[21:]
    me, half = ids[0], ids[1]
    d = xs.shape[1]
    rows = xs.shape[0] // 4
    dma = Copies(sems)
    loads = dma.start(
        [(g, dall.at[n]) for n, g in enumerate(ins)]
        + pack_copies(w0, me, half, wbuf0, lambda ref: ref)
        + pack_copies(w1, me, half, wbuf1, lambda ref: ref)
    )
    part = wbuf0.shape[2] // 3
    rest = dma.start([(xs, xv), (ghid, gv)])
    wait(loads)
    acc = None
    for i in range(3):
        for c in range(3):
            buf, at = (wbuf0, i) if c == 0 else (wbuf1, 3 * (c - 1) + i)
            wi = rows_of([buf[o, h, pl.ds(at * part, part), :] for o in range(4) for h in (0, 1)])
            term = nt(dall[3 * i + c], wi)
            acc = term if acc is None else acc + term
    gn[...] = acc
    wait(rest)
    total = jnp.zeros((1, d), F32)
    for a in range(4):
        at = pl.ds(a * rows, rows)
        x = xv[at, :].astype(F32)
        gf = gn[at, :]
        n = lax.rsqrt(jnp.mean(x * x, axis=-1, keepdims=True) + EPS)
        g = gf * gain[...]
        xn = x * n
        total = total + jnp.sum(gf * xn, axis=0, keepdims=True)
        gi[at, :] = (gv[at, :] + n * (g - xn * (n * jnp.mean(g * x, axis=-1, keepdims=True)))).astype(BF)
    ggain[...] = total


def tokens_kernel(ids, tokens, out, gin):
    out[...] = tokens[:, 0]
    gin[...] = tokens[:, 1].astype(F32)


def ff_shares_kernel(quad, thirds, starts, ids, *refs):
    ins, (out_in, out_back, buf, part_in, part_back, sems) = refs, refs[-6:]
    here, far = ids[1], ids[3]
    sh = out_in.shape[0]
    dma = Copies(sems)
    n = (2 * sh + 384) // 8
    copies = []
    for k in range(len(thirds)):
        pairs = []
        for m, h in ((2 * k, here), (2 * k + 1, 1 - here)):
            src = ins[m].at[pl.ds(starts[m], 8 * n)]
            if not quad:
                pairs.append((src, buf.at[k, h]))
                continue
            for p in (0, 1):
                for q, i in enumerate(Sum.ORDER):
                    row = pl.multiple_of(p * 4 * n + (far ^ i) * n, 16)
                    pairs.append((src.at[pl.ds((4 * p + q) * n, n)], buf.at[k, h, pl.ds(row, n)]))
        copies.append(dma.start(pairs))
    stores = []
    for m, k in enumerate(thirds):
        wait(copies[m])
        for b in range(4):
            part_in[m, :, pl.ds(b * 256, 256)] = buf[m, 0, pl.ds(b * sh, sh), :].astype(F32)
        stores += dma.start([
            (part_in.at[m, :, pl.ds(b * 256, 256)], out_in.at[:, pl.ds((b * 3 + k) * 256, 256)]) for b in range(4)
        ])
        for j in range(3):
            part_back[m, :, pl.ds(j * 256, 256)] = buf[m, 1, pl.ds(j * 256, 256), :].astype(F32)
        stores += dma.start([(part_back.at[m], out_back.at[pl.ds(k * 256, 256)])])
    wait(stores)


def attn_shares_kernel(plain, ids, *refs):
    ins, (wq, wk, wv, wo, buf, sems) = refs[:-6], refs[-6:]
    here, far = ids[1], ids[3]
    sh = wq.shape[0]
    pairs = []
    for m, h in ((0, here), (1, 1 - here)):
        if plain:
            pairs.append((ins[m], buf.at[h]))
            continue
        n = ins[m].shape[1]
        pairs += [(ins[m].at[i], buf.at[h, pl.ds(pl.multiple_of((far ^ i) * n, 16), n)]) for i in range(4)]
    wait(Copies(sems).start(pairs))
    at = lambda half, n: buf[half, pl.ds(n * sh, sh), :].astype(F32)
    for i in range(3):
        wo[:, pl.ds(i * 256, 256)] = at(0, i)
    for i, out in enumerate((wq, wk, wv)):
        out[:, pl.ds(0, 256)] = at(1, i)
        out[:, pl.ds(256, 256)] = at(0, 3 + i)
        out[:, pl.ds(512, 256)] = at(1, 3 + i)


def bucket_of(offset, bucket_count):
    distance = jnp.abs(offset)
    bucket = jnp.where(offset > 0, bucket_count // 2, 0).astype(jnp.int32)
    for edge in EDGES:
        bucket = bucket + (distance >= edge).astype(jnp.int32)
    return bucket


def shards(inputs, segments, gain_attn, w_query, w_key, w_value, w_out, bucket_bias_table, gain_ff, w_in, w_back, cotangent):
    seqs, rows, d = inputs.shape
    sh = w_query.shape[0]
    hw = sh // 2
    ffs = w_in.shape[1]
    bucket_count, heads = bucket_bias_table.shape
    length = rows * seqs
    places = [lax.axis_index(a).astype(jnp.int32) for a in ("near", "side", "core", "far")]
    near_at, side_at, core_at, far_at = places
    line = Line(jnp.stack([2 * side_at + core_at, near_at, core_at, far_at]))
    gate = line.gate
    row_low, row_f32 = sds((length, d), BF), sds((length, d), F32)
    quad_low, tok_low = sds((length, 256), BF), sds((rows, d), BF)
    gain1, gain2 = gain_attn.reshape(1, d), gain_ff.reshape(1, d)
    pack_rows = [4 * hw + 384 + 3 * hw, 4 * hw + 384, 4 * hw + 384]

    m0, m1, m2, m3, own_a, own_b, y_a, y_b = call(
        prep_a_kernel,
        "prep_a",
        [sds((rows + 16, d), BF)] * 4
        + [sds((2, 3 * hw, 256), BF), sds((2, 6 * hw, 256), BF), sds((3 * hw, 256), BF), sds((6 * hw, 256), BF)],
        [SM, VM] + [HBM] * 4,
        [VM] * 8,
        [DMA((31,))],
        (line.ids, segments, inputs, w_query, w_key, w_value),
    )
    wa = Gather(line, own_a, y_a)
    msgs = [swap(m1, "core"), swap(m2, "side"), swap(m3, "side", "core")]
    wb = Gather(line, own_b, y_b)

    own0, own1, own2, y0, y1, y2, k1, k2, k3 = call(
        prep_b_kernel,
        "prep_b",
        [sds((2, r, 256), BF) for r in pack_rows] + [sds((r, 256), BF) for r in pack_rows] + [tok_low] * 3,
        [SM] + [HBM] * 4,
        [VM] * 9,
        [DMA((75,))],
        (line.ids, w_in, w_back, w_out, cotangent),
    )

    (own0,) = gate(own0)
    wa.cross()
    *msgs, table_in = gate(*msgs, bucket_bias_table)
    wa.relay()

    offs = jnp.arange(4 * rows, dtype=jnp.int32)
    offs = jnp.where(offs < 3 * rows, offs - rows, offs - 5 * rows)
    hot = (bucket_of(offs, bucket_count)[None] == jnp.arange(bucket_count, dtype=jnp.int32)[:, None]).astype(F32)
    lines = jnp.einsum("up,uw->wp", hot, table_in, precision=lax.Precision.HIGHEST)

    y0, own0 = gate(y0, own0)
    wf = [Gather(line, own0, y0)]
    xs, nrm, nrm_t, seg = call(
        norm_kernel,
        "norm",
        [row_low, row_low, sds((d, length), BF), sds((1, length), F32)],
        [SM] + [HBM] * 4 + [VM],
        [VM] * 4,
        [scratch((64, d)), DMA((8,))],
        (line.ids, m0, *msgs, gain1),
    )
    nrm, lines = gate(nrm, lines)
    wb.cross()
    wa = wa.done()

    qs, ks, vs, probs, mixed = [], [], [], [], []
    for g in range(3):
        q, k, v, p, mx = call(
            functools.partial(attn_fwd_kernel, g),
            "attn_fwd",
            [quad_low] * 3 + [sds((4, length, length), BF), quad_low],
            [SM, SM, VM, VM] + [HBM] * 7,
            [HBM] * 4 + [VM],
            [
                scratch((4, rows, 3 * rows), F32),
                scratch((length, d)),
                scratch((4, 2, 3 * hw, 256)),
                scratch((length, 256)),
                scratch((length, 256)),
                scratch((length, 256)),
                scratch((4, length, length)),
                DMA((15,)),
            ],
            (line.ids, table_in, seg, lines, nrm, *(wa if g == 0 else wb)),
        )
        (mx,) = gate(mx)
        for have, new in ((qs, q), (ks, k), (vs, v), (probs, p), (mixed, mx)):
            have.append(new)
        if g == 0:
            wb.relay()
            wf[0].cross()
            own1, y1 = gate(own1, y1)
            wf.append(Gather(line, own1, y1))
            wb = wb.done()
        if g == 1:
            wf[0].relay()
            wf[1].cross()
            k1, k2, k3 = gate(k1, k2, k3)
            cots = [swap(k1, "core"), swap(k2, "side"), swap(k3, "side", "core")]
    packs = [wf[0].done()]
    cots = gate(*cots)
    wf[1].relay()
    own2, y2 = gate(own2, y2)
    wf.append(Gather(line, own2, y2))

    sums_f, acts, gpres = [], [], []
    for c in range(3):
        lead = c == 0
        *fresh, act, gpre, keep, send = call(
            functools.partial(ffn_kernel, lead),
            "ffn",
            ([row_f32, row_low, sds((d, length), BF)] if lead else [])
            + [sds((length, 1024), BF)] * 2
            + piece_shapes(4 * sh + 768),
            [SM] + ([VM] + [HBM] * 4 if lead else [HBM] * 2) + [HBM] * 10,
            [HBM] * (7 if lead else 4),
            (
                [scratch((length, d)), scratch((length, d)), scratch((4, 2, 3 * hw, 256)), scratch((length, d), F32)]
                if lead
                else []
            )
            + [
                scratch((length, d)),
                scratch((d, length)),
                scratch((length, d)),
                scratch((4, 2, 4 * hw + 384, 256)),
                scratch((length, 1024)),
                scratch((length, 1024)),
                scratch((4, 2, 2 * sh + 384, 256)),
                DMA((60,)),
            ],
            (line.ids, *((gain2, xs, *mixed) if lead else (ff, ff_t)), cotangent, *cots, *packs[c]),
        )
        if lead:
            hid, ff, ff_t = fresh
        piece = (keep, send)
        acts.append(act)
        (gpre,) = gate(gpre)
        gpres.append(gpre)
        if c == 0:
            packs.append(wf[1].done())
            wf[2].cross()
        if c == 1:
            wf[2].relay()
        moves = [[], [("first",)], [("second",), ("first",)]][c]
        sums_f.append(advance(line, *[(f, *m) for f, m in zip(sums_f, moves)], new=piece))
        if c == 1:
            packs.append(wf[2].done())

    ghid, *gmix, ggain_ff, gwo = call(
        after_ff_kernel,
        "after_ff",
        [row_f32] + [quad_low] * 3 + [sds((1, d), F32), sds((4, 3 * sh, 256), BF)],
        [SM, VM] + [HBM] * 29,
        [HBM] * 4 + [VM, HBM],
        [
            scratch((length, d), F32),
            scratch((3, length, 1024)),
            scratch((length, d)),
            scratch((length, d)),
            scratch((4, 2, 3 * hw, 256)),
            scratch((3, 4, 2, 4 * hw, 256)),
            scratch((length, d)),
            scratch((length, d), F32),
            scratch((length, d), F32),
            scratch((3, length, 256)),
            scratch((4, 3 * sh, 256)),
            DMA((52,)),
        ],
        (line.ids, gain2, hid, *gpres, cotangent, *cots, *mixed, *packs[0], *packs[1], *packs[2]),
    )
    gmix[0], ggain_ff = gate(gmix[0], ggain_ff)
    quad = lax.axis_size("far") == 4
    third = "spread" if quad else "third"
    far_steps = lambda *steps: steps if quad else ()
    advance(line, (sums_f[0], third), (sums_f[1], "second"), (sums_f[2], "first"))

    dqs, dks, dvs, diags, sums_a = [], [], [], [], []
    for first, groups in ((0, 1), (1, 2)):
        carry = (gwo,) if first == 0 else ()
        body = 3 * sh * (groups + len(carry))
        some = range(first, first + groups)
        keep, send, *grads, diag = call(
            functools.partial(attn_bwd_kernel, groups, len(carry)),
            "attn_bwd",
            piece_shapes(body) + [quad_low] * (3 * groups) + [sds((4 * groups, 6 * rows), F32)],
            [SM] + [HBM] * (1 + 5 * groups + len(carry)),
            [HBM] * (2 + 3 * groups) + [VM],
            [scratch((groups, length, 256))] * 3
            + [scratch((4 * groups, length, length)), scratch((groups, length, 256)), scratch((d, length))]
            + [scratch((groups, length, 256))] * 3
            + [scratch((2, rows, 5 * rows), F32), scratch((4, 2, body // 2, 256)), DMA((48,))],
            (line.ids, nrm_t, *[a for g in some for a in (qs[g], ks[g], vs[g], probs[g], gmix[g])], *carry),
            us=10 * groups,
        )
        (grads[0],) = gate(grads[0])
        for n in range(groups):
            for have, new in zip((dqs, dks, dvs), grads[3 * n : 3 * n + 3]):
                have.append(new)
        diags.append(diag)
        if first == 0:
            steps = ((sums_f[1], third), (sums_f[2], "second"), *far_steps((sums_f[0], "pair")))
        else:
            steps = ((sums_a[0], "first"), (sums_f[2], third))
            steps += far_steps((sums_f[0], "back"), (sums_f[1], "pair"))
        sums_a.append(advance(line, *steps, new=(keep, send)))

    gin, ggain_attn = call(
        first_norm_kernel,
        "first_norm",
        [row_low, sds((1, d), F32)],
        [SM, VM] + [HBM] * 23,
        [VM] * 2,
        [
            scratch((length, d)),
            scratch((length, d), F32),
            scratch((9, length, 256)),
            scratch((4, 2, 3 * hw, 256)),
            scratch((4, 2, 6 * hw, 256)),
            scratch((length, d), F32),
            DMA((27,)),
        ],
        (line.ids, gain1, xs, ghid, *dqs, *dks, *dvs, *wa, *wb),
    )
    gin, ggain_attn = gate(gin, ggain_attn)
    steps = far_steps((sums_f[0], "last"), (sums_f[1], "back"), (sums_f[2], "pair"))
    advance(line, (sums_a[1], "first"), (sums_a[0], "second"), *steps)
    (tokens,) = call(
        out_kernel,
        "out",
        [sds((seqs, 2, rows, d), BF)],
        [SM] + [HBM] * 23,
        [VM],
        [
            scratch((length, d), F32),
            scratch((3, length, 1024)),
            scratch((3, 4, 2, 384, 256)),
            DMA((32,)),
        ],
        (line.ids, hid, gin, *acts, *packs[0], *packs[1], *packs[2]),
    )
    tokens, ggain_attn = gate(tokens, ggain_attn)
    steps = far_steps((sums_f[0], "finish"), (sums_f[1], "last"), (sums_f[2], "back"))
    advance(line, (sums_a[1], "second"), (sums_a[0], "third"), *steps)
    first_total = sums_a[0].buffer


    hot6 = jnp.concatenate(
        [
            hot,
            jnp.zeros((bucket_count, rows), F32).at[bucket_count // 2 - 1].set(1.0),
            jnp.zeros((bucket_count, rows), F32).at[bucket_count - 1].set(1.0),
        ],
        axis=1,
    )
    table = jnp.einsum("up,wp->uw", hot6, jnp.concatenate(diags, axis=0), precision=lax.Precision.HIGHEST)
    small = jnp.concatenate([ggain_attn.reshape(-1), ggain_ff.reshape(-1), table.reshape(-1)])
    tokens = lax.all_to_all(tokens, ("side", "core"), 0, 0, tiled=True)
    advance(line, (sums_a[1], "third"), *far_steps((sums_f[1], "finish"), (sums_f[2], "last")))
    far_c = FarSum([first_total, sums_a[1].buffer])

    sums_f[1].land(line)
    far_c.land(line)
    far_c.back()
    if quad:
        advance(line, (sums_f[2], "finish"))
    else:
        for f in sums_f:
            whole = lax.psum(f.buffer, "far")
            f.buffer, f.flying = whole, {0: (swap(whole, "near"), ())}
    (small,) = gate(small)
    small = small + swap(small, "core")

    def ff_shares(thirds, have):
        parts, starts = [], []
        for f in [sums_f[k] for k in thirds]:
            arr, at = next(iter(f.flying.values()))
            parts += [f.buffer, *gate(arr)]
            starts += [0, at[0].start if at else 0]
        n = len(thirds)
        return call(
            functools.partial(ff_shares_kernel, quad, thirds, starts),
            "ff_shares",
            [sds((sh, ffs), F32), sds(w_back.shape, F32)],
            [SM] + [HBM] * (2 * n + len(have)),
            [HBM] * 2,
            [
                scratch((n, 2, 2 * sh + 384, 256)),
                scratch((n, sh, 1024), F32),
                scratch((n, 256, d), F32),
                DMA((21 * n,)),
            ],
            (line.ids, *parts, *have),
            aliases={1 + 2 * n + i: i for i in range(len(have))},
            us=1,
        )

    shares = gate(*ff_shares((0, 1), ()))
    sums_f[2].land(line)
    far_c.land(line)
    far_c.finish(line)
    (small,) = gate(small)
    small = small + swap(small, "side")
    tokens, small = gate(tokens, small)
    small = small + swap_far(small, 1) if quad else lax.psum(small, "far")
    output, grad_inputs = call(
        tokens_kernel,
        "tokens",
        [sds((seqs, rows, d), BF), sds((seqs, rows, d), F32)],
        [SM, VM],
        [VM] * 2,
        [],
        (line.ids, tokens),
        us=1,
    )
    output, small = gate(output, small)
    if quad:
        small = small + swap_far(small, 2)
    share_in, share_back = gate(*ff_shares((2,), shares))
    *shares_c, small = gate(*far_c.result, small)
    small = small + swap(small, "near")
    share_q, share_k, share_v, share_o = call(
        functools.partial(attn_shares_kernel, far_c.plain),
        "attn_shares",
        [sds((sh, d), F32)] * 4,
        [SM] + [HBM] * len(shares_c),
        [VM] * 4,
        [scratch((2, 6 * sh, 256)), DMA((8,))],
        (line.ids, *shares_c),
        us=1,
    )
    total_gain_attn, total_gain_ff = small[:d], small[d : 2 * d]
    total_table = small[2 * d :].reshape(bucket_count, heads)


    return (
        output,
        grad_inputs,
        total_gain_attn,
        share_q,
        share_k,
        share_v,
        share_o,
        total_table,
        total_gain_ff,
        share_in,
        share_back,
    )


def solution(mesh):
    far = mesh.shape["rows"] // 2
    inner = jax.sharding.Mesh(mesh.devices.reshape(far, 2, 2, 2), AXES)
    over_rows, over_blk = ("far", "near"), ("side", "core")
    tok, row, rep = P(over_rows, over_blk, None), P(over_blk, None), P()
    return jax.shard_map(
        shards,
        mesh=inner,
        in_specs=(tok, P(over_rows, over_blk), rep, row, row, row, row, rep, rep, row, row, tok),
        out_specs=(tok, tok, rep, row, row, row, row, rep, rep, row, row),
        check_vma=False,
    )
```
